32 devices in a mesh: ctx: 8 (over z, y), ws: 4 (over x, core).
Axes of the slice: x: 2, y: 2, z: 4, core: 2. Of those that a mesh axis runs over, the one named last changes fastest.
Arguments:
- inputs: bfloat16 [4, 1024, 2048], P('ws', 'ctx'), may hold values from -6 to 6
- grad_output: bfloat16 [4, 1024, 2048], P('ws', 'ctx'), may hold values from -6 to 6
- routes: int32 [4, 1024, 8], P('ws', 'ctx'), may hold values from 0 to 31, all different within a row; in each aligned block of 128 rows (0 to 127, 128 to 255, ..., all dimensions but the last counted through in order) at most 48 rows name the same one
- doc_lengths: int32 [4, 4], P('ws'), may hold values from 32 to 576, as said below
- norm_attn: bfloat16 [2048], P(('ctx', 'ws')), may hold values from 0.099609375 to 1.8984375
- w_query: bfloat16 [2048, 4096], P(('ctx', 'ws')), may hold values from -0.125 to 0.125
- key_projection: bfloat16 [2048, 512], P(('ctx', 'ws')), may hold values from -0.125 to 0.125
- value_projection: bfloat16 [2048, 512], P(('ctx', 'ws')), may hold values from -0.125 to 0.125
- query_norm: bfloat16 [128], P(('ctx', 'ws')), may hold values from 0.099609375 to 1.8984375
- key_norm: bfloat16 [128], P(('ctx', 'ws')), may hold values from 0.099609375 to 1.8984375
- w_out: bfloat16 [4096, 2048], P(('ctx', 'ws')), may hold values from -0.5 to 0.5
- norm_ffn: bfloat16 [2048], P(('ctx', 'ws')), may hold values from 0.099609375 to 1.8984375
- w_router: bfloat16 [2048, 32], P(('ctx', 'ws')), may hold values from -0.0625 to 0.0625
- expert_gate: bfloat16 [32, 2048, 768], P(('ctx', 'ws')), may hold values from -0.125 to 0.125
- expert_up: bfloat16 [32, 2048, 768], P(('ctx', 'ws')), may hold values from -0.125 to 0.125
- expert_down: bfloat16 [32, 768, 2048], P(('ctx', 'ws')), may hold values from -1.25 to 1.25
Outputs:
- output: bfloat16 [4, 1024, 2048], P('ws', 'ctx')
- grad_input: float32 [4, 1024, 2048], P('ws', 'ctx')
- grad_norm_attn: float32 [2048], P(('ctx', 'ws'))
- grad_w_query: float32 [2048, 4096], P(('ctx', 'ws'))
- grad_w_key: float32 [2048, 512], P(('ctx', 'ws'))
- grad_w_value: float32 [2048, 512], P(('ctx', 'ws'))
- grad_query_norm: float32 [128], P(('ctx', 'ws'))
- grad_key_norm: float32 [128], P(('ctx', 'ws'))
- grad_w_out: float32 [4096, 2048], P(('ctx', 'ws'))
- grad_norm_ffn: float32 [2048], P(('ctx', 'ws'))
- grad_w_router: float32 [2048, 32], P(('ctx', 'ws'))
- grad_expert_gate: float32 [32, 2048, 768], P(('ctx', 'ws'))
- grad_expert_up: float32 [32, 2048, 768], P(('ctx', 'ws'))
- grad_expert_down: float32 [32, 768, 2048], P(('ctx', 'ws'))
The draws below stay inside these ranges and needn't reach their ends.
Inputs may be any that keep to these rules, and one draw needn't show every extreme that they name: `routes`: each row names 8 different experts. Among the rows of one device no expert is named more than 48 times, and in every draw some expert is named exactly 48 times there. `doc_lengths`: the first document of each sequence has between 513 and 576 tokens, the others between 32 and 128; rows whose place lies past the sum are padding.
All inputs are finite; a program needn't handle non-finite values.
Results may differ from the reference program's by a relative error of at most 0.025.
Values may be sent and summed in bfloat16 or wider, within the bound.
A program may use at most 256 MiB of HBM per device.

```python
import math
from functools import partial
import jax
import jax.numpy as jnp
import numpy as np
from jax import lax

MODEL_DIM = 2048
QUERY_HEADS = 32
KEY_VALUE_HEADS = 4
HEAD_DIM = 128
FF = 768
TOPK = 8
NDOC = 4
TOK_DEV = 128
HALF = 64
SEQUENCE_LENGTH = 1024
SEQUENCE_COUNT = 4
EXPERTS = 32
CAP = 48
DOC_HI = 128
DOC_LO = 32
N_CTX = 8
N_WS = 4


def draw_doc_lengths(key, part):
    key = jax.random.fold_in(key, 11)
    first_key, rest_key, pick_key = jax.random.split(key, 3)
    longest = SEQUENCE_LENGTH // 2 + HALF - jax.random.randint(first_key, (SEQUENCE_COUNT, 1), 0, HALF)
    others = jax.random.randint(rest_key, (SEQUENCE_COUNT, NDOC - 1), DOC_LO, DOC_HI + 1)
    chosen = jax.random.randint(pick_key, (), 0, SEQUENCE_COUNT)
    row_index = jnp.arange(SEQUENCE_COUNT)[:, None]
    column_index = jnp.arange(NDOC - 1)[None, :]
    longest = jnp.where(row_index == chosen, SEQUENCE_LENGTH // 2 + HALF, longest)
    others = jnp.where((row_index == chosen) & (column_index == 0), DOC_LO, others)
    return jnp.concatenate([longest, others], axis=1).astype(jnp.int32)


def block_levels(own_key, dims, cuts, least, top_value):
    gain, own = 1.0, jax.random.fold_in(own_key, 6)
    for dim, blocks in cuts:
        heights = jnp.exp(jax.random.uniform(jax.random.fold_in(own, dim), (blocks,), jnp.float32, least / len(cuts), top_value / len(cuts)))
        gain = gain * jnp.repeat(heights, dims[dim] // blocks).reshape([-1 if axis == dim else 1 for axis in range(len(dims))])
    return gain


def deal_out(rng, own, number, rows, amount, top, reach, slope):
    sequence = jax.random.permutation(rng, amount)
    crowded, usual = portions_of(amount, rows * top, reach, slope, True), portions_of(amount, rows * top, reach, slope, False)
    places = jnp.arange(amount)

    def named(lengths, turn):
        used = int((lengths > 0).sum())
        fixed = max(1, used // 4)
        moved = fixed + (places - fixed + turn * (used - fixed)) % max(1, amount - fixed)
        return jnp.zeros((amount,), jnp.int32).at[sequence[jnp.where(places < fixed, places, moved)]].set(jnp.asarray(lengths, jnp.int32))

    lengths = jnp.where(number % 4 == 0, named(crowded, number // 4), named(usual, number - number // 4 - 1))
    mixed = jax.random.permutation(jax.random.fold_in(own, 3), amount)
    donor, sink = mixed[0:amount // 2 * 2:2], mixed[1:amount // 2 * 2:2]
    room = jnp.minimum(lengths[donor] - 1, reach - lengths[sink]) // 2
    room = jnp.where((donor == sequence[0]) | (sink == sequence[0]) | (lengths[sink] == 0), 0, jnp.maximum(room, 0))
    moved = jax.random.randint(jax.random.fold_in(own, 4), (amount // 2,), 0, 1 << 20) % (room + 1)
    lengths = lengths.at[donor].add(-moved).at[sink].add(moved)
    members = jnp.searchsorted(jnp.cumsum(lengths), jnp.arange(rows * top), side="right").astype(jnp.int32)
    grid = members.reshape(top, rows).T
    grid = grid[jax.random.permutation(jax.random.fold_in(own, 1), rows)]
    turn = jax.random.randint(jax.random.fold_in(own, 2), (rows, 1), 0, top)
    return jnp.take_along_axis(grid, (jnp.arange(top)[None, :] + turn) % top, axis=1)


def portions_of(amount, total, bound, slope, full):
    portions = [(1 << 20) // math.isqrt(standing ** slope) + 1 for standing in range(1, amount + 1)]
    largest = bound if full else min(bound, max(-(-total // amount), total * portions[0] // sum(portions)))
    least = 1 if total - largest >= amount - 1 else 0
    counts, rest = [largest] + [least] * (amount - 1), total - largest - least * (amount - 1)
    while rest > 0:
        movable = [i for i in range(1, amount) if counts[i] < largest] or [i for i in range(1, amount) if counts[i] < bound]
        mass, left = sum([portions[i] for i in movable]), rest
        for i in movable:
            more = min(bound - counts[i], max(1, left * portions[i] // mass), rest)
            counts[i] = counts[i] + more
            rest = rest - more
    return np.array(counts)


def scatter_about(rng, shape, width, limit, cuts=(), held_as=jnp.bfloat16):
    values = width * jax.random.normal(rng, shape, jnp.float32)
    if cuts:
        values = values * block_levels(rng, shape, cuts, -0.22, 0.18)
    return jnp.clip(values, -limit, limit).astype(held_as)


def setup_inputs(seed: int = 0) -> dict:
    keys = jax.random.split(jax.random.key(seed), 17)
    inputs = scatter_about(keys[0], (SEQUENCE_COUNT, SEQUENCE_LENGTH, MODEL_DIM), 1.0, 6.0, ((0, 4), (1, 8)))
    grad_output = scatter_about(keys[1], (SEQUENCE_COUNT, SEQUENCE_LENGTH, MODEL_DIM), 1.0, 6.0, ((0, 4), (1, 8)))
    routes_keys = jax.random.split(jax.random.fold_in(keys[2], 1), SEQUENCE_COUNT * SEQUENCE_LENGTH // TOK_DEV)
    routes_turns = jax.random.permutation(jax.random.fold_in(keys[2], 3), SEQUENCE_COUNT * SEQUENCE_LENGTH // TOK_DEV)
    routes = jax.vmap(lambda own, number: deal_out(jax.random.fold_in(keys[2], 2), own, number, TOK_DEV, EXPERTS, TOPK, CAP, 1))(routes_keys, routes_turns).reshape((SEQUENCE_COUNT, SEQUENCE_LENGTH, TOPK))
    doc_lengths = draw_doc_lengths(jax.random.fold_in(keys[16], 71), 0)
    norm_attn = jnp.clip(1.0 + 0.18 * jax.random.normal(keys[4], (MODEL_DIM,), jnp.float32), 0.099609375, 1.8984375).astype(jnp.bfloat16)
    w_query = scatter_about(keys[5], (MODEL_DIM, QUERY_HEADS * HEAD_DIM), MODEL_DIM ** -0.5, 0.125, ((0, 32),))
    key_projection = scatter_about(keys[6], (MODEL_DIM, KEY_VALUE_HEADS * HEAD_DIM), MODEL_DIM ** -0.5, 0.125, ((0, 32),))
    value_projection = scatter_about(keys[7], (MODEL_DIM, KEY_VALUE_HEADS * HEAD_DIM), MODEL_DIM ** -0.5, 0.125, ((0, 32),))
    query_norm = jnp.clip(1.0 + 0.18 * jax.random.normal(keys[8], (HEAD_DIM,), jnp.float32), 0.099609375, 1.8984375).astype(jnp.bfloat16)
    key_norm = jnp.clip(1.0 + 0.18 * jax.random.normal(keys[9], (HEAD_DIM,), jnp.float32), 0.099609375, 1.8984375).astype(jnp.bfloat16)
    w_out = scatter_about(keys[10], (QUERY_HEADS * HEAD_DIM, MODEL_DIM), (QUERY_HEADS * HEAD_DIM // 32) ** -0.5, 0.5, ((0, 32),))
    norm_ffn = jnp.clip(1.0 + 0.18 * jax.random.normal(keys[11], (MODEL_DIM,), jnp.float32), 0.099609375, 1.8984375).astype(jnp.bfloat16)
    w_router = scatter_about(keys[12], (MODEL_DIM, EXPERTS), (4 * MODEL_DIM) ** -0.5, 0.0625, ((0, 32),))
    expert_gate = scatter_about(keys[13], (EXPERTS, MODEL_DIM, FF), MODEL_DIM ** -0.5, 0.125, ((0, 32),))
    expert_up = scatter_about(keys[14], (EXPERTS, MODEL_DIM, FF), MODEL_DIM ** -0.5, 0.125, ((0, 32),))
    expert_down = scatter_about(keys[15], (EXPERTS, FF, MODEL_DIM), (FF // 32) ** -0.5, 1.25, ((0, 32),))
    return dict(inputs=inputs, grad_output=grad_output, routes=routes, doc_lengths=doc_lengths, norm_attn=norm_attn, w_query=w_query, key_projection=key_projection, value_projection=value_projection, query_norm=query_norm, key_norm=key_norm, w_out=w_out, norm_ffn=norm_ffn, w_router=w_router, expert_gate=expert_gate, expert_up=expert_up, expert_down=expert_down)


EPS = 1e-06
THETA = 1000000.0
MASK_FILL = -1e+30
TOP_PRECISION = lax.Precision.HIGHEST

@jax.custom_vjp
def lowered_precision(v):
    return lax.optimization_barrier(v.astype(jnp.bfloat16)).astype(jnp.float32)

@jax.custom_vjp
def lowered_backward(v):
    return v

def low_keep(v):
    return (lowered_precision(v), None)

def low_pass(kept, grad):
    return (grad,)

def back_keep(v):
    return (v, None)

def back_low(kept, grad):
    return (lowered_precision(grad),)
lowered_precision.defvjp(low_keep, low_pass)
lowered_backward.defvjp(back_keep, back_low)

def rms_scale(values, norm_gain):
    return values * lax.rsqrt(lax.optimization_barrier(jnp.mean(values * values, axis=-1, keepdims=True)) + EPS) * norm_gain

def rotate(values, positions):
    half_dim = values.shape[-1] // 2
    frequency = THETA ** (-2.0 * jnp.arange(half_dim, dtype=jnp.float32) / values.shape[-1])
    angle = positions.astype(jnp.float32)[:, None] * frequency[None, :]
    cosine = jnp.cos(angle)[:, None, :]
    sine_part = jnp.sin(angle)[:, None, :]
    first_half = values[..., :half_dim]
    second_half = values[..., half_dim:]
    return jnp.concatenate([first_half * cosine - second_half * sine_part, second_half * cosine + first_half * sine_part], axis=-1)

def head_prepare(raw_heads, norm_gain, positions):
    return rotate(rms_scale(raw_heads, norm_gain), positions)

def stored_positions(row_index, tokens_per_shard, ctx_count):
    device_row = row_index // tokens_per_shard
    within = row_index % tokens_per_shard
    half_block = tokens_per_shard // 2
    block_index = jnp.where(within < half_block, device_row, 2 * ctx_count - 1 - device_row)
    return block_index * half_block + within % half_block

def segment_ids(doc_lengths, positions):
    doc_ends = jnp.cumsum(doc_lengths, dtype=jnp.int32)
    return lax.optimization_barrier(jnp.sum((positions[:, None] >= doc_ends[None, :]).astype(jnp.int32), axis=1, dtype=jnp.int32))

def slot_ranks(flat_routes, expert_count):
    expert_hits = (flat_routes[:, None] == jnp.arange(expert_count, dtype=jnp.int32)[None, :]).astype(jnp.int32)
    running = jnp.cumsum(expert_hits, axis=0, dtype=jnp.int32) - 1
    return lax.optimization_barrier(jnp.sum(expert_hits * running, axis=1, dtype=jnp.int32))

def route_tables(routes):
    device_count = N_CTX * N_WS
    per_device = routes.reshape(SEQUENCE_COUNT, N_CTX, TOK_DEV * TOPK).astype(jnp.int32)
    slot_rank = jax.vmap(jax.vmap(partial(slot_ranks, expert_count=EXPERTS)))(per_device)
    owner_device = jnp.arange(N_CTX, dtype=jnp.int32)[None, :] * N_WS + jnp.arange(SEQUENCE_COUNT, dtype=jnp.int32)[:, None]
    slot_index = ((per_device * device_count + owner_device[:, :, None]) * CAP + slot_rank).reshape(-1)
    entries = SEQUENCE_COUNT * SEQUENCE_LENGTH * TOPK
    slot_table = jnp.full((EXPERTS * device_count * CAP,), entries, jnp.int32).at[slot_index].set(jnp.arange(entries, dtype=jnp.int32))
    return (slot_table, slot_index)

def reference(inputs, grad_output, routes, doc_lengths, norm_attn, w_query, key_projection, value_projection, query_norm, key_norm, w_out, norm_ffn, w_router, expert_gate, expert_up, expert_down):
    positions = stored_positions(jnp.arange(SEQUENCE_LENGTH, dtype=jnp.int32), TOK_DEV, N_CTX)
    segments = jax.vmap(segment_ids, in_axes=(0, None))(doc_lengths, positions)
    validity = (segments < NDOC).astype(jnp.float32)
    slot_table, slot_index = route_tables(routes)
    query_group_size = QUERY_HEADS // KEY_VALUE_HEADS
    logit_scale = HEAD_DIM ** (-0.5)

    def attend(pieces):
        query_rows, key_heads, values, segment_row = pieces
        grouped_queries = query_rows.reshape(SEQUENCE_LENGTH, KEY_VALUE_HEADS, query_group_size, HEAD_DIM)
        scores = lowered_backward(jnp.einsum('tkgd,jkd->kgtj', grouped_queries, key_heads, precision=TOP_PRECISION) * logit_scale)
        allowed = (segment_row[:, None] == segment_row[None, :]) & (positions[None, :] <= positions[:, None])
        scores = jnp.where(allowed[None, None], scores, MASK_FILL)
        exponent = jnp.exp(scores - lax.optimization_barrier(jnp.max(scores, axis=-1, keepdims=True)))
        softmaxed = lowered_precision(exponent / lax.optimization_barrier(jnp.sum(exponent, axis=-1, keepdims=True)))
        attended = jnp.einsum('kgtj,jkd->tkgd', softmaxed, values, precision=TOP_PRECISION)
        return lowered_precision(lowered_backward(attended.reshape(SEQUENCE_LENGTH, QUERY_HEADS * HEAD_DIM)))

    def expert(pieces):
        rows_in, gate_matrix, up_matrix, down_matrix = pieces
        gate_hidden = lowered_backward(jnp.dot(rows_in, gate_matrix, precision=TOP_PRECISION, preferred_element_type=jnp.float32))
        up_hidden = lowered_backward(jnp.dot(rows_in, up_matrix, precision=TOP_PRECISION, preferred_element_type=jnp.float32))
        hidden = lowered_precision(jax.nn.silu(gate_hidden) * up_hidden)
        return lowered_precision(lowered_backward(jnp.dot(hidden, down_matrix, precision=TOP_PRECISION, preferred_element_type=jnp.float32)))

    def forward(layer_in, attn_gain, query_matrix, key_matrix, value_matrix, query_gain, key_norm_gain, output_matrix, ffn_gain, router_matrix, gate_weights, up_weights, down_weights):
        normalized_rows = lowered_precision(rms_scale(layer_in, attn_gain))
        unnormed_queries = lowered_backward(jnp.einsum('mpt,tr->mpr', normalized_rows, query_matrix, precision=TOP_PRECISION)).reshape(SEQUENCE_COUNT, SEQUENCE_LENGTH, QUERY_HEADS, HEAD_DIM)
        unnormed_keys = lowered_backward(jnp.einsum('mpt,tr->mpr', normalized_rows, key_matrix, precision=TOP_PRECISION)).reshape(SEQUENCE_COUNT, SEQUENCE_LENGTH, KEY_VALUE_HEADS, HEAD_DIM)
        value_head_rows = lowered_precision(lowered_backward(jnp.einsum('mpt,tr->mpr', normalized_rows, value_matrix, precision=TOP_PRECISION))).reshape(SEQUENCE_COUNT, SEQUENCE_LENGTH, KEY_VALUE_HEADS, HEAD_DIM)
        query_rows = lowered_precision(head_prepare(unnormed_queries, query_gain, positions))
        key_heads = lowered_precision(head_prepare(unnormed_keys, key_norm_gain, positions))
        attention_result = lax.map(jax.checkpoint(attend), (query_rows, key_heads, value_head_rows, segments))
        branch_choice = lowered_backward(jnp.einsum('ehk,ko->eho', attention_result, output_matrix, precision=TOP_PRECISION))
        hidden_state = layer_in + branch_choice
        combined_rows = lowered_precision(rms_scale(hidden_state, ffn_gain))
        router_scores = lowered_backward(jnp.einsum('coy,yz->coz', combined_rows, router_matrix, precision=TOP_PRECISION))
        chosen = jnp.take_along_axis(router_scores, routes, axis=-1)
        exponent = jnp.exp(chosen - lax.optimization_barrier(jnp.max(chosen, axis=-1, keepdims=True)))
        gate_share = exponent / lax.optimization_barrier(jnp.sum(exponent, axis=-1, keepdims=True))
        copies = lowered_backward(jnp.broadcast_to(combined_rows[:, :, None, :], (SEQUENCE_COUNT, SEQUENCE_LENGTH, TOPK, MODEL_DIM)).reshape(SEQUENCE_COUNT * SEQUENCE_LENGTH * TOPK, MODEL_DIM))
        padded = jnp.concatenate([copies, jnp.zeros((1, MODEL_DIM), jnp.float32)], axis=0)
        expert_rows = padded[slot_table].reshape(EXPERTS, N_CTX * N_WS * CAP, MODEL_DIM)
        expert_outs = lax.map(jax.checkpoint(expert), (expert_rows, gate_weights, up_weights, down_weights))
        picked = expert_outs.reshape(-1, MODEL_DIM)[slot_index].reshape(SEQUENCE_COUNT, SEQUENCE_LENGTH, TOPK, MODEL_DIM)
        return hidden_state + lax.optimization_barrier(jnp.sum(gate_share[..., None] * picked, axis=2))
    arrays = tuple((argument.astype(jnp.float32) for argument in (inputs, norm_attn, w_query, key_projection, value_projection, query_norm, key_norm, w_out, norm_ffn, w_router, expert_gate, expert_up, expert_down)))
    result, backward = jax.vjp(forward, *arrays)
    cotangent = grad_output.astype(jnp.float32) * validity[..., None]
    gradients = backward(cotangent)
    return (result.astype(jnp.bfloat16), gradients[0], gradients[1], gradients[2], gradients[3], gradients[4], gradients[5], gradients[6], gradients[7], gradients[8], gradients[9], gradients[10], gradients[11], gradients[12])
```

```python
import jax
import jax.numpy as jnp
from jax import lax
from jax.experimental import pallas as pl
from jax.experimental.pallas import tpu as pltpu
from jax.sharding import PartitionSpec as P

QUERY_HEADS = 32
KEY_VALUE_HEADS = 4
HEAD_DIM = 128
TOPK = 8


EPS = 1e-06
THETA = 1000000.0
MASK_FILL = -1e30
TOP_PRECISION = lax.Precision.HIGHEST
SINGLE_FLOAT = jnp.float32
BRAIN_FLOAT_TYPE = jnp.bfloat16


def rms_scale(values, norm_gain):
    return values * lax.rsqrt(jnp.mean(values * values, axis=-1, keepdims=True) + EPS) * norm_gain


def rotate(values, positions):
    half_dim = values.shape[-1] // 2
    frequency = THETA ** (-2.0 * jnp.arange(half_dim, dtype=jnp.float32) / values.shape[-1])
    angle = positions.astype(jnp.float32)[:, None] * frequency[None, :]
    cosine = jnp.cos(angle)[:, None, :]
    sine_part = jnp.sin(angle)[:, None, :]
    first_half = values[..., :half_dim]
    second_half = values[..., half_dim:]
    return jnp.concatenate(
        [
            first_half * cosine - second_half * sine_part,
            second_half * cosine + first_half * sine_part,
        ],
        axis=-1,
    )


def head_prepare(raw_heads, norm_gain, positions):
    return rotate(rms_scale(raw_heads, norm_gain), positions)


def swiglu(gate_part, up_part):
    return jax.nn.silu(gate_part) * up_part


def stored_positions(row_index, tokens_per_shard, ctx_count):
    device_row = row_index // tokens_per_shard
    within = row_index % tokens_per_shard
    half_block = tokens_per_shard // 2
    block_index = jnp.where(within < half_block, device_row, 2 * ctx_count - 1 - device_row)
    return block_index * half_block + within % half_block


def segment_ids(doc_lengths, positions):
    doc_ends = jnp.cumsum(doc_lengths, dtype=jnp.int32)
    return jnp.sum(
        (positions[:, None] >= doc_ends[None, :]).astype(jnp.int32), axis=1, dtype=jnp.int32
    )


def slot_ranks(flat_routes, expert_count):
    expert_hits = (
        flat_routes[:, None] == jnp.arange(expert_count, dtype=jnp.int32)[None, :]
    ).astype(jnp.int32)
    running = jnp.cumsum(expert_hits, axis=0, dtype=jnp.int32) - 1
    return jnp.sum(expert_hits * running, axis=1, dtype=jnp.int32)


def send_inputs(flat_rows):
    moved = lax.all_to_all(flat_rows, ("ctx", "ws"), split_axis=0, concat_axis=0, tiled=True)
    return moved


def send_outputs(flat_rows):
    moved = lax.all_to_all(flat_rows, ("ctx", "ws"), split_axis=0, concat_axis=0, tiled=True)
    return moved


def send_out_grads(flat_rows):
    moved = lax.all_to_all(flat_rows, ("ctx", "ws"), split_axis=0, concat_axis=0, tiled=True)
    return moved


def send_in_grads(flat_rows):
    moved = lax.all_to_all(flat_rows, ("ctx", "ws"), split_axis=0, concat_axis=0, tiled=True)
    return moved


def flat_rows(grid_sum):
    return grid_sum.reshape((-1,) + grid_sum.shape[3:])


def to_expert_major(arrived, expert_local):
    device_count, row_span, model_width = arrived.shape
    capacity = row_span // expert_local
    shaped = arrived.reshape(device_count, expert_local, capacity, model_width)
    return shaped.transpose(1, 0, 2, 3).reshape(expert_local, device_count * capacity, model_width)


def to_device_major(expert_rows, device_count):
    expert_local, row_span, model_width = expert_rows.shape
    capacity = row_span // device_count
    shaped = expert_rows.reshape(expert_local, device_count, capacity, model_width)
    return shaped.transpose(1, 0, 2, 3).reshape(device_count, expert_local * capacity, model_width)


def general_body(
    inputs,
    grad_output,
    routes,
    doc_lengths,
    norm_attn,
    w_query,
    key_projection,
    value_projection,
    query_norm,
    key_norm,
    w_out,
    norm_ffn,
    w_router,
    expert_gate,
    expert_up,
    expert_down,
):
    ctx_count = lax.axis_size("ctx")
    device_count = ctx_count * lax.axis_size("ws")
    tokens_per_shard = inputs.shape[1]
    model_width = inputs.shape[2]
    sequence_tokens = tokens_per_shard * ctx_count
    expert_count = w_router.shape[1]
    expert_local = expert_gate.shape[0]
    capacity = max(2, tokens_per_shard * TOPK * 3 // (2 * device_count))
    query_group_size = QUERY_HEADS // KEY_VALUE_HEADS
    logit_scale = HEAD_DIM ** (-0.5)
    single_key_block = min(512, sequence_tokens)
    count_of_blocks = sequence_tokens // single_key_block
    ctx_index = lax.axis_index("ctx")
    positions_all = stored_positions(
        jnp.arange(sequence_tokens, dtype=jnp.int32), tokens_per_shard, ctx_count
    )
    segments_all = segment_ids(doc_lengths[0], positions_all)
    local_positions = lax.dynamic_slice_in_dim(
        positions_all, ctx_index * tokens_per_shard, tokens_per_shard
    )
    segments_own = lax.dynamic_slice_in_dim(
        segments_all, ctx_index * tokens_per_shard, tokens_per_shard
    )
    validity = (segments_own < doc_lengths.shape[1]).astype(SINGLE_FLOAT)
    shards = (
        norm_attn,
        w_query,
        key_projection,
        value_projection,
        query_norm,
        key_norm,
        w_out,
        norm_ffn,
        w_router,
    )
    gathered = (
        lax.all_gather(shards[0], ("ctx", "ws"), axis=0, tiled=True),
        lax.all_gather(shards[1], ("ctx", "ws"), axis=0, tiled=True),
        lax.all_gather(shards[2], ("ctx", "ws"), axis=0, tiled=True),
        lax.all_gather(shards[3], ("ctx", "ws"), axis=0, tiled=True),
        lax.all_gather(shards[4], ("ctx", "ws"), axis=0, tiled=True),
        lax.all_gather(shards[5], ("ctx", "ws"), axis=0, tiled=True),
        lax.all_gather(shards[6], ("ctx", "ws"), axis=0, tiled=True),
        lax.all_gather(shards[7], ("ctx", "ws"), axis=0, tiled=True),
        lax.all_gather(shards[8], ("ctx", "ws"), axis=0, tiled=True),
    )
    (
        attn_gain,
        query_matrix,
        key_matrix,
        value_matrix,
        query_gain,
        key_norm_gain,
        output_matrix,
        ffn_gain,
        router_matrix,
    ) = gathered
    attn_gain = attn_gain.astype(SINGLE_FLOAT)
    query_gain = query_gain.astype(SINGLE_FLOAT)
    key_norm_gain = key_norm_gain.astype(SINGLE_FLOAT)
    ffn_gain = ffn_gain.astype(SINGLE_FLOAT)
    layer_in = inputs[0].astype(SINGLE_FLOAT)
    normalized_rows = rms_scale(layer_in, attn_gain).astype(BRAIN_FLOAT_TYPE)
    unnormed_queries = jnp.dot(
        normalized_rows, query_matrix, preferred_element_type=SINGLE_FLOAT
    ).reshape(tokens_per_shard, QUERY_HEADS, HEAD_DIM)
    unnormed_keys = jnp.dot(
        normalized_rows, key_matrix, preferred_element_type=SINGLE_FLOAT
    ).reshape(tokens_per_shard, KEY_VALUE_HEADS, HEAD_DIM)
    value_low = jnp.dot(normalized_rows, value_matrix, preferred_element_type=SINGLE_FLOAT).astype(
        BRAIN_FLOAT_TYPE
    )
    query_rows = head_prepare(unnormed_queries, query_gain, local_positions).astype(
        BRAIN_FLOAT_TYPE
    )
    key_low = (
        head_prepare(unnormed_keys, key_norm_gain, local_positions)
        .astype(BRAIN_FLOAT_TYPE)
        .reshape(tokens_per_shard, KEY_VALUE_HEADS * HEAD_DIM)
    )
    every_key, every_value = (
        lax.all_gather(key_low, "ctx", axis=0, tiled=True),
        lax.all_gather(value_low, "ctx", axis=0, tiled=True),
    )
    grouped_queries = query_rows.reshape(
        tokens_per_shard, KEY_VALUE_HEADS, query_group_size, HEAD_DIM
    )
    blocked_keys = every_key.reshape(count_of_blocks, single_key_block, KEY_VALUE_HEADS, HEAD_DIM)
    blocked_values = every_value.reshape(
        count_of_blocks, single_key_block, KEY_VALUE_HEADS, HEAD_DIM
    )
    position_blocks = positions_all.reshape(count_of_blocks, single_key_block)
    segment_blocks = segments_all.reshape(count_of_blocks, single_key_block)

    def scores_for(block_keys, block_positions, block_segments):
        raw_scores = (
            jnp.einsum(
                "tkgd,jkd->kgtj", grouped_queries, block_keys, preferred_element_type=SINGLE_FLOAT
            )
            * logit_scale
        )
        allowed = (segments_own[:, None] == block_segments[None, :]) & (
            block_positions[None, :] <= local_positions[:, None]
        )
        return (raw_scores, allowed[None, None])

    def stats_step(running, pieces):
        maximum, denominator = running
        block_keys, block_positions, block_segments = pieces
        raw_scores, allowed = scores_for(block_keys, block_positions, block_segments)
        masked = jnp.where(allowed, raw_scores, MASK_FILL)
        new_maximum = jnp.maximum(maximum, jnp.max(masked, axis=-1))
        weights = jnp.where(allowed, jnp.exp(masked - new_maximum[..., None]), 0.0)
        denominator = denominator * jnp.exp(maximum - new_maximum) + jnp.sum(weights, axis=-1)
        return ((new_maximum, denominator), None)

    stats_init = (
        jnp.full((KEY_VALUE_HEADS, query_group_size, tokens_per_shard), MASK_FILL, SINGLE_FLOAT),
        jnp.zeros((KEY_VALUE_HEADS, query_group_size, tokens_per_shard), SINGLE_FLOAT),
    )
    (maximum, denominator), _ = lax.scan(
        stats_step, stats_init, (blocked_keys, position_blocks, segment_blocks)
    )

    def probs_for(raw_scores, allowed):
        return (
            jnp.where(allowed, jnp.exp(raw_scores - maximum[..., None]), 0.0)
            / denominator[..., None]
        )

    def value_update(running, pieces):
        block_keys, block_values, block_positions, block_segments = pieces
        raw_scores, allowed = scores_for(block_keys, block_positions, block_segments)
        softmaxed = probs_for(raw_scores, allowed).astype(BRAIN_FLOAT_TYPE)
        running = running + jnp.einsum(
            "kgtj,jkd->tkgd", softmaxed, block_values, preferred_element_type=SINGLE_FLOAT
        )
        return (running, None)

    inputs_per_block = (blocked_keys, blocked_values, position_blocks, segment_blocks)
    attended, _ = lax.scan(
        value_update,
        jnp.zeros((tokens_per_shard, KEY_VALUE_HEADS, query_group_size, HEAD_DIM), SINGLE_FLOAT),
        inputs_per_block,
    )
    attn_low = attended.reshape(tokens_per_shard, QUERY_HEADS * HEAD_DIM).astype(BRAIN_FLOAT_TYPE)
    hidden_state = layer_in + jnp.dot(attn_low, output_matrix, preferred_element_type=SINGLE_FLOAT)
    combined_rows = rms_scale(hidden_state, ffn_gain).astype(BRAIN_FLOAT_TYPE)
    router_scores = jnp.dot(combined_rows, router_matrix, preferred_element_type=SINGLE_FLOAT)
    own_routes = routes[0]
    route_mask = (
        own_routes[:, :, None] == jnp.arange(expert_count, dtype=jnp.int32)[None, None, :]
    ).astype(SINGLE_FLOAT)
    chosen = jnp.einsum("tke,te->tk", route_mask, router_scores, precision=TOP_PRECISION)
    gate_share = jax.nn.softmax(chosen, axis=-1)
    flat_routes = own_routes.reshape(-1)
    slot_index = flat_routes * capacity + slot_ranks(flat_routes, expert_count)
    entries = tokens_per_shard * TOPK
    source_slot = (
        jnp.full((expert_count * capacity,), entries, jnp.int32)
        .at[slot_index]
        .set(jnp.arange(entries, dtype=jnp.int32))
    )
    padded_in = jnp.concatenate(
        [combined_rows, jnp.zeros((1, model_width), BRAIN_FLOAT_TYPE)], axis=0
    )
    outgoing = padded_in[source_slot // TOPK].reshape(device_count, -1, model_width)
    expert_in = to_expert_major(send_inputs(outgoing), expert_local)
    gate_hidden = jnp.einsum(
        "erd,edf->erf", expert_in, expert_gate, preferred_element_type=SINGLE_FLOAT
    )
    up_hidden = jnp.einsum(
        "erd,edf->erf", expert_in, expert_up, preferred_element_type=SINGLE_FLOAT
    )
    hidden = swiglu(gate_hidden, up_hidden).astype(BRAIN_FLOAT_TYPE)
    expert_out = jnp.einsum(
        "erf,efd->erd", hidden, expert_down, preferred_element_type=SINGLE_FLOAT
    ).astype(BRAIN_FLOAT_TYPE)
    returned = send_outputs(to_device_major(expert_out, device_count)).reshape(
        expert_count * capacity, model_width
    )
    picked = returned[slot_index].reshape(tokens_per_shard, TOPK, model_width)
    moe_sum = jnp.sum(gate_share[:, :, None] * picked.astype(SINGLE_FLOAT), axis=1)
    output = (hidden_state + moe_sum).astype(BRAIN_FLOAT_TYPE)
    d_layer = grad_output[0].astype(SINGLE_FLOAT) * validity[:, None]
    d_gate_share = jnp.sum(d_layer[:, None, :] * picked.astype(SINGLE_FLOAT), axis=-1)
    d_chosen = gate_share * (
        d_gate_share - jnp.sum(gate_share * d_gate_share, axis=-1, keepdims=True)
    )
    d_logits = jnp.einsum("tke,tk->te", route_mask, d_chosen, precision=TOP_PRECISION).astype(
        BRAIN_FLOAT_TYPE
    )
    d_copies = (
        (gate_share[:, :, None] * d_layer[:, None, :])
        .astype(BRAIN_FLOAT_TYPE)
        .reshape(entries, model_width)
    )
    d_padded = jnp.concatenate([d_copies, jnp.zeros((1, model_width), BRAIN_FLOAT_TYPE)], axis=0)
    d_outgoing = d_padded[source_slot].reshape(device_count, -1, model_width)
    d_expert_out = to_expert_major(send_out_grads(d_outgoing), expert_local)
    d_hidden = jnp.einsum(
        "erd,efd->erf", d_expert_out, expert_down, preferred_element_type=SINGLE_FLOAT
    )
    grad_down = jnp.einsum(
        "erf,erd->efd", hidden, d_expert_out, preferred_element_type=SINGLE_FLOAT
    )
    _, swiglu_back = jax.vjp(swiglu, gate_hidden, up_hidden)
    d_gate_hidden, d_up_hidden = swiglu_back(d_hidden)
    d_gate_low = d_gate_hidden.astype(BRAIN_FLOAT_TYPE)
    d_up_low = d_up_hidden.astype(BRAIN_FLOAT_TYPE)
    grad_gate = jnp.einsum(
        "erd,erf->edf", expert_in, d_gate_low, preferred_element_type=SINGLE_FLOAT
    )
    grad_up = jnp.einsum("erd,erf->edf", expert_in, d_up_low, preferred_element_type=SINGLE_FLOAT)
    d_expert_in = jnp.einsum(
        "erf,edf->erd", d_gate_low, expert_gate, preferred_element_type=SINGLE_FLOAT
    )
    d_expert_in = (
        d_expert_in
        + jnp.einsum("erf,edf->erd", d_up_low, expert_up, preferred_element_type=SINGLE_FLOAT)
    ).astype(BRAIN_FLOAT_TYPE)
    d_returned = send_in_grads(to_device_major(d_expert_in, device_count)).reshape(
        expert_count * capacity, model_width
    )
    d_slots = d_returned[slot_index].reshape(tokens_per_shard, TOPK, model_width)
    d_mixed = jnp.sum(d_slots.astype(SINGLE_FLOAT), axis=1) + jnp.einsum(
        "te,de->td", d_logits, router_matrix, preferred_element_type=SINGLE_FLOAT
    )
    grad_router = jnp.einsum(
        "td,te->de", combined_rows, d_logits, preferred_element_type=SINGLE_FLOAT
    )
    _, ffn_norm_back = jax.vjp(rms_scale, hidden_state, ffn_gain)
    d_state_norm, grad_ffn_gain = ffn_norm_back(d_mixed)
    d_state = d_layer + d_state_norm
    d_state_low = d_state.astype(BRAIN_FLOAT_TYPE)
    grad_out_weight = jnp.einsum(
        "tc,td->cd", attn_low, d_state_low, preferred_element_type=SINGLE_FLOAT
    )
    attention_gradient = jnp.einsum(
        "td,cd->tc", d_state_low, output_matrix, preferred_element_type=SINGLE_FLOAT
    ).astype(BRAIN_FLOAT_TYPE)
    attention_gradient = attention_gradient.reshape(
        tokens_per_shard, KEY_VALUE_HEADS, query_group_size, HEAD_DIM
    )
    row_delta = jnp.sum(attention_gradient.astype(SINGLE_FLOAT) * attended, axis=-1).transpose(
        1, 2, 0
    )

    def backward_step(d_query_acc, pieces):
        block_keys, block_values, block_positions, block_segments = pieces
        raw_scores, allowed = scores_for(block_keys, block_positions, block_segments)
        softmaxed = probs_for(raw_scores, allowed)
        d_probs = jnp.einsum(
            "tkgd,jkd->kgtj", attention_gradient, block_values, preferred_element_type=SINGLE_FLOAT
        )
        d_scores = (softmaxed * (d_probs - row_delta[..., None])).astype(BRAIN_FLOAT_TYPE)
        d_query_acc = d_query_acc + jnp.einsum(
            "kgtj,jkd->tkgd", d_scores, block_keys, preferred_element_type=SINGLE_FLOAT
        )
        d_key_block = jnp.einsum(
            "kgtj,tkgd->jkd", d_scores, grouped_queries, preferred_element_type=SINGLE_FLOAT
        )
        d_value_block = jnp.einsum(
            "kgtj,tkgd->jkd",
            softmaxed.astype(BRAIN_FLOAT_TYPE),
            attention_gradient,
            preferred_element_type=SINGLE_FLOAT,
        )
        return (d_query_acc, (d_key_block, d_value_block))

    d_query_acc, (key_block_gradients, value_block_gradients) = lax.scan(
        backward_step,
        jnp.zeros((tokens_per_shard, KEY_VALUE_HEADS, query_group_size, HEAD_DIM), SINGLE_FLOAT),
        inputs_per_block,
    )
    every_key_gradient = (key_block_gradients * logit_scale).reshape(
        sequence_tokens, KEY_VALUE_HEADS * HEAD_DIM
    )
    every_value_gradient = value_block_gradients.reshape(
        sequence_tokens, KEY_VALUE_HEADS * HEAD_DIM
    )
    key_gradients, d_values = (
        lax.psum_scatter(
            every_key_gradient.astype(jnp.bfloat16), "ctx", scatter_dimension=0, tiled=True
        ).astype(jnp.float32),
        lax.psum_scatter(
            every_value_gradient.astype(jnp.bfloat16), "ctx", scatter_dimension=0, tiled=True
        ).astype(jnp.float32),
    )
    _, query_back = jax.vjp(
        lambda raw_heads, norm_gain: head_prepare(raw_heads, norm_gain, local_positions),
        unnormed_queries,
        query_gain,
    )
    d_query_raw, grad_query_gain = query_back(
        (d_query_acc * logit_scale).reshape(tokens_per_shard, QUERY_HEADS, HEAD_DIM)
    )
    _, key_backward = jax.vjp(
        lambda raw_heads, norm_gain: head_prepare(raw_heads, norm_gain, local_positions),
        unnormed_keys,
        key_norm_gain,
    )
    raw_key_gradient, key_gain_gradient = key_backward(
        key_gradients.reshape(tokens_per_shard, KEY_VALUE_HEADS, HEAD_DIM)
    )
    d_query_low = d_query_raw.reshape(tokens_per_shard, QUERY_HEADS * HEAD_DIM).astype(
        BRAIN_FLOAT_TYPE
    )
    key_gradient_lowprec = raw_key_gradient.reshape(
        tokens_per_shard, KEY_VALUE_HEADS * HEAD_DIM
    ).astype(BRAIN_FLOAT_TYPE)
    d_value_low = d_values.astype(BRAIN_FLOAT_TYPE)
    grad_query_weight = jnp.einsum(
        "td,tc->dc", normalized_rows, d_query_low, preferred_element_type=SINGLE_FLOAT
    )
    grad_key_weight = jnp.einsum(
        "td,tc->dc", normalized_rows, key_gradient_lowprec, preferred_element_type=SINGLE_FLOAT
    )
    grad_value_weight = jnp.einsum(
        "td,tc->dc", normalized_rows, d_value_low, preferred_element_type=SINGLE_FLOAT
    )
    d_normed = jnp.einsum(
        "tc,dc->td", d_query_low, query_matrix, preferred_element_type=SINGLE_FLOAT
    )
    d_normed = d_normed + jnp.einsum(
        "tc,dc->td", key_gradient_lowprec, key_matrix, preferred_element_type=SINGLE_FLOAT
    )
    d_normed = d_normed + jnp.einsum(
        "tc,dc->td", d_value_low, value_matrix, preferred_element_type=SINGLE_FLOAT
    )
    _, attn_norm_back = jax.vjp(rms_scale, layer_in, attn_gain)
    d_input_norm, grad_attn_gain = attn_norm_back(d_normed)
    grad_input = d_state + d_input_norm
    reduced = (
        lax.psum_scatter(grad_attn_gain, ("ctx", "ws"), scatter_dimension=0, tiled=True),
        lax.psum_scatter(grad_query_weight, ("ctx", "ws"), scatter_dimension=0, tiled=True),
        lax.psum_scatter(grad_key_weight, ("ctx", "ws"), scatter_dimension=0, tiled=True),
        lax.psum_scatter(grad_value_weight, ("ctx", "ws"), scatter_dimension=0, tiled=True),
        lax.psum_scatter(grad_query_gain, ("ctx", "ws"), scatter_dimension=0, tiled=True),
        lax.psum_scatter(key_gain_gradient, ("ctx", "ws"), scatter_dimension=0, tiled=True),
        lax.psum_scatter(grad_out_weight, ("ctx", "ws"), scatter_dimension=0, tiled=True),
        lax.psum_scatter(grad_ffn_gain, ("ctx", "ws"), scatter_dimension=0, tiled=True),
        lax.psum_scatter(grad_router, ("ctx", "ws"), scatter_dimension=0, tiled=True),
    )
    return (
        output[None],
        grad_input[None],
        reduced[0],
        reduced[1],
        reduced[2],
        reduced[3],
        reduced[4],
        reduced[5],
        reduced[6],
        reduced[7],
        reduced[8],
        grad_gate,
        grad_up,
        grad_down,
    )


VMEM_WHOLE = pl.BlockSpec(memory_space=pltpu.VMEM)
VMEM_BYTES = 60 * 2**20
EXTRA = 128


def compiler_params():
    return pltpu.CompilerParams(vmem_limit_bytes=VMEM_BYTES)


def dot_rows(left, right):
    return lax.dot_general(
        left, right, (((1,), (0,)), ((), ())), preferred_element_type=SINGLE_FLOAT
    )


def dot_right_transposed(left, right):
    return lax.dot_general(
        left, right, (((1,), (1,)), ((), ())), preferred_element_type=SINGLE_FLOAT
    )


def dot_left_transposed(left, right):
    return lax.dot_general(
        left, right, (((0,), (0,)), ((), ())), preferred_element_type=SINGLE_FLOAT
    )


def key_range(tile, tile_rows, sequence_tokens, slack):
    half = sequence_tokens // 2
    first_row = tile * tile_rows
    low = 0 if first_row < half + slack else half
    return low, first_row + tile_rows


def stacked_heads(ref, rows, heads):
    return jnp.concatenate(
        [ref[rows, h * HEAD_DIM : (h + 1) * HEAD_DIM] for h in range(heads)], axis=0
    )


def tile_scores(q4, k_ref, segc_ref, segr_ref, low, high, first_row, tile_rows, heads):
    scale = HEAD_DIM ** (-0.5)
    scores = dot_right_transposed(q4, k_ref[low:high, :]) * scale
    span = high - low
    query_place = first_row + lax.broadcasted_iota(jnp.int32, (tile_rows, span), 0)
    key_place = low + lax.broadcasted_iota(jnp.int32, (tile_rows, span), 1)
    allowed = (segc_ref[first_row : first_row + tile_rows, :] == segr_ref[:, low:high]) & (
        key_place <= query_place
    )
    fill = jnp.where(allowed, 0.0, MASK_FILL)
    scores = scores + jnp.concatenate([fill] * heads, axis=0)
    exponent = jnp.exp(scores - jnp.max(scores, axis=-1, keepdims=True))
    return exponent * (1.0 / jnp.sum(exponent, axis=-1, keepdims=True))


def attention_forward_kernel(
    slack,
    x_ref,
    gain_ref,
    w_ref,
    qg_ref,
    kg_ref,
    cos_ref,
    sin_ref,
    segc_ref,
    segr_ref,
    wo_ref,
    normed_ref,
    raw_ref,
    q_ref,
    k_ref,
    v_ref,
    attn_ref,
    part_ref,
):
    tokens = x_ref.shape[0]
    heads = q_ref.shape[1] // HEAD_DIM
    rows_step = 256

    def project(i, carry):
        rows = pl.ds(pl.multiple_of(i * rows_step, rows_step), rows_step)
        x = x_ref[rows, :].astype(SINGLE_FLOAT)
        inverse = lax.rsqrt(jnp.mean(x * x, axis=-1, keepdims=True) + EPS)
        normed = (x * inverse * gain_ref[...]).astype(BRAIN_FLOAT_TYPE)
        normed_ref[rows, :] = normed
        raw = dot_rows(normed, w_ref[...])
        raw_ref[rows, :] = raw[:, : (heads + 1) * HEAD_DIM]
        v_ref[rows, :] = raw[:, (heads + 1) * HEAD_DIM :].astype(BRAIN_FLOAT_TYPE)
        cosine, sine = cos_ref[rows, :], sin_ref[rows, :]
        for h in range(heads + 1):
            part = raw[:, h * HEAD_DIM : (h + 1) * HEAD_DIM]
            gain = qg_ref[...] if h < heads else kg_ref[...]
            scaled = (
                part * lax.rsqrt(jnp.mean(part * part, axis=-1, keepdims=True) + EPS) * gain
            )
            turned = scaled * cosine + pltpu.roll(scaled, HEAD_DIM // 2, 1) * sine
            turned = turned.astype(BRAIN_FLOAT_TYPE)
            if h < heads:
                q_ref[rows, h * HEAD_DIM : (h + 1) * HEAD_DIM] = turned
            else:
                k_ref[rows, :] = turned
        return carry

    lax.fori_loop(0, tokens // rows_step, project, 0)
    tile_rows = 128
    for tile in range(tokens // tile_rows):
        first_row = tile * tile_rows
        rows = slice(first_row, first_row + tile_rows)
        low, high = key_range(tile, tile_rows, tokens, slack)
        probs = tile_scores(
            stacked_heads(q_ref, rows, heads),
            k_ref,
            segc_ref,
            segr_ref,
            low,
            high,
            first_row,
            tile_rows,
            heads,
        )
        attended = dot_rows(probs.astype(BRAIN_FLOAT_TYPE), v_ref[low:high, :])
        for h in range(heads):
            attn_ref[rows, h * HEAD_DIM : (h + 1) * HEAD_DIM] = attended[
                h * tile_rows : (h + 1) * tile_rows
            ].astype(BRAIN_FLOAT_TYPE)

    def project_out(i, carry):
        rows = pl.ds(pl.multiple_of(i * rows_step, rows_step), rows_step)
        part_ref[rows, :] = dot_rows(attn_ref[rows, :], wo_ref[...]).astype(BRAIN_FLOAT_TYPE)
        return carry

    lax.fori_loop(0, tokens // rows_step, project_out, 0)


def attention_forward(slack, x, gain, w, qg, kg, cosine, sine, segc, segr, wo):
    tokens, width = x.shape
    channels = w.shape[1] - 2 * HEAD_DIM
    low = BRAIN_FLOAT_TYPE
    shapes = (
        jax.ShapeDtypeStruct((tokens, width), low),
        jax.ShapeDtypeStruct((tokens, channels + HEAD_DIM), SINGLE_FLOAT),
        jax.ShapeDtypeStruct((tokens, channels), low),
        jax.ShapeDtypeStruct((tokens, HEAD_DIM), low),
        jax.ShapeDtypeStruct((tokens, HEAD_DIM), low),
        jax.ShapeDtypeStruct((tokens, channels), low),
        jax.ShapeDtypeStruct((tokens, width), low),
    )

    def kernel(*refs):
        attention_forward_kernel(slack, *refs)

    return pl.pallas_call(
        kernel,
        out_shape=shapes,
        in_specs=[VMEM_WHOLE] * 10,
        out_specs=[VMEM_WHOLE] * 7,
        compiler_params=compiler_params(),
        name="attention_forward",
    )(x, gain, w, qg, kg, cosine, sine, segc, segr, wo)


def head_backward(turned_gradient, part, gain, cosine, sine):
    scaled_gradient = turned_gradient * cosine - (
        pltpu.roll(turned_gradient, HEAD_DIM // 2, 1) * sine
    )
    inverse = lax.rsqrt(jnp.mean(part * part, axis=-1, keepdims=True) + EPS)
    unit = part * inverse
    gain_gradient = jnp.sum(scaled_gradient * unit, axis=0, keepdims=True)
    unit_gradient = scaled_gradient * gain
    raw_gradient = inverse * (
        unit_gradient - unit * jnp.mean(unit * unit_gradient, axis=-1, keepdims=True)
    )
    return raw_gradient, gain_gradient


def attention_backward_kernel(
    slack,
    dh_ref,
    wo_ref,
    attn_ref,
    q_ref,
    k_ref,
    v_ref,
    raw_ref,
    normed_ref,
    x_ref,
    w_ref,
    qg_ref,
    kg_ref,
    cos_ref,
    sin_ref,
    segc_ref,
    segr_ref,
    gwo_ref,
    gw_ref,
    dpart_ref,
    ggain_ref,
    gheads_ref,
    da_ref,
    draw_ref,
    dk_ref,
    dv_ref,
):
    tokens = x_ref.shape[0]
    heads = q_ref.shape[1] // HEAD_DIM
    scale = HEAD_DIM ** (-0.5)
    rows_step = 256

    def attended_gradient(i, carry):
        rows = pl.ds(pl.multiple_of(i * rows_step, rows_step), rows_step)
        da_ref[rows, :] = dot_right_transposed(dh_ref[rows, :], wo_ref[...]).astype(
            BRAIN_FLOAT_TYPE
        )
        return carry

    lax.fori_loop(0, tokens // rows_step, attended_gradient, 0)

    def out_weight(i, carry):
        columns = pl.ds(pl.multiple_of(i * 512, 512), 512)
        gwo_ref[:, columns] = dot_left_transposed(attn_ref[...], dh_ref[:, columns]).astype(
            gwo_ref.dtype
        )
        return carry

    lax.fori_loop(0, dh_ref.shape[1] // 512, out_weight, 0)
    dk_ref[...] = jnp.zeros_like(dk_ref)
    dv_ref[...] = jnp.zeros_like(dv_ref)
    query_gain_gradient = jnp.zeros((1, HEAD_DIM), SINGLE_FLOAT)
    tile_rows = 128
    for tile in range(tokens // tile_rows):
        first_row = tile * tile_rows
        rows = slice(first_row, first_row + tile_rows)
        low, high = key_range(tile, tile_rows, tokens, slack)
        q4 = stacked_heads(q_ref, rows, heads)
        da4 = stacked_heads(da_ref, rows, heads)
        probs = tile_scores(
            q4, k_ref, segc_ref, segr_ref, low, high, first_row, tile_rows, heads
        )
        d_probs = dot_right_transposed(da4, v_ref[low:high, :])
        delta = jnp.sum(probs * d_probs, axis=-1, keepdims=True)
        d_scores = (probs * (d_probs - delta)).astype(BRAIN_FLOAT_TYPE)
        dq4 = dot_rows(d_scores, k_ref[low:high, :]) * scale
        dk_ref[low:high, :] += dot_left_transposed(d_scores, q4)
        dv_ref[low:high, :] += dot_left_transposed(probs.astype(BRAIN_FLOAT_TYPE), da4)
        for h in range(heads):
            columns = slice(h * HEAD_DIM, (h + 1) * HEAD_DIM)
            raw_gradient, gain_gradient = head_backward(
                dq4[h * tile_rows : (h + 1) * tile_rows],
                raw_ref[rows, columns],
                qg_ref[...],
                cos_ref[rows, :],
                sin_ref[rows, :],
            )
            draw_ref[rows, columns] = raw_gradient.astype(BRAIN_FLOAT_TYPE)
            query_gain_gradient = query_gain_gradient + gain_gradient
    key_columns = slice(heads * HEAD_DIM, (heads + 1) * HEAD_DIM)
    raw_gradient, key_gain_gradient = head_backward(
        dk_ref[...] * scale, raw_ref[:, key_columns], kg_ref[...], cos_ref[...], sin_ref[...]
    )
    draw_ref[:, key_columns] = raw_gradient.astype(BRAIN_FLOAT_TYPE)
    draw_ref[:, (heads + 1) * HEAD_DIM :] = dv_ref[...].astype(BRAIN_FLOAT_TYPE)
    gheads_ref[...] = jnp.concatenate(
        [query_gain_gradient, key_gain_gradient, jnp.zeros((6, HEAD_DIM), SINGLE_FLOAT)], axis=0
    )

    def projection_weight(i, carry):
        columns = pl.ds(pl.multiple_of(i * 256, 256), 256)
        gw_ref[columns, :] = dot_left_transposed(normed_ref[:, columns], draw_ref[...]).astype(
            gw_ref.dtype
        )
        return carry

    lax.fori_loop(0, normed_ref.shape[1] // 256, projection_weight, 0)
    ggain_ref[...] = jnp.zeros_like(ggain_ref)

    def input_gradient(i, carry):
        rows = pl.ds(pl.multiple_of(i * rows_step, rows_step), rows_step)
        d_normed = dot_right_transposed(draw_ref[rows, :], w_ref[...])
        dpart_ref[rows, :] = d_normed.astype(BRAIN_FLOAT_TYPE)
        x = x_ref[rows, :].astype(SINGLE_FLOAT)
        inverse = lax.rsqrt(jnp.mean(x * x, axis=-1, keepdims=True) + EPS)
        ggain_ref[...] += jnp.sum(d_normed * (x * inverse), axis=0, keepdims=True)
        return carry

    lax.fori_loop(0, tokens // rows_step, input_gradient, 0)


def attention_backward(
    slack, dh, wo, attn, q, k, v, raw, normed, x, w, qg, kg, cosine, sine, segc, segr
):
    tokens, width = x.shape
    channels = q.shape[1]
    low = BRAIN_FLOAT_TYPE
    shapes = (
        jax.ShapeDtypeStruct((channels, width), low),
        jax.ShapeDtypeStruct((width, channels + 2 * HEAD_DIM), low),
        jax.ShapeDtypeStruct((tokens, width), low),
        jax.ShapeDtypeStruct((1, width), SINGLE_FLOAT),
        jax.ShapeDtypeStruct((8, HEAD_DIM), SINGLE_FLOAT),
    )

    def kernel(*refs):
        attention_backward_kernel(slack, *refs)

    return pl.pallas_call(
        kernel,
        out_shape=shapes,
        in_specs=[VMEM_WHOLE] * 16,
        out_specs=[VMEM_WHOLE] * 5,
        scratch_shapes=[
            pltpu.VMEM((tokens, channels), low),
            pltpu.VMEM((tokens, channels + 2 * HEAD_DIM), low),
            pltpu.VMEM((tokens, HEAD_DIM), SINGLE_FLOAT),
            pltpu.VMEM((tokens, HEAD_DIM), SINGLE_FLOAT),
        ],
        compiler_params=compiler_params(),
        name="attention_backward",
    )(dh, wo, attn, q, k, v, raw, normed, x, w, qg, kg, cosine, sine, segc, segr)


def expert_kernel(
    capacity,
    expert_ref,
    pay_ref,
    dout_ref,
    wg_ref,
    wu_ref,
    wd_ref,
    outp_ref,
    dp_ref,
    x_ref,
    deo_ref,
    hid_ref,
    dgl_ref,
    dul_ref,
    d_ref,
    g_ref,
    st_ref,
):
    sources, tokens, payload = pay_ref.shape
    width = wg_ref.shape[0]
    experts = (payload - width) // 4
    e = expert_ref[0]
    lane = lax.broadcasted_iota(jnp.int32, (tokens, payload - width), 1)
    slot_lane = lax.broadcasted_iota(jnp.int32, (tokens, capacity), 1).astype(SINGLE_FLOAT)
    row_lane = lax.broadcasted_iota(jnp.int32, (capacity, payload - width), 1)
    is_gate = (row_lane == e) | (row_lane == experts + e)
    for s in range(sources):
        rows = slice(s * capacity, (s + 1) * capacity)
        table = pay_ref[s, :, width:].astype(SINGLE_FLOAT)
        rank = jnp.sum(jnp.where(lane == 2 * experts + e, table, 0.0), axis=-1, keepdims=True)
        pick = (rank == slot_lane).astype(BRAIN_FLOAT_TYPE)
        st_ref[s] = pick
        chosen = dot_left_transposed(pick, pay_ref[s])
        x_ref[rows, :] = chosen[:, :width].astype(BRAIN_FLOAT_TYPE)
        gate = jnp.sum(jnp.where(is_gate, chosen[:, width:], 0.0), axis=-1, keepdims=True)
        g_ref[rows, :] = gate
        d_rows = dot_left_transposed(pick, dout_ref[s])
        d_ref[rows, :] = d_rows.astype(BRAIN_FLOAT_TYPE)
        deo_ref[rows, :] = (gate * d_rows).astype(BRAIN_FLOAT_TYPE)
    x = x_ref[...]
    gate_hidden = dot_rows(x, wg_ref[...])
    up_hidden = dot_rows(x, wu_ref[...])
    sigmoid = 1.0 / (1.0 + jnp.exp(-gate_hidden))
    silu = gate_hidden * sigmoid
    hidden = (silu * up_hidden).astype(BRAIN_FLOAT_TYPE)
    hid_ref[...] = hidden
    d_hidden = dot_right_transposed(deo_ref[...], wd_ref[...])
    d_gate = (d_hidden * up_hidden * sigmoid * (1.0 + gate_hidden * (1.0 - sigmoid))).astype(
        BRAIN_FLOAT_TYPE
    )
    d_up = (d_hidden * silu).astype(BRAIN_FLOAT_TYPE)
    dgl_ref[...] = d_gate
    dul_ref[...] = d_up
    expert_out = dot_rows(hidden, wd_ref[...]).astype(BRAIN_FLOAT_TYPE)
    d_copy = (
        dot_right_transposed(d_gate, wg_ref[...]) + dot_right_transposed(d_up, wu_ref[...])
    ).astype(BRAIN_FLOAT_TYPE)
    for s in range(sources):
        rows = slice(s * capacity, (s + 1) * capacity)
        pick = st_ref[s]
        e_rows = expert_out[rows].astype(SINGLE_FLOAT)
        gate = g_ref[rows, :]
        d_gate_rows = jnp.sum(
            d_ref[rows, :].astype(SINGLE_FLOAT) * e_rows, axis=-1, keepdims=True
        )
        high = d_gate_rows.astype(BRAIN_FLOAT_TYPE).astype(SINGLE_FLOAT)
        extra = jnp.where(row_lane == e, high, 0.0) + jnp.where(
            row_lane == experts + e, d_gate_rows - high, 0.0
        )
        outp_ref[s] = dot_rows(pick, (gate * e_rows).astype(BRAIN_FLOAT_TYPE)).astype(
            BRAIN_FLOAT_TYPE
        )
        dp_ref[s, :, :width] = dot_rows(pick, d_copy[rows]).astype(BRAIN_FLOAT_TYPE)
        dp_ref[s, :, width:] = dot_rows(pick, extra.astype(BRAIN_FLOAT_TYPE)).astype(
            BRAIN_FLOAT_TYPE
        )


def expert_compute(capacity, step_sources, expert, pay, dout, wg, wu, wd):
    sources, tokens, payload = pay.shape
    width, ff = wg.shape
    low = BRAIN_FLOAT_TYPE
    rows = step_sources * capacity
    total = sources * capacity
    once = pl.Buffered(1)
    grid_spec = pltpu.PrefetchScalarGridSpec(
        num_scalar_prefetch=1,
        grid=(sources // step_sources,),
        in_specs=[
            pl.BlockSpec((step_sources, tokens, payload), lambda i, e: (i, 0, 0)),
            pl.BlockSpec((step_sources, tokens, width), lambda i, e: (i, 0, 0)),
            pl.BlockSpec((width, ff), lambda i, e: (0, 0), pipeline_mode=once),
            pl.BlockSpec((width, ff), lambda i, e: (0, 0), pipeline_mode=once),
            pl.BlockSpec((ff, width), lambda i, e: (0, 0), pipeline_mode=once),
        ],
        out_specs=[
            pl.BlockSpec((step_sources, tokens, width), lambda i, e: (i, 0, 0)),
            pl.BlockSpec((step_sources, tokens, payload), lambda i, e: (i, 0, 0)),
            pl.BlockSpec((rows, width), lambda i, e: (i, 0)),
            pl.BlockSpec((rows, width), lambda i, e: (i, 0)),
            pl.BlockSpec((rows, ff), lambda i, e: (i, 0)),
            pl.BlockSpec((rows, ff), lambda i, e: (i, 0)),
            pl.BlockSpec((rows, ff), lambda i, e: (i, 0)),
        ],
        scratch_shapes=[
            pltpu.VMEM((rows, width), low),
            pltpu.VMEM((rows, 1), SINGLE_FLOAT),
            pltpu.VMEM((step_sources, tokens, capacity), low),
        ],
    )

    def kernel(*refs):
        expert_kernel(capacity, *refs)

    return pl.pallas_call(
        kernel,
        grid_spec=grid_spec,
        out_shape=(
            jax.ShapeDtypeStruct((sources, tokens, width), low),
            jax.ShapeDtypeStruct((sources, tokens, payload), low),
            jax.ShapeDtypeStruct((total, width), low),
            jax.ShapeDtypeStruct((total, width), low),
            jax.ShapeDtypeStruct((total, ff), low),
            jax.ShapeDtypeStruct((total, ff), low),
            jax.ShapeDtypeStruct((total, ff), low),
        ),
        compiler_params=compiler_params(),
        name="expert_compute",
    )(expert, pay, dout, wg, wu, wd)


def natural_order(blocks):
    count, rows, width = blocks.shape
    half = rows // 2
    first = blocks[:, :half].reshape(count * half, width)
    second = blocks[::-1, half:].reshape(count * half, width)
    return jnp.concatenate([first, second], axis=0)


def device_order(rows, count):
    total, width = rows.shape
    half = total // count // 2
    first = rows[: total // 2].reshape(count, half, width)
    second = rows[total // 2 :].reshape(count, half, width)[::-1]
    return jnp.concatenate([first, second], axis=1)


def norm_backward(gradient, values, gain):
    inverse = lax.rsqrt(jnp.mean(values * values, axis=-1, keepdims=True) + EPS)
    unit = values * inverse
    scaled = gradient * gain
    d_values = inverse * (scaled - unit * jnp.mean(unit * scaled, axis=-1, keepdims=True))
    return d_values, jnp.sum(gradient * unit, axis=0)


def tensor_body(
    inputs,
    grad_output,
    routes,
    doc_lengths,
    norm_attn,
    w_query,
    key_projection,
    value_projection,
    query_norm,
    key_norm,
    w_out,
    norm_ffn,
    w_router,
    expert_gate,
    expert_up,
    expert_down,
):
    ctx_count = lax.axis_size("ctx")
    ws_count = lax.axis_size("ws")
    device_count = ctx_count * ws_count
    tokens = inputs.shape[1]
    width = inputs.shape[2]
    sequence_tokens = tokens * ctx_count
    expert_count = w_router.shape[1]
    capacity = tokens * TOPK * 3 // (2 * device_count)
    heads = QUERY_HEADS // ctx_count
    group = QUERY_HEADS // KEY_VALUE_HEADS
    slack = tokens // 2
    ctx_index = lax.axis_index("ctx")
    both = ("ctx", "ws")
    me = ctx_index * ws_count + lax.axis_index("ws")
    slabs = []
    for c in range(ctx_count):
        kv = c * heads // group
        slabs.append(
            jnp.concatenate(
                [
                    w_query[:, c * heads * HEAD_DIM : (c + 1) * heads * HEAD_DIM],
                    key_projection[:, kv * HEAD_DIM : (kv + 1) * HEAD_DIM],
                    value_projection[:, kv * HEAD_DIM : (kv + 1) * HEAD_DIM],
                ],
                axis=1,
            )
        )
    slabs = jnp.stack(slabs)
    moved = lax.all_to_all(slabs, "ctx", split_axis=0, concat_axis=0)
    w_all = lax.all_gather(moved, "ws", axis=1).reshape(width, (heads + 2) * HEAD_DIM)
    wo_all = lax.all_gather(w_out, "ws", axis=0, tiled=True)
    x_blocks = lax.all_gather(inputs[0], "ctx", axis=0)
    x_all = natural_order(x_blocks)
    attn_gain = lax.all_gather(norm_attn, both, tiled=True).astype(SINGLE_FLOAT)
    ffn_gain = lax.all_gather(norm_ffn, both, tiled=True).astype(SINGLE_FLOAT)
    query_gain = lax.all_gather(query_norm, both, tiled=True).astype(SINGLE_FLOAT)
    key_gain = lax.all_gather(key_norm, both, tiled=True).astype(SINGLE_FLOAT)
    router_matrix = lax.all_gather(w_router, both, axis=0, tiled=True)

    places = jnp.arange(sequence_tokens, dtype=jnp.int32)
    segments = segment_ids(doc_lengths[0], places)
    half = HEAD_DIM // 2
    frequency = THETA ** (-2.0 * jnp.arange(half, dtype=SINGLE_FLOAT) / HEAD_DIM)
    angle = places.astype(SINGLE_FLOAT)[:, None] * frequency[None, :]
    cosine, sine = jnp.cos(angle), jnp.sin(angle)
    cosine = jnp.concatenate([cosine, cosine], axis=1)
    sine = jnp.concatenate([-sine, sine], axis=1)
    segc, segr = segments[:, None], segments[None, :]
    qg, kg = query_gain[None, :], key_gain[None, :]
    own_places = jnp.arange(tokens, dtype=jnp.int32)
    own_places = jnp.where(
        own_places < tokens // 2,
        ctx_index * (tokens // 2) + own_places,
        (2 * ctx_count - 2 - ctx_index) * (tokens // 2) + own_places,
    )
    own_segments = segment_ids(doc_lengths[0], own_places)
    validity = own_segments < doc_lengths.shape[1]
    d_layer = jnp.where(validity[:, None], grad_output[0], 0.0).astype(BRAIN_FLOAT_TYPE)
    dout_all = lax.all_gather(d_layer, both, axis=0)

    normed, raw, q, k, v, attn, part = attention_forward(
        slack, x_all, attn_gain[None, :], w_all, qg, kg, cosine, sine, segc, segr, wo_all
    )
    branch = lax.psum_scatter(
        device_order(part, ctx_count), "ctx", scatter_dimension=0, tiled=False
    )
    layer_in = inputs[0].astype(SINGLE_FLOAT)
    hidden_state = layer_in + branch.astype(SINGLE_FLOAT)
    mixed = rms_scale(hidden_state, ffn_gain).astype(BRAIN_FLOAT_TYPE)
    logits = jnp.dot(mixed, router_matrix, preferred_element_type=SINGLE_FLOAT)
    own_routes = routes[0]
    hit = jnp.any(
        own_routes[:, :, None] == jnp.arange(expert_count, dtype=jnp.int32)[None, None, :], axis=1
    )
    masked = jnp.where(hit, logits, MASK_FILL)
    exponent = jnp.exp(masked - jnp.max(masked, axis=-1, keepdims=True))
    gates = exponent / jnp.sum(exponent, axis=-1, keepdims=True)
    hits = hit.astype(BRAIN_FLOAT_TYPE)
    earlier = jnp.tril(jnp.ones((tokens, tokens), BRAIN_FLOAT_TYPE), -1)
    rank = jnp.dot(earlier, hits, preferred_element_type=SINGLE_FLOAT)
    rank = jnp.where(hit, rank, -1.0).astype(BRAIN_FLOAT_TYPE)
    gate_high = gates.astype(BRAIN_FLOAT_TYPE)
    gate_low = (gates - gate_high.astype(SINGLE_FLOAT)).astype(BRAIN_FLOAT_TYPE)
    payload = jnp.concatenate(
        [mixed, gate_high, gate_low, rank, jnp.zeros_like(rank)], axis=1
    )
    pay_all = lax.all_gather(payload, both, axis=0)
    out_part, d_part, x_rows, d_rows, hidden, d_gate, d_up = expert_compute(
        capacity, 4, me.astype(jnp.int32).reshape(1), pay_all, dout_all, expert_gate[0], expert_up[0], expert_down[0]
    )
    d_back = lax.psum_scatter(d_part, both, scatter_dimension=0, tiled=False)
    moe_sum = lax.psum_scatter(out_part, both, scatter_dimension=0, tiled=False)
    output = (hidden_state + moe_sum.astype(SINGLE_FLOAT)).astype(BRAIN_FLOAT_TYPE)
    grad_gate = dot_left_transposed(x_rows, d_gate)[None]
    grad_up = dot_left_transposed(x_rows, d_up)[None]
    grad_down = dot_left_transposed(hidden, d_rows)[None]

    table = d_back[:, width:].astype(SINGLE_FLOAT)
    d_gates = table[:, :expert_count] + table[:, expert_count : 2 * expert_count]
    d_chosen = gates * (d_gates - jnp.sum(gates * d_gates, axis=-1, keepdims=True))
    d_logits = d_chosen.astype(BRAIN_FLOAT_TYPE)
    d_mixed = d_back[:, :width].astype(SINGLE_FLOAT) + dot_right_transposed(
        d_logits, router_matrix
    )
    grad_router = dot_left_transposed(mixed, d_logits)
    d_state_norm, grad_ffn_gain = norm_backward(d_mixed, hidden_state, ffn_gain)
    d_state = d_layer.astype(SINGLE_FLOAT) + d_state_norm
    d_state_low = d_state.astype(BRAIN_FLOAT_TYPE)
    dh_all = natural_order(lax.all_gather(d_state_low, "ctx", axis=0))
    gwo, gw, dpart, ggain, gheads = attention_backward(
        slack, dh_all, wo_all, attn, q, k, v, raw, normed, x_all, w_all, qg, kg, cosine, sine, segc, segr
    )
    d_normed = lax.psum_scatter(
        device_order(dpart, ctx_count), "ctx", scatter_dimension=0, tiled=False
    ).astype(SINGLE_FLOAT)
    d_input_norm, _ = norm_backward(d_normed, layer_in, attn_gain)
    grad_input = d_state + d_input_norm
    grad_wo = lax.psum_scatter(gwo, "ws", scatter_dimension=0, tiled=True).astype(SINGLE_FLOAT)
    owned = width // device_count
    gw = gw.reshape(ctx_count, ws_count, owned, (heads + 2) * HEAD_DIM)
    gw = lax.psum_scatter(gw, "ws", scatter_dimension=1, tiled=False)
    gw = lax.all_to_all(gw, "ctx", split_axis=0, concat_axis=0).astype(SINGLE_FLOAT)
    channels = heads * HEAD_DIM
    grad_wq = gw[:, :, :channels].transpose(1, 0, 2).reshape(owned, ctx_count * channels)
    shared = ctx_count // KEY_VALUE_HEADS
    kv = gw[:, :, channels:].reshape(KEY_VALUE_HEADS, shared, owned, 2, HEAD_DIM).sum(1)
    grad_wk = kv[:, :, 0].transpose(1, 0, 2).reshape(owned, KEY_VALUE_HEADS * HEAD_DIM)
    grad_wv = kv[:, :, 1].transpose(1, 0, 2).reshape(owned, KEY_VALUE_HEADS * HEAD_DIM)
    small = [ggain[0], gheads[0], gheads[1], grad_ffn_gain]
    small = [lax.psum_scatter(g, both, scatter_dimension=0, tiled=True) for g in small]
    grad_router = lax.psum_scatter(grad_router, both, scatter_dimension=0, tiled=True)
    return (
        output[None],
        grad_input[None],
        small[0],
        grad_wq,
        grad_wk,
        grad_wv,
        small[1],
        small[2],
        grad_wo,
        small[3],
        grad_router,
        grad_gate,
        grad_up,
        grad_down,
    )


def planned_body(mesh):
    if mesh.shape["ctx"] == 8 and mesh.shape["ws"] == 4:
        return tensor_body
    return general_body


def solution(mesh):
    placed = (
        P("ws", "ctx", None),
        P("ws", "ctx", None),
        P("ws", "ctx", None),
        P("ws", None),
        P(("ctx", "ws")),
        P(("ctx", "ws"), None),
        P(("ctx", "ws"), None),
        P(("ctx", "ws"), None),
        P(("ctx", "ws")),
        P(("ctx", "ws")),
        P(("ctx", "ws"), None),
        P(("ctx", "ws")),
        P(("ctx", "ws"), None),
        P(("ctx", "ws"), None, None),
        P(("ctx", "ws"), None, None),
        P(("ctx", "ws"), None, None),
    )
    return jax.shard_map(
        planned_body(mesh),
        mesh=mesh,
        in_specs=placed,
        out_specs=(
            P("ws", "ctx", None),
            P("ws", "ctx", None),
            P(("ctx", "ws")),
            P(("ctx", "ws"), None),
            P(("ctx", "ws"), None),
            P(("ctx", "ws"), None),
            P(("ctx", "ws")),
            P(("ctx", "ws")),
            P(("ctx", "ws"), None),
            P(("ctx", "ws")),
            P(("ctx", "ws"), None),
            P(("ctx", "ws"), None, None),
            P(("ctx", "ws"), None, None),
            P(("ctx", "ws"), None, None),
        ),
        check_vma=False,
    )
```

```python
import jax
import jax.numpy as jnp
from jax import lax
from jax.experimental import pallas as pl
from jax.experimental.pallas import tpu as pltpu
from jax.sharding import PartitionSpec as P

QUERY_HEADS = 32
KEY_VALUE_HEADS = 4
HEAD_DIM = 128
TOPK = 8


EPS = 1e-06
THETA = 1000000.0
MASK_FILL = -1e30
TOP_PRECISION = lax.Precision.HIGHEST
SINGLE_FLOAT = jnp.float32
BRAIN_FLOAT_TYPE = jnp.bfloat16


def rms_scale(values, norm_gain):
    return values * lax.rsqrt(jnp.mean(values * values, axis=-1, keepdims=True) + EPS) * norm_gain


def rotate(values, positions):
    half_dim = values.shape[-1] // 2
    frequency = THETA ** (-2.0 * jnp.arange(half_dim, dtype=jnp.float32) / values.shape[-1])
    angle = positions.astype(jnp.float32)[:, None] * frequency[None, :]
    cosine = jnp.cos(angle)[:, None, :]
    sine_part = jnp.sin(angle)[:, None, :]
    first_half = values[..., :half_dim]
    second_half = values[..., half_dim:]
    return jnp.concatenate(
        [
            first_half * cosine - second_half * sine_part,
            second_half * cosine + first_half * sine_part,
        ],
        axis=-1,
    )


def head_prepare(raw_heads, norm_gain, positions):
    return rotate(rms_scale(raw_heads, norm_gain), positions)


def swiglu(gate_part, up_part):
    return jax.nn.silu(gate_part) * up_part


def stored_positions(row_index, tokens_per_shard, ctx_count):
    device_row = row_index // tokens_per_shard
    within = row_index % tokens_per_shard
    half_block = tokens_per_shard // 2
    block_index = jnp.where(within < half_block, device_row, 2 * ctx_count - 1 - device_row)
    return block_index * half_block + within % half_block


def segment_ids(doc_lengths, positions):
    doc_ends = jnp.cumsum(doc_lengths, dtype=jnp.int32)
    return jnp.sum(
        (positions[:, None] >= doc_ends[None, :]).astype(jnp.int32), axis=1, dtype=jnp.int32
    )


def slot_ranks(flat_routes, expert_count):
    expert_hits = (
        flat_routes[:, None] == jnp.arange(expert_count, dtype=jnp.int32)[None, :]
    ).astype(jnp.int32)
    running = jnp.cumsum(expert_hits, axis=0, dtype=jnp.int32) - 1
    return jnp.sum(expert_hits * running, axis=1, dtype=jnp.int32)


def send_inputs(flat_rows):
    moved = lax.all_to_all(flat_rows, ("ctx", "ws"), split_axis=0, concat_axis=0, tiled=True)
    return moved


def send_outputs(flat_rows):
    moved = lax.all_to_all(flat_rows, ("ctx", "ws"), split_axis=0, concat_axis=0, tiled=True)
    return moved


def send_out_grads(flat_rows):
    moved = lax.all_to_all(flat_rows, ("ctx", "ws"), split_axis=0, concat_axis=0, tiled=True)
    return moved


def send_in_grads(flat_rows):
    moved = lax.all_to_all(flat_rows, ("ctx", "ws"), split_axis=0, concat_axis=0, tiled=True)
    return moved


def flat_rows(grid_sum):
    return grid_sum.reshape((-1,) + grid_sum.shape[3:])


def to_expert_major(arrived, expert_local):
    device_count, row_span, model_width = arrived.shape
    capacity = row_span // expert_local
    shaped = arrived.reshape(device_count, expert_local, capacity, model_width)
    return shaped.transpose(1, 0, 2, 3).reshape(expert_local, device_count * capacity, model_width)


def to_device_major(expert_rows, device_count):
    expert_local, row_span, model_width = expert_rows.shape
    capacity = row_span // device_count
    shaped = expert_rows.reshape(expert_local, device_count, capacity, model_width)
    return shaped.transpose(1, 0, 2, 3).reshape(device_count, expert_local * capacity, model_width)


def general_body(
    inputs,
    grad_output,
    routes,
    doc_lengths,
    norm_attn,
    w_query,
    key_projection,
    value_projection,
    query_norm,
    key_norm,
    w_out,
    norm_ffn,
    w_router,
    expert_gate,
    expert_up,
    expert_down,
):
    ctx_count = lax.axis_size("ctx")
    device_count = ctx_count * lax.axis_size("ws")
    tokens_per_shard = inputs.shape[1]
    model_width = inputs.shape[2]
    sequence_tokens = tokens_per_shard * ctx_count
    expert_count = w_router.shape[1]
    expert_local = expert_gate.shape[0]
    capacity = max(2, tokens_per_shard * TOPK * 3 // (2 * device_count))
    query_group_size = QUERY_HEADS // KEY_VALUE_HEADS
    logit_scale = HEAD_DIM ** (-0.5)
    single_key_block = min(512, sequence_tokens)
    count_of_blocks = sequence_tokens // single_key_block
    ctx_index = lax.axis_index("ctx")
    positions_all = stored_positions(
        jnp.arange(sequence_tokens, dtype=jnp.int32), tokens_per_shard, ctx_count
    )
    segments_all = segment_ids(doc_lengths[0], positions_all)
    local_positions = lax.dynamic_slice_in_dim(
        positions_all, ctx_index * tokens_per_shard, tokens_per_shard
    )
    segments_own = lax.dynamic_slice_in_dim(
        segments_all, ctx_index * tokens_per_shard, tokens_per_shard
    )
    validity = (segments_own < doc_lengths.shape[1]).astype(SINGLE_FLOAT)
    shards = (
        norm_attn,
        w_query,
        key_projection,
        value_projection,
        query_norm,
        key_norm,
        w_out,
        norm_ffn,
        w_router,
    )
    gathered = (
        lax.all_gather(shards[0], ("ctx", "ws"), axis=0, tiled=True),
        lax.all_gather(shards[1], ("ctx", "ws"), axis=0, tiled=True),
        lax.all_gather(shards[2], ("ctx", "ws"), axis=0, tiled=True),
        lax.all_gather(shards[3], ("ctx", "ws"), axis=0, tiled=True),
        lax.all_gather(shards[4], ("ctx", "ws"), axis=0, tiled=True),
        lax.all_gather(shards[5], ("ctx", "ws"), axis=0, tiled=True),
        lax.all_gather(shards[6], ("ctx", "ws"), axis=0, tiled=True),
        lax.all_gather(shards[7], ("ctx", "ws"), axis=0, tiled=True),
        lax.all_gather(shards[8], ("ctx", "ws"), axis=0, tiled=True),
    )
    (
        attn_gain,
        query_matrix,
        key_matrix,
        value_matrix,
        query_gain,
        key_norm_gain,
        output_matrix,
        ffn_gain,
        router_matrix,
    ) = gathered
    attn_gain = attn_gain.astype(SINGLE_FLOAT)
    query_gain = query_gain.astype(SINGLE_FLOAT)
    key_norm_gain = key_norm_gain.astype(SINGLE_FLOAT)
    ffn_gain = ffn_gain.astype(SINGLE_FLOAT)
    layer_in = inputs[0].astype(SINGLE_FLOAT)
    normalized_rows = rms_scale(layer_in, attn_gain).astype(BRAIN_FLOAT_TYPE)
    unnormed_queries = jnp.dot(
        normalized_rows, query_matrix, preferred_element_type=SINGLE_FLOAT
    ).reshape(tokens_per_shard, QUERY_HEADS, HEAD_DIM)
    unnormed_keys = jnp.dot(
        normalized_rows, key_matrix, preferred_element_type=SINGLE_FLOAT
    ).reshape(tokens_per_shard, KEY_VALUE_HEADS, HEAD_DIM)
    value_low = jnp.dot(normalized_rows, value_matrix, preferred_element_type=SINGLE_FLOAT).astype(
        BRAIN_FLOAT_TYPE
    )
    query_rows = head_prepare(unnormed_queries, query_gain, local_positions).astype(
        BRAIN_FLOAT_TYPE
    )
    key_low = (
        head_prepare(unnormed_keys, key_norm_gain, local_positions)
        .astype(BRAIN_FLOAT_TYPE)
        .reshape(tokens_per_shard, KEY_VALUE_HEADS * HEAD_DIM)
    )
    every_key, every_value = (
        lax.all_gather(key_low, "ctx", axis=0, tiled=True),
        lax.all_gather(value_low, "ctx", axis=0, tiled=True),
    )
    grouped_queries = query_rows.reshape(
        tokens_per_shard, KEY_VALUE_HEADS, query_group_size, HEAD_DIM
    )
    blocked_keys = every_key.reshape(count_of_blocks, single_key_block, KEY_VALUE_HEADS, HEAD_DIM)
    blocked_values = every_value.reshape(
        count_of_blocks, single_key_block, KEY_VALUE_HEADS, HEAD_DIM
    )
    position_blocks = positions_all.reshape(count_of_blocks, single_key_block)
    segment_blocks = segments_all.reshape(count_of_blocks, single_key_block)

    def scores_for(block_keys, block_positions, block_segments):
        raw_scores = (
            jnp.einsum(
                "tkgd,jkd->kgtj", grouped_queries, block_keys, preferred_element_type=SINGLE_FLOAT
            )
            * logit_scale
        )
        allowed = (segments_own[:, None] == block_segments[None, :]) & (
            block_positions[None, :] <= local_positions[:, None]
        )
        return (raw_scores, allowed[None, None])

    def stats_step(running, pieces):
        maximum, denominator = running
        block_keys, block_positions, block_segments = pieces
        raw_scores, allowed = scores_for(block_keys, block_positions, block_segments)
        masked = jnp.where(allowed, raw_scores, MASK_FILL)
        new_maximum = jnp.maximum(maximum, jnp.max(masked, axis=-1))
        weights = jnp.where(allowed, jnp.exp(masked - new_maximum[..., None]), 0.0)
        denominator = denominator * jnp.exp(maximum - new_maximum) + jnp.sum(weights, axis=-1)
        return ((new_maximum, denominator), None)

    stats_init = (
        jnp.full((KEY_VALUE_HEADS, query_group_size, tokens_per_shard), MASK_FILL, SINGLE_FLOAT),
        jnp.zeros((KEY_VALUE_HEADS, query_group_size, tokens_per_shard), SINGLE_FLOAT),
    )
    (maximum, denominator), _ = lax.scan(
        stats_step, stats_init, (blocked_keys, position_blocks, segment_blocks)
    )

    def probs_for(raw_scores, allowed):
        return (
            jnp.where(allowed, jnp.exp(raw_scores - maximum[..., None]), 0.0)
            / denominator[..., None]
        )

    def value_update(running, pieces):
        block_keys, block_values, block_positions, block_segments = pieces
        raw_scores, allowed = scores_for(block_keys, block_positions, block_segments)
        softmaxed = probs_for(raw_scores, allowed).astype(BRAIN_FLOAT_TYPE)
        running = running + jnp.einsum(
            "kgtj,jkd->tkgd", softmaxed, block_values, preferred_element_type=SINGLE_FLOAT
        )
        return (running, None)

    inputs_per_block = (blocked_keys, blocked_values, position_blocks, segment_blocks)
    attended, _ = lax.scan(
        value_update,
        jnp.zeros((tokens_per_shard, KEY_VALUE_HEADS, query_group_size, HEAD_DIM), SINGLE_FLOAT),
        inputs_per_block,
    )
    attn_low = attended.reshape(tokens_per_shard, QUERY_HEADS * HEAD_DIM).astype(BRAIN_FLOAT_TYPE)
    hidden_state = layer_in + jnp.dot(attn_low, output_matrix, preferred_element_type=SINGLE_FLOAT)
    combined_rows = rms_scale(hidden_state, ffn_gain).astype(BRAIN_FLOAT_TYPE)
    router_scores = jnp.dot(combined_rows, router_matrix, preferred_element_type=SINGLE_FLOAT)
    own_routes = routes[0]
    route_mask = (
        own_routes[:, :, None] == jnp.arange(expert_count, dtype=jnp.int32)[None, None, :]
    ).astype(SINGLE_FLOAT)
    chosen = jnp.einsum("tke,te->tk", route_mask, router_scores, precision=TOP_PRECISION)
    gate_share = jax.nn.softmax(chosen, axis=-1)
    flat_routes = own_routes.reshape(-1)
    slot_index = flat_routes * capacity + slot_ranks(flat_routes, expert_count)
    entries = tokens_per_shard * TOPK
    source_slot = (
        jnp.full((expert_count * capacity,), entries, jnp.int32)
        .at[slot_index]
        .set(jnp.arange(entries, dtype=jnp.int32))
    )
    padded_in = jnp.concatenate(
        [combined_rows, jnp.zeros((1, model_width), BRAIN_FLOAT_TYPE)], axis=0
    )
    outgoing = padded_in[source_slot // TOPK].reshape(device_count, -1, model_width)
    expert_in = to_expert_major(send_inputs(outgoing), expert_local)
    gate_hidden = jnp.einsum(
        "erd,edf->erf", expert_in, expert_gate, preferred_element_type=SINGLE_FLOAT
    )
    up_hidden = jnp.einsum(
        "erd,edf->erf", expert_in, expert_up, preferred_element_type=SINGLE_FLOAT
    )
    hidden = swiglu(gate_hidden, up_hidden).astype(BRAIN_FLOAT_TYPE)
    expert_out = jnp.einsum(
        "erf,efd->erd", hidden, expert_down, preferred_element_type=SINGLE_FLOAT
    ).astype(BRAIN_FLOAT_TYPE)
    returned = send_outputs(to_device_major(expert_out, device_count)).reshape(
        expert_count * capacity, model_width
    )
    picked = returned[slot_index].reshape(tokens_per_shard, TOPK, model_width)
    moe_sum = jnp.sum(gate_share[:, :, None] * picked.astype(SINGLE_FLOAT), axis=1)
    output = (hidden_state + moe_sum).astype(BRAIN_FLOAT_TYPE)
    d_layer = grad_output[0].astype(SINGLE_FLOAT) * validity[:, None]
    d_gate_share = jnp.sum(d_layer[:, None, :] * picked.astype(SINGLE_FLOAT), axis=-1)
    d_chosen = gate_share * (
        d_gate_share - jnp.sum(gate_share * d_gate_share, axis=-1, keepdims=True)
    )
    d_logits = jnp.einsum("tke,tk->te", route_mask, d_chosen, precision=TOP_PRECISION).astype(
        BRAIN_FLOAT_TYPE
    )
    d_copies = (
        (gate_share[:, :, None] * d_layer[:, None, :])
        .astype(BRAIN_FLOAT_TYPE)
        .reshape(entries, model_width)
    )
    d_padded = jnp.concatenate([d_copies, jnp.zeros((1, model_width), BRAIN_FLOAT_TYPE)], axis=0)
    d_outgoing = d_padded[source_slot].reshape(device_count, -1, model_width)
    d_expert_out = to_expert_major(send_out_grads(d_outgoing), expert_local)
    d_hidden = jnp.einsum(
        "erd,efd->erf", d_expert_out, expert_down, preferred_element_type=SINGLE_FLOAT
    )
    grad_down = jnp.einsum(
        "erf,erd->efd", hidden, d_expert_out, preferred_element_type=SINGLE_FLOAT
    )
    _, swiglu_back = jax.vjp(swiglu, gate_hidden, up_hidden)
    d_gate_hidden, d_up_hidden = swiglu_back(d_hidden)
    d_gate_low = d_gate_hidden.astype(BRAIN_FLOAT_TYPE)
    d_up_low = d_up_hidden.astype(BRAIN_FLOAT_TYPE)
    grad_gate = jnp.einsum(
        "erd,erf->edf", expert_in, d_gate_low, preferred_element_type=SINGLE_FLOAT
    )
    grad_up = jnp.einsum("erd,erf->edf", expert_in, d_up_low, preferred_element_type=SINGLE_FLOAT)
    d_expert_in = jnp.einsum(
        "erf,edf->erd", d_gate_low, expert_gate, preferred_element_type=SINGLE_FLOAT
    )
    d_expert_in = (
        d_expert_in
        + jnp.einsum("erf,edf->erd", d_up_low, expert_up, preferred_element_type=SINGLE_FLOAT)
    ).astype(BRAIN_FLOAT_TYPE)
    d_returned = send_in_grads(to_device_major(d_expert_in, device_count)).reshape(
        expert_count * capacity, model_width
    )
    d_slots = d_returned[slot_index].reshape(tokens_per_shard, TOPK, model_width)
    d_mixed = jnp.sum(d_slots.astype(SINGLE_FLOAT), axis=1) + jnp.einsum(
        "te,de->td", d_logits, router_matrix, preferred_element_type=SINGLE_FLOAT
    )
    grad_router = jnp.einsum(
        "td,te->de", combined_rows, d_logits, preferred_element_type=SINGLE_FLOAT
    )
    _, ffn_norm_back = jax.vjp(rms_scale, hidden_state, ffn_gain)
    d_state_norm, grad_ffn_gain = ffn_norm_back(d_mixed)
    d_state = d_layer + d_state_norm
    d_state_low = d_state.astype(BRAIN_FLOAT_TYPE)
    grad_out_weight = jnp.einsum(
        "tc,td->cd", attn_low, d_state_low, preferred_element_type=SINGLE_FLOAT
    )
    attention_gradient = jnp.einsum(
        "td,cd->tc", d_state_low, output_matrix, preferred_element_type=SINGLE_FLOAT
    ).astype(BRAIN_FLOAT_TYPE)
    attention_gradient = attention_gradient.reshape(
        tokens_per_shard, KEY_VALUE_HEADS, query_group_size, HEAD_DIM
    )
    row_delta = jnp.sum(attention_gradient.astype(SINGLE_FLOAT) * attended, axis=-1).transpose(
        1, 2, 0
    )

    def backward_step(d_query_acc, pieces):
        block_keys, block_values, block_positions, block_segments = pieces
        raw_scores, allowed = scores_for(block_keys, block_positions, block_segments)
        softmaxed = probs_for(raw_scores, allowed)
        d_probs = jnp.einsum(
            "tkgd,jkd->kgtj", attention_gradient, block_values, preferred_element_type=SINGLE_FLOAT
        )
        d_scores = (softmaxed * (d_probs - row_delta[..., None])).astype(BRAIN_FLOAT_TYPE)
        d_query_acc = d_query_acc + jnp.einsum(
            "kgtj,jkd->tkgd", d_scores, block_keys, preferred_element_type=SINGLE_FLOAT
        )
        d_key_block = jnp.einsum(
            "kgtj,tkgd->jkd", d_scores, grouped_queries, preferred_element_type=SINGLE_FLOAT
        )
        d_value_block = jnp.einsum(
            "kgtj,tkgd->jkd",
            softmaxed.astype(BRAIN_FLOAT_TYPE),
            attention_gradient,
            preferred_element_type=SINGLE_FLOAT,
        )
        return (d_query_acc, (d_key_block, d_value_block))

    d_query_acc, (key_block_gradients, value_block_gradients) = lax.scan(
        backward_step,
        jnp.zeros((tokens_per_shard, KEY_VALUE_HEADS, query_group_size, HEAD_DIM), SINGLE_FLOAT),
        inputs_per_block,
    )
    every_key_gradient = (key_block_gradients * logit_scale).reshape(
        sequence_tokens, KEY_VALUE_HEADS * HEAD_DIM
    )
    every_value_gradient = value_block_gradients.reshape(
        sequence_tokens, KEY_VALUE_HEADS * HEAD_DIM
    )
    key_gradients, d_values = (
        lax.psum_scatter(
            every_key_gradient.astype(jnp.bfloat16), "ctx", scatter_dimension=0, tiled=True
        ).astype(jnp.float32),
        lax.psum_scatter(
            every_value_gradient.astype(jnp.bfloat16), "ctx", scatter_dimension=0, tiled=True
        ).astype(jnp.float32),
    )
    _, query_back = jax.vjp(
        lambda raw_heads, norm_gain: head_prepare(raw_heads, norm_gain, local_positions),
        unnormed_queries,
        query_gain,
    )
    d_query_raw, grad_query_gain = query_back(
        (d_query_acc * logit_scale).reshape(tokens_per_shard, QUERY_HEADS, HEAD_DIM)
    )
    _, key_backward = jax.vjp(
        lambda raw_heads, norm_gain: head_prepare(raw_heads, norm_gain, local_positions),
        unnormed_keys,
        key_norm_gain,
    )
    raw_key_gradient, key_gain_gradient = key_backward(
        key_gradients.reshape(tokens_per_shard, KEY_VALUE_HEADS, HEAD_DIM)
    )
    d_query_low = d_query_raw.reshape(tokens_per_shard, QUERY_HEADS * HEAD_DIM).astype(
        BRAIN_FLOAT_TYPE
    )
    key_gradient_lowprec = raw_key_gradient.reshape(
        tokens_per_shard, KEY_VALUE_HEADS * HEAD_DIM
    ).astype(BRAIN_FLOAT_TYPE)
    d_value_low = d_values.astype(BRAIN_FLOAT_TYPE)
    grad_query_weight = jnp.einsum(
        "td,tc->dc", normalized_rows, d_query_low, preferred_element_type=SINGLE_FLOAT
    )
    grad_key_weight = jnp.einsum(
        "td,tc->dc", normalized_rows, key_gradient_lowprec, preferred_element_type=SINGLE_FLOAT
    )
    grad_value_weight = jnp.einsum(
        "td,tc->dc", normalized_rows, d_value_low, preferred_element_type=SINGLE_FLOAT
    )
    d_normed = jnp.einsum(
        "tc,dc->td", d_query_low, query_matrix, preferred_element_type=SINGLE_FLOAT
    )
    d_normed = d_normed + jnp.einsum(
        "tc,dc->td", key_gradient_lowprec, key_matrix, preferred_element_type=SINGLE_FLOAT
    )
    d_normed = d_normed + jnp.einsum(
        "tc,dc->td", d_value_low, value_matrix, preferred_element_type=SINGLE_FLOAT
    )
    _, attn_norm_back = jax.vjp(rms_scale, layer_in, attn_gain)
    d_input_norm, grad_attn_gain = attn_norm_back(d_normed)
    grad_input = d_state + d_input_norm
    reduced = (
        lax.psum_scatter(grad_attn_gain, ("ctx", "ws"), scatter_dimension=0, tiled=True),
        lax.psum_scatter(grad_query_weight, ("ctx", "ws"), scatter_dimension=0, tiled=True),
        lax.psum_scatter(grad_key_weight, ("ctx", "ws"), scatter_dimension=0, tiled=True),
        lax.psum_scatter(grad_value_weight, ("ctx", "ws"), scatter_dimension=0, tiled=True),
        lax.psum_scatter(grad_query_gain, ("ctx", "ws"), scatter_dimension=0, tiled=True),
        lax.psum_scatter(key_gain_gradient, ("ctx", "ws"), scatter_dimension=0, tiled=True),
        lax.psum_scatter(grad_out_weight, ("ctx", "ws"), scatter_dimension=0, tiled=True),
        lax.psum_scatter(grad_ffn_gain, ("ctx", "ws"), scatter_dimension=0, tiled=True),
        lax.psum_scatter(grad_router, ("ctx", "ws"), scatter_dimension=0, tiled=True),
    )
    return (
        output[None],
        grad_input[None],
        reduced[0],
        reduced[1],
        reduced[2],
        reduced[3],
        reduced[4],
        reduced[5],
        reduced[6],
        reduced[7],
        reduced[8],
        grad_gate,
        grad_up,
        grad_down,
    )


VMEM_WHOLE = pl.BlockSpec(memory_space=pltpu.VMEM)
VMEM_BYTES = 60 * 2**20
EXTRA = 128


def compiler_params():
    return pltpu.CompilerParams(vmem_limit_bytes=VMEM_BYTES)


def dot_rows(left, right):
    return lax.dot_general(
        left, right, (((1,), (0,)), ((), ())), preferred_element_type=SINGLE_FLOAT
    )


def dot_right_transposed(left, right):
    return lax.dot_general(
        left, right, (((1,), (1,)), ((), ())), preferred_element_type=SINGLE_FLOAT
    )


def dot_left_transposed(left, right):
    return lax.dot_general(
        left, right, (((0,), (0,)), ((), ())), preferred_element_type=SINGLE_FLOAT
    )


def key_range(tile, tile_rows, sequence_tokens, slack):
    half = sequence_tokens // 2
    first_row = tile * tile_rows
    low = 0 if first_row < half + slack else half
    return low, first_row + tile_rows


def stacked_heads(ref, rows, heads):
    return jnp.concatenate(
        [ref[rows, h * HEAD_DIM : (h + 1) * HEAD_DIM] for h in range(heads)], axis=0
    )


def tile_scores(q4, k_ref, segc_ref, segr_ref, low, high, first_row, tile_rows, heads):
    scale = HEAD_DIM ** (-0.5)
    scores = dot_right_transposed(q4, k_ref[low:high, :]) * scale
    span = high - low
    query_place = first_row + lax.broadcasted_iota(jnp.int32, (tile_rows, span), 0)
    key_place = low + lax.broadcasted_iota(jnp.int32, (tile_rows, span), 1)
    allowed = (segc_ref[first_row : first_row + tile_rows, :] == segr_ref[:, low:high]) & (
        key_place <= query_place
    )
    fill = jnp.where(allowed, 0.0, MASK_FILL)
    scores = scores + jnp.concatenate([fill] * heads, axis=0)
    exponent = jnp.exp(scores - jnp.max(scores, axis=-1, keepdims=True))
    return exponent * (1.0 / jnp.sum(exponent, axis=-1, keepdims=True))


def attention_forward_kernel(
    slack,
    x_ref,
    gain_ref,
    w_ref,
    qg_ref,
    kg_ref,
    cos_ref,
    sin_ref,
    segc_ref,
    segr_ref,
    wo_ref,
    normed_ref,
    raw_ref,
    q_ref,
    k_ref,
    v_ref,
    attn_ref,
    part_ref,
):
    tokens = x_ref.shape[0]
    heads = q_ref.shape[1] // HEAD_DIM
    rows_step = 256

    def project(i, carry):
        rows = pl.ds(pl.multiple_of(i * rows_step, rows_step), rows_step)
        x = x_ref[rows, :].astype(SINGLE_FLOAT)
        inverse = lax.rsqrt(jnp.mean(x * x, axis=-1, keepdims=True) + EPS)
        normed = (x * inverse * gain_ref[...]).astype(BRAIN_FLOAT_TYPE)
        normed_ref[rows, :] = normed
        raw = dot_rows(normed, w_ref[...])
        raw_ref[rows, :] = raw[:, : (heads + 1) * HEAD_DIM]
        v_ref[rows, :] = raw[:, (heads + 1) * HEAD_DIM :].astype(BRAIN_FLOAT_TYPE)
        cosine, sine = cos_ref[rows, :], sin_ref[rows, :]
        for h in range(heads + 1):
            part = raw[:, h * HEAD_DIM : (h + 1) * HEAD_DIM]
            gain = qg_ref[...] if h < heads else kg_ref[...]
            scaled = (
                part * lax.rsqrt(jnp.mean(part * part, axis=-1, keepdims=True) + EPS) * gain
            )
            turned = scaled * cosine + pltpu.roll(scaled, HEAD_DIM // 2, 1) * sine
            turned = turned.astype(BRAIN_FLOAT_TYPE)
            if h < heads:
                q_ref[rows, h * HEAD_DIM : (h + 1) * HEAD_DIM] = turned
            else:
                k_ref[rows, :] = turned
        return carry

    lax.fori_loop(0, tokens // rows_step, project, 0)
    tile_rows = 128
    for tile in range(tokens // tile_rows):
        first_row = tile * tile_rows
        rows = slice(first_row, first_row + tile_rows)
        low, high = key_range(tile, tile_rows, tokens, slack)
        probs = tile_scores(
            stacked_heads(q_ref, rows, heads),
            k_ref,
            segc_ref,
            segr_ref,
            low,
            high,
            first_row,
            tile_rows,
            heads,
        )
        attended = dot_rows(probs.astype(BRAIN_FLOAT_TYPE), v_ref[low:high, :])
        for h in range(heads):
            attn_ref[rows, h * HEAD_DIM : (h + 1) * HEAD_DIM] = attended[
                h * tile_rows : (h + 1) * tile_rows
            ].astype(BRAIN_FLOAT_TYPE)

    def project_out(i, carry):
        rows = pl.ds(pl.multiple_of(i * rows_step, rows_step), rows_step)
        part_ref[rows, :] = dot_rows(attn_ref[rows, :], wo_ref[...]).astype(BRAIN_FLOAT_TYPE)
        return carry

    lax.fori_loop(0, tokens // rows_step, project_out, 0)


def attention_forward(slack, x, gain, w, qg, kg, cosine, sine, segc, segr, wo):
    tokens, width = x.shape
    channels = w.shape[1] - 2 * HEAD_DIM
    low = BRAIN_FLOAT_TYPE
    shapes = (
        jax.ShapeDtypeStruct((tokens, width), low),
        jax.ShapeDtypeStruct((tokens, channels + HEAD_DIM), SINGLE_FLOAT),
        jax.ShapeDtypeStruct((tokens, channels), low),
        jax.ShapeDtypeStruct((tokens, HEAD_DIM), low),
        jax.ShapeDtypeStruct((tokens, HEAD_DIM), low),
        jax.ShapeDtypeStruct((tokens, channels), low),
        jax.ShapeDtypeStruct((tokens, width), low),
    )

    def kernel(*refs):
        attention_forward_kernel(slack, *refs)

    return pl.pallas_call(
        kernel,
        out_shape=shapes,
        in_specs=[VMEM_WHOLE] * 10,
        out_specs=[VMEM_WHOLE] * 7,
        compiler_params=compiler_params(),
        name="attention_forward",
    )(x, gain, w, qg, kg, cosine, sine, segc, segr, wo)


def head_backward(turned_gradient, part, gain, cosine, sine):
    scaled_gradient = turned_gradient * cosine - (
        pltpu.roll(turned_gradient, HEAD_DIM // 2, 1) * sine
    )
    inverse = lax.rsqrt(jnp.mean(part * part, axis=-1, keepdims=True) + EPS)
    unit = part * inverse
    gain_gradient = jnp.sum(scaled_gradient * unit, axis=0, keepdims=True)
    unit_gradient = scaled_gradient * gain
    raw_gradient = inverse * (
        unit_gradient - unit * jnp.mean(unit * unit_gradient, axis=-1, keepdims=True)
    )
    return raw_gradient, gain_gradient


def attention_backward_kernel(
    slack,
    dh_ref,
    wo_ref,
    attn_ref,
    q_ref,
    k_ref,
    v_ref,
    raw_ref,
    normed_ref,
    x_ref,
    w_ref,
    qg_ref,
    kg_ref,
    cos_ref,
    sin_ref,
    segc_ref,
    segr_ref,
    gwo_ref,
    gw_ref,
    dpart_ref,
    ggain_ref,
    gheads_ref,
    da_ref,
    draw_ref,
    dk_ref,
    dv_ref,
):
    tokens = x_ref.shape[0]
    heads = q_ref.shape[1] // HEAD_DIM
    scale = HEAD_DIM ** (-0.5)
    rows_step = 256

    def attended_gradient(i, carry):
        rows = pl.ds(pl.multiple_of(i * rows_step, rows_step), rows_step)
        da_ref[rows, :] = dot_right_transposed(dh_ref[rows, :], wo_ref[...]).astype(
            BRAIN_FLOAT_TYPE
        )
        return carry

    lax.fori_loop(0, tokens // rows_step, attended_gradient, 0)

    def out_weight(i, carry):
        columns = pl.ds(pl.multiple_of(i * 512, 512), 512)
        gwo_ref[:, columns] = dot_left_transposed(attn_ref[...], dh_ref[:, columns]).astype(
            gwo_ref.dtype
        )
        return carry

    lax.fori_loop(0, dh_ref.shape[1] // 512, out_weight, 0)
    dk_ref[...] = jnp.zeros_like(dk_ref)
    dv_ref[...] = jnp.zeros_like(dv_ref)
    query_gain_gradient = jnp.zeros((1, HEAD_DIM), SINGLE_FLOAT)
    tile_rows = 128
    for tile in range(tokens // tile_rows):
        first_row = tile * tile_rows
        rows = slice(first_row, first_row + tile_rows)
        low, high = key_range(tile, tile_rows, tokens, slack)
        q4 = stacked_heads(q_ref, rows, heads)
        da4 = stacked_heads(da_ref, rows, heads)
        probs = tile_scores(
            q4, k_ref, segc_ref, segr_ref, low, high, first_row, tile_rows, heads
        )
        d_probs = dot_right_transposed(da4, v_ref[low:high, :])
        delta = jnp.sum(probs * d_probs, axis=-1, keepdims=True)
        d_scores = (probs * (d_probs - delta)).astype(BRAIN_FLOAT_TYPE)
        dq4 = dot_rows(d_scores, k_ref[low:high, :]) * scale
        dk_ref[low:high, :] += dot_left_transposed(d_scores, q4)
        dv_ref[low:high, :] += dot_left_transposed(probs.astype(BRAIN_FLOAT_TYPE), da4)
        for h in range(heads):
            columns = slice(h * HEAD_DIM, (h + 1) * HEAD_DIM)
            raw_gradient, gain_gradient = head_backward(
                dq4[h * tile_rows : (h + 1) * tile_rows],
                raw_ref[rows, columns],
                qg_ref[...],
                cos_ref[rows, :],
                sin_ref[rows, :],
            )
            draw_ref[rows, columns] = raw_gradient.astype(BRAIN_FLOAT_TYPE)
            query_gain_gradient = query_gain_gradient + gain_gradient
    key_columns = slice(heads * HEAD_DIM, (heads + 1) * HEAD_DIM)
    raw_gradient, key_gain_gradient = head_backward(
        dk_ref[...] * scale, raw_ref[:, key_columns], kg_ref[...], cos_ref[...], sin_ref[...]
    )
    draw_ref[:, key_columns] = raw_gradient.astype(BRAIN_FLOAT_TYPE)
    draw_ref[:, (heads + 1) * HEAD_DIM :] = dv_ref[...].astype(BRAIN_FLOAT_TYPE)
    gheads_ref[...] = jnp.concatenate(
        [query_gain_gradient, key_gain_gradient, jnp.zeros((6, HEAD_DIM), SINGLE_FLOAT)], axis=0
    )

    def projection_weight(i, carry):
        columns = pl.ds(pl.multiple_of(i * 256, 256), 256)
        gw_ref[columns, :] = dot_left_transposed(normed_ref[:, columns], draw_ref[...]).astype(
            gw_ref.dtype
        )
        return carry

    lax.fori_loop(0, normed_ref.shape[1] // 256, projection_weight, 0)
    ggain_ref[...] = jnp.zeros_like(ggain_ref)

    def input_gradient(i, carry):
        rows = pl.ds(pl.multiple_of(i * rows_step, rows_step), rows_step)
        d_normed = dot_right_transposed(draw_ref[rows, :], w_ref[...])
        dpart_ref[rows, :] = d_normed.astype(BRAIN_FLOAT_TYPE)
        x = x_ref[rows, :].astype(SINGLE_FLOAT)
        inverse = lax.rsqrt(jnp.mean(x * x, axis=-1, keepdims=True) + EPS)
        ggain_ref[...] += jnp.sum(d_normed * (x * inverse), axis=0, keepdims=True)
        return carry

    lax.fori_loop(0, tokens // rows_step, input_gradient, 0)


def attention_backward(
    slack, dh, wo, attn, q, k, v, raw, normed, x, w, qg, kg, cosine, sine, segc, segr
):
    tokens, width = x.shape
    channels = q.shape[1]
    low = BRAIN_FLOAT_TYPE
    shapes = (
        jax.ShapeDtypeStruct((channels, width), low),
        jax.ShapeDtypeStruct((width, channels + 2 * HEAD_DIM), low),
        jax.ShapeDtypeStruct((tokens, width), low),
        jax.ShapeDtypeStruct((1, width), SINGLE_FLOAT),
        jax.ShapeDtypeStruct((8, HEAD_DIM), SINGLE_FLOAT),
    )

    def kernel(*refs):
        attention_backward_kernel(slack, *refs)

    return pl.pallas_call(
        kernel,
        out_shape=shapes,
        in_specs=[VMEM_WHOLE] * 16,
        out_specs=[VMEM_WHOLE] * 5,
        scratch_shapes=[
            pltpu.VMEM((tokens, channels), low),
            pltpu.VMEM((tokens, channels + 2 * HEAD_DIM), low),
            pltpu.VMEM((tokens, HEAD_DIM), SINGLE_FLOAT),
            pltpu.VMEM((tokens, HEAD_DIM), SINGLE_FLOAT),
        ],
        compiler_params=compiler_params(),
        name="attention_backward",
    )(dh, wo, attn, q, k, v, raw, normed, x, w, qg, kg, cosine, sine, segc, segr)


def expert_kernel(
    capacity,
    expert_ref,
    pay_ref,
    dout_ref,
    wg_ref,
    wu_ref,
    wd_ref,
    outp_ref,
    dp_ref,
    x_ref,
    deo_ref,
    hid_ref,
    dgl_ref,
    dul_ref,
    d_ref,
    g_ref,
    st_ref,
):
    sources, tokens, payload = pay_ref.shape
    width = wg_ref.shape[0]
    experts = (payload - width) // 4
    e = expert_ref[0]
    lane = lax.broadcasted_iota(jnp.int32, (tokens, payload - width), 1)
    slot_lane = lax.broadcasted_iota(jnp.int32, (tokens, capacity), 1).astype(SINGLE_FLOAT)
    row_lane = lax.broadcasted_iota(jnp.int32, (capacity, payload - width), 1)
    is_gate = (row_lane == e) | (row_lane == experts + e)
    for s in range(sources):
        rows = slice(s * capacity, (s + 1) * capacity)
        table = pay_ref[s, :, width:].astype(SINGLE_FLOAT)
        rank = jnp.sum(jnp.where(lane == 2 * experts + e, table, 0.0), axis=-1, keepdims=True)
        pick = (rank == slot_lane).astype(BRAIN_FLOAT_TYPE)
        st_ref[s] = pick
        chosen = dot_left_transposed(pick, pay_ref[s])
        x_ref[rows, :] = chosen[:, :width].astype(BRAIN_FLOAT_TYPE)
        gate = jnp.sum(jnp.where(is_gate, chosen[:, width:], 0.0), axis=-1, keepdims=True)
        g_ref[rows, :] = gate
        d_rows = dot_left_transposed(pick, dout_ref[s])
        d_ref[rows, :] = d_rows.astype(BRAIN_FLOAT_TYPE)
        deo_ref[rows, :] = (gate * d_rows).astype(BRAIN_FLOAT_TYPE)
    x = x_ref[...]
    gate_hidden = dot_rows(x, wg_ref[...])
    up_hidden = dot_rows(x, wu_ref[...])
    sigmoid = 1.0 / (1.0 + jnp.exp(-gate_hidden))
    silu = gate_hidden * sigmoid
    hidden = (silu * up_hidden).astype(BRAIN_FLOAT_TYPE)
    hid_ref[...] = hidden
    d_hidden = dot_right_transposed(deo_ref[...], wd_ref[...])
    d_gate = (d_hidden * up_hidden * sigmoid * (1.0 + gate_hidden * (1.0 - sigmoid))).astype(
        BRAIN_FLOAT_TYPE
    )
    d_up = (d_hidden * silu).astype(BRAIN_FLOAT_TYPE)
    dgl_ref[...] = d_gate
    dul_ref[...] = d_up
    expert_out = dot_rows(hidden, wd_ref[...]).astype(BRAIN_FLOAT_TYPE)
    d_copy = (
        dot_right_transposed(d_gate, wg_ref[...]) + dot_right_transposed(d_up, wu_ref[...])
    ).astype(BRAIN_FLOAT_TYPE)
    for s in range(sources):
        rows = slice(s * capacity, (s + 1) * capacity)
        pick = st_ref[s]
        e_rows = expert_out[rows].astype(SINGLE_FLOAT)
        gate = g_ref[rows, :]
        d_gate_rows = jnp.sum(
            d_ref[rows, :].astype(SINGLE_FLOAT) * e_rows, axis=-1, keepdims=True
        )
        high = d_gate_rows.astype(BRAIN_FLOAT_TYPE).astype(SINGLE_FLOAT)
        extra = jnp.where(row_lane == e, high, 0.0) + jnp.where(
            row_lane == experts + e, d_gate_rows - high, 0.0
        )
        outp_ref[s] = dot_rows(pick, (gate * e_rows).astype(BRAIN_FLOAT_TYPE)).astype(
            BRAIN_FLOAT_TYPE
        )
        dp_ref[s, :, :width] = dot_rows(pick, d_copy[rows]).astype(BRAIN_FLOAT_TYPE)
        dp_ref[s, :, width:] = dot_rows(pick, extra.astype(BRAIN_FLOAT_TYPE)).astype(
            BRAIN_FLOAT_TYPE
        )


def expert_compute(capacity, step_sources, expert, pay, dout, wg, wu, wd):
    sources, tokens, payload = pay.shape
    width, ff = wg.shape
    low = BRAIN_FLOAT_TYPE
    rows = step_sources * capacity
    total = sources * capacity
    once = pl.Buffered(1)
    grid_spec = pltpu.PrefetchScalarGridSpec(
        num_scalar_prefetch=1,
        grid=(sources // step_sources,),
        in_specs=[
            pl.BlockSpec((step_sources, tokens, payload), lambda i, e: (i, 0, 0)),
            pl.BlockSpec((step_sources, tokens, width), lambda i, e: (i, 0, 0)),
            pl.BlockSpec((width, ff), lambda i, e: (0, 0), pipeline_mode=once),
            pl.BlockSpec((width, ff), lambda i, e: (0, 0), pipeline_mode=once),
            pl.BlockSpec((ff, width), lambda i, e: (0, 0), pipeline_mode=once),
        ],
        out_specs=[
            pl.BlockSpec((step_sources, tokens, width), lambda i, e: (i, 0, 0)),
            pl.BlockSpec((step_sources, tokens, payload), lambda i, e: (i, 0, 0)),
            pl.BlockSpec((rows, width), lambda i, e: (i, 0)),
            pl.BlockSpec((rows, width), lambda i, e: (i, 0)),
            pl.BlockSpec((rows, ff), lambda i, e: (i, 0)),
            pl.BlockSpec((rows, ff), lambda i, e: (i, 0)),
            pl.BlockSpec((rows, ff), lambda i, e: (i, 0)),
        ],
        scratch_shapes=[
            pltpu.VMEM((rows, width), low),
            pltpu.VMEM((rows, 1), SINGLE_FLOAT),
            pltpu.VMEM((step_sources, tokens, capacity), low),
        ],
    )

    def kernel(*refs):
        expert_kernel(capacity, *refs)

    return pl.pallas_call(
        kernel,
        grid_spec=grid_spec,
        out_shape=(
            jax.ShapeDtypeStruct((sources, tokens, width), low),
            jax.ShapeDtypeStruct((sources, tokens, payload), low),
            jax.ShapeDtypeStruct((total, width), low),
            jax.ShapeDtypeStruct((total, width), low),
            jax.ShapeDtypeStruct((total, ff), low),
            jax.ShapeDtypeStruct((total, ff), low),
            jax.ShapeDtypeStruct((total, ff), low),
        ),
        compiler_params=compiler_params(),
        name="expert_compute",
    )(expert, pay, dout, wg, wu, wd)


MESH = pl.DeviceIdType.MESH
ANYWHERE = pl.BlockSpec(memory_space=pl.ANY)
LINE = 4


def place():
    c, w = lax.axis_index("ctx"), lax.axis_index("ws")
    return c // 2, c % 2, w // 2, w % 2


def device_at(z, y, x, k):
    return (z * 2 + y, x * 2 + k)


def slot_of(z, y, x, k):
    return ((z * 2 + y) * 2 + x) * 2 + k


def line_order(z):
    upper = z // 2
    return [z, z + 1 - 2 * upper, 2 - 2 * (z % 2) + upper, 3 - 3 * upper]


def remote(source, target, send, recv, device):
    return pltpu.make_async_remote_copy(
        src_ref=source,
        dst_ref=target,
        send_sem=send,
        recv_sem=recv,
        device_id=device,
        device_id_type=MESH,
    )


def meet(z, y, x, k, around):
    barrier = pltpu.get_barrier_semaphore()

    def greet(device):
        pl.semaphore_signal(barrier, inc=1, device_id=device, device_id_type=MESH)

    @pl.when(z < LINE - 1)
    def _():
        greet(device_at(z + 1, y, x, k))

    @pl.when(z > 0)
    def _():
        greet(device_at(z - 1, y, x, k))

    for device in around:
        greet(device)
    pl.semaphore_wait(barrier, len(around) + 1 + z * (LINE - 1 - z) // 2)


class Sends:
    def __init__(self, semaphores):
        self.semaphores = semaphores
        self.started = []

    def start(self, source, target, recv, device, condition=None):
        copy = remote(source, target, self.semaphores.at[len(self.started)], recv, device)
        if condition is None:
            copy.start()
        else:
            pl.when(condition)(copy.start)
        self.started.append((condition, copy))

    def finish(self):
        for condition, copy in self.started:
            if condition is None:
                copy.wait_send()
            else:
                pl.when(condition)(copy.wait_send)


def arrived(target, recv, device):
    remote(target, target, recv, recv, device).wait_recv()


def along_line(z, y, x, k, block, i, order, start):
    if i == 0:
        up, down = z < LINE - 1, z > 0
    else:
        below = order[i] < z
        up, down = below & (z < LINE - 1), jnp.logical_not(below) & (z > 0)
    start(block, device_at(z + 1, y, x, k), up)
    start(block, device_at(z - 1, y, x, k), down)


def gather_all_kernel(source, out, local, send_sems, recv_sems):
    z, y, x, k = place()
    order = line_order(z)
    along_x, along_y = device_at(z, y, 1 - x, k), device_at(z, 1 - y, x, k)
    sibling = device_at(z, y, x, 1 - k)
    meet(z, y, x, k, (along_x, along_y, sibling))
    sends = Sends(send_sems)
    mine = slot_of(z, y, x, k)
    own = pltpu.make_async_copy(source, out.at[mine], local)
    own.start()

    def pass_on(slot, device, condition=None):
        block = source if slot is mine else out.at[slot]
        sends.start(block, out.at[slot], recv_sems.at[slot], device, condition)

    def wait(slot):
        arrived(out.at[slot], recv_sems.at[slot], along_x)

    def column(i):
        slot = mine if i == 0 else slot_of(order[i], y, x, k)
        if i > 0:
            wait(slot)
        along_line(z, y, x, k, slot, i, order, pass_on)
        pass_on(slot, along_x)
        pass_on(slot, along_y)
        pass_on(slot, sibling)

    def from_x(i):
        slot = slot_of(order[i], y, 1 - x, k)
        wait(slot)
        pass_on(slot, sibling)
        if i == 3:
            for j in (0, 1):
                pass_on(slot_of(order[j], y, 1 - x, k), along_y)

    def from_y(i):
        slot = slot_of(order[i], 1 - y, x, k)
        wait(slot)
        pass_on(slot, sibling)
        if i == 3:
            for j in (2, 3):
                pass_on(slot_of(order[j], 1 - y, x, k), along_x)

    def from_corner(i):
        slot = slot_of(order[i], 1 - y, 1 - x, k)
        wait(slot)
        pass_on(slot, sibling)

    column(0)
    for i in (1, 2, 3):
        column(i)
        from_x(i - 1)
        from_y(i - 1)
    from_x(3)
    from_y(3)
    for i in range(4):
        from_corner(i)
    for i in range(4):
        for dy in (y, 1 - y):
            for dx in (x, 1 - x):
                wait(slot_of(order[i], dy, dx, 1 - k))
    own.wait()
    sends.finish()


def gather_all(block, collective_id):
    return pl.pallas_call(
        gather_all_kernel,
        out_shape=jax.ShapeDtypeStruct((32,) + block.shape, block.dtype),
        in_specs=[ANYWHERE],
        out_specs=ANYWHERE,
        scratch_shapes=[
            pltpu.SemaphoreType.DMA,
            pltpu.SemaphoreType.DMA((40,)),
            pltpu.SemaphoreType.DMA((32,)),
        ],
        compiler_params=pltpu.CompilerParams(collective_id=collective_id, has_side_effects=True),
        name="gather_all",
    )(block)


def add_blocks(target, *terms):
    rows = target.shape[0]

    def step(i, carry):
        part = pl.ds(pl.multiple_of(i * 16, 16), 16)
        total = terms[0][part, :].astype(SINGLE_FLOAT)
        for term in terms[1:]:
            total = total + term[part, :].astype(SINGLE_FLOAT)
        target[part, :] = total.astype(target.dtype)
        return carry

    lax.fori_loop(0, rows // 16, step, 0)


def scatter_line(z, y, x, k, order, total, owned, up_ref, down_ref, up_sems, down_sems, sends, out, after):
    above, below = device_at(z + 1, y, x, k), device_at(z - 1, y, x, k)
    for i in (3, 2, 1):
        total(i)
        chip = order[i]
        upward = chip > z
        block = owned(i)

        @pl.when(upward & (z > 0))
        def _():
            arrived(up_ref.at[chip], up_sems.at[chip], below)
            add_blocks(block, block, up_ref.at[chip])

        @pl.when(jnp.logical_not(upward) & (z < LINE - 1))
        def _():
            arrived(down_ref.at[chip], down_sems.at[chip], above)
            add_blocks(block, block, down_ref.at[chip])

        sends.start(block, up_ref.at[chip], up_sems.at[chip], above, upward)
        sends.start(
            block, down_ref.at[chip], down_sems.at[chip], below, jnp.logical_not(upward)
        )
        after(i)
    total(0)
    block = owned(0)

    @pl.when(z > 0)
    def _():
        arrived(up_ref.at[z], up_sems.at[z], below)

    @pl.when(z < LINE - 1)
    def _():
        arrived(down_ref.at[z], down_sems.at[z], above)

    @pl.when(z == 0)
    def _():
        add_blocks(out, block, down_ref.at[z])

    @pl.when(z == LINE - 1)
    def _():
        add_blocks(out, block, up_ref.at[z])

    @pl.when((z > 0) & (z < LINE - 1))
    def _():
        add_blocks(out, block, up_ref.at[z], down_ref.at[z])


def scatter_all_kernel(
    part,
    out,
    own_ref,
    sibling_ref,
    corner_ref,
    x_ref,
    y_ref,
    up_ref,
    down_ref,
    load_sems,
    sibling_sems,
    corner_sems,
    x_sems,
    y_sems,
    up_sems,
    down_sems,
    send_sems,
):
    z, y, x, k = place()
    order = line_order(z)
    along_x, along_y = device_at(z, y, 1 - x, k), device_at(z, 1 - y, x, k)
    sibling = device_at(z, y, x, 1 - k)
    meet(z, y, x, k, (along_x, along_y, sibling))
    sends = Sends(send_sems)
    home, on_x, on_y, corner = 0, 1, 2, 3
    where = {home: (y, x), on_x: (y, 1 - x), on_y: (1 - y, x), corner: (1 - y, 1 - x)}
    turn = [(i, corner) for i in (3, 2, 1, 0)]
    for i in (3, 2, 1, 0):
        turn += [(i, on_x), (i, on_y)]
    turn += [(i, home) for i in (3, 2, 1, 0)]
    loads = {}
    for i, r in turn:
        j = i * 4 + r
        dy, dx = where[r]
        sends.start(
            part.at[slot_of(order[i], dy, dx, 1 - k)],
            sibling_ref.at[j],
            sibling_sems.at[j],
            sibling,
        )
        loads[j] = pltpu.make_async_copy(
            part.at[slot_of(order[i], dy, dx, k)], own_ref.at[j], load_sems.at[j]
        )
        loads[j].start()

    def gather(i, r, *extra):
        j = i * 4 + r
        loads[j].wait()
        arrived(sibling_ref.at[j], sibling_sems.at[j], sibling)
        add_blocks(own_ref.at[j], own_ref.at[j], sibling_ref.at[j], *extra)
        return own_ref.at[j]

    for i in (3, 2, 1, 0):
        sends.start(
            gather(i, corner), corner_ref.at[i], corner_sems.at[i], along_y if i < 2 else along_x
        )

    def cross(i):
        arrived(corner_ref.at[i], corner_sems.at[i], along_x)
        extra = (corner_ref.at[i],)
        for_x = gather(i, on_x, *(extra if i < 2 else ()))
        for_y = gather(i, on_y, *(extra if i >= 2 else ()))
        sends.start(for_x, x_ref.at[i], x_sems.at[i], along_x)
        sends.start(for_y, y_ref.at[i], y_sems.at[i], along_y)

    def total(i):
        arrived(x_ref.at[i], x_sems.at[i], along_x)
        arrived(y_ref.at[i], y_sems.at[i], along_y)
        if i > 0:
            cross(i - 1)
        gather(i, home, x_ref.at[i], y_ref.at[i])

    cross(3)
    scatter_line(
        z, y, x, k, order, total, lambda i: own_ref.at[i * 4 + home],
        up_ref, down_ref, up_sems, down_sems, sends, out, lambda i: None,
    )
    sends.finish()


def scatter_all(part, collective_id, dtype):
    shape, low = part.shape[1:], part.dtype
    dma = pltpu.SemaphoreType.DMA
    return pl.pallas_call(
        scatter_all_kernel,
        out_shape=jax.ShapeDtypeStruct(shape, dtype),
        in_specs=[ANYWHERE],
        out_specs=VMEM_WHOLE,
        scratch_shapes=[pltpu.VMEM((n,) + shape, low) for n in (16, 16, 4, 4, 4, 4, 4)]
        + [dma((n,)) for n in (16, 16, 4, 4, 4, 4, 4)]
        + [dma((40,))],
        compiler_params=pltpu.CompilerParams(
            collective_id=collective_id, has_side_effects=True, vmem_limit_bytes=VMEM_BYTES
        ),
        name="scatter_all",
    )(part)


def halves(ref, z, y):
    half = ref.shape[0] // 16
    c = z * 2 + y
    return [
        ref.at[pl.ds(pl.multiple_of(half * b, half), half), :] for b in (c, 15 - c)
    ]


def split_rows(ref):
    half = ref.shape[0] // 2
    return [ref.at[0:half, :], ref.at[half : 2 * half, :]]


class RowGather:
    def __init__(self, source, out, sends, locals_, semaphores, at, order, along_y):
        self.source, self.out, self.sends, self.semaphores = source, out, sends, semaphores
        self.at, self.order, self.along_y = at, order, along_y
        z, y, x, k = at
        self.own = [
            pltpu.make_async_copy(a, b, locals_.at[n])
            for n, (a, b) in enumerate(zip(split_rows(source), halves(out, z, y)))
        ]
        for copy in self.own:
            copy.start()

    def column(self, i):
        z, y, x, k = self.at
        chip = self.order[i]
        pieces = halves(self.out, chip, y)
        if i > 0:
            self.wait(chip, y)
        for n in (0, 1):
            block = split_rows(self.source)[n] if i == 0 else pieces[n]
            recv = self.semaphores.at[n, chip * 2 + y]

            def start(_, device, condition=None):
                self.sends.start(block, pieces[n], recv, device, condition)

            along_line(z, y, x, k, None, i, self.order, start)
            start(None, self.along_y)

    def wait(self, chip, y):
        for n, piece in enumerate(halves(self.out, chip, y)):
            arrived(piece, self.semaphores.at[n, chip * 2 + y], self.along_y)

    def finish(self):
        y = self.at[1]
        for i in range(4):
            self.wait(self.order[i], 1 - y)
        for copy in self.own:
            copy.wait()


def gather_rows_kernel(source, out, local_sems, send_sems, recv_sems):
    at = place()
    z, y, x, k = at
    along_y = device_at(z, 1 - y, x, k)
    meet(z, y, x, k, (along_y,))
    sends = Sends(send_sems)
    rows = RowGather(source, out, sends, local_sems, recv_sems, at, line_order(z), along_y)
    for i in range(4):
        rows.column(i)
    rows.finish()
    sends.finish()


def gather_rows(block, collective_id):
    rows, width = block.shape
    dma = pltpu.SemaphoreType.DMA
    return pl.pallas_call(
        gather_rows_kernel,
        out_shape=jax.ShapeDtypeStruct((8 * rows, width), block.dtype),
        in_specs=[ANYWHERE],
        out_specs=ANYWHERE,
        scratch_shapes=[dma((2,)), dma((24,)), dma((2, 8))],
        compiler_params=pltpu.CompilerParams(collective_id=collective_id, has_side_effects=True),
        name="gather_rows",
    )(block)


class RowScatter:
    def __init__(self, part, out, buffers, semaphores, sends, at, order, along_y):
        self.part, self.out, self.sends, self.at, self.order = part, out, sends, at, order
        self.along_y = along_y
        self.own_ref, self.y_ref, self.up_ref, self.down_ref = buffers
        self.load_sems, self.y_sems, self.up_sems, self.down_sems = semaphores
        z, y, x, k = at
        self.loads = {}
        for i in (3, 2, 1, 0):
            self.loads[i] = [
                pltpu.make_async_copy(a, b, self.load_sems.at[n, i])
                for n, (a, b) in enumerate(
                    zip(halves(part, order[i], y), split_rows(self.own_ref.at[i]))
                )
            ]
            for copy in self.loads[i]:
                copy.start()
        self.cross(3)

    def cross(self, i):
        y = self.at[1]
        for n, (a, b) in enumerate(
            zip(halves(self.part, self.order[i], 1 - y), split_rows(self.y_ref.at[i]))
        ):
            self.sends.start(a, b, self.y_sems.at[n, i], self.along_y)

    def total(self, i):
        for copy in self.loads[i]:
            copy.wait()
        for n, piece in enumerate(split_rows(self.y_ref.at[i])):
            arrived(piece, self.y_sems.at[n, i], self.along_y)
        if i > 0:
            self.cross(i - 1)
        add_blocks(self.own_ref.at[i], self.own_ref.at[i], self.y_ref.at[i])

    def run(self, after=lambda i: None):
        z, y, x, k = self.at
        scatter_line(
            z, y, x, k, self.order, self.total, lambda i: self.own_ref.at[i],
            self.up_ref, self.down_ref, self.up_sems, self.down_sems, self.sends, self.out,
            after,
        )


def row_scatter_scratch(rows, width, low):
    dma = pltpu.SemaphoreType.DMA
    return [pltpu.VMEM((4, rows, width), low)] * 4 + [
        dma((2, 4)),
        dma((2, 4)),
        dma((4,)),
        dma((4,)),
    ]


def scatter_rows_kernel(part, out, *scratch):
    at = place()
    z, y, x, k = at
    along_y = device_at(z, 1 - y, x, k)
    meet(z, y, x, k, (along_y,))
    sends = Sends(scratch[8])
    rows = RowScatter(part, out, scratch[:4], scratch[4:8], sends, at, line_order(z), along_y)
    rows.run()
    sends.finish()


def scatter_rows(part, collective_id):
    rows, width = part.shape[0] // 8, part.shape[1]
    return pl.pallas_call(
        scatter_rows_kernel,
        out_shape=jax.ShapeDtypeStruct((rows, width), SINGLE_FLOAT),
        in_specs=[ANYWHERE],
        out_specs=VMEM_WHOLE,
        scratch_shapes=row_scatter_scratch(rows, width, part.dtype)
        + [pltpu.SemaphoreType.DMA((16,))],
        compiler_params=pltpu.CompilerParams(
            collective_id=collective_id, has_side_effects=True, vmem_limit_bytes=VMEM_BYTES
        ),
        name="scatter_rows",
    )(part)


def ring_of(c, w):
    return [((c + t) % 8, w) for t in range(1, 8)]


def gather_start_kernel(
    x_in,
    slab_in,
    wo_in,
    x_out,
    slab_out,
    wo_out,
    local_sems,
    send_sems,
    x_sems,
    slab_sems,
    wo_sems,
):
    at = place()
    z, y, x, k = at
    c, w = z * 2 + y, x * 2 + k
    along_x, along_y = device_at(z, y, 1 - x, k), device_at(z, 1 - y, x, k)
    sibling = device_at(z, y, x, 1 - k)
    others = ring_of(c, w)
    barrier = pltpu.get_barrier_semaphore()
    for device in others + [along_x, sibling]:
        pl.semaphore_signal(barrier, inc=1, device_id=device, device_id_type=MESH)
    pl.semaphore_wait(barrier, 9)
    sends = Sends(send_sems)
    rows = RowGather(
        x_in, x_out, sends, local_sems.at[pl.ds(0, 2)], x_sems, at, line_order(z), along_y
    )
    wo_rows = wo_in.shape[0]

    def wo_at(w):
        return wo_out.at[pl.ds(pl.multiple_of(w * wo_rows, wo_rows), wo_rows), :]

    mine = c * 4 + w
    local = [
        pltpu.make_async_copy(slab_in.at[c], slab_out.at[mine], local_sems.at[2]),
        pltpu.make_async_copy(wo_in, wo_at(w), local_sems.at[3]),
    ]
    for copy in local:
        copy.start()

    def pass_on(slot, device, block=None):
        block = slab_out.at[slot] if block is None else block
        sends.start(block, slab_out.at[slot], slab_sems.at[slot], device)

    def take(source, w):
        slot = source * 4 + w
        arrived(slab_out.at[slot], slab_sems.at[slot], along_x)
        return slot

    rows.column(0)
    for device in (along_x, sibling):
        sends.start(wo_in, wo_at(w), wo_sems.at[w], device)
        pass_on(mine, device, slab_in.at[c])
    for device in others:
        sends.start(slab_in.at[device[0]], slab_out.at[mine], slab_sems.at[mine], device)

    def onward():
        for t in range(1, 8):
            slot = take((c + 8 - t) % 8, w)
            pass_on(slot, along_x)
            pass_on(slot, sibling)

    def across():
        beside = (1 - x) * 2 + k
        arrived(wo_at(beside), wo_sems.at[beside], along_x)
        sends.start(wo_at(beside), wo_at(beside), wo_sems.at[beside], sibling)
        for t in range(8):
            pass_on(take((c + 8 - t) % 8, beside), sibling)

    rows.column(1)
    rows.column(2)
    onward()
    rows.column(3)
    across()
    for other in (x * 2 + 1 - k, (1 - x) * 2 + 1 - k):
        for t in range(8):
            take((c + 8 - t) % 8, other)
        arrived(wo_at(other), wo_sems.at[other], along_x)
    rows.finish()
    for copy in local:
        copy.wait()
    sends.finish()


def gather_start(x, slabs, wo, collective_id):
    tokens, width = x.shape
    low = BRAIN_FLOAT_TYPE
    dma = pltpu.SemaphoreType.DMA
    return pl.pallas_call(
        gather_start_kernel,
        out_shape=(
            jax.ShapeDtypeStruct((8 * tokens, width), low),
            jax.ShapeDtypeStruct((32,) + slabs.shape[1:], low),
            jax.ShapeDtypeStruct((4 * wo.shape[0], width), low),
        ),
        in_specs=[ANYWHERE] * 3,
        out_specs=[ANYWHERE] * 3,
        scratch_shapes=[dma((4,)), dma((64,)), dma((2, 8)), dma((32,)), dma((4,))],
        compiler_params=pltpu.CompilerParams(collective_id=collective_id, has_side_effects=True),
        name="gather_start",
    )(x, slabs, wo)


def scatter_end_kernel(
    part,
    gw,
    gwo,
    small,
    rows_out,
    gw_out,
    gwo_out,
    small_out,
    *scratch,
):
    row_scratch, row_sems = scratch[:4], scratch[4:8]
    (
        send_sems,
        load_sems,
        core_sems,
        x_sems,
        to_sems,
        small_to_sems,
        gw_own,
        gw_core,
        gw_x,
        gwo_own,
        gwo_core,
        gwo_x,
        small_own,
        small_core,
        small_x,
        small_to,
    ) = scratch[8:]
    at = place()
    z, y, x, k = at
    c, w = z * 2 + y, x * 2 + k
    along_x, along_y = device_at(z, y, 1 - x, k), device_at(z, 1 - y, x, k)
    sibling = device_at(z, y, x, 1 - k)
    others = ring_of(c, w)
    barrier = pltpu.get_barrier_semaphore()
    for device in others + [along_x, sibling]:
        pl.semaphore_signal(barrier, inc=1, device_id=device, device_id_type=MESH)
    pl.semaphore_wait(barrier, 9)
    sends = Sends(send_sems)
    rows = RowScatter(
        part, rows_out, row_scratch, row_sems, sends, at, line_order(z), along_y
    )
    loads = []
    for n, (source, core, own) in enumerate(
        (
            (small, small_core, small_own),
            (gw, gw_core, gw_own),
            (gwo, gwo_core, gwo_own),
        )
    ):
        outer = (slice(None),) * (len(source.shape) - 3)
        sends.start(source.at[(*outer, 1 - k)], core, core_sems.at[n], sibling)
        loads.append(pltpu.make_async_copy(source.at[(*outer, k)], own, load_sems.at[n]))
        loads[-1].start()

    def fold(n, own, core):
        loads[n].wait()
        arrived(core, core_sems.at[n], sibling)
        flat = [(i,) for i in range(own.shape[0])]
        for extent in own.shape[1:-2]:
            flat = [index + (j,) for index in flat for j in range(extent)]
        for i in flat:
            add_blocks(own.at[i], own.at[i], core.at[i])

    fold(0, small_own, small_core)
    sends.start(small_own.at[:, 1 - x], small_x, x_sems.at[0], along_x)
    fold(1, gw_own, gw_core)
    sends.start(gw_own.at[:, 1 - x], gw_x, x_sems.at[1], along_x)
    fold(2, gwo_own, gwo_core)
    keep = []

    def weights(i):
        if i == 2:
            sends.start(gwo_own.at[1 - x], gwo_x, x_sems.at[2], along_x)
            spread()

    def spread():
        for n, own, far in ((0, small_own, small_x), (1, gw_own, gw_x)):
            arrived(far, x_sems.at[n], along_x)
            for i in range(8):
                add_blocks(own.at[i, x], own.at[i, x], far.at[i])
            target, sems = (small_to, small_to_sems) if n == 0 else (gw_out, to_sems)
            keep.append(
                pltpu.make_async_copy(own.at[c, x], target.at[c], load_sems.at[3 + n])
            )
            keep[-1].start()
            for device in others:
                sends.start(own.at[device[0], x], target.at[c], sems.at[c], device)

    rows.run(weights)
    arrived(gwo_x, x_sems.at[2], along_x)
    add_blocks(gwo_out, gwo_own.at[x], gwo_x)
    for copy in keep:
        copy.wait()
    for t in range(1, 8):
        source = (c + 8 - t) % 8
        arrived(small_to.at[source], small_to_sems.at[source], along_x)
        arrived(gw_out.at[source], to_sems.at[source], along_x)
    total = small_to[0]
    for i in range(1, 8):
        total = total + small_to[i]
    small_out[...] = total
    sends.finish()


def scatter_end(part, gw, gwo, small, collective_id):
    rows, width = part.shape[0] // 8, part.shape[1]
    low = part.dtype
    dma, vmem = pltpu.SemaphoreType.DMA, pltpu.VMEM
    r, n = gw.shape[3:]
    ro, no = gwo.shape[2:]
    rs, ns = small.shape[3:]
    return pl.pallas_call(
        scatter_end_kernel,
        out_shape=(
            jax.ShapeDtypeStruct((rows, width), SINGLE_FLOAT),
            jax.ShapeDtypeStruct((8, r, n), low),
            jax.ShapeDtypeStruct((ro, no), SINGLE_FLOAT),
            jax.ShapeDtypeStruct((rs, ns), SINGLE_FLOAT),
        ),
        in_specs=[ANYWHERE] * 4,
        out_specs=[VMEM_WHOLE, ANYWHERE, VMEM_WHOLE, VMEM_WHOLE],
        scratch_shapes=row_scatter_scratch(rows, width, low)
        + [dma((48,)), dma((5,)), dma((3,)), dma((3,)), dma((8,)), dma((8,))]
        + [vmem((8, 2, r, n), low), vmem((8, 2, r, n), low), vmem((8, r, n), low)]
        + [vmem((2, ro, no), low), vmem((2, ro, no), low), vmem((ro, no), low)]
        + [vmem((8, 2, rs, ns), SINGLE_FLOAT), vmem((8, 2, rs, ns), SINGLE_FLOAT)]
        + [vmem((8, rs, ns), SINGLE_FLOAT), vmem((8, rs, ns), SINGLE_FLOAT)],
        compiler_params=pltpu.CompilerParams(
            collective_id=collective_id, has_side_effects=True, vmem_limit_bytes=VMEM_BYTES
        ),
        name="scatter_end",
    )(part, gw, gwo, small)


def natural_order(blocks):
    count, rows, width = blocks.shape
    half = rows // 2
    first = blocks[:, :half].reshape(count * half, width)
    second = blocks[::-1, half:].reshape(count * half, width)
    return jnp.concatenate([first, second], axis=0)


def device_order(rows, count):
    total, width = rows.shape
    half = total // count // 2
    first = rows[: total // 2].reshape(count, half, width)
    second = rows[total // 2 :].reshape(count, half, width)[::-1]
    return jnp.concatenate([first, second], axis=1)


def norm_backward(gradient, values, gain):
    inverse = lax.rsqrt(jnp.mean(values * values, axis=-1, keepdims=True) + EPS)
    unit = values * inverse
    scaled = gradient * gain
    d_values = inverse * (scaled - unit * jnp.mean(unit * scaled, axis=-1, keepdims=True))
    return d_values, jnp.sum(gradient * unit, axis=0)


def tensor_body(
    inputs,
    grad_output,
    routes,
    doc_lengths,
    norm_attn,
    w_query,
    key_projection,
    value_projection,
    query_norm,
    key_norm,
    w_out,
    norm_ffn,
    w_router,
    expert_gate,
    expert_up,
    expert_down,
):
    ctx_count = lax.axis_size("ctx")
    ws_count = lax.axis_size("ws")
    device_count = ctx_count * ws_count
    tokens = inputs.shape[1]
    width = inputs.shape[2]
    sequence_tokens = tokens * ctx_count
    expert_count = w_router.shape[1]
    capacity = tokens * TOPK * 3 // (2 * device_count)
    heads = QUERY_HEADS // ctx_count
    group = QUERY_HEADS // KEY_VALUE_HEADS
    slack = tokens // 2
    ctx_index = lax.axis_index("ctx")
    both = ("ctx", "ws")
    me = ctx_index * ws_count + lax.axis_index("ws")
    small = jnp.concatenate([norm_attn, norm_ffn, query_norm, key_norm, w_router.reshape(-1)])
    columns = (heads + 2) * HEAD_DIM
    small = jnp.pad(small, (0, 16 * columns - small.shape[0])).reshape(16, columns)
    slabs = []
    for c in range(ctx_count):
        kv = c * heads // group
        slab = jnp.concatenate(
            [
                w_query[:, c * heads * HEAD_DIM : (c + 1) * heads * HEAD_DIM],
                key_projection[:, kv * HEAD_DIM : (kv + 1) * HEAD_DIM],
                value_projection[:, kv * HEAD_DIM : (kv + 1) * HEAD_DIM],
            ],
            axis=1,
        )
        slabs.append(jnp.concatenate([slab, small], axis=0))
    owned, few = width // device_count, query_norm.shape[0]
    x_all, slabs, wo_all = gather_start(inputs[0], jnp.stack(slabs), w_out, 1)
    w_all = slabs[:, :owned].reshape(width, columns)
    small = slabs[:, owned:].reshape(device_count, 16 * columns)
    attn_gain = small[:, :owned].reshape(width).astype(SINGLE_FLOAT)
    ffn_gain = small[:, owned : 2 * owned].reshape(width).astype(SINGLE_FLOAT)
    at = 2 * owned
    query_gain = small[:, at : at + few].reshape(HEAD_DIM).astype(SINGLE_FLOAT)
    key_gain = small[:, at + few : at + 2 * few].reshape(HEAD_DIM).astype(SINGLE_FLOAT)
    at = at + 2 * few
    router_matrix = small[:, at : at + owned * expert_count].reshape(width, expert_count)

    places = jnp.arange(sequence_tokens, dtype=jnp.int32)
    segments = segment_ids(doc_lengths[0], places)
    half = HEAD_DIM // 2
    frequency = THETA ** (-2.0 * jnp.arange(half, dtype=SINGLE_FLOAT) / HEAD_DIM)
    angle = places.astype(SINGLE_FLOAT)[:, None] * frequency[None, :]
    cosine, sine = jnp.cos(angle), jnp.sin(angle)
    cosine = jnp.concatenate([cosine, cosine], axis=1)
    sine = jnp.concatenate([-sine, sine], axis=1)
    segc, segr = segments[:, None], segments[None, :]
    qg, kg = query_gain[None, :], key_gain[None, :]
    own_places = jnp.arange(tokens, dtype=jnp.int32)
    own_places = jnp.where(
        own_places < tokens // 2,
        ctx_index * (tokens // 2) + own_places,
        (2 * ctx_count - 2 - ctx_index) * (tokens // 2) + own_places,
    )
    own_segments = segment_ids(doc_lengths[0], own_places)
    validity = own_segments < doc_lengths.shape[1]
    d_layer = jnp.where(validity[:, None], grad_output[0], 0.0).astype(BRAIN_FLOAT_TYPE)

    normed, raw, q, k, v, attn, part = attention_forward(
        slack, x_all, attn_gain[None, :], w_all, qg, kg, cosine, sine, segc, segr, wo_all
    )
    branch = scatter_rows(part, 2)
    layer_in = inputs[0].astype(SINGLE_FLOAT)
    hidden_state = layer_in + branch
    mixed = rms_scale(hidden_state, ffn_gain).astype(BRAIN_FLOAT_TYPE)
    logits = jnp.dot(mixed, router_matrix, preferred_element_type=SINGLE_FLOAT)
    own_routes = routes[0]
    hit = jnp.any(
        own_routes[:, :, None] == jnp.arange(expert_count, dtype=jnp.int32)[None, None, :], axis=1
    )
    masked = jnp.where(hit, logits, MASK_FILL)
    exponent = jnp.exp(masked - jnp.max(masked, axis=-1, keepdims=True))
    gates = exponent / jnp.sum(exponent, axis=-1, keepdims=True)
    hits = hit.astype(BRAIN_FLOAT_TYPE)
    earlier = jnp.tril(jnp.ones((tokens, tokens), BRAIN_FLOAT_TYPE), -1)
    rank = jnp.dot(earlier, hits, preferred_element_type=SINGLE_FLOAT)
    rank = jnp.where(hit, rank, -1.0).astype(BRAIN_FLOAT_TYPE)
    gate_high = gates.astype(BRAIN_FLOAT_TYPE)
    gate_low = (gates - gate_high.astype(SINGLE_FLOAT)).astype(BRAIN_FLOAT_TYPE)
    payload = jnp.concatenate(
        [mixed, gate_high, gate_low, rank, jnp.zeros_like(rank)], axis=1
    )
    pay_all = gather_all(payload, 3)
    dout_all = gather_all(d_layer, 7)
    out_part, d_part, x_rows, d_rows, hidden, d_gate, d_up = expert_compute(
        capacity, 4, me.astype(jnp.int32).reshape(1), pay_all, dout_all, expert_gate[0], expert_up[0], expert_down[0]
    )
    d_back = scatter_all(d_part, 4, SINGLE_FLOAT)
    moe_sum = scatter_all(out_part, 8, SINGLE_FLOAT)
    output = (hidden_state + moe_sum).astype(BRAIN_FLOAT_TYPE)
    grad_gate = dot_left_transposed(x_rows, d_gate)[None]
    grad_up = dot_left_transposed(x_rows, d_up)[None]
    grad_down = dot_left_transposed(hidden, d_rows)[None]

    table = d_back[:, width:]
    d_gates = table[:, :expert_count] + table[:, expert_count : 2 * expert_count]
    d_chosen = gates * (d_gates - jnp.sum(gates * d_gates, axis=-1, keepdims=True))
    d_logits = d_chosen.astype(BRAIN_FLOAT_TYPE)
    d_mixed = d_back[:, :width] + dot_right_transposed(
        d_logits, router_matrix
    )
    grad_router = dot_left_transposed(mixed, d_logits)
    d_state_norm, grad_ffn_gain = norm_backward(d_mixed, hidden_state, ffn_gain)
    d_state = d_layer.astype(SINGLE_FLOAT) + d_state_norm
    d_state_low = d_state.astype(BRAIN_FLOAT_TYPE)
    dh_all = gather_rows(d_state_low, 5)
    gwo, gw, dpart, ggain, gheads = attention_backward(
        slack, dh_all, wo_all, attn, q, k, v, raw, normed, x_all, w_all, qg, kg, cosine, sine, segc, segr
    )
    blocks = (ctx_count, ws_count // 2, 2)
    small = jnp.concatenate(
        [
            ggain.reshape(device_count, owned),
            grad_ffn_gain.reshape(device_count, owned),
            gheads[0].reshape(device_count, few),
            gheads[1].reshape(device_count, few),
            grad_router.reshape(device_count, owned * expert_count),
        ],
        axis=1,
    )
    small = jnp.pad(small, ((0, 0), (0, 32 * 128 - small.shape[1]))).reshape(*blocks, 32, 128)
    d_normed, gw, grad_wo, small = scatter_end(
        dpart,
        gw.reshape(*blocks, owned, columns),
        gwo.reshape(*blocks[1:], w_out.shape[0], width),
        small,
        6,
    )
    small = small.reshape(-1)
    d_input_norm, _ = norm_backward(d_normed, layer_in, attn_gain)
    grad_input = d_state + d_input_norm
    gw = gw.astype(SINGLE_FLOAT)
    channels = heads * HEAD_DIM
    grad_wq = gw[:, :, :channels].transpose(1, 0, 2).reshape(owned, ctx_count * channels)
    shared = ctx_count // KEY_VALUE_HEADS
    kv = gw[:, :, channels:].reshape(KEY_VALUE_HEADS, shared, owned, 2, HEAD_DIM).sum(1)
    grad_wk = kv[:, :, 0].transpose(1, 0, 2).reshape(owned, KEY_VALUE_HEADS * HEAD_DIM)
    grad_wv = kv[:, :, 1].transpose(1, 0, 2).reshape(owned, KEY_VALUE_HEADS * HEAD_DIM)
    return (
        output[None],
        grad_input[None],
        small[:owned],
        grad_wq,
        grad_wk,
        grad_wv,
        small[2 * owned : at - few],
        small[at - few : at],
        grad_wo,
        small[owned : 2 * owned],
        small[at : at + owned * expert_count].reshape(owned, expert_count),
        grad_gate,
        grad_up,
        grad_down,
    )


def planned_body(mesh):
    if mesh.shape["ctx"] == 8 and mesh.shape["ws"] == 4:
        return tensor_body
    return general_body


def solution(mesh):
    placed = (
        P("ws", "ctx", None),
        P("ws", "ctx", None),
        P("ws", "ctx", None),
        P("ws", None),
        P(("ctx", "ws")),
        P(("ctx", "ws"), None),
        P(("ctx", "ws"), None),
        P(("ctx", "ws"), None),
        P(("ctx", "ws")),
        P(("ctx", "ws")),
        P(("ctx", "ws"), None),
        P(("ctx", "ws")),
        P(("ctx", "ws"), None),
        P(("ctx", "ws"), None, None),
        P(("ctx", "ws"), None, None),
        P(("ctx", "ws"), None, None),
    )
    return jax.shard_map(
        planned_body(mesh),
        mesh=mesh,
        in_specs=placed,
        out_specs=(
            P("ws", "ctx", None),
            P("ws", "ctx", None),
            P(("ctx", "ws")),
            P(("ctx", "ws"), None),
            P(("ctx", "ws"), None),
            P(("ctx", "ws"), None),
            P(("ctx", "ws")),
            P(("ctx", "ws")),
            P(("ctx", "ws"), None),
            P(("ctx", "ws")),
            P(("ctx", "ws"), None),
            P(("ctx", "ws"), None, None),
            P(("ctx", "ws"), None, None),
            P(("ctx", "ws"), None, None),
        ),
        check_vma=False,
    )
```

```python
import jax
import jax.numpy as jnp
from jax import lax
from jax.experimental import pallas as pl
from jax.experimental.pallas import tpu as pltpu
from jax.sharding import PartitionSpec as P

QUERY_HEADS = 32
KEY_VALUE_HEADS = 4
HEAD_DIM = 128
TOPK = 8


EPS = 1e-06
THETA = 1000000.0
MASK_FILL = -1e30
TOP_PRECISION = lax.Precision.HIGHEST
SINGLE_FLOAT = jnp.float32
BRAIN_FLOAT_TYPE = jnp.bfloat16


def rms_scale(values, norm_gain):
    return values * lax.rsqrt(jnp.mean(values * values, axis=-1, keepdims=True) + EPS) * norm_gain


def rotate(values, positions):
    half_dim = values.shape[-1] // 2
    frequency = THETA ** (-2.0 * jnp.arange(half_dim, dtype=jnp.float32) / values.shape[-1])
    angle = positions.astype(jnp.float32)[:, None] * frequency[None, :]
    cosine = jnp.cos(angle)[:, None, :]
    sine_part = jnp.sin(angle)[:, None, :]
    first_half = values[..., :half_dim]
    second_half = values[..., half_dim:]
    return jnp.concatenate(
        [
            first_half * cosine - second_half * sine_part,
            second_half * cosine + first_half * sine_part,
        ],
        axis=-1,
    )


def head_prepare(raw_heads, norm_gain, positions):
    return rotate(rms_scale(raw_heads, norm_gain), positions)


def swiglu(gate_part, up_part):
    return jax.nn.silu(gate_part) * up_part


def stored_positions(row_index, tokens_per_shard, ctx_count):
    device_row = row_index // tokens_per_shard
    within = row_index % tokens_per_shard
    half_block = tokens_per_shard // 2
    block_index = jnp.where(within < half_block, device_row, 2 * ctx_count - 1 - device_row)
    return block_index * half_block + within % half_block


def segment_ids(doc_lengths, positions):
    doc_ends = jnp.cumsum(doc_lengths, dtype=jnp.int32)
    return jnp.sum(
        (positions[:, None] >= doc_ends[None, :]).astype(jnp.int32), axis=1, dtype=jnp.int32
    )


def slot_ranks(flat_routes, expert_count):
    expert_hits = (
        flat_routes[:, None] == jnp.arange(expert_count, dtype=jnp.int32)[None, :]
    ).astype(jnp.int32)
    running = jnp.cumsum(expert_hits, axis=0, dtype=jnp.int32) - 1
    return jnp.sum(expert_hits * running, axis=1, dtype=jnp.int32)


def send_inputs(flat_rows):
    moved = lax.all_to_all(flat_rows, ("ctx", "ws"), split_axis=0, concat_axis=0, tiled=True)
    return moved


def send_outputs(flat_rows):
    moved = lax.all_to_all(flat_rows, ("ctx", "ws"), split_axis=0, concat_axis=0, tiled=True)
    return moved


def send_out_grads(flat_rows):
    moved = lax.all_to_all(flat_rows, ("ctx", "ws"), split_axis=0, concat_axis=0, tiled=True)
    return moved


def send_in_grads(flat_rows):
    moved = lax.all_to_all(flat_rows, ("ctx", "ws"), split_axis=0, concat_axis=0, tiled=True)
    return moved


def flat_rows(grid_sum):
    return grid_sum.reshape((-1,) + grid_sum.shape[3:])


def to_expert_major(arrived, expert_local):
    device_count, row_span, model_width = arrived.shape
    capacity = row_span // expert_local
    shaped = arrived.reshape(device_count, expert_local, capacity, model_width)
    return shaped.transpose(1, 0, 2, 3).reshape(expert_local, device_count * capacity, model_width)


def to_device_major(expert_rows, device_count):
    expert_local, row_span, model_width = expert_rows.shape
    capacity = row_span // device_count
    shaped = expert_rows.reshape(expert_local, device_count, capacity, model_width)
    return shaped.transpose(1, 0, 2, 3).reshape(device_count, expert_local * capacity, model_width)


def general_body(
    inputs,
    grad_output,
    routes,
    doc_lengths,
    norm_attn,
    w_query,
    key_projection,
    value_projection,
    query_norm,
    key_norm,
    w_out,
    norm_ffn,
    w_router,
    expert_gate,
    expert_up,
    expert_down,
):
    ctx_count = lax.axis_size("ctx")
    device_count = ctx_count * lax.axis_size("ws")
    tokens_per_shard = inputs.shape[1]
    model_width = inputs.shape[2]
    sequence_tokens = tokens_per_shard * ctx_count
    expert_count = w_router.shape[1]
    expert_local = expert_gate.shape[0]
    capacity = max(2, tokens_per_shard * TOPK * 3 // (2 * device_count))
    query_group_size = QUERY_HEADS // KEY_VALUE_HEADS
    logit_scale = HEAD_DIM ** (-0.5)
    single_key_block = min(512, sequence_tokens)
    count_of_blocks = sequence_tokens // single_key_block
    ctx_index = lax.axis_index("ctx")
    positions_all = stored_positions(
        jnp.arange(sequence_tokens, dtype=jnp.int32), tokens_per_shard, ctx_count
    )
    segments_all = segment_ids(doc_lengths[0], positions_all)
    local_positions = lax.dynamic_slice_in_dim(
        positions_all, ctx_index * tokens_per_shard, tokens_per_shard
    )
    segments_own = lax.dynamic_slice_in_dim(
        segments_all, ctx_index * tokens_per_shard, tokens_per_shard
    )
    validity = (segments_own < doc_lengths.shape[1]).astype(SINGLE_FLOAT)
    shards = (
        norm_attn,
        w_query,
        key_projection,
        value_projection,
        query_norm,
        key_norm,
        w_out,
        norm_ffn,
        w_router,
    )
    gathered = (
        lax.all_gather(shards[0], ("ctx", "ws"), axis=0, tiled=True),
        lax.all_gather(shards[1], ("ctx", "ws"), axis=0, tiled=True),
        lax.all_gather(shards[2], ("ctx", "ws"), axis=0, tiled=True),
        lax.all_gather(shards[3], ("ctx", "ws"), axis=0, tiled=True),
        lax.all_gather(shards[4], ("ctx", "ws"), axis=0, tiled=True),
        lax.all_gather(shards[5], ("ctx", "ws"), axis=0, tiled=True),
        lax.all_gather(shards[6], ("ctx", "ws"), axis=0, tiled=True),
        lax.all_gather(shards[7], ("ctx", "ws"), axis=0, tiled=True),
        lax.all_gather(shards[8], ("ctx", "ws"), axis=0, tiled=True),
    )
    (
        attn_gain,
        query_matrix,
        key_matrix,
        value_matrix,
        query_gain,
        key_norm_gain,
        output_matrix,
        ffn_gain,
        router_matrix,
    ) = gathered
    attn_gain = attn_gain.astype(SINGLE_FLOAT)
    query_gain = query_gain.astype(SINGLE_FLOAT)
    key_norm_gain = key_norm_gain.astype(SINGLE_FLOAT)
    ffn_gain = ffn_gain.astype(SINGLE_FLOAT)
    layer_in = inputs[0].astype(SINGLE_FLOAT)
    normalized_rows = rms_scale(layer_in, attn_gain).astype(BRAIN_FLOAT_TYPE)
    unnormed_queries = jnp.dot(
        normalized_rows, query_matrix, preferred_element_type=SINGLE_FLOAT
    ).reshape(tokens_per_shard, QUERY_HEADS, HEAD_DIM)
    unnormed_keys = jnp.dot(
        normalized_rows, key_matrix, preferred_element_type=SINGLE_FLOAT
    ).reshape(tokens_per_shard, KEY_VALUE_HEADS, HEAD_DIM)
    value_low = jnp.dot(normalized_rows, value_matrix, preferred_element_type=SINGLE_FLOAT).astype(
        BRAIN_FLOAT_TYPE
    )
    query_rows = head_prepare(unnormed_queries, query_gain, local_positions).astype(
        BRAIN_FLOAT_TYPE
    )
    key_low = (
        head_prepare(unnormed_keys, key_norm_gain, local_positions)
        .astype(BRAIN_FLOAT_TYPE)
        .reshape(tokens_per_shard, KEY_VALUE_HEADS * HEAD_DIM)
    )
    every_key, every_value = (
        lax.all_gather(key_low, "ctx", axis=0, tiled=True),
        lax.all_gather(value_low, "ctx", axis=0, tiled=True),
    )
    grouped_queries = query_rows.reshape(
        tokens_per_shard, KEY_VALUE_HEADS, query_group_size, HEAD_DIM
    )
    blocked_keys = every_key.reshape(count_of_blocks, single_key_block, KEY_VALUE_HEADS, HEAD_DIM)
    blocked_values = every_value.reshape(
        count_of_blocks, single_key_block, KEY_VALUE_HEADS, HEAD_DIM
    )
    position_blocks = positions_all.reshape(count_of_blocks, single_key_block)
    segment_blocks = segments_all.reshape(count_of_blocks, single_key_block)

    def scores_for(block_keys, block_positions, block_segments):
        raw_scores = (
            jnp.einsum(
                "tkgd,jkd->kgtj", grouped_queries, block_keys, preferred_element_type=SINGLE_FLOAT
            )
            * logit_scale
        )
        allowed = (segments_own[:, None] == block_segments[None, :]) & (
            block_positions[None, :] <= local_positions[:, None]
        )
        return (raw_scores, allowed[None, None])

    def stats_step(running, pieces):
        maximum, denominator = running
        block_keys, block_positions, block_segments = pieces
        raw_scores, allowed = scores_for(block_keys, block_positions, block_segments)
        masked = jnp.where(allowed, raw_scores, MASK_FILL)
        new_maximum = jnp.maximum(maximum, jnp.max(masked, axis=-1))
        weights = jnp.where(allowed, jnp.exp(masked - new_maximum[..., None]), 0.0)
        denominator = denominator * jnp.exp(maximum - new_maximum) + jnp.sum(weights, axis=-1)
        return ((new_maximum, denominator), None)

    stats_init = (
        jnp.full((KEY_VALUE_HEADS, query_group_size, tokens_per_shard), MASK_FILL, SINGLE_FLOAT),
        jnp.zeros((KEY_VALUE_HEADS, query_group_size, tokens_per_shard), SINGLE_FLOAT),
    )
    (maximum, denominator), _ = lax.scan(
        stats_step, stats_init, (blocked_keys, position_blocks, segment_blocks)
    )

    def probs_for(raw_scores, allowed):
        return (
            jnp.where(allowed, jnp.exp(raw_scores - maximum[..., None]), 0.0)
            / denominator[..., None]
        )

    def value_update(running, pieces):
        block_keys, block_values, block_positions, block_segments = pieces
        raw_scores, allowed = scores_for(block_keys, block_positions, block_segments)
        softmaxed = probs_for(raw_scores, allowed).astype(BRAIN_FLOAT_TYPE)
        running = running + jnp.einsum(
            "kgtj,jkd->tkgd", softmaxed, block_values, preferred_element_type=SINGLE_FLOAT
        )
        return (running, None)

    inputs_per_block = (blocked_keys, blocked_values, position_blocks, segment_blocks)
    attended, _ = lax.scan(
        value_update,
        jnp.zeros((tokens_per_shard, KEY_VALUE_HEADS, query_group_size, HEAD_DIM), SINGLE_FLOAT),
        inputs_per_block,
    )
    attn_low = attended.reshape(tokens_per_shard, QUERY_HEADS * HEAD_DIM).astype(BRAIN_FLOAT_TYPE)
    hidden_state = layer_in + jnp.dot(attn_low, output_matrix, preferred_element_type=SINGLE_FLOAT)
    combined_rows = rms_scale(hidden_state, ffn_gain).astype(BRAIN_FLOAT_TYPE)
    router_scores = jnp.dot(combined_rows, router_matrix, preferred_element_type=SINGLE_FLOAT)
    own_routes = routes[0]
    route_mask = (
        own_routes[:, :, None] == jnp.arange(expert_count, dtype=jnp.int32)[None, None, :]
    ).astype(SINGLE_FLOAT)
    chosen = jnp.einsum("tke,te->tk", route_mask, router_scores, precision=TOP_PRECISION)
    gate_share = jax.nn.softmax(chosen, axis=-1)
    flat_routes = own_routes.reshape(-1)
    slot_index = flat_routes * capacity + slot_ranks(flat_routes, expert_count)
    entries = tokens_per_shard * TOPK
    source_slot = (
        jnp.full((expert_count * capacity,), entries, jnp.int32)
        .at[slot_index]
        .set(jnp.arange(entries, dtype=jnp.int32))
    )
    padded_in = jnp.concatenate(
        [combined_rows, jnp.zeros((1, model_width), BRAIN_FLOAT_TYPE)], axis=0
    )
    outgoing = padded_in[source_slot // TOPK].reshape(device_count, -1, model_width)
    expert_in = to_expert_major(send_inputs(outgoing), expert_local)
    gate_hidden = jnp.einsum(
        "erd,edf->erf", expert_in, expert_gate, preferred_element_type=SINGLE_FLOAT
    )
    up_hidden = jnp.einsum(
        "erd,edf->erf", expert_in, expert_up, preferred_element_type=SINGLE_FLOAT
    )
    hidden = swiglu(gate_hidden, up_hidden).astype(BRAIN_FLOAT_TYPE)
    expert_out = jnp.einsum(
        "erf,efd->erd", hidden, expert_down, preferred_element_type=SINGLE_FLOAT
    ).astype(BRAIN_FLOAT_TYPE)
    returned = send_outputs(to_device_major(expert_out, device_count)).reshape(
        expert_count * capacity, model_width
    )
    picked = returned[slot_index].reshape(tokens_per_shard, TOPK, model_width)
    moe_sum = jnp.sum(gate_share[:, :, None] * picked.astype(SINGLE_FLOAT), axis=1)
    output = (hidden_state + moe_sum).astype(BRAIN_FLOAT_TYPE)
    d_layer = grad_output[0].astype(SINGLE_FLOAT) * validity[:, None]
    d_gate_share = jnp.sum(d_layer[:, None, :] * picked.astype(SINGLE_FLOAT), axis=-1)
    d_chosen = gate_share * (
        d_gate_share - jnp.sum(gate_share * d_gate_share, axis=-1, keepdims=True)
    )
    d_logits = jnp.einsum("tke,tk->te", route_mask, d_chosen, precision=TOP_PRECISION).astype(
        BRAIN_FLOAT_TYPE
    )
    d_copies = (
        (gate_share[:, :, None] * d_layer[:, None, :])
        .astype(BRAIN_FLOAT_TYPE)
        .reshape(entries, model_width)
    )
    d_padded = jnp.concatenate([d_copies, jnp.zeros((1, model_width), BRAIN_FLOAT_TYPE)], axis=0)
    d_outgoing = d_padded[source_slot].reshape(device_count, -1, model_width)
    d_expert_out = to_expert_major(send_out_grads(d_outgoing), expert_local)
    d_hidden = jnp.einsum(
        "erd,efd->erf", d_expert_out, expert_down, preferred_element_type=SINGLE_FLOAT
    )
    grad_down = jnp.einsum(
        "erf,erd->efd", hidden, d_expert_out, preferred_element_type=SINGLE_FLOAT
    )
    _, swiglu_back = jax.vjp(swiglu, gate_hidden, up_hidden)
    d_gate_hidden, d_up_hidden = swiglu_back(d_hidden)
    d_gate_low = d_gate_hidden.astype(BRAIN_FLOAT_TYPE)
    d_up_low = d_up_hidden.astype(BRAIN_FLOAT_TYPE)
    grad_gate = jnp.einsum(
        "erd,erf->edf", expert_in, d_gate_low, preferred_element_type=SINGLE_FLOAT
    )
    grad_up = jnp.einsum("erd,erf->edf", expert_in, d_up_low, preferred_element_type=SINGLE_FLOAT)
    d_expert_in = jnp.einsum(
        "erf,edf->erd", d_gate_low, expert_gate, preferred_element_type=SINGLE_FLOAT
    )
    d_expert_in = (
        d_expert_in
        + jnp.einsum("erf,edf->erd", d_up_low, expert_up, preferred_element_type=SINGLE_FLOAT)
    ).astype(BRAIN_FLOAT_TYPE)
    d_returned = send_in_grads(to_device_major(d_expert_in, device_count)).reshape(
        expert_count * capacity, model_width
    )
    d_slots = d_returned[slot_index].reshape(tokens_per_shard, TOPK, model_width)
    d_mixed = jnp.sum(d_slots.astype(SINGLE_FLOAT), axis=1) + jnp.einsum(
        "te,de->td", d_logits, router_matrix, preferred_element_type=SINGLE_FLOAT
    )
    grad_router = jnp.einsum(
        "td,te->de", combined_rows, d_logits, preferred_element_type=SINGLE_FLOAT
    )
    _, ffn_norm_back = jax.vjp(rms_scale, hidden_state, ffn_gain)
    d_state_norm, grad_ffn_gain = ffn_norm_back(d_mixed)
    d_state = d_layer + d_state_norm
    d_state_low = d_state.astype(BRAIN_FLOAT_TYPE)
    grad_out_weight = jnp.einsum(
        "tc,td->cd", attn_low, d_state_low, preferred_element_type=SINGLE_FLOAT
    )
    attention_gradient = jnp.einsum(
        "td,cd->tc", d_state_low, output_matrix, preferred_element_type=SINGLE_FLOAT
    ).astype(BRAIN_FLOAT_TYPE)
    attention_gradient = attention_gradient.reshape(
        tokens_per_shard, KEY_VALUE_HEADS, query_group_size, HEAD_DIM
    )
    row_delta = jnp.sum(attention_gradient.astype(SINGLE_FLOAT) * attended, axis=-1).transpose(
        1, 2, 0
    )

    def backward_step(d_query_acc, pieces):
        block_keys, block_values, block_positions, block_segments = pieces
        raw_scores, allowed = scores_for(block_keys, block_positions, block_segments)
        softmaxed = probs_for(raw_scores, allowed)
        d_probs = jnp.einsum(
            "tkgd,jkd->kgtj", attention_gradient, block_values, preferred_element_type=SINGLE_FLOAT
        )
        d_scores = (softmaxed * (d_probs - row_delta[..., None])).astype(BRAIN_FLOAT_TYPE)
        d_query_acc = d_query_acc + jnp.einsum(
            "kgtj,jkd->tkgd", d_scores, block_keys, preferred_element_type=SINGLE_FLOAT
        )
        d_key_block = jnp.einsum(
            "kgtj,tkgd->jkd", d_scores, grouped_queries, preferred_element_type=SINGLE_FLOAT
        )
        d_value_block = jnp.einsum(
            "kgtj,tkgd->jkd",
            softmaxed.astype(BRAIN_FLOAT_TYPE),
            attention_gradient,
            preferred_element_type=SINGLE_FLOAT,
        )
        return (d_query_acc, (d_key_block, d_value_block))

    d_query_acc, (key_block_gradients, value_block_gradients) = lax.scan(
        backward_step,
        jnp.zeros((tokens_per_shard, KEY_VALUE_HEADS, query_group_size, HEAD_DIM), SINGLE_FLOAT),
        inputs_per_block,
    )
    every_key_gradient = (key_block_gradients * logit_scale).reshape(
        sequence_tokens, KEY_VALUE_HEADS * HEAD_DIM
    )
    every_value_gradient = value_block_gradients.reshape(
        sequence_tokens, KEY_VALUE_HEADS * HEAD_DIM
    )
    key_gradients, d_values = (
        lax.psum_scatter(
            every_key_gradient.astype(jnp.bfloat16), "ctx", scatter_dimension=0, tiled=True
        ).astype(jnp.float32),
        lax.psum_scatter(
            every_value_gradient.astype(jnp.bfloat16), "ctx", scatter_dimension=0, tiled=True
        ).astype(jnp.float32),
    )
    _, query_back = jax.vjp(
        lambda raw_heads, norm_gain: head_prepare(raw_heads, norm_gain, local_positions),
        unnormed_queries,
        query_gain,
    )
    d_query_raw, grad_query_gain = query_back(
        (d_query_acc * logit_scale).reshape(tokens_per_shard, QUERY_HEADS, HEAD_DIM)
    )
    _, key_backward = jax.vjp(
        lambda raw_heads, norm_gain: head_prepare(raw_heads, norm_gain, local_positions),
        unnormed_keys,
        key_norm_gain,
    )
    raw_key_gradient, key_gain_gradient = key_backward(
        key_gradients.reshape(tokens_per_shard, KEY_VALUE_HEADS, HEAD_DIM)
    )
    d_query_low = d_query_raw.reshape(tokens_per_shard, QUERY_HEADS * HEAD_DIM).astype(
        BRAIN_FLOAT_TYPE
    )
    key_gradient_lowprec = raw_key_gradient.reshape(
        tokens_per_shard, KEY_VALUE_HEADS * HEAD_DIM
    ).astype(BRAIN_FLOAT_TYPE)
    d_value_low = d_values.astype(BRAIN_FLOAT_TYPE)
    grad_query_weight = jnp.einsum(
        "td,tc->dc", normalized_rows, d_query_low, preferred_element_type=SINGLE_FLOAT
    )
    grad_key_weight = jnp.einsum(
        "td,tc->dc", normalized_rows, key_gradient_lowprec, preferred_element_type=SINGLE_FLOAT
    )
    grad_value_weight = jnp.einsum(
        "td,tc->dc", normalized_rows, d_value_low, preferred_element_type=SINGLE_FLOAT
    )
    d_normed = jnp.einsum(
        "tc,dc->td", d_query_low, query_matrix, preferred_element_type=SINGLE_FLOAT
    )
    d_normed = d_normed + jnp.einsum(
        "tc,dc->td", key_gradient_lowprec, key_matrix, preferred_element_type=SINGLE_FLOAT
    )
    d_normed = d_normed + jnp.einsum(
        "tc,dc->td", d_value_low, value_matrix, preferred_element_type=SINGLE_FLOAT
    )
    _, attn_norm_back = jax.vjp(rms_scale, layer_in, attn_gain)
    d_input_norm, grad_attn_gain = attn_norm_back(d_normed)
    grad_input = d_state + d_input_norm
    reduced = (
        lax.psum_scatter(grad_attn_gain, ("ctx", "ws"), scatter_dimension=0, tiled=True),
        lax.psum_scatter(grad_query_weight, ("ctx", "ws"), scatter_dimension=0, tiled=True),
        lax.psum_scatter(grad_key_weight, ("ctx", "ws"), scatter_dimension=0, tiled=True),
        lax.psum_scatter(grad_value_weight, ("ctx", "ws"), scatter_dimension=0, tiled=True),
        lax.psum_scatter(grad_query_gain, ("ctx", "ws"), scatter_dimension=0, tiled=True),
        lax.psum_scatter(key_gain_gradient, ("ctx", "ws"), scatter_dimension=0, tiled=True),
        lax.psum_scatter(grad_out_weight, ("ctx", "ws"), scatter_dimension=0, tiled=True),
        lax.psum_scatter(grad_ffn_gain, ("ctx", "ws"), scatter_dimension=0, tiled=True),
        lax.psum_scatter(grad_router, ("ctx", "ws"), scatter_dimension=0, tiled=True),
    )
    return (
        output[None],
        grad_input[None],
        reduced[0],
        reduced[1],
        reduced[2],
        reduced[3],
        reduced[4],
        reduced[5],
        reduced[6],
        reduced[7],
        reduced[8],
        grad_gate,
        grad_up,
        grad_down,
    )


VMEM_WHOLE = pl.BlockSpec(memory_space=pltpu.VMEM)
VMEM_BYTES = 60 * 2**20
EXTRA = 128


def compiler_params():
    return pltpu.CompilerParams(vmem_limit_bytes=VMEM_BYTES)


def dot_rows(left, right):
    return lax.dot_general(
        left, right, (((1,), (0,)), ((), ())), preferred_element_type=SINGLE_FLOAT
    )


def dot_right_transposed(left, right):
    return lax.dot_general(
        left, right, (((1,), (1,)), ((), ())), preferred_element_type=SINGLE_FLOAT
    )


def dot_left_transposed(left, right):
    return lax.dot_general(
        left, right, (((0,), (0,)), ((), ())), preferred_element_type=SINGLE_FLOAT
    )


def key_range(tile, tile_rows, sequence_tokens, slack):
    half = sequence_tokens // 2
    first_row = tile * tile_rows
    low = 0 if first_row < half + slack else half
    return low, first_row + tile_rows


def stacked_heads(ref, rows, heads):
    return jnp.concatenate(
        [ref[rows, h * HEAD_DIM : (h + 1) * HEAD_DIM] for h in range(heads)], axis=0
    )


def tile_scores(q4, k_ref, segc_ref, segr_ref, low, high, first_row, tile_rows, heads):
    scale = HEAD_DIM ** (-0.5)
    scores = dot_right_transposed(q4, k_ref[low:high, :]) * scale
    span = high - low
    query_place = first_row + lax.broadcasted_iota(jnp.int32, (tile_rows, span), 0)
    key_place = low + lax.broadcasted_iota(jnp.int32, (tile_rows, span), 1)
    allowed = (segc_ref[first_row : first_row + tile_rows, :] == segr_ref[:, low:high]) & (
        key_place <= query_place
    )
    fill = jnp.where(allowed, 0.0, MASK_FILL)
    scores = scores + jnp.concatenate([fill] * heads, axis=0)
    exponent = jnp.exp(scores - jnp.max(scores, axis=-1, keepdims=True))
    return exponent * (1.0 / jnp.sum(exponent, axis=-1, keepdims=True))


def attention_forward_kernel(
    slack,
    x_ref,
    gain_ref,
    w_ref,
    qg_ref,
    kg_ref,
    cos_ref,
    sin_ref,
    segc_ref,
    segr_ref,
    wo_ref,
    normed_ref,
    raw_ref,
    q_ref,
    k_ref,
    v_ref,
    attn_ref,
    part_ref,
):
    tokens = x_ref.shape[0]
    heads = q_ref.shape[1] // HEAD_DIM
    rows_step = 256

    def project(i, carry):
        rows = pl.ds(pl.multiple_of(i * rows_step, rows_step), rows_step)
        x = x_ref[rows, :].astype(SINGLE_FLOAT)
        inverse = lax.rsqrt(jnp.mean(x * x, axis=-1, keepdims=True) + EPS)
        normed = (x * inverse * gain_ref[...]).astype(BRAIN_FLOAT_TYPE)
        normed_ref[rows, :] = normed
        raw = dot_rows(normed, w_ref[...])
        raw_ref[rows, :] = raw[:, : (heads + 1) * HEAD_DIM]
        v_ref[rows, :] = raw[:, (heads + 1) * HEAD_DIM :].astype(BRAIN_FLOAT_TYPE)
        cosine, sine = cos_ref[rows, :], sin_ref[rows, :]
        for h in range(heads + 1):
            part = raw[:, h * HEAD_DIM : (h + 1) * HEAD_DIM]
            gain = qg_ref[...] if h < heads else kg_ref[...]
            scaled = (
                part * lax.rsqrt(jnp.mean(part * part, axis=-1, keepdims=True) + EPS) * gain
            )
            turned = scaled * cosine + pltpu.roll(scaled, HEAD_DIM // 2, 1) * sine
            turned = turned.astype(BRAIN_FLOAT_TYPE)
            if h < heads:
                q_ref[rows, h * HEAD_DIM : (h + 1) * HEAD_DIM] = turned
            else:
                k_ref[rows, :] = turned
        return carry

    lax.fori_loop(0, tokens // rows_step, project, 0)
    tile_rows = 128
    for tile in range(tokens // tile_rows):
        first_row = tile * tile_rows
        rows = slice(first_row, first_row + tile_rows)
        low, high = key_range(tile, tile_rows, tokens, slack)
        probs = tile_scores(
            stacked_heads(q_ref, rows, heads),
            k_ref,
            segc_ref,
            segr_ref,
            low,
            high,
            first_row,
            tile_rows,
            heads,
        )
        attended = dot_rows(probs.astype(BRAIN_FLOAT_TYPE), v_ref[low:high, :])
        for h in range(heads):
            attn_ref[rows, h * HEAD_DIM : (h + 1) * HEAD_DIM] = attended[
                h * tile_rows : (h + 1) * tile_rows
            ].astype(BRAIN_FLOAT_TYPE)

    def project_out(i, carry):
        rows = pl.ds(pl.multiple_of(i * rows_step, rows_step), rows_step)
        part_ref[rows, :] = dot_rows(attn_ref[rows, :], wo_ref[...]).astype(BRAIN_FLOAT_TYPE)
        return carry

    lax.fori_loop(0, tokens // rows_step, project_out, 0)


def attention_forward(slack, x, gain, w, qg, kg, cosine, sine, segc, segr, wo):
    tokens, width = x.shape
    channels = w.shape[1] - 2 * HEAD_DIM
    low = BRAIN_FLOAT_TYPE
    shapes = (
        jax.ShapeDtypeStruct((tokens, width), low),
        jax.ShapeDtypeStruct((tokens, channels + HEAD_DIM), SINGLE_FLOAT),
        jax.ShapeDtypeStruct((tokens, channels), low),
        jax.ShapeDtypeStruct((tokens, HEAD_DIM), low),
        jax.ShapeDtypeStruct((tokens, HEAD_DIM), low),
        jax.ShapeDtypeStruct((tokens, channels), low),
        jax.ShapeDtypeStruct((tokens, width), low),
    )

    def kernel(*refs):
        attention_forward_kernel(slack, *refs)

    return pl.pallas_call(
        kernel,
        out_shape=shapes,
        in_specs=[VMEM_WHOLE] * 10,
        out_specs=[VMEM_WHOLE] * 7,
        compiler_params=compiler_params(),
        name="attention_forward",
    )(x, gain, w, qg, kg, cosine, sine, segc, segr, wo)


def head_backward(turned_gradient, part, gain, cosine, sine):
    scaled_gradient = turned_gradient * cosine - (
        pltpu.roll(turned_gradient, HEAD_DIM // 2, 1) * sine
    )
    inverse = lax.rsqrt(jnp.mean(part * part, axis=-1, keepdims=True) + EPS)
    unit = part * inverse
    gain_gradient = jnp.sum(scaled_gradient * unit, axis=0, keepdims=True)
    unit_gradient = scaled_gradient * gain
    raw_gradient = inverse * (
        unit_gradient - unit * jnp.mean(unit * unit_gradient, axis=-1, keepdims=True)
    )
    return raw_gradient, gain_gradient


def attention_backward_kernel(
    slack,
    dh_ref,
    wo_ref,
    attn_ref,
    q_ref,
    k_ref,
    v_ref,
    raw_ref,
    normed_ref,
    x_ref,
    w_ref,
    qg_ref,
    kg_ref,
    cos_ref,
    sin_ref,
    segc_ref,
    segr_ref,
    gwo_ref,
    gw_ref,
    dpart_ref,
    ggain_ref,
    gheads_ref,
    da_ref,
    draw_ref,
    dk_ref,
    dv_ref,
):
    tokens = x_ref.shape[0]
    heads = q_ref.shape[1] // HEAD_DIM
    scale = HEAD_DIM ** (-0.5)
    rows_step = 256

    def attended_gradient(i, carry):
        rows = pl.ds(pl.multiple_of(i * rows_step, rows_step), rows_step)
        da_ref[rows, :] = dot_right_transposed(dh_ref[rows, :], wo_ref[...]).astype(
            BRAIN_FLOAT_TYPE
        )
        return carry

    lax.fori_loop(0, tokens // rows_step, attended_gradient, 0)

    def out_weight(i, carry):
        columns = pl.ds(pl.multiple_of(i * 512, 512), 512)
        gwo_ref[:, columns] = dot_left_transposed(attn_ref[...], dh_ref[:, columns]).astype(
            gwo_ref.dtype
        )
        return carry

    lax.fori_loop(0, dh_ref.shape[1] // 512, out_weight, 0)
    dk_ref[...] = jnp.zeros_like(dk_ref)
    dv_ref[...] = jnp.zeros_like(dv_ref)
    query_gain_gradient = jnp.zeros((1, HEAD_DIM), SINGLE_FLOAT)
    tile_rows = 128
    for tile in range(tokens // tile_rows):
        first_row = tile * tile_rows
        rows = slice(first_row, first_row + tile_rows)
        low, high = key_range(tile, tile_rows, tokens, slack)
        q4 = stacked_heads(q_ref, rows, heads)
        da4 = stacked_heads(da_ref, rows, heads)
        probs = tile_scores(
            q4, k_ref, segc_ref, segr_ref, low, high, first_row, tile_rows, heads
        )
        d_probs = dot_right_transposed(da4, v_ref[low:high, :])
        delta = jnp.sum(probs * d_probs, axis=-1, keepdims=True)
        d_scores = (probs * (d_probs - delta)).astype(BRAIN_FLOAT_TYPE)
        dq4 = dot_rows(d_scores, k_ref[low:high, :]) * scale
        dk_ref[low:high, :] += dot_left_transposed(d_scores, q4)
        dv_ref[low:high, :] += dot_left_transposed(probs.astype(BRAIN_FLOAT_TYPE), da4)
        for h in range(heads):
            columns = slice(h * HEAD_DIM, (h + 1) * HEAD_DIM)
            raw_gradient, gain_gradient = head_backward(
                dq4[h * tile_rows : (h + 1) * tile_rows],
                raw_ref[rows, columns],
                qg_ref[...],
                cos_ref[rows, :],
                sin_ref[rows, :],
            )
            draw_ref[rows, columns] = raw_gradient.astype(BRAIN_FLOAT_TYPE)
            query_gain_gradient = query_gain_gradient + gain_gradient
    key_columns = slice(heads * HEAD_DIM, (heads + 1) * HEAD_DIM)
    raw_gradient, key_gain_gradient = head_backward(
        dk_ref[...] * scale, raw_ref[:, key_columns], kg_ref[...], cos_ref[...], sin_ref[...]
    )
    draw_ref[:, key_columns] = raw_gradient.astype(BRAIN_FLOAT_TYPE)
    draw_ref[:, (heads + 1) * HEAD_DIM :] = dv_ref[...].astype(BRAIN_FLOAT_TYPE)
    gheads_ref[...] = jnp.concatenate(
        [query_gain_gradient, key_gain_gradient, jnp.zeros((6, HEAD_DIM), SINGLE_FLOAT)], axis=0
    )

    def projection_weight(i, carry):
        columns = pl.ds(pl.multiple_of(i * 256, 256), 256)
        gw_ref[columns, :] = dot_left_transposed(normed_ref[:, columns], draw_ref[...]).astype(
            gw_ref.dtype
        )
        return carry

    lax.fori_loop(0, normed_ref.shape[1] // 256, projection_weight, 0)
    ggain_ref[...] = jnp.zeros_like(ggain_ref)

    def input_gradient(i, carry):
        rows = pl.ds(pl.multiple_of(i * rows_step, rows_step), rows_step)
        d_normed = dot_right_transposed(draw_ref[rows, :], w_ref[...])
        dpart_ref[rows, :] = d_normed.astype(BRAIN_FLOAT_TYPE)
        x = x_ref[rows, :].astype(SINGLE_FLOAT)
        inverse = lax.rsqrt(jnp.mean(x * x, axis=-1, keepdims=True) + EPS)
        ggain_ref[...] += jnp.sum(d_normed * (x * inverse), axis=0, keepdims=True)
        return carry

    lax.fori_loop(0, tokens // rows_step, input_gradient, 0)


def attention_backward(
    slack, dh, wo, attn, q, k, v, raw, normed, x, w, qg, kg, cosine, sine, segc, segr
):
    tokens, width = x.shape
    channels = q.shape[1]
    low = BRAIN_FLOAT_TYPE
    shapes = (
        jax.ShapeDtypeStruct((channels, width), low),
        jax.ShapeDtypeStruct((width, channels + 2 * HEAD_DIM), low),
        jax.ShapeDtypeStruct((tokens, width), low),
        jax.ShapeDtypeStruct((1, width), SINGLE_FLOAT),
        jax.ShapeDtypeStruct((8, HEAD_DIM), SINGLE_FLOAT),
    )

    def kernel(*refs):
        attention_backward_kernel(slack, *refs)

    return pl.pallas_call(
        kernel,
        out_shape=shapes,
        in_specs=[VMEM_WHOLE] * 16,
        out_specs=[VMEM_WHOLE] * 5,
        scratch_shapes=[
            pltpu.VMEM((tokens, channels), low),
            pltpu.VMEM((tokens, channels + 2 * HEAD_DIM), low),
            pltpu.VMEM((tokens, HEAD_DIM), SINGLE_FLOAT),
            pltpu.VMEM((tokens, HEAD_DIM), SINGLE_FLOAT),
        ],
        compiler_params=compiler_params(),
        name="attention_backward",
    )(dh, wo, attn, q, k, v, raw, normed, x, w, qg, kg, cosine, sine, segc, segr)


MESH = pl.DeviceIdType.MESH
ANYWHERE = pl.BlockSpec(memory_space=pl.ANY)
LINE = 4


def place():
    c, w = lax.axis_index("ctx"), lax.axis_index("ws")
    return c // 2, c % 2, w // 2, w % 2


def device_at(z, y, x, k):
    return (z * 2 + y, x * 2 + k)


def slot_of(z, y, x, k):
    return ((z * 2 + y) * 2 + x) * 2 + k


def line_order(z):
    upper = z // 2
    return [z, z + 1 - 2 * upper, 2 - 2 * (z % 2) + upper, 3 - 3 * upper]


def remote(source, target, send, recv, device):
    return pltpu.make_async_remote_copy(
        src_ref=source,
        dst_ref=target,
        send_sem=send,
        recv_sem=recv,
        device_id=device,
        device_id_type=MESH,
    )


def meet(z, y, x, k, around):
    barrier = pltpu.get_barrier_semaphore()

    def greet(device):
        pl.semaphore_signal(barrier, inc=1, device_id=device, device_id_type=MESH)

    @pl.when(z < LINE - 1)
    def _():
        greet(device_at(z + 1, y, x, k))

    @pl.when(z > 0)
    def _():
        greet(device_at(z - 1, y, x, k))

    for device in around:
        greet(device)
    pl.semaphore_wait(barrier, len(around) + 1 + z * (LINE - 1 - z) // 2)


class Sends:
    def __init__(self, semaphores):
        self.semaphores = semaphores
        self.started = []

    def start(self, source, target, recv, device, condition=None):
        copy = remote(source, target, self.semaphores.at[len(self.started)], recv, device)
        if condition is None:
            copy.start()
        else:
            pl.when(condition)(copy.start)
        self.started.append((condition, copy))

    def finish(self):
        for condition, copy in self.started:
            if condition is None:
                copy.wait_send()
            else:
                pl.when(condition)(copy.wait_send)


def arrived(target, recv, device):
    remote(target, target, recv, recv, device).wait_recv()


def along_line(z, y, x, k, block, i, order, start):
    if i == 0:
        up, down = z < LINE - 1, z > 0
    else:
        below = order[i] < z
        up, down = below & (z < LINE - 1), jnp.logical_not(below) & (z > 0)
    start(block, device_at(z + 1, y, x, k), up)
    start(block, device_at(z - 1, y, x, k), down)


def gather_all_kernel(source, out, local, send_sems, recv_sems):
    z, y, x, k = place()
    order = line_order(z)
    along_x, along_y = device_at(z, y, 1 - x, k), device_at(z, 1 - y, x, k)
    sibling = device_at(z, y, x, 1 - k)
    meet(z, y, x, k, (along_x, along_y, sibling))
    sends = Sends(send_sems)
    mine = slot_of(z, y, x, k)
    own = pltpu.make_async_copy(source, out.at[mine], local)
    own.start()

    def pass_on(slot, device, condition=None):
        block = source if slot is mine else out.at[slot]
        sends.start(block, out.at[slot], recv_sems.at[slot], device, condition)

    def wait(slot):
        arrived(out.at[slot], recv_sems.at[slot], along_x)

    def column(i):
        slot = mine if i == 0 else slot_of(order[i], y, x, k)
        if i > 0:
            wait(slot)
        along_line(z, y, x, k, slot, i, order, pass_on)
        pass_on(slot, along_x)
        pass_on(slot, along_y)
        pass_on(slot, sibling)

    def from_x(i):
        slot = slot_of(order[i], y, 1 - x, k)
        wait(slot)
        pass_on(slot, sibling)
        if i == 3:
            for j in (0, 1):
                pass_on(slot_of(order[j], y, 1 - x, k), along_y)

    def from_y(i):
        slot = slot_of(order[i], 1 - y, x, k)
        wait(slot)
        pass_on(slot, sibling)
        if i == 3:
            for j in (2, 3):
                pass_on(slot_of(order[j], 1 - y, x, k), along_x)

    def from_corner(i):
        slot = slot_of(order[i], 1 - y, 1 - x, k)
        wait(slot)
        pass_on(slot, sibling)

    column(0)
    for i in (1, 2, 3):
        column(i)
        from_x(i - 1)
        from_y(i - 1)
    from_x(3)
    from_y(3)
    for i in range(4):
        from_corner(i)
    for i in range(4):
        for dy in (y, 1 - y):
            for dx in (x, 1 - x):
                wait(slot_of(order[i], dy, dx, 1 - k))
    own.wait()
    sends.finish()


def gather_all(block, collective_id):
    return pl.pallas_call(
        gather_all_kernel,
        out_shape=jax.ShapeDtypeStruct((32,) + block.shape, block.dtype),
        in_specs=[ANYWHERE],
        out_specs=ANYWHERE,
        scratch_shapes=[
            pltpu.SemaphoreType.DMA,
            pltpu.SemaphoreType.DMA((40,)),
            pltpu.SemaphoreType.DMA((32,)),
        ],
        compiler_params=pltpu.CompilerParams(collective_id=collective_id, has_side_effects=True),
        name="gather_all",
    )(block)


def add_blocks(target, *terms):
    rows = target.shape[0]

    def step(i, carry):
        part = pl.ds(pl.multiple_of(i * 16, 16), 16)
        total = terms[0][part, :].astype(SINGLE_FLOAT)
        for term in terms[1:]:
            total = total + term[part, :].astype(SINGLE_FLOAT)
        target[part, :] = total.astype(target.dtype)
        return carry

    lax.fori_loop(0, rows // 16, step, 0)


def scatter_line(z, y, x, k, order, total, owned, up_ref, down_ref, up_sems, down_sems, sends, out, after):
    above, below = device_at(z + 1, y, x, k), device_at(z - 1, y, x, k)
    for i in (3, 2, 1):
        total(i)
        chip = order[i]
        upward = chip > z
        block = owned(i)

        @pl.when(upward & (z > 0))
        def _():
            arrived(up_ref.at[chip], up_sems.at[chip], below)
            add_blocks(block, block, up_ref.at[chip])

        @pl.when(jnp.logical_not(upward) & (z < LINE - 1))
        def _():
            arrived(down_ref.at[chip], down_sems.at[chip], above)
            add_blocks(block, block, down_ref.at[chip])

        sends.start(block, up_ref.at[chip], up_sems.at[chip], above, upward)
        sends.start(
            block, down_ref.at[chip], down_sems.at[chip], below, jnp.logical_not(upward)
        )
        after(i)
    total(0)
    block = owned(0)

    @pl.when(z > 0)
    def _():
        arrived(up_ref.at[z], up_sems.at[z], below)

    @pl.when(z < LINE - 1)
    def _():
        arrived(down_ref.at[z], down_sems.at[z], above)

    @pl.when(z == 0)
    def _():
        add_blocks(out, block, down_ref.at[z])

    @pl.when(z == LINE - 1)
    def _():
        add_blocks(out, block, up_ref.at[z])

    @pl.when((z > 0) & (z < LINE - 1))
    def _():
        add_blocks(out, block, up_ref.at[z], down_ref.at[z])


def scatter_picked_kernel(
    rows_in,
    pick_in,
    out,
    rows_ref,
    pick_ref,
    own_ref,
    corner_ref,
    x_ref,
    y_ref,
    up_ref,
    down_ref,
    load_sems,
    corner_sems,
    x_sems,
    y_sems,
    up_sems,
    down_sems,
    send_sems,
):
    z, y, x, k = place()
    order = line_order(z)
    along_x, along_y = device_at(z, y, 1 - x, k), device_at(z, 1 - y, x, k)
    pick_load = pltpu.make_async_copy(pick_in, pick_ref, load_sems.at[16])
    pick_load.start()
    turn = [i * 4 + r for r in (3, 1, 2, 0) for i in (3, 2, 1, 0)]
    loads = {j: pltpu.make_async_copy(rows_in.at[j], rows_ref.at[j], load_sems.at[j]) for j in turn}
    for j in turn:
        loads[j].start()
    meet(z, y, x, k, (along_x, along_y))
    sends = Sends(send_sems)
    pick_load.wait()

    def gather(i, r, *extra):
        j = i * 4 + r
        loads[j].wait()
        spread_rows(own_ref.at[j], pick_ref.at[j], rows_ref.at[j], *extra)
        return own_ref.at[j]

    for i in (3, 2, 1, 0):
        sends.start(
            gather(i, 3), corner_ref.at[i], corner_sems.at[i], along_y if i < 2 else along_x
        )

    def cross(i):
        arrived(corner_ref.at[i], corner_sems.at[i], along_x)
        extra = (corner_ref.at[i],)
        for_x = gather(i, 1, *(extra if i < 2 else ()))
        for_y = gather(i, 2, *(extra if i >= 2 else ()))
        sends.start(for_x, x_ref.at[i], x_sems.at[i], along_x)
        sends.start(for_y, y_ref.at[i], y_sems.at[i], along_y)

    def total(i):
        arrived(x_ref.at[i], x_sems.at[i], along_x)
        arrived(y_ref.at[i], y_sems.at[i], along_y)
        if i > 0:
            cross(i - 1)
        gather(i, 0, x_ref.at[i], y_ref.at[i])

    cross(3)
    scatter_line(
        z, y, x, k, order, total, lambda i: own_ref.at[i * 4],
        up_ref, down_ref, up_sems, down_sems, sends, out, lambda i: None,
    )
    sends.finish()


def scatter_picked(rows, pick, collective_id, dtype):
    slots, width = rows.shape[1:]
    tokens = pick.shape[2]
    shape, low = (tokens, width), rows.dtype
    dma = pltpu.SemaphoreType.DMA
    return pl.pallas_call(
        scatter_picked_kernel,
        out_shape=jax.ShapeDtypeStruct(shape, dtype),
        in_specs=[ANYWHERE, ANYWHERE],
        out_specs=VMEM_WHOLE,
        scratch_shapes=[pltpu.VMEM(rows.shape, low), pltpu.VMEM(pick.shape, low)]
        + [pltpu.VMEM((n,) + shape, low) for n in (16, 4, 4, 4, 4, 4)]
        + [dma((n,)) for n in (17, 4, 4, 4, 4, 4, 24)],
        compiler_params=pltpu.CompilerParams(
            collective_id=collective_id, has_side_effects=True, vmem_limit_bytes=VMEM_BYTES
        ),
        name="scatter_picked",
    )(rows, pick)


def halves(ref, z, y):
    half = ref.shape[0] // 16
    c = z * 2 + y
    return [
        ref.at[pl.ds(pl.multiple_of(half * b, half), half), :] for b in (c, 15 - c)
    ]


def split_rows(ref):
    half = ref.shape[0] // 2
    return [ref.at[0:half, :], ref.at[half : 2 * half, :]]


class RowGather:
    def __init__(self, source, out, sends, locals_, semaphores, at, order, along_y):
        self.source, self.out, self.sends, self.semaphores = source, out, sends, semaphores
        self.at, self.order, self.along_y = at, order, along_y
        z, y, x, k = at
        self.own = [
            pltpu.make_async_copy(a, b, locals_.at[n])
            for n, (a, b) in enumerate(zip(split_rows(source), halves(out, z, y)))
        ]
        for copy in self.own:
            copy.start()

    def column(self, i):
        z, y, x, k = self.at
        chip = self.order[i]
        pieces = halves(self.out, chip, y)
        if i > 0:
            self.wait(chip, y)
        for n in (0, 1):
            block = split_rows(self.source)[n] if i == 0 else pieces[n]
            recv = self.semaphores.at[n, chip * 2 + y]

            def start(_, device, condition=None):
                self.sends.start(block, pieces[n], recv, device, condition)

            along_line(z, y, x, k, None, i, self.order, start)
            start(None, self.along_y)

    def wait(self, chip, y):
        for n, piece in enumerate(halves(self.out, chip, y)):
            arrived(piece, self.semaphores.at[n, chip * 2 + y], self.along_y)

    def finish(self):
        y = self.at[1]
        for i in range(4):
            self.wait(self.order[i], 1 - y)
        for copy in self.own:
            copy.wait()


def gather_rows_kernel(source, out, local_sems, send_sems, recv_sems):
    at = place()
    z, y, x, k = at
    along_y = device_at(z, 1 - y, x, k)
    meet(z, y, x, k, (along_y,))
    sends = Sends(send_sems)
    rows = RowGather(source, out, sends, local_sems, recv_sems, at, line_order(z), along_y)
    for i in range(4):
        rows.column(i)
    rows.finish()
    sends.finish()


def gather_rows(block, collective_id):
    rows, width = block.shape
    dma = pltpu.SemaphoreType.DMA
    return pl.pallas_call(
        gather_rows_kernel,
        out_shape=jax.ShapeDtypeStruct((8 * rows, width), block.dtype),
        in_specs=[ANYWHERE],
        out_specs=ANYWHERE,
        scratch_shapes=[dma((2,)), dma((24,)), dma((2, 8))],
        compiler_params=pltpu.CompilerParams(collective_id=collective_id, has_side_effects=True),
        name="gather_rows",
    )(block)


class RowScatter:
    def __init__(self, part, out, buffers, semaphores, sends, at, order, along_y):
        self.part, self.out, self.sends, self.at, self.order = part, out, sends, at, order
        self.along_y = along_y
        self.own_ref, self.y_ref, self.up_ref, self.down_ref = buffers
        self.load_sems, self.y_sems, self.up_sems, self.down_sems = semaphores
        z, y, x, k = at
        self.loads = {}
        for i in (3, 2, 1, 0):
            self.loads[i] = [
                pltpu.make_async_copy(a, b, self.load_sems.at[n, i])
                for n, (a, b) in enumerate(
                    zip(halves(part, order[i], y), split_rows(self.own_ref.at[i]))
                )
            ]
            for copy in self.loads[i]:
                copy.start()
        self.cross(3)

    def cross(self, i):
        y = self.at[1]
        for n, (a, b) in enumerate(
            zip(halves(self.part, self.order[i], 1 - y), split_rows(self.y_ref.at[i]))
        ):
            self.sends.start(a, b, self.y_sems.at[n, i], self.along_y)

    def total(self, i):
        for copy in self.loads[i]:
            copy.wait()
        for n, piece in enumerate(split_rows(self.y_ref.at[i])):
            arrived(piece, self.y_sems.at[n, i], self.along_y)
        if i > 0:
            self.cross(i - 1)
        add_blocks(self.own_ref.at[i], self.own_ref.at[i], self.y_ref.at[i])

    def run(self, after=lambda i: None):
        z, y, x, k = self.at
        scatter_line(
            z, y, x, k, self.order, self.total, lambda i: self.own_ref.at[i],
            self.up_ref, self.down_ref, self.up_sems, self.down_sems, self.sends, self.out,
            after,
        )


def row_scatter_scratch(rows, width, low):
    dma = pltpu.SemaphoreType.DMA
    return [pltpu.VMEM((4, rows, width), low)] * 4 + [
        dma((2, 4)),
        dma((2, 4)),
        dma((4,)),
        dma((4,)),
    ]


def scatter_rows_kernel(part, out, *scratch):
    at = place()
    z, y, x, k = at
    along_y = device_at(z, 1 - y, x, k)
    meet(z, y, x, k, (along_y,))
    sends = Sends(scratch[8])
    rows = RowScatter(part, out, scratch[:4], scratch[4:8], sends, at, line_order(z), along_y)
    rows.run()
    sends.finish()


def scatter_rows(part, collective_id):
    rows, width = part.shape[0] // 8, part.shape[1]
    return pl.pallas_call(
        scatter_rows_kernel,
        out_shape=jax.ShapeDtypeStruct((rows, width), SINGLE_FLOAT),
        in_specs=[ANYWHERE],
        out_specs=VMEM_WHOLE,
        scratch_shapes=row_scatter_scratch(rows, width, part.dtype)
        + [pltpu.SemaphoreType.DMA((16,))],
        compiler_params=pltpu.CompilerParams(
            collective_id=collective_id, has_side_effects=True, vmem_limit_bytes=VMEM_BYTES
        ),
        name="scatter_rows",
    )(part)


def ring_of(c, w):
    return [((c + t) % 8, w) for t in range(1, 8)]


def gather_start_kernel(
    x_in,
    slab_in,
    wo_in,
    x_out,
    slab_out,
    wo_out,
    local_sems,
    send_sems,
    x_sems,
    slab_sems,
    wo_sems,
):
    at = place()
    z, y, x, k = at
    c, w = z * 2 + y, x * 2 + k
    along_x, along_y = device_at(z, y, 1 - x, k), device_at(z, 1 - y, x, k)
    sibling = device_at(z, y, x, 1 - k)
    others = ring_of(c, w)
    barrier = pltpu.get_barrier_semaphore()
    for device in others + [along_x, sibling]:
        pl.semaphore_signal(barrier, inc=1, device_id=device, device_id_type=MESH)
    pl.semaphore_wait(barrier, 9)
    sends = Sends(send_sems)
    rows = RowGather(
        x_in, x_out, sends, local_sems.at[pl.ds(0, 2)], x_sems, at, line_order(z), along_y
    )
    wo_rows = wo_in.shape[0]

    def wo_at(w):
        return wo_out.at[pl.ds(pl.multiple_of(w * wo_rows, wo_rows), wo_rows), :]

    mine = c * 4 + w
    local = [
        pltpu.make_async_copy(slab_in.at[c], slab_out.at[mine], local_sems.at[2]),
        pltpu.make_async_copy(wo_in, wo_at(w), local_sems.at[3]),
    ]
    for copy in local:
        copy.start()

    def pass_on(slot, device, block=None):
        block = slab_out.at[slot] if block is None else block
        sends.start(block, slab_out.at[slot], slab_sems.at[slot], device)

    def take(source, w):
        slot = source * 4 + w
        arrived(slab_out.at[slot], slab_sems.at[slot], along_x)
        return slot

    rows.column(0)
    for device in (along_x, sibling):
        sends.start(wo_in, wo_at(w), wo_sems.at[w], device)
        pass_on(mine, device, slab_in.at[c])
    for device in others:
        sends.start(slab_in.at[device[0]], slab_out.at[mine], slab_sems.at[mine], device)

    def onward():
        for t in range(1, 8):
            slot = take((c + 8 - t) % 8, w)
            pass_on(slot, along_x)
            pass_on(slot, sibling)

    def across():
        beside = (1 - x) * 2 + k
        arrived(wo_at(beside), wo_sems.at[beside], along_x)
        sends.start(wo_at(beside), wo_at(beside), wo_sems.at[beside], sibling)
        for t in range(8):
            pass_on(take((c + 8 - t) % 8, beside), sibling)

    rows.column(1)
    rows.column(2)
    onward()
    rows.column(3)
    across()
    for other in (x * 2 + 1 - k, (1 - x) * 2 + 1 - k):
        for t in range(8):
            take((c + 8 - t) % 8, other)
        arrived(wo_at(other), wo_sems.at[other], along_x)
    rows.finish()
    for copy in local:
        copy.wait()
    sends.finish()


def gather_start(x, slabs, wo, collective_id):
    tokens, width = x.shape
    low = BRAIN_FLOAT_TYPE
    dma = pltpu.SemaphoreType.DMA
    return pl.pallas_call(
        gather_start_kernel,
        out_shape=(
            jax.ShapeDtypeStruct((8 * tokens, width), low),
            jax.ShapeDtypeStruct((32,) + slabs.shape[1:], low),
            jax.ShapeDtypeStruct((4 * wo.shape[0], width), low),
        ),
        in_specs=[ANYWHERE] * 3,
        out_specs=[ANYWHERE] * 3,
        scratch_shapes=[dma((4,)), dma((64,)), dma((2, 8)), dma((32,)), dma((4,))],
        compiler_params=pltpu.CompilerParams(collective_id=collective_id, has_side_effects=True),
        name="gather_start",
    )(x, slabs, wo)


def scatter_end_kernel(
    part,
    gw,
    gwo,
    small,
    rows_out,
    gw_out,
    gwo_out,
    small_out,
    *scratch,
):
    row_scratch, row_sems = scratch[:4], scratch[4:8]
    (
        send_sems,
        load_sems,
        core_sems,
        x_sems,
        to_sems,
        small_to_sems,
        gw_own,
        gw_core,
        gw_x,
        gwo_own,
        gwo_core,
        gwo_x,
        small_own,
        small_core,
        small_x,
        small_to,
    ) = scratch[8:]
    at = place()
    z, y, x, k = at
    c, w = z * 2 + y, x * 2 + k
    along_x, along_y = device_at(z, y, 1 - x, k), device_at(z, 1 - y, x, k)
    sibling = device_at(z, y, x, 1 - k)
    others = ring_of(c, w)
    barrier = pltpu.get_barrier_semaphore()
    for device in others + [along_x, sibling]:
        pl.semaphore_signal(barrier, inc=1, device_id=device, device_id_type=MESH)
    pl.semaphore_wait(barrier, 9)
    sends = Sends(send_sems)
    rows = RowScatter(
        part, rows_out, row_scratch, row_sems, sends, at, line_order(z), along_y
    )
    loads = []
    for n, (source, core, own) in enumerate(
        (
            (small, small_core, small_own),
            (gw, gw_core, gw_own),
            (gwo, gwo_core, gwo_own),
        )
    ):
        outer = (slice(None),) * (len(source.shape) - 3)
        sends.start(source.at[(*outer, 1 - k)], core, core_sems.at[n], sibling)
        loads.append(pltpu.make_async_copy(source.at[(*outer, k)], own, load_sems.at[n]))
        loads[-1].start()

    def fold(n, own, core):
        loads[n].wait()
        arrived(core, core_sems.at[n], sibling)
        flat = [(i,) for i in range(own.shape[0])]
        for extent in own.shape[1:-2]:
            flat = [index + (j,) for index in flat for j in range(extent)]
        for i in flat:
            add_blocks(own.at[i], own.at[i], core.at[i])

    fold(0, small_own, small_core)
    sends.start(small_own.at[:, 1 - x], small_x, x_sems.at[0], along_x)
    fold(1, gw_own, gw_core)
    sends.start(gw_own.at[:, 1 - x], gw_x, x_sems.at[1], along_x)
    fold(2, gwo_own, gwo_core)
    keep = []

    def weights(i):
        if i == 2:
            sends.start(gwo_own.at[1 - x], gwo_x, x_sems.at[2], along_x)
            spread()

    def spread():
        for n, own, far in ((0, small_own, small_x), (1, gw_own, gw_x)):
            arrived(far, x_sems.at[n], along_x)
            for i in range(8):
                add_blocks(own.at[i, x], own.at[i, x], far.at[i])
            target, sems = (small_to, small_to_sems) if n == 0 else (gw_out, to_sems)
            keep.append(
                pltpu.make_async_copy(own.at[c, x], target.at[c], load_sems.at[3 + n])
            )
            keep[-1].start()
            for device in others:
                sends.start(own.at[device[0], x], target.at[c], sems.at[c], device)

    rows.run(weights)
    arrived(gwo_x, x_sems.at[2], along_x)
    add_blocks(gwo_out, gwo_own.at[x], gwo_x)
    for copy in keep:
        copy.wait()
    for t in range(1, 8):
        source = (c + 8 - t) % 8
        arrived(small_to.at[source], small_to_sems.at[source], along_x)
        arrived(gw_out.at[source], to_sems.at[source], along_x)
    total = small_to[0]
    for i in range(1, 8):
        total = total + small_to[i]
    small_out[...] = total
    sends.finish()


def scatter_end(part, gw, gwo, small, collective_id):
    rows, width = part.shape[0] // 8, part.shape[1]
    low = part.dtype
    dma, vmem = pltpu.SemaphoreType.DMA, pltpu.VMEM
    r, n = gw.shape[3:]
    ro, no = gwo.shape[2:]
    rs, ns = small.shape[3:]
    return pl.pallas_call(
        scatter_end_kernel,
        out_shape=(
            jax.ShapeDtypeStruct((rows, width), SINGLE_FLOAT),
            jax.ShapeDtypeStruct((8, r, n), low),
            jax.ShapeDtypeStruct((ro, no), SINGLE_FLOAT),
            jax.ShapeDtypeStruct((rs, ns), SINGLE_FLOAT),
        ),
        in_specs=[ANYWHERE] * 4,
        out_specs=[VMEM_WHOLE, ANYWHERE, VMEM_WHOLE, VMEM_WHOLE],
        scratch_shapes=row_scatter_scratch(rows, width, low)
        + [dma((48,)), dma((5,)), dma((3,)), dma((3,)), dma((8,)), dma((8,))]
        + [vmem((8, 2, r, n), low), vmem((8, 2, r, n), low), vmem((8, r, n), low)]
        + [vmem((2, ro, no), low), vmem((2, ro, no), low), vmem((ro, no), low)]
        + [vmem((8, 2, rs, ns), SINGLE_FLOAT), vmem((8, 2, rs, ns), SINGLE_FLOAT)]
        + [vmem((8, rs, ns), SINGLE_FLOAT), vmem((8, rs, ns), SINGLE_FLOAT)],
        compiler_params=pltpu.CompilerParams(
            collective_id=collective_id, has_side_effects=True, vmem_limit_bytes=VMEM_BYTES
        ),
        name="scatter_end",
    )(part, gw, gwo, small)


GROUPS = 8


def order_at(z, i):
    upper = z // 2
    inner = (z % 2) * (1 - upper) + (1 - z % 2) * upper
    along = i * (1 - inner) + inner * ((i + 1) % 3 + 2 * (i // 3))
    return 3 * upper + (1 - 2 * upper) * along


def group_blocks(g):
    later = ((g + 1) // 4) * (1 - g // 7)
    g = g * (1 - later) + later * (3 + g % 4)
    kind, turn = (g + 2) // 4, (g + 2) % 4
    far, side, near = 1 - (kind + 1) // 2, kind % 2, kind // 2
    return (
        (far * (turn - 2) + side * (3 - turn) + near * (3 - 2 * turn), 3 - 2 * kind + near),
        (far * turn + side * (3 - turn) + near * (2 - 2 * turn), 3 - kind - near),
    )


def spread_rows(target, pick, rows, *terms):
    step = 4 * HEAD_DIM
    width = target.shape[1]
    at = jnp.transpose(pick[...].astype(SINGLE_FLOAT)).astype(BRAIN_FLOAT_TYPE)
    for start in range(0, width, step):
        part = slice(start, min(start + step, width))
        total = dot_rows(at, rows[:, part])
        for term in terms:
            total = total + term[:, part].astype(SINGLE_FLOAT)
        target[:, part] = total.astype(target.dtype)


def expert_exchange_kernel(
    capacity,
    pay_all,
    dout_all,
    wg_in,
    wu_in,
    wd_in,
    back_ref,
    rows_out,
    pick_out,
    x_out,
    deo_out,
    hid_out,
    dgl_out,
    dul_out,
    wg_ref,
    wu_ref,
    wd_ref,
    pay_ref,
    dout_ref,
    x_ref,
    deo_ref,
    hid_ref,
    dgl_ref,
    dul_ref,
    d_ref,
    g_ref,
    far_pick_ref,
    far_d_ref,
    far_o_ref,
    near_o_ref,
    pick_ref,
    rows_ref,
    own_ref,
    corner_ref,
    x_sum_ref,
    y_sum_ref,
    up_ref,
    down_ref,
    weight_sems,
    load_sems,
    row_sems,
    near_sems,
    far_sems,
    sibling_sems,
    corner_sems,
    x_sums,
    y_sums,
    up_sems,
    down_sems,
    sum_send_sems,
    pick_sem,
):
    z, y, x, k = place()
    order = line_order(z)
    along_x, along_y = device_at(z, y, 1 - x, k), device_at(z, 1 - y, x, k)
    sibling = device_at(z, y, x, 1 - k)
    weights = [
        pltpu.make_async_copy(a, b, weight_sems.at[n])
        for n, (a, b) in enumerate(((wg_in, wg_ref), (wu_in, wu_ref), (wd_in, wd_ref)))
    ]
    for copy in weights:
        copy.start()
    meet(z, y, x, k, (along_x, along_y, sibling))
    mine = slot_of(z, y, x, k)
    width = wg_in.shape[0]
    _, tokens, payload = pay_all.shape
    experts = (payload - width) // 4
    rows = 4 * capacity
    above, below = device_at(z + 1, y, x, k), device_at(z - 1, y, x, k)

    def far_copies(n, j):
        half = pl.ds(capacity, capacity)
        return [
            remote(a, b, far_sems.at[n, m], sibling_sems.at[m, j], sibling)
            for m, (a, b) in enumerate(
                (
                    (far_pick_ref.at[n], pick_ref.at[j, half, :]),
                    (far_d_ref.at[n], rows_ref.at[j, half, :]),
                    (far_o_ref.at[n], rows_out.at[j, half, :]),
                )
            )
        ]

    def gather(i, r, *extra):
        j = i * 4 + r
        for copy in far_copies(0, j)[:2]:
            copy.wait_recv()
        spread_rows(own_ref.at[j], pick_ref.at[j], rows_ref.at[j], *extra)
        return own_ref.at[j]

    def sum_send(n, j, target, recv, device):
        return remote(own_ref.at[j], target, sum_send_sems.at[n], recv, device)

    corner_sends = [
        sum_send(i, i * 4 + 3, corner_ref.at[i], corner_sems.at[i], along_y if i < 2 else along_x)
        for i in range(4)
    ]
    x_sends = [
        sum_send(4 + i, i * 4 + 1, x_sum_ref.at[i], x_sums.at[i], along_x) for i in range(4)
    ]
    y_sends = [
        sum_send(8 + i, i * 4 + 2, y_sum_ref.at[i], y_sums.at[i], along_y) for i in range(4)
    ]
    line_sends = []
    for i in (1, 2, 3):
        chip = order[i]
        upward = chip > z
        line_sends.append(
            (upward, sum_send(12 + i, i * 4, up_ref.at[chip], up_sems.at[chip], above))
        )
        line_sends.append(
            (
                jnp.logical_not(upward),
                sum_send(16 + i, i * 4, down_ref.at[chip], down_sems.at[chip], below),
            )
        )

    def corners(*which):
        for i in which:
            gather(i, 3)
            corner_sends[i].start()

    def cross(i):
        arrived(corner_ref.at[i], corner_sems.at[i], along_x)
        extra = (corner_ref.at[i],)
        gather(i, 1, *(extra if i < 2 else ()))
        x_sends[i].start()
        gather(i, 2, *(extra if i >= 2 else ()))
        y_sends[i].start()

    def total(i):
        arrived(x_sum_ref.at[i], x_sums.at[i], along_x)
        arrived(y_sum_ref.at[i], y_sums.at[i], along_y)
        gather(i, 0, x_sum_ref.at[i], y_sum_ref.at[i])

    def along(i):
        total(i)
        chip, block = order[i], own_ref.at[i * 4]
        upward = chip > z

        @pl.when(upward & (z > 0))
        def _():
            arrived(up_ref.at[chip], up_sems.at[chip], below)
            add_blocks(block, block, up_ref.at[chip])

        @pl.when(jnp.logical_not(upward) & (z < LINE - 1))
        def _():
            arrived(down_ref.at[chip], down_sems.at[chip], above)
            add_blocks(block, block, down_ref.at[chip])

        for condition, copy in line_sends[2 * i - 2 : 2 * i]:
            pl.when(condition)(copy.start)

    def sixth():
        cross(1)
        along(3)

    def last():
        cross(0)
        along(2)

    at_start = {5: lambda: cross(2), 6: sixth, 7: last}
    at_middle = {1: lambda: corners(2, 0), 2: lambda: corners(3, 1), 3: lambda: cross(3)}

    def at(g, table):
        for n, work in table.items():
            pl.when(g == n)(work)

    for copy in weights:
        copy.wait()
    slot_row = lax.broadcasted_iota(jnp.int32, (capacity, tokens), 0).astype(SINGLE_FLOAT)
    row_lane = lax.broadcasted_iota(jnp.int32, (capacity, payload - width), 1)
    e = mine
    is_gate = (row_lane == e) | (row_lane == experts + e)
    rank_lane = (
        lax.broadcasted_iota(jnp.int32, (8, payload - width), 1) == 2 * experts + e
    ).astype(BRAIN_FLOAT_TYPE)

    def row_copies(g):
        out_rows = pl.ds(pl.multiple_of(g * rows, rows), rows)
        pairs = (
            (x_ref, x_out), (deo_ref, deo_out), (hid_ref, hid_out), (dgl_ref, dgl_out),
            (dul_ref, dul_out),
        )
        return [
            pltpu.make_async_copy(a, b.at[out_rows, :], row_sems.at[n])
            for n, (a, b) in enumerate(pairs)
        ]

    def blocks_of(g):
        found = []
        for lane_k in (k, 1 - k):
            for i, r in group_blocks(g):
                dy, dx = r // 2, r % 2
                slot = slot_of(
                    order_at(z, i), y + dy * (1 - 2 * y), x + dx * (1 - 2 * x), lane_k
                )
                found.append((slot, i * 4 + r))
        return found

    def near_copies(g):
        return [
            pltpu.make_async_copy(
                near_o_ref.at[n], rows_out.at[blocks_of(g)[n][1], pl.ds(0, capacity), :], near_sems.at[n]
            )
            for n in (0, 1)
        ]

    def settle(g):
        for copy in row_copies(g) + near_copies(g):
            copy.wait()
        for n in (0, 1):
            for copy in far_copies(n, blocks_of(g)[2 + n][1]):
                copy.wait_send()

    def load_copies(g):
        return [
            (
                pltpu.make_async_copy(pay_all.at[slot], pay_ref.at[n], load_sems.at[n]),
                pltpu.make_async_copy(dout_all.at[slot], dout_ref.at[n], load_sems.at[4 + n]),
            )
            for n, (slot, _) in enumerate(blocks_of(g))
        ]

    def load(g):
        for pair in load_copies(g):
            for copy in pair:
                copy.start()

    def step(g, carry):
        blocks = blocks_of(g)
        at(g, at_start)

        @pl.when(g > 0)
        def _():
            settle(g - 1)

        loads = load_copies(g)
        for n in range(4):
            for copy in loads[n]:
                copy.wait()
            part = slice(n * capacity, (n + 1) * capacity)
            rank = dot_right_transposed(rank_lane, pay_ref[n, :, width:])
            pick = (rank[0:1, :] == slot_row).astype(BRAIN_FLOAT_TYPE)
            if n < 2:
                pick_ref[blocks[n][1], 0:capacity, :] = pick
            else:
                far_pick_ref[n - 2] = pick
            chosen = dot_rows(pick, pay_ref[n])
            x_ref[part, :] = chosen[:, :width].astype(BRAIN_FLOAT_TYPE)
            gate = jnp.sum(jnp.where(is_gate, chosen[:, width:], 0.0), axis=-1, keepdims=True)
            g_ref[part, :] = gate
            d_rows = dot_rows(pick, dout_ref[n])
            d_ref[part, :] = d_rows.astype(BRAIN_FLOAT_TYPE)
            deo_ref[part, :] = (gate * d_rows).astype(BRAIN_FLOAT_TYPE)

        @pl.when(g < GROUPS - 1)
        def _():
            load(g + 1)

        at(g, at_middle)
        rows_in = x_ref[...]
        gate_hidden = dot_rows(rows_in, wg_ref[...])
        up_hidden = dot_rows(rows_in, wu_ref[...])
        sigmoid = 1.0 / (1.0 + jnp.exp(-gate_hidden))
        silu = gate_hidden * sigmoid
        hidden = (silu * up_hidden).astype(BRAIN_FLOAT_TYPE)
        hid_ref[...] = hidden
        d_hidden = dot_right_transposed(deo_ref[...], wd_ref[...])
        d_gate = (d_hidden * up_hidden * sigmoid * (1.0 + gate_hidden * (1.0 - sigmoid))).astype(
            BRAIN_FLOAT_TYPE
        )
        d_up = (d_hidden * silu).astype(BRAIN_FLOAT_TYPE)
        dgl_ref[...] = d_gate
        dul_ref[...] = d_up
        for copy in row_copies(g):
            copy.start()
        expert_out = dot_rows(hidden, wd_ref[...]).astype(BRAIN_FLOAT_TYPE)
        d_copy = (
            dot_right_transposed(d_gate, wg_ref[...]) + dot_right_transposed(d_up, wu_ref[...])
        ).astype(BRAIN_FLOAT_TYPE)
        for n in (2, 3, 0, 1):
            j = blocks[n][1]
            part = slice(n * capacity, (n + 1) * capacity)
            e_rows = expert_out[part].astype(SINGLE_FLOAT)
            d_gate_rows = jnp.sum(
                d_ref[part, :].astype(SINGLE_FLOAT) * e_rows, axis=-1, keepdims=True
            )
            high = d_gate_rows.astype(BRAIN_FLOAT_TYPE).astype(SINGLE_FLOAT)
            extra = jnp.where(row_lane == e, high, 0.0) + jnp.where(
                row_lane == experts + e, d_gate_rows - high, 0.0
            )
            if n >= 2:
                d_target, o_target = far_d_ref.at[n - 2], far_o_ref.at[n - 2]
            else:
                d_target, o_target = rows_ref.at[j, pl.ds(0, capacity), :], near_o_ref.at[n]
            d_target[:, :width] = d_copy[part]
            d_target[:, width:] = extra.astype(BRAIN_FLOAT_TYPE)
            o_target[...] = (g_ref[part, :] * e_rows).astype(BRAIN_FLOAT_TYPE)
            if n >= 2:
                for copy in far_copies(n - 2, j):
                    copy.start()
        for copy in near_copies(g):
            copy.start()
        return carry

    load(0)
    lax.fori_loop(0, GROUPS, step, 0)
    along(1)
    total(0)
    block = own_ref.at[0]

    @pl.when(z > 0)
    def _():
        arrived(up_ref.at[z], up_sems.at[z], below)

    @pl.when(z < LINE - 1)
    def _():
        arrived(down_ref.at[z], down_sems.at[z], above)

    @pl.when(z == 0)
    def _():
        add_blocks(back_ref, block, down_ref.at[z])

    @pl.when(z == LINE - 1)
    def _():
        add_blocks(back_ref, block, up_ref.at[z])

    @pl.when((z > 0) & (z < LINE - 1))
    def _():
        add_blocks(back_ref, block, up_ref.at[z], down_ref.at[z])

    settle(GROUPS - 1)
    keep = pltpu.make_async_copy(pick_ref, pick_out, pick_sem)
    keep.start()
    for j in range(16):
        far_copies(0, j)[2].wait_recv()
    keep.wait()
    for copy in corner_sends + x_sends + y_sends:
        copy.wait_send()
    for condition, copy in line_sends:
        pl.when(condition)(copy.wait_send)


def expert_exchange(capacity, pay_all, dout_all, wg, wu, wd, collective_id):
    _, tokens, wide = pay_all.shape
    width, ff = wg.shape
    low = BRAIN_FLOAT_TYPE
    rows = 4 * capacity
    total = GROUPS * rows
    dma, vmem = pltpu.SemaphoreType.DMA, pltpu.VMEM

    def kernel(*refs):
        expert_exchange_kernel(capacity, *refs)

    shape = jax.ShapeDtypeStruct
    return pl.pallas_call(
        kernel,
        out_shape=(
            shape((tokens, wide), SINGLE_FLOAT),
            shape((16, 2 * capacity, width), low),
            shape((16, 2 * capacity, tokens), low),
            shape((total, width), low),
            shape((total, width), low),
            shape((total, ff), low),
            shape((total, ff), low),
            shape((total, ff), low),
        ),
        in_specs=[ANYWHERE] * 5,
        out_specs=[VMEM_WHOLE] + [ANYWHERE] * 7,
        scratch_shapes=[vmem((width, ff), low), vmem((width, ff), low), vmem((ff, width), low)]
        + [vmem((4, tokens, wide), low), vmem((4, tokens, width), low)]
        + [vmem((rows, width), low), vmem((rows, width), low)]
        + [vmem((rows, ff), low)] * 3
        + [vmem((rows, width), low), vmem((rows, 1), SINGLE_FLOAT)]
        + [vmem((2, capacity, n), low) for n in (tokens, wide, width, width)]
        + [vmem((16, 2 * capacity, tokens), low), vmem((16, 2 * capacity, wide), low)]
        + [vmem((n, tokens, wide), low) for n in (16, 4, 4, 4, 4, 4)]
        + [dma((3,)), dma((8,)), dma((5,)), dma((2,)), dma((2, 3))]
        + [dma((3, 16)), dma((4,)), dma((4,)), dma((4,)), dma((4,)), dma((4,)), dma((20,)), dma],
        compiler_params=pltpu.CompilerParams(
            collective_id=collective_id, has_side_effects=True, vmem_limit_bytes=VMEM_BYTES
        ),
        name="expert_exchange",
    )(pay_all, dout_all, wg, wu, wd)


def natural_order(blocks):
    count, rows, width = blocks.shape
    half = rows // 2
    first = blocks[:, :half].reshape(count * half, width)
    second = blocks[::-1, half:].reshape(count * half, width)
    return jnp.concatenate([first, second], axis=0)


def device_order(rows, count):
    total, width = rows.shape
    half = total // count // 2
    first = rows[: total // 2].reshape(count, half, width)
    second = rows[total // 2 :].reshape(count, half, width)[::-1]
    return jnp.concatenate([first, second], axis=1)


def norm_backward(gradient, values, gain):
    inverse = lax.rsqrt(jnp.mean(values * values, axis=-1, keepdims=True) + EPS)
    unit = values * inverse
    scaled = gradient * gain
    d_values = inverse * (scaled - unit * jnp.mean(unit * scaled, axis=-1, keepdims=True))
    return d_values, jnp.sum(gradient * unit, axis=0)


def tensor_body(
    inputs,
    grad_output,
    routes,
    doc_lengths,
    norm_attn,
    w_query,
    key_projection,
    value_projection,
    query_norm,
    key_norm,
    w_out,
    norm_ffn,
    w_router,
    expert_gate,
    expert_up,
    expert_down,
):
    ctx_count = lax.axis_size("ctx")
    ws_count = lax.axis_size("ws")
    device_count = ctx_count * ws_count
    tokens = inputs.shape[1]
    width = inputs.shape[2]
    sequence_tokens = tokens * ctx_count
    expert_count = w_router.shape[1]
    capacity = tokens * TOPK * 3 // (2 * device_count)
    heads = QUERY_HEADS // ctx_count
    group = QUERY_HEADS // KEY_VALUE_HEADS
    slack = tokens // 2
    ctx_index = lax.axis_index("ctx")
    both = ("ctx", "ws")
    me = ctx_index * ws_count + lax.axis_index("ws")
    small = jnp.concatenate([norm_attn, norm_ffn, query_norm, key_norm, w_router.reshape(-1)])
    columns = (heads + 2) * HEAD_DIM
    small = jnp.pad(small, (0, 16 * columns - small.shape[0])).reshape(16, columns)
    slabs = []
    for c in range(ctx_count):
        kv = c * heads // group
        slab = jnp.concatenate(
            [
                w_query[:, c * heads * HEAD_DIM : (c + 1) * heads * HEAD_DIM],
                key_projection[:, kv * HEAD_DIM : (kv + 1) * HEAD_DIM],
                value_projection[:, kv * HEAD_DIM : (kv + 1) * HEAD_DIM],
            ],
            axis=1,
        )
        slabs.append(jnp.concatenate([slab, small], axis=0))
    owned, few = width // device_count, query_norm.shape[0]
    x_all, slabs, wo_all = gather_start(inputs[0], jnp.stack(slabs), w_out, 1)
    w_all = slabs[:, :owned].reshape(width, columns)
    small = slabs[:, owned:].reshape(device_count, 16 * columns)
    attn_gain = small[:, :owned].reshape(width).astype(SINGLE_FLOAT)
    ffn_gain = small[:, owned : 2 * owned].reshape(width).astype(SINGLE_FLOAT)
    at = 2 * owned
    query_gain = small[:, at : at + few].reshape(HEAD_DIM).astype(SINGLE_FLOAT)
    key_gain = small[:, at + few : at + 2 * few].reshape(HEAD_DIM).astype(SINGLE_FLOAT)
    at = at + 2 * few
    router_matrix = small[:, at : at + owned * expert_count].reshape(width, expert_count)

    places = jnp.arange(sequence_tokens, dtype=jnp.int32)
    segments = segment_ids(doc_lengths[0], places)
    half = HEAD_DIM // 2
    frequency = THETA ** (-2.0 * jnp.arange(half, dtype=SINGLE_FLOAT) / HEAD_DIM)
    angle = places.astype(SINGLE_FLOAT)[:, None] * frequency[None, :]
    cosine, sine = jnp.cos(angle), jnp.sin(angle)
    cosine = jnp.concatenate([cosine, cosine], axis=1)
    sine = jnp.concatenate([-sine, sine], axis=1)
    segc, segr = segments[:, None], segments[None, :]
    qg, kg = query_gain[None, :], key_gain[None, :]
    own_places = jnp.arange(tokens, dtype=jnp.int32)
    own_places = jnp.where(
        own_places < tokens // 2,
        ctx_index * (tokens // 2) + own_places,
        (2 * ctx_count - 2 - ctx_index) * (tokens // 2) + own_places,
    )
    own_segments = segment_ids(doc_lengths[0], own_places)
    validity = own_segments < doc_lengths.shape[1]
    d_layer = jnp.where(validity[:, None], grad_output[0], 0.0).astype(BRAIN_FLOAT_TYPE)
    dout_all = gather_all(d_layer, 7)

    normed, raw, q, k, v, attn, part = attention_forward(
        slack, x_all, attn_gain[None, :], w_all, qg, kg, cosine, sine, segc, segr, wo_all
    )
    branch = scatter_rows(part, 2)
    layer_in = inputs[0].astype(SINGLE_FLOAT)
    hidden_state = layer_in + branch
    mixed = rms_scale(hidden_state, ffn_gain).astype(BRAIN_FLOAT_TYPE)
    logits = jnp.dot(mixed, router_matrix, preferred_element_type=SINGLE_FLOAT)
    own_routes = routes[0]
    hit = jnp.any(
        own_routes[:, :, None] == jnp.arange(expert_count, dtype=jnp.int32)[None, None, :], axis=1
    )
    masked = jnp.where(hit, logits, MASK_FILL)
    exponent = jnp.exp(masked - jnp.max(masked, axis=-1, keepdims=True))
    gates = exponent / jnp.sum(exponent, axis=-1, keepdims=True)
    hits = hit.astype(BRAIN_FLOAT_TYPE)
    earlier = jnp.tril(jnp.ones((tokens, tokens), BRAIN_FLOAT_TYPE), -1)
    rank = jnp.dot(earlier, hits, preferred_element_type=SINGLE_FLOAT)
    rank = jnp.where(hit, rank, -1.0).astype(BRAIN_FLOAT_TYPE)
    gate_high = gates.astype(BRAIN_FLOAT_TYPE)
    gate_low = (gates - gate_high.astype(SINGLE_FLOAT)).astype(BRAIN_FLOAT_TYPE)
    payload = jnp.concatenate(
        [mixed, gate_high, gate_low, rank, jnp.zeros_like(rank)], axis=1
    )
    pay_all = gather_all(payload, 3)
    d_back, out_rows, out_pick, x_rows, d_rows, hidden, d_gate, d_up = expert_exchange(
        capacity, pay_all, dout_all, expert_gate[0], expert_up[0], expert_down[0], 4
    )
    moe_sum = scatter_picked(out_rows, out_pick, 8, SINGLE_FLOAT)
    output = (hidden_state + moe_sum).astype(BRAIN_FLOAT_TYPE)
    grad_gate = dot_left_transposed(x_rows, d_gate)[None]
    grad_up = dot_left_transposed(x_rows, d_up)[None]
    grad_down = dot_left_transposed(hidden, d_rows)[None]

    table = d_back[:, width:]
    d_gates = table[:, :expert_count] + table[:, expert_count : 2 * expert_count]
    d_chosen = gates * (d_gates - jnp.sum(gates * d_gates, axis=-1, keepdims=True))
    d_logits = d_chosen.astype(BRAIN_FLOAT_TYPE)
    d_mixed = d_back[:, :width] + dot_right_transposed(
        d_logits, router_matrix
    )
    grad_router = dot_left_transposed(mixed, d_logits)
    d_state_norm, grad_ffn_gain = norm_backward(d_mixed, hidden_state, ffn_gain)
    d_state = d_layer.astype(SINGLE_FLOAT) + d_state_norm
    d_state_low = d_state.astype(BRAIN_FLOAT_TYPE)
    dh_all = gather_rows(d_state_low, 5)
    gwo, gw, dpart, ggain, gheads = attention_backward(
        slack, dh_all, wo_all, attn, q, k, v, raw, normed, x_all, w_all, qg, kg, cosine, sine, segc, segr
    )
    blocks = (ctx_count, ws_count // 2, 2)
    small = jnp.concatenate(
        [
            ggain.reshape(device_count, owned),
            grad_ffn_gain.reshape(device_count, owned),
            gheads[0].reshape(device_count, few),
            gheads[1].reshape(device_count, few),
            grad_router.reshape(device_count, owned * expert_count),
        ],
        axis=1,
    )
    small = jnp.pad(small, ((0, 0), (0, 32 * 128 - small.shape[1]))).reshape(*blocks, 32, 128)
    d_normed, gw, grad_wo, small = scatter_end(
        dpart,
        gw.reshape(*blocks, owned, columns),
        gwo.reshape(*blocks[1:], w_out.shape[0], width),
        small,
        6,
    )
    small = small.reshape(-1)
    d_input_norm, _ = norm_backward(d_normed, layer_in, attn_gain)
    grad_input = d_state + d_input_norm
    gw = gw.astype(SINGLE_FLOAT)
    channels = heads * HEAD_DIM
    grad_wq = gw[:, :, :channels].transpose(1, 0, 2).reshape(owned, ctx_count * channels)
    shared = ctx_count // KEY_VALUE_HEADS
    kv = gw[:, :, channels:].reshape(KEY_VALUE_HEADS, shared, owned, 2, HEAD_DIM).sum(1)
    grad_wk = kv[:, :, 0].transpose(1, 0, 2).reshape(owned, KEY_VALUE_HEADS * HEAD_DIM)
    grad_wv = kv[:, :, 1].transpose(1, 0, 2).reshape(owned, KEY_VALUE_HEADS * HEAD_DIM)
    return (
        output[None],
        grad_input[None],
        small[:owned],
        grad_wq,
        grad_wk,
        grad_wv,
        small[2 * owned : at - few],
        small[at - few : at],
        grad_wo,
        small[owned : 2 * owned],
        small[at : at + owned * expert_count].reshape(owned, expert_count),
        grad_gate,
        grad_up,
        grad_down,
    )


def planned_body(mesh):
    if mesh.shape["ctx"] == 8 and mesh.shape["ws"] == 4:
        return tensor_body
    return general_body


def solution(mesh):
    placed = (
        P("ws", "ctx", None),
        P("ws", "ctx", None),
        P("ws", "ctx", None),
        P("ws", None),
        P(("ctx", "ws")),
        P(("ctx", "ws"), None),
        P(("ctx", "ws"), None),
        P(("ctx", "ws"), None),
        P(("ctx", "ws")),
        P(("ctx", "ws")),
        P(("ctx", "ws"), None),
        P(("ctx", "ws")),
        P(("ctx", "ws"), None),
        P(("ctx", "ws"), None, None),
        P(("ctx", "ws"), None, None),
        P(("ctx", "ws"), None, None),
    )
    return jax.shard_map(
        planned_body(mesh),
        mesh=mesh,
        in_specs=placed,
        out_specs=(
            P("ws", "ctx", None),
            P("ws", "ctx", None),
            P(("ctx", "ws")),
            P(("ctx", "ws"), None),
            P(("ctx", "ws"), None),
            P(("ctx", "ws"), None),
            P(("ctx", "ws")),
            P(("ctx", "ws")),
            P(("ctx", "ws"), None),
            P(("ctx", "ws")),
            P(("ctx", "ws"), None),
            P(("ctx", "ws"), None, None),
            P(("ctx", "ws"), None, None),
            P(("ctx", "ws"), None, None),
        ),
        check_vma=False,
    )
```

```python
import jax
import jax.numpy as jnp
from jax import lax
from jax.experimental import pallas as pl
from jax.experimental.pallas import tpu as pltpu
from jax.sharding import PartitionSpec as P

QUERY_HEADS = 32
KEY_VALUE_HEADS = 4
HEAD_DIM = 128
TOPK = 8


EPS = 1e-06
THETA = 1000000.0
MASK_FILL = -1e30
TOP_PRECISION = lax.Precision.HIGHEST
SINGLE_FLOAT = jnp.float32
BRAIN_FLOAT_TYPE = jnp.bfloat16


def rms_scale(values, norm_gain):
    return values * lax.rsqrt(jnp.mean(values * values, axis=-1, keepdims=True) + EPS) * norm_gain


def rotate(values, positions):
    half_dim = values.shape[-1] // 2
    frequency = THETA ** (-2.0 * jnp.arange(half_dim, dtype=jnp.float32) / values.shape[-1])
    angle = positions.astype(jnp.float32)[:, None] * frequency[None, :]
    cosine = jnp.cos(angle)[:, None, :]
    sine_part = jnp.sin(angle)[:, None, :]
    first_half = values[..., :half_dim]
    second_half = values[..., half_dim:]
    return jnp.concatenate(
        [
            first_half * cosine - second_half * sine_part,
            second_half * cosine + first_half * sine_part,
        ],
        axis=-1,
    )


def head_prepare(raw_heads, norm_gain, positions):
    return rotate(rms_scale(raw_heads, norm_gain), positions)


def swiglu(gate_part, up_part):
    return jax.nn.silu(gate_part) * up_part


def stored_positions(row_index, tokens_per_shard, ctx_count):
    device_row = row_index // tokens_per_shard
    within = row_index % tokens_per_shard
    half_block = tokens_per_shard // 2
    block_index = jnp.where(within < half_block, device_row, 2 * ctx_count - 1 - device_row)
    return block_index * half_block + within % half_block


def segment_ids(doc_lengths, positions):
    doc_ends = jnp.cumsum(doc_lengths, dtype=jnp.int32)
    return jnp.sum(
        (positions[:, None] >= doc_ends[None, :]).astype(jnp.int32), axis=1, dtype=jnp.int32
    )


def slot_ranks(flat_routes, expert_count):
    expert_hits = (
        flat_routes[:, None] == jnp.arange(expert_count, dtype=jnp.int32)[None, :]
    ).astype(jnp.int32)
    running = jnp.cumsum(expert_hits, axis=0, dtype=jnp.int32) - 1
    return jnp.sum(expert_hits * running, axis=1, dtype=jnp.int32)


def send_inputs(flat_rows):
    moved = lax.all_to_all(flat_rows, ("ctx", "ws"), split_axis=0, concat_axis=0, tiled=True)
    return moved


def send_outputs(flat_rows):
    moved = lax.all_to_all(flat_rows, ("ctx", "ws"), split_axis=0, concat_axis=0, tiled=True)
    return moved


def send_out_grads(flat_rows):
    moved = lax.all_to_all(flat_rows, ("ctx", "ws"), split_axis=0, concat_axis=0, tiled=True)
    return moved


def send_in_grads(flat_rows):
    moved = lax.all_to_all(flat_rows, ("ctx", "ws"), split_axis=0, concat_axis=0, tiled=True)
    return moved


def flat_rows(grid_sum):
    return grid_sum.reshape((-1,) + grid_sum.shape[3:])


def to_expert_major(arrived, expert_local):
    device_count, row_span, model_width = arrived.shape
    capacity = row_span // expert_local
    shaped = arrived.reshape(device_count, expert_local, capacity, model_width)
    return shaped.transpose(1, 0, 2, 3).reshape(expert_local, device_count * capacity, model_width)


def to_device_major(expert_rows, device_count):
    expert_local, row_span, model_width = expert_rows.shape
    capacity = row_span // device_count
    shaped = expert_rows.reshape(expert_local, device_count, capacity, model_width)
    return shaped.transpose(1, 0, 2, 3).reshape(device_count, expert_local * capacity, model_width)


def general_body(
    inputs,
    grad_output,
    routes,
    doc_lengths,
    norm_attn,
    w_query,
    key_projection,
    value_projection,
    query_norm,
    key_norm,
    w_out,
    norm_ffn,
    w_router,
    expert_gate,
    expert_up,
    expert_down,
):
    ctx_count = lax.axis_size("ctx")
    device_count = ctx_count * lax.axis_size("ws")
    tokens_per_shard = inputs.shape[1]
    model_width = inputs.shape[2]
    sequence_tokens = tokens_per_shard * ctx_count
    expert_count = w_router.shape[1]
    expert_local = expert_gate.shape[0]
    capacity = max(2, tokens_per_shard * TOPK * 3 // (2 * device_count))
    query_group_size = QUERY_HEADS // KEY_VALUE_HEADS
    logit_scale = HEAD_DIM ** (-0.5)
    single_key_block = min(512, sequence_tokens)
    count_of_blocks = sequence_tokens // single_key_block
    ctx_index = lax.axis_index("ctx")
    positions_all = stored_positions(
        jnp.arange(sequence_tokens, dtype=jnp.int32), tokens_per_shard, ctx_count
    )
    segments_all = segment_ids(doc_lengths[0], positions_all)
    local_positions = lax.dynamic_slice_in_dim(
        positions_all, ctx_index * tokens_per_shard, tokens_per_shard
    )
    segments_own = lax.dynamic_slice_in_dim(
        segments_all, ctx_index * tokens_per_shard, tokens_per_shard
    )
    validity = (segments_own < doc_lengths.shape[1]).astype(SINGLE_FLOAT)
    shards = (
        norm_attn,
        w_query,
        key_projection,
        value_projection,
        query_norm,
        key_norm,
        w_out,
        norm_ffn,
        w_router,
    )
    gathered = (
        lax.all_gather(shards[0], ("ctx", "ws"), axis=0, tiled=True),
        lax.all_gather(shards[1], ("ctx", "ws"), axis=0, tiled=True),
        lax.all_gather(shards[2], ("ctx", "ws"), axis=0, tiled=True),
        lax.all_gather(shards[3], ("ctx", "ws"), axis=0, tiled=True),
        lax.all_gather(shards[4], ("ctx", "ws"), axis=0, tiled=True),
        lax.all_gather(shards[5], ("ctx", "ws"), axis=0, tiled=True),
        lax.all_gather(shards[6], ("ctx", "ws"), axis=0, tiled=True),
        lax.all_gather(shards[7], ("ctx", "ws"), axis=0, tiled=True),
        lax.all_gather(shards[8], ("ctx", "ws"), axis=0, tiled=True),
    )
    (
        attn_gain,
        query_matrix,
        key_matrix,
        value_matrix,
        query_gain,
        key_norm_gain,
        output_matrix,
        ffn_gain,
        router_matrix,
    ) = gathered
    attn_gain = attn_gain.astype(SINGLE_FLOAT)
    query_gain = query_gain.astype(SINGLE_FLOAT)
    key_norm_gain = key_norm_gain.astype(SINGLE_FLOAT)
    ffn_gain = ffn_gain.astype(SINGLE_FLOAT)
    layer_in = inputs[0].astype(SINGLE_FLOAT)
    normalized_rows = rms_scale(layer_in, attn_gain).astype(BRAIN_FLOAT_TYPE)
    unnormed_queries = jnp.dot(
        normalized_rows, query_matrix, preferred_element_type=SINGLE_FLOAT
    ).reshape(tokens_per_shard, QUERY_HEADS, HEAD_DIM)
    unnormed_keys = jnp.dot(
        normalized_rows, key_matrix, preferred_element_type=SINGLE_FLOAT
    ).reshape(tokens_per_shard, KEY_VALUE_HEADS, HEAD_DIM)
    value_low = jnp.dot(normalized_rows, value_matrix, preferred_element_type=SINGLE_FLOAT).astype(
        BRAIN_FLOAT_TYPE
    )
    query_rows = head_prepare(unnormed_queries, query_gain, local_positions).astype(
        BRAIN_FLOAT_TYPE
    )
    key_low = (
        head_prepare(unnormed_keys, key_norm_gain, local_positions)
        .astype(BRAIN_FLOAT_TYPE)
        .reshape(tokens_per_shard, KEY_VALUE_HEADS * HEAD_DIM)
    )
    every_key, every_value = (
        lax.all_gather(key_low, "ctx", axis=0, tiled=True),
        lax.all_gather(value_low, "ctx", axis=0, tiled=True),
    )
    grouped_queries = query_rows.reshape(
        tokens_per_shard, KEY_VALUE_HEADS, query_group_size, HEAD_DIM
    )
    blocked_keys = every_key.reshape(count_of_blocks, single_key_block, KEY_VALUE_HEADS, HEAD_DIM)
    blocked_values = every_value.reshape(
        count_of_blocks, single_key_block, KEY_VALUE_HEADS, HEAD_DIM
    )
    position_blocks = positions_all.reshape(count_of_blocks, single_key_block)
    segment_blocks = segments_all.reshape(count_of_blocks, single_key_block)

    def scores_for(block_keys, block_positions, block_segments):
        raw_scores = (
            jnp.einsum(
                "tkgd,jkd->kgtj", grouped_queries, block_keys, preferred_element_type=SINGLE_FLOAT
            )
            * logit_scale
        )
        allowed = (segments_own[:, None] == block_segments[None, :]) & (
            block_positions[None, :] <= local_positions[:, None]
        )
        return (raw_scores, allowed[None, None])

    def stats_step(running, pieces):
        maximum, denominator = running
        block_keys, block_positions, block_segments = pieces
        raw_scores, allowed = scores_for(block_keys, block_positions, block_segments)
        masked = jnp.where(allowed, raw_scores, MASK_FILL)
        new_maximum = jnp.maximum(maximum, jnp.max(masked, axis=-1))
        weights = jnp.where(allowed, jnp.exp(masked - new_maximum[..., None]), 0.0)
        denominator = denominator * jnp.exp(maximum - new_maximum) + jnp.sum(weights, axis=-1)
        return ((new_maximum, denominator), None)

    stats_init = (
        jnp.full((KEY_VALUE_HEADS, query_group_size, tokens_per_shard), MASK_FILL, SINGLE_FLOAT),
        jnp.zeros((KEY_VALUE_HEADS, query_group_size, tokens_per_shard), SINGLE_FLOAT),
    )
    (maximum, denominator), _ = lax.scan(
        stats_step, stats_init, (blocked_keys, position_blocks, segment_blocks)
    )

    def probs_for(raw_scores, allowed):
        return (
            jnp.where(allowed, jnp.exp(raw_scores - maximum[..., None]), 0.0)
            / denominator[..., None]
        )

    def value_update(running, pieces):
        block_keys, block_values, block_positions, block_segments = pieces
        raw_scores, allowed = scores_for(block_keys, block_positions, block_segments)
        softmaxed = probs_for(raw_scores, allowed).astype(BRAIN_FLOAT_TYPE)
        running = running + jnp.einsum(
            "kgtj,jkd->tkgd", softmaxed, block_values, preferred_element_type=SINGLE_FLOAT
        )
        return (running, None)

    inputs_per_block = (blocked_keys, blocked_values, position_blocks, segment_blocks)
    attended, _ = lax.scan(
        value_update,
        jnp.zeros((tokens_per_shard, KEY_VALUE_HEADS, query_group_size, HEAD_DIM), SINGLE_FLOAT),
        inputs_per_block,
    )
    attn_low = attended.reshape(tokens_per_shard, QUERY_HEADS * HEAD_DIM).astype(BRAIN_FLOAT_TYPE)
    hidden_state = layer_in + jnp.dot(attn_low, output_matrix, preferred_element_type=SINGLE_FLOAT)
    combined_rows = rms_scale(hidden_state, ffn_gain).astype(BRAIN_FLOAT_TYPE)
    router_scores = jnp.dot(combined_rows, router_matrix, preferred_element_type=SINGLE_FLOAT)
    own_routes = routes[0]
    route_mask = (
        own_routes[:, :, None] == jnp.arange(expert_count, dtype=jnp.int32)[None, None, :]
    ).astype(SINGLE_FLOAT)
    chosen = jnp.einsum("tke,te->tk", route_mask, router_scores, precision=TOP_PRECISION)
    gate_share = jax.nn.softmax(chosen, axis=-1)
    flat_routes = own_routes.reshape(-1)
    slot_index = flat_routes * capacity + slot_ranks(flat_routes, expert_count)
    entries = tokens_per_shard * TOPK
    source_slot = (
        jnp.full((expert_count * capacity,), entries, jnp.int32)
        .at[slot_index]
        .set(jnp.arange(entries, dtype=jnp.int32))
    )
    padded_in = jnp.concatenate(
        [combined_rows, jnp.zeros((1, model_width), BRAIN_FLOAT_TYPE)], axis=0
    )
    outgoing = padded_in[source_slot // TOPK].reshape(device_count, -1, model_width)
    expert_in = to_expert_major(send_inputs(outgoing), expert_local)
    gate_hidden = jnp.einsum(
        "erd,edf->erf", expert_in, expert_gate, preferred_element_type=SINGLE_FLOAT
    )
    up_hidden = jnp.einsum(
        "erd,edf->erf", expert_in, expert_up, preferred_element_type=SINGLE_FLOAT
    )
    hidden = swiglu(gate_hidden, up_hidden).astype(BRAIN_FLOAT_TYPE)
    expert_out = jnp.einsum(
        "erf,efd->erd", hidden, expert_down, preferred_element_type=SINGLE_FLOAT
    ).astype(BRAIN_FLOAT_TYPE)
    returned = send_outputs(to_device_major(expert_out, device_count)).reshape(
        expert_count * capacity, model_width
    )
    picked = returned[slot_index].reshape(tokens_per_shard, TOPK, model_width)
    moe_sum = jnp.sum(gate_share[:, :, None] * picked.astype(SINGLE_FLOAT), axis=1)
    output = (hidden_state + moe_sum).astype(BRAIN_FLOAT_TYPE)
    d_layer = grad_output[0].astype(SINGLE_FLOAT) * validity[:, None]
    d_gate_share = jnp.sum(d_layer[:, None, :] * picked.astype(SINGLE_FLOAT), axis=-1)
    d_chosen = gate_share * (
        d_gate_share - jnp.sum(gate_share * d_gate_share, axis=-1, keepdims=True)
    )
    d_logits = jnp.einsum("tke,tk->te", route_mask, d_chosen, precision=TOP_PRECISION).astype(
        BRAIN_FLOAT_TYPE
    )
    d_copies = (
        (gate_share[:, :, None] * d_layer[:, None, :])
        .astype(BRAIN_FLOAT_TYPE)
        .reshape(entries, model_width)
    )
    d_padded = jnp.concatenate([d_copies, jnp.zeros((1, model_width), BRAIN_FLOAT_TYPE)], axis=0)
    d_outgoing = d_padded[source_slot].reshape(device_count, -1, model_width)
    d_expert_out = to_expert_major(send_out_grads(d_outgoing), expert_local)
    d_hidden = jnp.einsum(
        "erd,efd->erf", d_expert_out, expert_down, preferred_element_type=SINGLE_FLOAT
    )
    grad_down = jnp.einsum(
        "erf,erd->efd", hidden, d_expert_out, preferred_element_type=SINGLE_FLOAT
    )
    _, swiglu_back = jax.vjp(swiglu, gate_hidden, up_hidden)
    d_gate_hidden, d_up_hidden = swiglu_back(d_hidden)
    d_gate_low = d_gate_hidden.astype(BRAIN_FLOAT_TYPE)
    d_up_low = d_up_hidden.astype(BRAIN_FLOAT_TYPE)
    grad_gate = jnp.einsum(
        "erd,erf->edf", expert_in, d_gate_low, preferred_element_type=SINGLE_FLOAT
    )
    grad_up = jnp.einsum("erd,erf->edf", expert_in, d_up_low, preferred_element_type=SINGLE_FLOAT)
    d_expert_in = jnp.einsum(
        "erf,edf->erd", d_gate_low, expert_gate, preferred_element_type=SINGLE_FLOAT
    )
    d_expert_in = (
        d_expert_in
        + jnp.einsum("erf,edf->erd", d_up_low, expert_up, preferred_element_type=SINGLE_FLOAT)
    ).astype(BRAIN_FLOAT_TYPE)
    d_returned = send_in_grads(to_device_major(d_expert_in, device_count)).reshape(
        expert_count * capacity, model_width
    )
    d_slots = d_returned[slot_index].reshape(tokens_per_shard, TOPK, model_width)
    d_mixed = jnp.sum(d_slots.astype(SINGLE_FLOAT), axis=1) + jnp.einsum(
        "te,de->td", d_logits, router_matrix, preferred_element_type=SINGLE_FLOAT
    )
    grad_router = jnp.einsum(
        "td,te->de", combined_rows, d_logits, preferred_element_type=SINGLE_FLOAT
    )
    _, ffn_norm_back = jax.vjp(rms_scale, hidden_state, ffn_gain)
    d_state_norm, grad_ffn_gain = ffn_norm_back(d_mixed)
    d_state = d_layer + d_state_norm
    d_state_low = d_state.astype(BRAIN_FLOAT_TYPE)
    grad_out_weight = jnp.einsum(
        "tc,td->cd", attn_low, d_state_low, preferred_element_type=SINGLE_FLOAT
    )
    attention_gradient = jnp.einsum(
        "td,cd->tc", d_state_low, output_matrix, preferred_element_type=SINGLE_FLOAT
    ).astype(BRAIN_FLOAT_TYPE)
    attention_gradient = attention_gradient.reshape(
        tokens_per_shard, KEY_VALUE_HEADS, query_group_size, HEAD_DIM
    )
    row_delta = jnp.sum(attention_gradient.astype(SINGLE_FLOAT) * attended, axis=-1).transpose(
        1, 2, 0
    )

    def backward_step(d_query_acc, pieces):
        block_keys, block_values, block_positions, block_segments = pieces
        raw_scores, allowed = scores_for(block_keys, block_positions, block_segments)
        softmaxed = probs_for(raw_scores, allowed)
        d_probs = jnp.einsum(
            "tkgd,jkd->kgtj", attention_gradient, block_values, preferred_element_type=SINGLE_FLOAT
        )
        d_scores = (softmaxed * (d_probs - row_delta[..., None])).astype(BRAIN_FLOAT_TYPE)
        d_query_acc = d_query_acc + jnp.einsum(
            "kgtj,jkd->tkgd", d_scores, block_keys, preferred_element_type=SINGLE_FLOAT
        )
        d_key_block = jnp.einsum(
            "kgtj,tkgd->jkd", d_scores, grouped_queries, preferred_element_type=SINGLE_FLOAT
        )
        d_value_block = jnp.einsum(
            "kgtj,tkgd->jkd",
            softmaxed.astype(BRAIN_FLOAT_TYPE),
            attention_gradient,
            preferred_element_type=SINGLE_FLOAT,
        )
        return (d_query_acc, (d_key_block, d_value_block))

    d_query_acc, (key_block_gradients, value_block_gradients) = lax.scan(
        backward_step,
        jnp.zeros((tokens_per_shard, KEY_VALUE_HEADS, query_group_size, HEAD_DIM), SINGLE_FLOAT),
        inputs_per_block,
    )
    every_key_gradient = (key_block_gradients * logit_scale).reshape(
        sequence_tokens, KEY_VALUE_HEADS * HEAD_DIM
    )
    every_value_gradient = value_block_gradients.reshape(
        sequence_tokens, KEY_VALUE_HEADS * HEAD_DIM
    )
    key_gradients, d_values = (
        lax.psum_scatter(
            every_key_gradient.astype(jnp.bfloat16), "ctx", scatter_dimension=0, tiled=True
        ).astype(jnp.float32),
        lax.psum_scatter(
            every_value_gradient.astype(jnp.bfloat16), "ctx", scatter_dimension=0, tiled=True
        ).astype(jnp.float32),
    )
    _, query_back = jax.vjp(
        lambda raw_heads, norm_gain: head_prepare(raw_heads, norm_gain, local_positions),
        unnormed_queries,
        query_gain,
    )
    d_query_raw, grad_query_gain = query_back(
        (d_query_acc * logit_scale).reshape(tokens_per_shard, QUERY_HEADS, HEAD_DIM)
    )
    _, key_backward = jax.vjp(
        lambda raw_heads, norm_gain: head_prepare(raw_heads, norm_gain, local_positions),
        unnormed_keys,
        key_norm_gain,
    )
    raw_key_gradient, key_gain_gradient = key_backward(
        key_gradients.reshape(tokens_per_shard, KEY_VALUE_HEADS, HEAD_DIM)
    )
    d_query_low = d_query_raw.reshape(tokens_per_shard, QUERY_HEADS * HEAD_DIM).astype(
        BRAIN_FLOAT_TYPE
    )
    key_gradient_lowprec = raw_key_gradient.reshape(
        tokens_per_shard, KEY_VALUE_HEADS * HEAD_DIM
    ).astype(BRAIN_FLOAT_TYPE)
    d_value_low = d_values.astype(BRAIN_FLOAT_TYPE)
    grad_query_weight = jnp.einsum(
        "td,tc->dc", normalized_rows, d_query_low, preferred_element_type=SINGLE_FLOAT
    )
    grad_key_weight = jnp.einsum(
        "td,tc->dc", normalized_rows, key_gradient_lowprec, preferred_element_type=SINGLE_FLOAT
    )
    grad_value_weight = jnp.einsum(
        "td,tc->dc", normalized_rows, d_value_low, preferred_element_type=SINGLE_FLOAT
    )
    d_normed = jnp.einsum(
        "tc,dc->td", d_query_low, query_matrix, preferred_element_type=SINGLE_FLOAT
    )
    d_normed = d_normed + jnp.einsum(
        "tc,dc->td", key_gradient_lowprec, key_matrix, preferred_element_type=SINGLE_FLOAT
    )
    d_normed = d_normed + jnp.einsum(
        "tc,dc->td", d_value_low, value_matrix, preferred_element_type=SINGLE_FLOAT
    )
    _, attn_norm_back = jax.vjp(rms_scale, layer_in, attn_gain)
    d_input_norm, grad_attn_gain = attn_norm_back(d_normed)
    grad_input = d_state + d_input_norm
    reduced = (
        lax.psum_scatter(grad_attn_gain, ("ctx", "ws"), scatter_dimension=0, tiled=True),
        lax.psum_scatter(grad_query_weight, ("ctx", "ws"), scatter_dimension=0, tiled=True),
        lax.psum_scatter(grad_key_weight, ("ctx", "ws"), scatter_dimension=0, tiled=True),
        lax.psum_scatter(grad_value_weight, ("ctx", "ws"), scatter_dimension=0, tiled=True),
        lax.psum_scatter(grad_query_gain, ("ctx", "ws"), scatter_dimension=0, tiled=True),
        lax.psum_scatter(key_gain_gradient, ("ctx", "ws"), scatter_dimension=0, tiled=True),
        lax.psum_scatter(grad_out_weight, ("ctx", "ws"), scatter_dimension=0, tiled=True),
        lax.psum_scatter(grad_ffn_gain, ("ctx", "ws"), scatter_dimension=0, tiled=True),
        lax.psum_scatter(grad_router, ("ctx", "ws"), scatter_dimension=0, tiled=True),
    )
    return (
        output[None],
        grad_input[None],
        reduced[0],
        reduced[1],
        reduced[2],
        reduced[3],
        reduced[4],
        reduced[5],
        reduced[6],
        reduced[7],
        reduced[8],
        grad_gate,
        grad_up,
        grad_down,
    )


VMEM_WHOLE = pl.BlockSpec(memory_space=pltpu.VMEM)
VMEM_BYTES = 60 * 2**20
EXTRA = 128


def compiler_params():
    return pltpu.CompilerParams(vmem_limit_bytes=VMEM_BYTES)


def dot_rows(left, right):
    return lax.dot_general(
        left, right, (((1,), (0,)), ((), ())), preferred_element_type=SINGLE_FLOAT
    )


def dot_right_transposed(left, right):
    return lax.dot_general(
        left, right, (((1,), (1,)), ((), ())), preferred_element_type=SINGLE_FLOAT
    )


def dot_left_transposed(left, right):
    return lax.dot_general(
        left, right, (((0,), (0,)), ((), ())), preferred_element_type=SINGLE_FLOAT
    )


def key_range(tile, tile_rows, sequence_tokens, slack):
    half = sequence_tokens // 2
    first_row = tile * tile_rows
    low = 0 if first_row < half + slack else half
    return low, first_row + tile_rows


def stacked_heads(ref, rows, heads):
    return jnp.concatenate(
        [ref[rows, h * HEAD_DIM : (h + 1) * HEAD_DIM] for h in range(heads)], axis=0
    )


def tile_scores(q4, k_ref, segc_ref, segr_ref, low, high, first_row, tile_rows, heads):
    scale = HEAD_DIM ** (-0.5)
    scores = dot_right_transposed(q4, k_ref[low:high, :]) * scale
    span = high - low
    query_place = first_row + lax.broadcasted_iota(jnp.int32, (tile_rows, span), 0)
    key_place = low + lax.broadcasted_iota(jnp.int32, (tile_rows, span), 1)
    allowed = (segc_ref[first_row : first_row + tile_rows, :] == segr_ref[:, low:high]) & (
        key_place <= query_place
    )
    fill = jnp.where(allowed, 0.0, MASK_FILL)
    scores = scores + jnp.concatenate([fill] * heads, axis=0)
    exponent = jnp.exp(scores - jnp.max(scores, axis=-1, keepdims=True))
    return exponent * (1.0 / jnp.sum(exponent, axis=-1, keepdims=True))


def head_backward(turned_gradient, part, gain, cosine, sine):
    scaled_gradient = turned_gradient * cosine - (
        pltpu.roll(turned_gradient, HEAD_DIM // 2, 1) * sine
    )
    inverse = lax.rsqrt(jnp.mean(part * part, axis=-1, keepdims=True) + EPS)
    unit = part * inverse
    gain_gradient = jnp.sum(scaled_gradient * unit, axis=0, keepdims=True)
    unit_gradient = scaled_gradient * gain
    raw_gradient = inverse * (
        unit_gradient - unit * jnp.mean(unit * unit_gradient, axis=-1, keepdims=True)
    )
    return raw_gradient, gain_gradient


MESH = pl.DeviceIdType.MESH
ANYWHERE = pl.BlockSpec(memory_space=pl.ANY)
LINE = 4


def place():
    c, w = lax.axis_index("ctx"), lax.axis_index("ws")
    return c // 2, c % 2, w // 2, w % 2


def device_at(z, y, x, k):
    return (z * 2 + y, x * 2 + k)


def slot_of(z, y, x, k):
    return ((z * 2 + y) * 2 + x) * 2 + k


def line_order(z):
    upper = z // 2
    return [z, z + 1 - 2 * upper, 2 - 2 * (z % 2) + upper, 3 - 3 * upper]


def remote(source, target, send, recv, device):
    return pltpu.make_async_remote_copy(
        src_ref=source,
        dst_ref=target,
        send_sem=send,
        recv_sem=recv,
        device_id=device,
        device_id_type=MESH,
    )


def meet(z, y, x, k, around):
    barrier = pltpu.get_barrier_semaphore()

    def greet(device):
        pl.semaphore_signal(barrier, inc=1, device_id=device, device_id_type=MESH)

    @pl.when(z < LINE - 1)
    def _():
        greet(device_at(z + 1, y, x, k))

    @pl.when(z > 0)
    def _():
        greet(device_at(z - 1, y, x, k))

    for device in around:
        greet(device)
    pl.semaphore_wait(barrier, len(around) + 1 + z * (LINE - 1 - z) // 2)


class Sends:
    def __init__(self, semaphores):
        self.semaphores = semaphores
        self.started = []

    def start(self, source, target, recv, device, condition=None):
        copy = remote(source, target, self.semaphores.at[len(self.started)], recv, device)
        if condition is None:
            copy.start()
        else:
            pl.when(condition)(copy.start)
        self.started.append((condition, copy))

    def finish(self):
        for condition, copy in self.started:
            if condition is None:
                copy.wait_send()
            else:
                pl.when(condition)(copy.wait_send)


def arrived(target, recv, device):
    remote(target, target, recv, recv, device).wait_recv()


def along_line(z, y, x, k, block, i, order, start):
    if i == 0:
        up, down = z < LINE - 1, z > 0
    else:
        below = order[i] < z
        up, down = below & (z < LINE - 1), jnp.logical_not(below) & (z > 0)
    start(block, device_at(z + 1, y, x, k), up)
    start(block, device_at(z - 1, y, x, k), down)


class BlockGather:
    def __init__(self, source, out, local, send_sems, recv_sems):
        self.source, self.out, self.recv_sems = source, out, recv_sems
        z, y, x, k = self.at = place()
        self.order = line_order(z)
        self.along_x, self.along_y = device_at(z, y, 1 - x, k), device_at(z, 1 - y, x, k)
        self.sibling = device_at(z, y, x, 1 - k)
        self.sends = Sends(send_sems)
        self.mine = slot_of(z, y, x, k)
        self.own = pltpu.make_async_copy(source, out.at[self.mine], local)

    def pass_on(self, slot, device, condition=None):
        block = self.source if slot is self.mine else self.out.at[slot]
        self.sends.start(block, self.out.at[slot], self.recv_sems.at[slot], device, condition)

    def wait(self, slot):
        arrived(self.out.at[slot], self.recv_sems.at[slot], self.along_x)

    def column(self, i):
        z, y, x, k = self.at
        slot = self.mine if i == 0 else slot_of(self.order[i], y, x, k)
        if i > 0:
            self.wait(slot)
        along_line(z, y, x, k, slot, i, self.order, self.pass_on)
        for device in (self.along_x, self.along_y, self.sibling):
            self.pass_on(slot, device)

    def across(self, i, on_x, on_y):
        z, y, x, k = self.at
        return slot_of(self.order[i], 1 - y if on_y else y, 1 - x if on_x else x, k)

    def receive(self, slot):
        self.wait(slot)
        self.pass_on(slot, self.sibling)

    def begin(self):
        meet(*self.at, (self.along_x, self.along_y, self.sibling))
        self.own.start()
        self.column(0)

    def advance(self, i):
        self.column(i)
        self.receive(self.across(i - 1, True, False))
        self.receive(self.across(i - 1, False, True))

    def finish(self):
        self.receive(self.across(3, True, False))
        for j in (0, 1):
            self.pass_on(self.across(j, True, False), self.along_y)
        self.receive(self.across(3, False, True))
        for j in (2, 3):
            self.pass_on(self.across(j, False, True), self.along_x)
        for i in range(4):
            self.receive(self.across(i, True, True))
        z, y, x, k = self.at
        for i in range(4):
            for dy in (y, 1 - y):
                for dx in (x, 1 - x):
                    self.wait(slot_of(self.order[i], dy, dx, 1 - k))
        self.own.wait()
        self.sends.finish()


def gather_all_kernel(source, out, *semaphores):
    blocks = BlockGather(source, out, *semaphores)
    blocks.begin()
    for i in (1, 2, 3):
        blocks.advance(i)
    blocks.finish()


def gather_all(block, collective_id):
    return pl.pallas_call(
        gather_all_kernel,
        out_shape=jax.ShapeDtypeStruct((32,) + block.shape, block.dtype),
        in_specs=[ANYWHERE],
        out_specs=ANYWHERE,
        scratch_shapes=[
            pltpu.SemaphoreType.DMA,
            pltpu.SemaphoreType.DMA((40,)),
            pltpu.SemaphoreType.DMA((32,)),
        ],
        compiler_params=pltpu.CompilerParams(collective_id=collective_id, has_side_effects=True),
        name="gather_all",
    )(block)


def add_blocks(target, *terms):
    rows = target.shape[0]

    def step(i, carry):
        part = pl.ds(pl.multiple_of(i * 16, 16), 16)
        total = terms[0][part, :].astype(SINGLE_FLOAT)
        for term in terms[1:]:
            total = total + term[part, :].astype(SINGLE_FLOAT)
        target[part, :] = total.astype(target.dtype)
        return carry

    lax.fori_loop(0, rows // 16, step, 0)


def scatter_line(z, y, x, k, order, total, owned, up_ref, down_ref, up_sems, down_sems, sends, out, after):
    above, below = device_at(z + 1, y, x, k), device_at(z - 1, y, x, k)
    for i in (3, 2, 1):
        total(i)
        chip = order[i]
        upward = chip > z
        block = owned(i)

        @pl.when(upward & (z > 0))
        def _():
            arrived(up_ref.at[chip], up_sems.at[chip], below)
            add_blocks(block, block, up_ref.at[chip])

        @pl.when(jnp.logical_not(upward) & (z < LINE - 1))
        def _():
            arrived(down_ref.at[chip], down_sems.at[chip], above)
            add_blocks(block, block, down_ref.at[chip])

        sends.start(block, up_ref.at[chip], up_sems.at[chip], above, upward)
        sends.start(
            block, down_ref.at[chip], down_sems.at[chip], below, jnp.logical_not(upward)
        )
        after(i)
    total(0)
    block = owned(0)

    @pl.when(z > 0)
    def _():
        arrived(up_ref.at[z], up_sems.at[z], below)

    @pl.when(z < LINE - 1)
    def _():
        arrived(down_ref.at[z], down_sems.at[z], above)

    @pl.when(z == 0)
    def _():
        add_blocks(out, block, down_ref.at[z])

    @pl.when(z == LINE - 1)
    def _():
        add_blocks(out, block, up_ref.at[z])

    @pl.when((z > 0) & (z < LINE - 1))
    def _():
        add_blocks(out, block, up_ref.at[z], down_ref.at[z])


class PickedSums:
    def __init__(self, rows_in, pick_in, out, scratch):
        (
            self.rows_ref,
            self.pick_ref,
            self.own_ref,
            self.corner_ref,
            self.x_ref,
            self.y_ref,
            self.up_ref,
            self.down_ref,
            load_sems,
            self.corner_sems,
            self.x_sems,
            self.y_sems,
            self.up_sems,
            self.down_sems,
            send_sems,
        ) = scratch
        self.out = out
        z, y, x, k = self.at = place()
        self.order = line_order(z)
        self.along_x, self.along_y = device_at(z, y, 1 - x, k), device_at(z, 1 - y, x, k)
        self.pick_load = pltpu.make_async_copy(pick_in, self.pick_ref, load_sems.at[16])
        self.turn = [i * 4 + r for r in (3, 1, 2, 0) for i in (3, 2, 1, 0)]
        self.loads = {
            j: pltpu.make_async_copy(rows_in.at[j], self.rows_ref.at[j], load_sems.at[j])
            for j in self.turn
        }
        self.sends = Sends(send_sems)

    def begin(self):
        self.pick_load.start()
        for j in self.turn:
            self.loads[j].start()
        meet(*self.at, (self.along_x, self.along_y))
        self.pick_load.wait()

    def gather(self, i, r, *extra):
        j = i * 4 + r
        self.loads[j].wait()
        block = self.own_ref.at[j]
        spread_rows(block, self.pick_ref.at[j], self.rows_ref.at[j], *extra)
        return block

    def corners(self):
        for i in (3, 2, 1, 0):
            self.sends.start(
                self.gather(i, 3),
                self.corner_ref.at[i],
                self.corner_sems.at[i],
                self.along_y if i < 2 else self.along_x,
            )

    def cross(self, i):
        arrived(self.corner_ref.at[i], self.corner_sems.at[i], self.along_x)
        extra = (self.corner_ref.at[i],)
        for_x = self.gather(i, 1, *(extra if i < 2 else ()))
        self.sends.start(for_x, self.x_ref.at[i], self.x_sems.at[i], self.along_x)
        for_y = self.gather(i, 2, *(extra if i >= 2 else ()))
        self.sends.start(for_y, self.y_ref.at[i], self.y_sems.at[i], self.along_y)

    def total(self, i):
        arrived(self.x_ref.at[i], self.x_sems.at[i], self.along_x)
        arrived(self.y_ref.at[i], self.y_sems.at[i], self.along_y)
        if i > 0:
            self.cross(i - 1)
        self.gather(i, 0, self.x_ref.at[i], self.y_ref.at[i])

    def finish(self, between=lambda i: None):
        scatter_line(
            *self.at, self.order, self.total, lambda i: self.own_ref.at[i * 4],
            self.up_ref, self.down_ref, self.up_sems, self.down_sems, self.sends, self.out,
            between,
        )
        self.sends.finish()


def picked_scratch(rows, pick):
    shape, low = (pick.shape[2], rows.shape[2]), rows.dtype
    return (
        [pltpu.VMEM(rows.shape, low), pltpu.VMEM(pick.shape, low)]
        + [pltpu.VMEM((n,) + shape, low) for n in (16, 4, 4, 4, 4, 4)]
        + [pltpu.SemaphoreType.DMA((n,)) for n in (17, 4, 4, 4, 4, 4, 24)]
    )


def halves(ref, z, y):
    half = ref.shape[0] // 16
    c = z * 2 + y
    return [
        ref.at[pl.ds(pl.multiple_of(half * b, half), half), :] for b in (c, 15 - c)
    ]


def split_rows(ref):
    half = ref.shape[0] // 2
    return [ref.at[0:half, :], ref.at[half : 2 * half, :]]


class RowGather:
    def __init__(self, source, out, sends, locals_, semaphores, at, order, along_y):
        self.source, self.out, self.sends, self.semaphores = source, out, sends, semaphores
        self.at, self.order, self.along_y = at, order, along_y
        z, y, x, k = at
        self.own = [
            pltpu.make_async_copy(a, b, locals_.at[n])
            for n, (a, b) in enumerate(zip(split_rows(source), halves(out, z, y)))
        ]
        for copy in self.own:
            copy.start()

    def column(self, i):
        z, y, x, k = self.at
        chip = self.order[i]
        pieces = halves(self.out, chip, y)
        if i > 0:
            self.wait(chip, y)
        for n in (0, 1):
            block = split_rows(self.source)[n] if i == 0 else pieces[n]
            recv = self.semaphores.at[n, chip * 2 + y]

            def start(_, device, condition=None):
                self.sends.start(block, pieces[n], recv, device, condition)

            along_line(z, y, x, k, None, i, self.order, start)
            start(None, self.along_y)

    def wait(self, chip, y):
        for n, piece in enumerate(halves(self.out, chip, y)):
            arrived(piece, self.semaphores.at[n, chip * 2 + y], self.along_y)

    def finish(self):
        y = self.at[1]
        for i in range(4):
            self.wait(self.order[i], 1 - y)
        for copy in self.own:
            copy.wait()


def gather_rows_kernel(source, out, local_sems, send_sems, recv_sems):
    at = place()
    z, y, x, k = at
    along_y = device_at(z, 1 - y, x, k)
    meet(z, y, x, k, (along_y,))
    sends = Sends(send_sems)
    rows = RowGather(source, out, sends, local_sems, recv_sems, at, line_order(z), along_y)
    for i in range(4):
        rows.column(i)
    rows.finish()
    sends.finish()


def gather_rows(block, collective_id):
    rows, width = block.shape
    dma = pltpu.SemaphoreType.DMA
    return pl.pallas_call(
        gather_rows_kernel,
        out_shape=jax.ShapeDtypeStruct((8 * rows, width), block.dtype),
        in_specs=[ANYWHERE],
        out_specs=ANYWHERE,
        scratch_shapes=[dma((2,)), dma((24,)), dma((2, 8))],
        compiler_params=pltpu.CompilerParams(collective_id=collective_id, has_side_effects=True),
        name="gather_rows",
    )(block)


class RowScatter:
    def __init__(self, part, out, buffers, semaphores, sends, at, order, along_y):
        self.part, self.out, self.sends, self.at, self.order = part, out, sends, at, order
        self.along_y = along_y
        self.own_ref, self.y_ref, self.up_ref, self.down_ref = buffers
        self.load_sems, self.y_sems, self.up_sems, self.down_sems = semaphores
        z, y, x, k = at
        self.loads = {}
        for i in (3, 2, 1, 0):
            self.loads[i] = [
                pltpu.make_async_copy(a, b, self.load_sems.at[n, i])
                for n, (a, b) in enumerate(
                    zip(halves(part, order[i], y), split_rows(self.own_ref.at[i]))
                )
            ]
            for copy in self.loads[i]:
                copy.start()
        self.cross(3)

    def cross(self, i):
        y = self.at[1]
        for n, (a, b) in enumerate(
            zip(halves(self.part, self.order[i], 1 - y), split_rows(self.y_ref.at[i]))
        ):
            self.sends.start(a, b, self.y_sems.at[n, i], self.along_y)

    def total(self, i):
        for copy in self.loads[i]:
            copy.wait()
        for n, piece in enumerate(split_rows(self.y_ref.at[i])):
            arrived(piece, self.y_sems.at[n, i], self.along_y)
        if i > 0:
            self.cross(i - 1)
        add_blocks(self.own_ref.at[i], self.own_ref.at[i], self.y_ref.at[i])

    def run(self, after=lambda i: None):
        z, y, x, k = self.at
        scatter_line(
            z, y, x, k, self.order, self.total, lambda i: self.own_ref.at[i],
            self.up_ref, self.down_ref, self.up_sems, self.down_sems, self.sends, self.out,
            after,
        )


def row_scatter_scratch(rows, width, low):
    dma = pltpu.SemaphoreType.DMA
    return [pltpu.VMEM((4, rows, width), low)] * 4 + [
        dma((2, 4)),
        dma((2, 4)),
        dma((4,)),
        dma((4,)),
    ]


def scatter_rows_kernel(part, out, *scratch):
    at = place()
    z, y, x, k = at
    along_y = device_at(z, 1 - y, x, k)
    meet(z, y, x, k, (along_y,))
    sends = Sends(scratch[8])
    rows = RowScatter(part, out, scratch[:4], scratch[4:8], sends, at, line_order(z), along_y)
    rows.run()
    sends.finish()


def scatter_rows(part, collective_id):
    rows, width = part.shape[0] // 8, part.shape[1]
    return pl.pallas_call(
        scatter_rows_kernel,
        out_shape=jax.ShapeDtypeStruct((rows, width), SINGLE_FLOAT),
        in_specs=[ANYWHERE],
        out_specs=VMEM_WHOLE,
        scratch_shapes=row_scatter_scratch(rows, width, part.dtype)
        + [pltpu.SemaphoreType.DMA((16,))],
        compiler_params=pltpu.CompilerParams(
            collective_id=collective_id, has_side_effects=True, vmem_limit_bytes=VMEM_BYTES
        ),
        name="scatter_rows",
    )(part)


def ring_of(c, w):
    return [((c + t) % 8, w) for t in range(1, 8)]


def gather_start_kernel(
    x_in,
    slab_in,
    wo_in,
    x_out,
    slab_out,
    wo_out,
    local_sems,
    send_sems,
    x_sems,
    slab_sems,
    wo_sems,
):
    at = place()
    z, y, x, k = at
    c, w = z * 2 + y, x * 2 + k
    along_x, along_y = device_at(z, y, 1 - x, k), device_at(z, 1 - y, x, k)
    sibling = device_at(z, y, x, 1 - k)
    others = ring_of(c, w)
    barrier = pltpu.get_barrier_semaphore()
    for device in others + [along_x, sibling]:
        pl.semaphore_signal(barrier, inc=1, device_id=device, device_id_type=MESH)
    pl.semaphore_wait(barrier, 9)
    sends = Sends(send_sems)
    rows = RowGather(
        x_in, x_out, sends, local_sems.at[pl.ds(0, 2)], x_sems, at, line_order(z), along_y
    )
    wo_rows = wo_in.shape[0]

    def wo_at(w):
        return wo_out.at[pl.ds(pl.multiple_of(w * wo_rows, wo_rows), wo_rows), :]

    mine = c * 4 + w
    local = [
        pltpu.make_async_copy(slab_in.at[c], slab_out.at[mine], local_sems.at[2]),
        pltpu.make_async_copy(wo_in, wo_at(w), local_sems.at[3]),
    ]
    for copy in local:
        copy.start()

    def pass_on(slot, device, block=None):
        block = slab_out.at[slot] if block is None else block
        sends.start(block, slab_out.at[slot], slab_sems.at[slot], device)

    def take(source, w):
        slot = source * 4 + w
        arrived(slab_out.at[slot], slab_sems.at[slot], along_x)
        return slot

    rows.column(0)
    for device in (along_x, sibling):
        sends.start(wo_in, wo_at(w), wo_sems.at[w], device)
        pass_on(mine, device, slab_in.at[c])
    for device in others:
        sends.start(slab_in.at[device[0]], slab_out.at[mine], slab_sems.at[mine], device)

    def onward():
        for t in range(1, 8):
            slot = take((c + 8 - t) % 8, w)
            pass_on(slot, along_x)
            pass_on(slot, sibling)

    def across():
        beside = (1 - x) * 2 + k
        arrived(wo_at(beside), wo_sems.at[beside], along_x)
        sends.start(wo_at(beside), wo_at(beside), wo_sems.at[beside], sibling)
        for t in range(8):
            pass_on(take((c + 8 - t) % 8, beside), sibling)

    rows.column(1)
    rows.column(2)
    onward()
    rows.column(3)
    across()
    for other in (x * 2 + 1 - k, (1 - x) * 2 + 1 - k):
        for t in range(8):
            take((c + 8 - t) % 8, other)
        arrived(wo_at(other), wo_sems.at[other], along_x)
    rows.finish()
    for copy in local:
        copy.wait()
    sends.finish()


def gather_start(x, slabs, wo, collective_id):
    tokens, width = x.shape
    low = BRAIN_FLOAT_TYPE
    dma = pltpu.SemaphoreType.DMA
    return pl.pallas_call(
        gather_start_kernel,
        out_shape=(
            jax.ShapeDtypeStruct((8 * tokens, width), low),
            jax.ShapeDtypeStruct((32,) + slabs.shape[1:], low),
            jax.ShapeDtypeStruct((4 * wo.shape[0], width), low),
        ),
        in_specs=[ANYWHERE] * 3,
        out_specs=[ANYWHERE] * 3,
        scratch_shapes=[dma((4,)), dma((64,)), dma((2, 8)), dma((32,)), dma((4,))],
        compiler_params=pltpu.CompilerParams(collective_id=collective_id, has_side_effects=True),
        name="gather_start",
    )(x, slabs, wo)


def scatter_end_kernel(
    part,
    gw,
    gwo,
    small,
    rows_out,
    gw_out,
    gwo_out,
    small_out,
    *scratch,
):
    row_scratch, row_sems = scratch[:4], scratch[4:8]
    (
        send_sems,
        load_sems,
        core_sems,
        x_sems,
        to_sems,
        small_to_sems,
        gw_own,
        gw_core,
        gw_x,
        gwo_own,
        gwo_core,
        gwo_x,
        small_own,
        small_core,
        small_x,
        small_to,
    ) = scratch[8:]
    at = place()
    z, y, x, k = at
    c, w = z * 2 + y, x * 2 + k
    along_x, along_y = device_at(z, y, 1 - x, k), device_at(z, 1 - y, x, k)
    sibling = device_at(z, y, x, 1 - k)
    others = ring_of(c, w)
    barrier = pltpu.get_barrier_semaphore()
    for device in others + [along_x, sibling]:
        pl.semaphore_signal(barrier, inc=1, device_id=device, device_id_type=MESH)
    pl.semaphore_wait(barrier, 9)
    sends = Sends(send_sems)
    rows = RowScatter(
        part, rows_out, row_scratch, row_sems, sends, at, line_order(z), along_y
    )
    loads = []
    for n, (source, core, own) in enumerate(
        (
            (small, small_core, small_own),
            (gw, gw_core, gw_own),
            (gwo, gwo_core, gwo_own),
        )
    ):
        outer = (slice(None),) * (len(source.shape) - 3)
        sends.start(source.at[(*outer, 1 - k)], core, core_sems.at[n], sibling)
        loads.append(pltpu.make_async_copy(source.at[(*outer, k)], own, load_sems.at[n]))
        loads[-1].start()

    def fold(n, own, core):
        loads[n].wait()
        arrived(core, core_sems.at[n], sibling)
        flat = [(i,) for i in range(own.shape[0])]
        for extent in own.shape[1:-2]:
            flat = [index + (j,) for index in flat for j in range(extent)]
        for i in flat:
            add_blocks(own.at[i], own.at[i], core.at[i])

    fold(0, small_own, small_core)
    sends.start(small_own.at[:, 1 - x], small_x, x_sems.at[0], along_x)
    fold(1, gw_own, gw_core)
    sends.start(gw_own.at[:, 1 - x], gw_x, x_sems.at[1], along_x)
    fold(2, gwo_own, gwo_core)
    keep = []

    def weights(i):
        if i == 2:
            sends.start(gwo_own.at[1 - x], gwo_x, x_sems.at[2], along_x)
            spread()

    def spread():
        for n, own, far in ((0, small_own, small_x), (1, gw_own, gw_x)):
            arrived(far, x_sems.at[n], along_x)
            for i in range(8):
                add_blocks(own.at[i, x], own.at[i, x], far.at[i])
            target, sems = (small_to, small_to_sems) if n == 0 else (gw_out, to_sems)
            keep.append(
                pltpu.make_async_copy(own.at[c, x], target.at[c], load_sems.at[3 + n])
            )
            keep[-1].start()
            for device in others:
                sends.start(own.at[device[0], x], target.at[c], sems.at[c], device)

    rows.run(weights)
    arrived(gwo_x, x_sems.at[2], along_x)
    add_blocks(gwo_out, gwo_own.at[x], gwo_x)
    for copy in keep:
        copy.wait()
    for t in range(1, 8):
        source = (c + 8 - t) % 8
        arrived(small_to.at[source], small_to_sems.at[source], along_x)
        arrived(gw_out.at[source], to_sems.at[source], along_x)
    total = small_to[0]
    for i in range(1, 8):
        total = total + small_to[i]
    small_out[...] = total
    sends.finish()


def scatter_end(part, gw, gwo, small, collective_id):
    rows, width = part.shape[0] // 8, part.shape[1]
    low = part.dtype
    dma, vmem = pltpu.SemaphoreType.DMA, pltpu.VMEM
    r, n = gw.shape[3:]
    ro, no = gwo.shape[2:]
    rs, ns = small.shape[3:]
    return pl.pallas_call(
        scatter_end_kernel,
        out_shape=(
            jax.ShapeDtypeStruct((rows, width), SINGLE_FLOAT),
            jax.ShapeDtypeStruct((8, r, n), low),
            jax.ShapeDtypeStruct((ro, no), SINGLE_FLOAT),
            jax.ShapeDtypeStruct((rs, ns), SINGLE_FLOAT),
        ),
        in_specs=[ANYWHERE] * 4,
        out_specs=[VMEM_WHOLE, ANYWHERE, VMEM_WHOLE, VMEM_WHOLE],
        scratch_shapes=row_scatter_scratch(rows, width, low)
        + [dma((48,)), dma((5,)), dma((3,)), dma((3,)), dma((8,)), dma((8,))]
        + [vmem((8, 2, r, n), low), vmem((8, 2, r, n), low), vmem((8, r, n), low)]
        + [vmem((2, ro, no), low), vmem((2, ro, no), low), vmem((ro, no), low)]
        + [vmem((8, 2, rs, ns), SINGLE_FLOAT), vmem((8, 2, rs, ns), SINGLE_FLOAT)]
        + [vmem((8, rs, ns), SINGLE_FLOAT), vmem((8, rs, ns), SINGLE_FLOAT)],
        compiler_params=pltpu.CompilerParams(
            collective_id=collective_id, has_side_effects=True, vmem_limit_bytes=VMEM_BYTES
        ),
        name="scatter_end",
    )(part, gw, gwo, small)


def forward_gather_kernel(
    slack,
    block_in,
    x_in,
    slabs_in,
    wo_in,
    gain_ref,
    qg_ref,
    kg_ref,
    cos_ref,
    sin_ref,
    segc_ref,
    segr_ref,
    block_out,
    normed_out,
    raw_out,
    q_out,
    k_out,
    v_out,
    attn_out,
    part_out,
    *scratch,
):
    (
        x_ref,
        w_ref,
        wo_ref,
        normed_ref,
        raw_ref,
        q_ref,
        k_ref,
        v_ref,
        attn_ref,
        part_ref,
        in_sems,
        out_sems,
    ) = scratch[:12]
    tokens, width = x_ref.shape
    heads = q_ref.shape[1] // HEAD_DIM
    owned, columns = w_ref.shape[1:]
    rows_step = 256
    copies = [
        pltpu.make_async_copy(s, t, in_sems.at[n])
        for n, (s, t) in enumerate(
            ((x_in, x_ref), (slabs_in.at[:, pl.ds(0, owned), :], w_ref), (wo_in, wo_ref))
        )
    ]
    stores = [
        pltpu.make_async_copy(s, t, out_sems.at[n])
        for n, (s, t) in enumerate(
            (
                (normed_ref, normed_out),
                (raw_ref, raw_out),
                (q_ref, q_out),
                (k_ref, k_out),
                (v_ref, v_out),
                (attn_ref, attn_out),
                (part_ref, part_out),
            )
        )
    ]
    for copy in copies:
        copy.start()
    blocks = BlockGather(block_in, block_out, *scratch[12:])
    blocks.begin()
    copies[0].wait()
    copies[1].wait()

    def project(i, carry):
        rows = pl.ds(pl.multiple_of(i * rows_step, rows_step), rows_step)
        x = x_ref[rows, :].astype(SINGLE_FLOAT)
        inverse = lax.rsqrt(jnp.mean(x * x, axis=-1, keepdims=True) + EPS)
        normed = (x * inverse * gain_ref[...]).astype(BRAIN_FLOAT_TYPE)
        normed_ref[rows, :] = normed
        raw = dot_rows(normed, w_ref[...].reshape(width, columns))
        raw_ref[rows, :] = raw[:, : (heads + 1) * HEAD_DIM]
        v_ref[rows, :] = raw[:, (heads + 1) * HEAD_DIM :].astype(BRAIN_FLOAT_TYPE)
        cosine, sine = cos_ref[rows, :], sin_ref[rows, :]
        for h in range(heads + 1):
            part = raw[:, h * HEAD_DIM : (h + 1) * HEAD_DIM]
            gain = qg_ref[...] if h < heads else kg_ref[...]
            scaled = (
                part * lax.rsqrt(jnp.mean(part * part, axis=-1, keepdims=True) + EPS) * gain
            )
            turned = scaled * cosine + pltpu.roll(scaled, HEAD_DIM // 2, 1) * sine
            turned = turned.astype(BRAIN_FLOAT_TYPE)
            if h < heads:
                q_ref[rows, h * HEAD_DIM : (h + 1) * HEAD_DIM] = turned
            else:
                k_ref[rows, :] = turned
        return carry

    lax.fori_loop(0, tokens // rows_step, project, 0)
    for copy in stores[:5]:
        copy.start()
    blocks.advance(1)
    tile_rows = 128
    for tile in range(tokens // tile_rows):
        first_row = tile * tile_rows
        rows = slice(first_row, first_row + tile_rows)
        low, high = key_range(tile, tile_rows, tokens, slack)
        probs = tile_scores(
            stacked_heads(q_ref, rows, heads),
            k_ref,
            segc_ref,
            segr_ref,
            low,
            high,
            first_row,
            tile_rows,
            heads,
        )
        attended = dot_rows(probs.astype(BRAIN_FLOAT_TYPE), v_ref[low:high, :])
        for h in range(heads):
            attn_ref[rows, h * HEAD_DIM : (h + 1) * HEAD_DIM] = attended[
                h * tile_rows : (h + 1) * tile_rows
            ].astype(BRAIN_FLOAT_TYPE)
    stores[5].start()
    blocks.advance(2)
    copies[2].wait()

    def project_out(i, carry):
        rows = pl.ds(pl.multiple_of(i * rows_step, rows_step), rows_step)
        part_ref[rows, :] = dot_rows(attn_ref[rows, :], wo_ref[...]).astype(BRAIN_FLOAT_TYPE)
        return carry

    lax.fori_loop(0, tokens // rows_step, project_out, 0)
    stores[6].start()
    blocks.advance(3)
    blocks.finish()
    for copy in stores:
        copy.wait()


def forward_gather(slack, block, x, slabs, wo, gain, qg, kg, cosine, sine, segc, segr, collective_id):
    tokens, width = x.shape
    columns = slabs.shape[2]
    owned = width // slabs.shape[0]
    channels = columns - 2 * HEAD_DIM
    low = BRAIN_FLOAT_TYPE
    shape, vmem, dma = jax.ShapeDtypeStruct, pltpu.VMEM, pltpu.SemaphoreType.DMA
    sizes = (
        ((tokens, width), low),
        ((tokens, channels + HEAD_DIM), SINGLE_FLOAT),
        ((tokens, channels), low),
        ((tokens, HEAD_DIM), low),
        ((tokens, HEAD_DIM), low),
        ((tokens, channels), low),
        ((tokens, width), low),
    )

    def kernel(*refs):
        forward_gather_kernel(slack, *refs)

    return pl.pallas_call(
        kernel,
        out_shape=[shape((32,) + block.shape, low)] + [shape(*size) for size in sizes],
        in_specs=[ANYWHERE] * 4 + [VMEM_WHOLE] * 7,
        out_specs=[ANYWHERE] * 8,
        scratch_shapes=[
            vmem((tokens, width), low),
            vmem((slabs.shape[0], owned, columns), low),
            vmem(wo.shape, low),
        ]
        + [vmem(*size) for size in sizes]
        + [dma((3,)), dma((7,))]
        + [dma, dma((40,)), dma((32,))],
        compiler_params=pltpu.CompilerParams(
            collective_id=collective_id, has_side_effects=True, vmem_limit_bytes=VMEM_BYTES
        ),
        name="forward_gather",
    )(block, x, slabs, wo, gain, qg, kg, cosine, sine, segc, segr)


GROUPS = 8


def order_at(z, i):
    upper = z // 2
    inner = (z % 2) * (1 - upper) + (1 - z % 2) * upper
    along = i * (1 - inner) + inner * ((i + 1) % 3 + 2 * (i // 3))
    return 3 * upper + (1 - 2 * upper) * along


def group_blocks(g):
    later = ((g + 1) // 4) * (1 - g // 7)
    g = g * (1 - later) + later * (3 + g % 4)
    kind, turn = (g + 2) // 4, (g + 2) % 4
    far, side, near = 1 - (kind + 1) // 2, kind % 2, kind // 2
    return (
        (far * (turn - 2) + side * (3 - turn) + near * (3 - 2 * turn), 3 - 2 * kind + near),
        (far * turn + side * (3 - turn) + near * (2 - 2 * turn), 3 - kind - near),
    )


def spread_rows(target, pick, rows, *terms):
    step = 4 * HEAD_DIM
    width = target.shape[1]
    at = jnp.transpose(pick[...].astype(SINGLE_FLOAT)).astype(BRAIN_FLOAT_TYPE)
    for start in range(0, width, step):
        part = slice(start, min(start + step, width))
        total = dot_rows(at, rows[:, part])
        for term in terms:
            total = total + term[:, part].astype(SINGLE_FLOAT)
        target[:, part] = total.astype(target.dtype)


def expert_exchange_kernel(
    capacity,
    pay_all,
    dout_all,
    wg_in,
    wu_in,
    wd_in,
    back_ref,
    rows_out,
    pick_out,
    x_out,
    deo_out,
    hid_out,
    dgl_out,
    dul_out,
    wg_ref,
    wu_ref,
    wd_ref,
    pay_ref,
    dout_ref,
    x_ref,
    deo_ref,
    hid_ref,
    dgl_ref,
    dul_ref,
    d_ref,
    g_ref,
    far_pick_ref,
    far_d_ref,
    far_o_ref,
    near_o_ref,
    pick_ref,
    rows_ref,
    own_ref,
    corner_ref,
    x_sum_ref,
    y_sum_ref,
    up_ref,
    down_ref,
    weight_sems,
    load_sems,
    row_sems,
    near_sems,
    far_sems,
    sibling_sems,
    corner_sems,
    x_sums,
    y_sums,
    up_sems,
    down_sems,
    sum_send_sems,
    pick_sem,
):
    z, y, x, k = place()
    order = line_order(z)
    along_x, along_y = device_at(z, y, 1 - x, k), device_at(z, 1 - y, x, k)
    sibling = device_at(z, y, x, 1 - k)
    weights = [
        pltpu.make_async_copy(a, b, weight_sems.at[n])
        for n, (a, b) in enumerate(((wg_in, wg_ref), (wu_in, wu_ref), (wd_in, wd_ref)))
    ]
    for copy in weights:
        copy.start()
    meet(z, y, x, k, (along_x, along_y, sibling))
    mine = slot_of(z, y, x, k)
    width = wg_in.shape[0]
    _, tokens, payload = pay_all.shape
    experts = (payload - width) // 4
    rows = 4 * capacity
    above, below = device_at(z + 1, y, x, k), device_at(z - 1, y, x, k)

    def far_copies(n, j):
        half = pl.ds(capacity, capacity)
        return [
            remote(a, b, far_sems.at[n, m], sibling_sems.at[m, j], sibling)
            for m, (a, b) in enumerate(
                (
                    (far_pick_ref.at[n], pick_ref.at[j, half, :]),
                    (far_d_ref.at[n], rows_ref.at[j, half, :]),
                    (far_o_ref.at[n], rows_out.at[j, half, :]),
                )
            )
        ]

    def gather(i, r, *extra):
        j = i * 4 + r
        for copy in far_copies(0, j)[:2]:
            copy.wait_recv()
        spread_rows(own_ref.at[j], pick_ref.at[j], rows_ref.at[j], *extra)
        return own_ref.at[j]

    def sum_send(n, j, target, recv, device):
        return remote(own_ref.at[j], target, sum_send_sems.at[n], recv, device)

    corner_sends = [
        sum_send(i, i * 4 + 3, corner_ref.at[i], corner_sems.at[i], along_y if i < 2 else along_x)
        for i in range(4)
    ]
    x_sends = [
        sum_send(4 + i, i * 4 + 1, x_sum_ref.at[i], x_sums.at[i], along_x) for i in range(4)
    ]
    y_sends = [
        sum_send(8 + i, i * 4 + 2, y_sum_ref.at[i], y_sums.at[i], along_y) for i in range(4)
    ]
    line_sends = []
    for i in (1, 2, 3):
        chip = order[i]
        upward = chip > z
        line_sends.append(
            (upward, sum_send(12 + i, i * 4, up_ref.at[chip], up_sems.at[chip], above))
        )
        line_sends.append(
            (
                jnp.logical_not(upward),
                sum_send(16 + i, i * 4, down_ref.at[chip], down_sems.at[chip], below),
            )
        )

    def corners(*which):
        for i in which:
            gather(i, 3)
            corner_sends[i].start()

    def cross(i):
        arrived(corner_ref.at[i], corner_sems.at[i], along_x)
        extra = (corner_ref.at[i],)
        gather(i, 1, *(extra if i < 2 else ()))
        x_sends[i].start()
        gather(i, 2, *(extra if i >= 2 else ()))
        y_sends[i].start()

    def total(i):
        arrived(x_sum_ref.at[i], x_sums.at[i], along_x)
        arrived(y_sum_ref.at[i], y_sums.at[i], along_y)
        gather(i, 0, x_sum_ref.at[i], y_sum_ref.at[i])

    def along(i):
        total(i)
        chip, block = order[i], own_ref.at[i * 4]
        upward = chip > z

        @pl.when(upward & (z > 0))
        def _():
            arrived(up_ref.at[chip], up_sems.at[chip], below)
            add_blocks(block, block, up_ref.at[chip])

        @pl.when(jnp.logical_not(upward) & (z < LINE - 1))
        def _():
            arrived(down_ref.at[chip], down_sems.at[chip], above)
            add_blocks(block, block, down_ref.at[chip])

        for condition, copy in line_sends[2 * i - 2 : 2 * i]:
            pl.when(condition)(copy.start)

    def sixth():
        cross(1)
        along(3)

    def last():
        cross(0)
        along(2)

    at_start = {5: lambda: cross(2), 6: sixth, 7: last}
    at_middle = {1: lambda: corners(2, 0), 2: lambda: corners(3, 1), 3: lambda: cross(3)}

    def at(g, table):
        for n, work in table.items():
            pl.when(g == n)(work)

    for copy in weights:
        copy.wait()
    slot_row = lax.broadcasted_iota(jnp.int32, (capacity, tokens), 0).astype(SINGLE_FLOAT)
    row_lane = lax.broadcasted_iota(jnp.int32, (capacity, payload - width), 1)
    e = mine
    is_gate = (row_lane == e) | (row_lane == experts + e)
    rank_lane = (
        lax.broadcasted_iota(jnp.int32, (8, payload - width), 1) == 2 * experts + e
    ).astype(BRAIN_FLOAT_TYPE)

    def row_copies(g):
        out_rows = pl.ds(pl.multiple_of(g * rows, rows), rows)
        pairs = (
            (x_ref, x_out), (deo_ref, deo_out), (hid_ref, hid_out), (dgl_ref, dgl_out),
            (dul_ref, dul_out),
        )
        return [
            pltpu.make_async_copy(a, b.at[out_rows, :], row_sems.at[n])
            for n, (a, b) in enumerate(pairs)
        ]

    def blocks_of(g):
        found = []
        for lane_k in (k, 1 - k):
            for i, r in group_blocks(g):
                dy, dx = r // 2, r % 2
                slot = slot_of(
                    order_at(z, i), y + dy * (1 - 2 * y), x + dx * (1 - 2 * x), lane_k
                )
                found.append((slot, i * 4 + r))
        return found

    def near_copies(g):
        return [
            pltpu.make_async_copy(
                near_o_ref.at[n], rows_out.at[blocks_of(g)[n][1], pl.ds(0, capacity), :], near_sems.at[n]
            )
            for n in (0, 1)
        ]

    def settle(g):
        for copy in row_copies(g) + near_copies(g):
            copy.wait()
        for n in (0, 1):
            for copy in far_copies(n, blocks_of(g)[2 + n][1]):
                copy.wait_send()

    def load_copies(g):
        return [
            (
                pltpu.make_async_copy(pay_all.at[slot], pay_ref.at[n], load_sems.at[n]),
                pltpu.make_async_copy(dout_all.at[slot], dout_ref.at[n], load_sems.at[4 + n]),
            )
            for n, (slot, _) in enumerate(blocks_of(g))
        ]

    def load(g):
        for pair in load_copies(g):
            for copy in pair:
                copy.start()

    def step(g, carry):
        blocks = blocks_of(g)
        at(g, at_start)

        @pl.when(g > 0)
        def _():
            settle(g - 1)

        loads = load_copies(g)
        for n in range(4):
            for copy in loads[n]:
                copy.wait()
            part = slice(n * capacity, (n + 1) * capacity)
            rank = dot_right_transposed(rank_lane, pay_ref[n, :, width:])
            pick = (rank[0:1, :] == slot_row).astype(BRAIN_FLOAT_TYPE)
            if n < 2:
                pick_ref[blocks[n][1], 0:capacity, :] = pick
            else:
                far_pick_ref[n - 2] = pick
            chosen = dot_rows(pick, pay_ref[n])
            x_ref[part, :] = chosen[:, :width].astype(BRAIN_FLOAT_TYPE)
            gate = jnp.sum(jnp.where(is_gate, chosen[:, width:], 0.0), axis=-1, keepdims=True)
            g_ref[part, :] = gate
            d_rows = dot_rows(pick, dout_ref[n])
            d_ref[part, :] = d_rows.astype(BRAIN_FLOAT_TYPE)
            deo_ref[part, :] = (gate * d_rows).astype(BRAIN_FLOAT_TYPE)

        @pl.when(g < GROUPS - 1)
        def _():
            load(g + 1)

        at(g, at_middle)
        rows_in = x_ref[...]
        gate_hidden = dot_rows(rows_in, wg_ref[...])
        up_hidden = dot_rows(rows_in, wu_ref[...])
        sigmoid = 1.0 / (1.0 + jnp.exp(-gate_hidden))
        silu = gate_hidden * sigmoid
        hidden = (silu * up_hidden).astype(BRAIN_FLOAT_TYPE)
        hid_ref[...] = hidden
        d_hidden = dot_right_transposed(deo_ref[...], wd_ref[...])
        d_gate = (d_hidden * up_hidden * sigmoid * (1.0 + gate_hidden * (1.0 - sigmoid))).astype(
            BRAIN_FLOAT_TYPE
        )
        d_up = (d_hidden * silu).astype(BRAIN_FLOAT_TYPE)
        dgl_ref[...] = d_gate
        dul_ref[...] = d_up
        for copy in row_copies(g):
            copy.start()
        expert_out = dot_rows(hidden, wd_ref[...]).astype(BRAIN_FLOAT_TYPE)
        d_copy = (
            dot_right_transposed(d_gate, wg_ref[...]) + dot_right_transposed(d_up, wu_ref[...])
        ).astype(BRAIN_FLOAT_TYPE)
        for n in (2, 3, 0, 1):
            j = blocks[n][1]
            part = slice(n * capacity, (n + 1) * capacity)
            e_rows = expert_out[part].astype(SINGLE_FLOAT)
            d_gate_rows = jnp.sum(
                d_ref[part, :].astype(SINGLE_FLOAT) * e_rows, axis=-1, keepdims=True
            )
            high = d_gate_rows.astype(BRAIN_FLOAT_TYPE).astype(SINGLE_FLOAT)
            extra = jnp.where(row_lane == e, high, 0.0) + jnp.where(
                row_lane == experts + e, d_gate_rows - high, 0.0
            )
            if n >= 2:
                d_target, o_target = far_d_ref.at[n - 2], far_o_ref.at[n - 2]
            else:
                d_target, o_target = rows_ref.at[j, pl.ds(0, capacity), :], near_o_ref.at[n]
            d_target[:, :width] = d_copy[part]
            d_target[:, width:] = extra.astype(BRAIN_FLOAT_TYPE)
            o_target[...] = (g_ref[part, :] * e_rows).astype(BRAIN_FLOAT_TYPE)
            if n >= 2:
                for copy in far_copies(n - 2, j):
                    copy.start()
        for copy in near_copies(g):
            copy.start()
        return carry

    load(0)
    lax.fori_loop(0, GROUPS, step, 0)
    along(1)
    total(0)
    block = own_ref.at[0]

    @pl.when(z > 0)
    def _():
        arrived(up_ref.at[z], up_sems.at[z], below)

    @pl.when(z < LINE - 1)
    def _():
        arrived(down_ref.at[z], down_sems.at[z], above)

    @pl.when(z == 0)
    def _():
        add_blocks(back_ref, block, down_ref.at[z])

    @pl.when(z == LINE - 1)
    def _():
        add_blocks(back_ref, block, up_ref.at[z])

    @pl.when((z > 0) & (z < LINE - 1))
    def _():
        add_blocks(back_ref, block, up_ref.at[z], down_ref.at[z])

    settle(GROUPS - 1)
    keep = pltpu.make_async_copy(pick_ref, pick_out, pick_sem)
    keep.start()
    for j in range(16):
        far_copies(0, j)[2].wait_recv()
    keep.wait()
    for copy in corner_sends + x_sends + y_sends:
        copy.wait_send()
    for condition, copy in line_sends:
        pl.when(condition)(copy.wait_send)


def expert_exchange(capacity, pay_all, dout_all, wg, wu, wd, collective_id):
    _, tokens, wide = pay_all.shape
    width, ff = wg.shape
    low = BRAIN_FLOAT_TYPE
    rows = 4 * capacity
    total = GROUPS * rows
    dma, vmem = pltpu.SemaphoreType.DMA, pltpu.VMEM

    def kernel(*refs):
        expert_exchange_kernel(capacity, *refs)

    shape = jax.ShapeDtypeStruct
    return pl.pallas_call(
        kernel,
        out_shape=(
            shape((tokens, wide), SINGLE_FLOAT),
            shape((16, 2 * capacity, width), low),
            shape((16, 2 * capacity, tokens), low),
            shape((total, width), low),
            shape((total, width), low),
            shape((total, ff), low),
            shape((total, ff), low),
            shape((total, ff), low),
        ),
        in_specs=[ANYWHERE] * 5,
        out_specs=[VMEM_WHOLE] + [ANYWHERE] * 7,
        scratch_shapes=[vmem((width, ff), low), vmem((width, ff), low), vmem((ff, width), low)]
        + [vmem((4, tokens, wide), low), vmem((4, tokens, width), low)]
        + [vmem((rows, width), low), vmem((rows, width), low)]
        + [vmem((rows, ff), low)] * 3
        + [vmem((rows, width), low), vmem((rows, 1), SINGLE_FLOAT)]
        + [vmem((2, capacity, n), low) for n in (tokens, wide, width, width)]
        + [vmem((16, 2 * capacity, tokens), low), vmem((16, 2 * capacity, wide), low)]
        + [vmem((n, tokens, wide), low) for n in (16, 4, 4, 4, 4, 4)]
        + [dma((3,)), dma((8,)), dma((5,)), dma((2,)), dma((2, 3))]
        + [dma((3, 16)), dma((4,)), dma((4,)), dma((4,)), dma((4,)), dma((4,)), dma((20,)), dma],
        compiler_params=pltpu.CompilerParams(
            collective_id=collective_id, has_side_effects=True, vmem_limit_bytes=VMEM_BYTES
        ),
        name="expert_exchange",
    )(pay_all, dout_all, wg, wu, wd)


def backward_scatter_kernel(
    slack,
    rows_in,
    pick_in,
    dh_in,
    wo_in,
    attn_in,
    q_in,
    k_in,
    v_in,
    raw_in,
    normed_in,
    x_in,
    w_in,
    qg_ref,
    kg_ref,
    cos_ref,
    sin_ref,
    segc_ref,
    segr_ref,
    out,
    gwo_out,
    gw_out,
    dpart_out,
    ggain_ref,
    gheads_ref,
    *scratch,
):
    (
        dh_ref,
        wo_ref,
        attn_ref,
        q_ref,
        k_ref,
        v_ref,
        raw_ref,
        normed_ref,
        w_ref,
        x_ref,
        gwo_ref,
        gw_ref,
        da_ref,
        draw_ref,
        dk_ref,
        dv_ref,
        in_sems,
        x_load_sems,
        gwo_sems,
        gw_sems,
        dpart_sems,
    ) = scratch[:21]
    exchange = PickedSums(rows_in, pick_in, out, scratch[21:])
    owned, columns = w_ref.shape[1:]
    w_rows = w_in.at[:, pl.ds(0, owned), :]
    inputs = (dh_in, wo_in, attn_in, q_in, k_in, v_in, raw_in, normed_in, w_rows)
    held = (dh_ref, wo_ref, attn_ref, q_ref, k_ref, v_ref, raw_ref, normed_ref, w_ref)
    copies = [pltpu.make_async_copy(s, t, in_sems.at[n]) for n, (s, t) in enumerate(zip(inputs, held))]
    tokens = dh_ref.shape[0]
    heads = q_ref.shape[1] // HEAD_DIM
    scale = HEAD_DIM ** (-0.5)
    rows_step = 256
    row_steps = tokens // rows_step

    def x_load(i):
        rows = pl.ds(pl.multiple_of(i * rows_step, rows_step), rows_step)
        return pltpu.make_async_copy(x_in.at[rows, :], x_ref.at[i % 2], x_load_sems.at[i % 2])

    def dpart_store(i):
        rows = pl.ds(pl.multiple_of(i * rows_step, rows_step), rows_step)
        return pltpu.make_async_copy(dh_ref.at[rows, :], dpart_out.at[rows, :], dpart_sems.at[i])

    def gwo_store(i):
        columns = pl.ds(pl.multiple_of(i * 512, 512), 512)
        return pltpu.make_async_copy(
            gwo_ref.at[i % 2], gwo_out.at[:, columns], gwo_sems.at[i % 2]
        )

    def gw_store(i):
        part = pl.ds(pl.multiple_of(i * 256, 256), 256)
        return pltpu.make_async_copy(gw_ref.at[i % 2], gw_out.at[part, :], gw_sems.at[i % 2])

    def attended_gradient():
        def body(i, carry):
            rows = pl.ds(pl.multiple_of(i * rows_step, rows_step), rows_step)
            da_ref[rows, :] = dot_right_transposed(dh_ref[rows, :], wo_ref[...]).astype(
                BRAIN_FLOAT_TYPE
            )
            return carry

        for copy in copies[:2]:
            copy.wait()
        lax.fori_loop(0, row_steps, body, 0)

    def out_weight():
        copies[2].wait()
        for i in range(dh_ref.shape[1] // 512):
            if i >= 2:
                gwo_store(i - 2).wait()
            gwo_ref[i % 2] = dot_left_transposed(
                attn_ref[...], dh_ref[:, i * 512 : (i + 1) * 512]
            ).astype(gwo_ref.dtype)
            gwo_store(i).start()

    tile_rows = 128
    gains = []

    def tiles(first, last):
        for tile in range(first, last):
            first_row = tile * tile_rows
            rows = slice(first_row, first_row + tile_rows)
            low, high = key_range(tile, tile_rows, tokens, slack)
            q4 = stacked_heads(q_ref, rows, heads)
            da4 = stacked_heads(da_ref, rows, heads)
            probs = tile_scores(
                q4, k_ref, segc_ref, segr_ref, low, high, first_row, tile_rows, heads
            )
            d_probs = dot_right_transposed(da4, v_ref[low:high, :])
            delta = jnp.sum(probs * d_probs, axis=-1, keepdims=True)
            d_scores = (probs * (d_probs - delta)).astype(BRAIN_FLOAT_TYPE)
            dq4 = dot_rows(d_scores, k_ref[low:high, :]) * scale
            dk_ref[low:high, :] += dot_left_transposed(d_scores, q4)
            dv_ref[low:high, :] += dot_left_transposed(probs.astype(BRAIN_FLOAT_TYPE), da4)
            for h in range(heads):
                columns = slice(h * HEAD_DIM, (h + 1) * HEAD_DIM)
                raw_gradient, gain_gradient = head_backward(
                    dq4[h * tile_rows : (h + 1) * tile_rows],
                    raw_ref[rows, columns],
                    qg_ref[...],
                    cos_ref[rows, :],
                    sin_ref[rows, :],
                )
                draw_ref[rows, columns] = raw_gradient.astype(BRAIN_FLOAT_TYPE)
                gains.append(gain_gradient)

    def keys():
        columns = slice(heads * HEAD_DIM, (heads + 1) * HEAD_DIM)
        raw_gradient, key_gain_gradient = head_backward(
            dk_ref[...] * scale, raw_ref[:, columns], kg_ref[...], cos_ref[...], sin_ref[...]
        )
        draw_ref[:, columns] = raw_gradient.astype(BRAIN_FLOAT_TYPE)
        draw_ref[:, (heads + 1) * HEAD_DIM :] = dv_ref[...].astype(BRAIN_FLOAT_TYPE)
        query_gain_gradient = gains[0]
        for gain in gains[1:]:
            query_gain_gradient = query_gain_gradient + gain
        gheads_ref[...] = jnp.concatenate(
            [query_gain_gradient, key_gain_gradient, jnp.zeros((6, HEAD_DIM), SINGLE_FLOAT)],
            axis=0,
        )

    def projection_weight():
        copies[7].wait()
        count = normed_ref.shape[1] // 256
        for i in range(count):
            if i >= 2:
                gw_store(i - 2).wait()
            gw_ref[i % 2] = dot_left_transposed(
                normed_ref[:, i * 256 : (i + 1) * 256], draw_ref[...]
            ).astype(gw_ref.dtype)
            gw_store(i).start()

    def input_gradient():
        copies[8].wait()
        ggain_ref[...] = jnp.zeros_like(ggain_ref)
        for i in range(row_steps):
            x_load(i).wait()
            rows = slice(i * rows_step, (i + 1) * rows_step)
            d_normed = dot_right_transposed(
                draw_ref[rows, :], w_ref[...].reshape(normed_ref.shape[1], columns)
            )
            dh_ref[rows, :] = d_normed.astype(BRAIN_FLOAT_TYPE)
            dpart_store(i).start()
            x = x_ref[i % 2].astype(SINGLE_FLOAT)
            inverse = lax.rsqrt(jnp.mean(x * x, axis=-1, keepdims=True) + EPS)
            ggain_ref[...] += jnp.sum(d_normed * (x * inverse), axis=0, keepdims=True)
            if i + 2 < row_steps:
                x_load(i + 2).start()

    exchange.begin()
    for copy in copies:
        copy.start()
    x_load(0).start()
    x_load(1).start()
    dk_ref[...] = jnp.zeros_like(dk_ref)
    dv_ref[...] = jnp.zeros_like(dv_ref)
    exchange.corners()
    attended_gradient()
    out_weight()
    for copy in copies[3:7]:
        copy.wait()
    tiles(0, 5)
    exchange.cross(3)
    tiles(5, 8)
    keys()

    def between(i):
        if i == 3:
            projection_weight()
        elif i == 2:
            input_gradient()

    exchange.finish(between)
    for i in (2, 3):
        gwo_store(i).wait()
    for i in (6, 7):
        gw_store(i).wait()
    for i in range(row_steps):
        dpart_store(i).wait()


def backward_scatter(
    slack, rows, pick, dh, wo, attn, q, k, v, raw, normed, x, w, qg, kg, cosine, sine, segc, segr,
    collective_id,
):
    tokens, width = x.shape
    channels = q.shape[1]
    columns = channels + 2 * HEAD_DIM
    low = BRAIN_FLOAT_TYPE
    shape, vmem, dma = jax.ShapeDtypeStruct, pltpu.VMEM, pltpu.SemaphoreType.DMA
    shapes = (
        shape((pick.shape[2], width), SINGLE_FLOAT),
        shape((channels, width), low),
        shape((width, columns), low),
        shape((tokens, width), low),
        shape((1, width), SINGLE_FLOAT),
        shape((8, HEAD_DIM), SINGLE_FLOAT),
    )

    def kernel(*refs):
        backward_scatter_kernel(slack, *refs)

    return pl.pallas_call(
        kernel,
        out_shape=shapes,
        in_specs=[ANYWHERE] * 12 + [VMEM_WHOLE] * 6,
        out_specs=[VMEM_WHOLE] + [ANYWHERE] * 3 + [VMEM_WHOLE] * 2,
        scratch_shapes=[
            vmem((tokens, width), low),
            vmem((channels, width), low),
            vmem((tokens, channels), low),
            vmem((tokens, channels), low),
            vmem((tokens, HEAD_DIM), low),
            vmem((tokens, HEAD_DIM), low),
            vmem((tokens, channels + HEAD_DIM), SINGLE_FLOAT),
            vmem((tokens, width), low),
            vmem((w.shape[0], width // w.shape[0], columns), low),
            vmem((2, 256, width), low),
            vmem((2, channels, 512), low),
            vmem((2, 256, columns), low),
            vmem((tokens, channels), low),
            vmem((tokens, columns), low),
            vmem((tokens, HEAD_DIM), SINGLE_FLOAT),
            vmem((tokens, HEAD_DIM), SINGLE_FLOAT),
            dma((9,)),
            dma((2,)),
            dma((2,)),
            dma((2,)),
            dma((4,)),
        ]
        + picked_scratch(rows, pick),
        compiler_params=pltpu.CompilerParams(
            collective_id=collective_id, has_side_effects=True, vmem_limit_bytes=VMEM_BYTES
        ),
        name="backward_scatter",
    )(rows, pick, dh, wo, attn, q, k, v, raw, normed, x, w, qg, kg, cosine, sine, segc, segr)


def natural_order(blocks):
    count, rows, width = blocks.shape
    half = rows // 2
    first = blocks[:, :half].reshape(count * half, width)
    second = blocks[::-1, half:].reshape(count * half, width)
    return jnp.concatenate([first, second], axis=0)


def device_order(rows, count):
    total, width = rows.shape
    half = total // count // 2
    first = rows[: total // 2].reshape(count, half, width)
    second = rows[total // 2 :].reshape(count, half, width)[::-1]
    return jnp.concatenate([first, second], axis=1)


def norm_backward(gradient, values, gain):
    inverse = lax.rsqrt(jnp.mean(values * values, axis=-1, keepdims=True) + EPS)
    unit = values * inverse
    scaled = gradient * gain
    d_values = inverse * (scaled - unit * jnp.mean(unit * scaled, axis=-1, keepdims=True))
    return d_values, jnp.sum(gradient * unit, axis=0)


def tensor_body(
    inputs,
    grad_output,
    routes,
    doc_lengths,
    norm_attn,
    w_query,
    key_projection,
    value_projection,
    query_norm,
    key_norm,
    w_out,
    norm_ffn,
    w_router,
    expert_gate,
    expert_up,
    expert_down,
):
    ctx_count = lax.axis_size("ctx")
    ws_count = lax.axis_size("ws")
    device_count = ctx_count * ws_count
    tokens = inputs.shape[1]
    width = inputs.shape[2]
    sequence_tokens = tokens * ctx_count
    expert_count = w_router.shape[1]
    capacity = tokens * TOPK * 3 // (2 * device_count)
    heads = QUERY_HEADS // ctx_count
    group = QUERY_HEADS // KEY_VALUE_HEADS
    slack = tokens // 2
    ctx_index = lax.axis_index("ctx")
    both = ("ctx", "ws")
    me = ctx_index * ws_count + lax.axis_index("ws")
    small = jnp.concatenate([norm_attn, norm_ffn, query_norm, key_norm, w_router.reshape(-1)])
    columns = (heads + 2) * HEAD_DIM
    small = jnp.pad(small, (0, 16 * columns - small.shape[0])).reshape(16, columns)
    slabs = []
    for c in range(ctx_count):
        kv = c * heads // group
        slab = jnp.concatenate(
            [
                w_query[:, c * heads * HEAD_DIM : (c + 1) * heads * HEAD_DIM],
                key_projection[:, kv * HEAD_DIM : (kv + 1) * HEAD_DIM],
                value_projection[:, kv * HEAD_DIM : (kv + 1) * HEAD_DIM],
            ],
            axis=1,
        )
        slabs.append(jnp.concatenate([slab, small], axis=0))
    owned, few = width // device_count, query_norm.shape[0]
    x_all, slabs, wo_all = gather_start(inputs[0], jnp.stack(slabs), w_out, 1)
    small = slabs[:, owned:].reshape(device_count, 16 * columns)
    attn_gain = small[:, :owned].reshape(width).astype(SINGLE_FLOAT)
    ffn_gain = small[:, owned : 2 * owned].reshape(width).astype(SINGLE_FLOAT)
    at = 2 * owned
    query_gain = small[:, at : at + few].reshape(HEAD_DIM).astype(SINGLE_FLOAT)
    key_gain = small[:, at + few : at + 2 * few].reshape(HEAD_DIM).astype(SINGLE_FLOAT)
    at = at + 2 * few
    router_matrix = small[:, at : at + owned * expert_count].reshape(width, expert_count)

    places = jnp.arange(sequence_tokens, dtype=jnp.int32)
    segments = segment_ids(doc_lengths[0], places)
    half = HEAD_DIM // 2
    frequency = THETA ** (-2.0 * jnp.arange(half, dtype=SINGLE_FLOAT) / HEAD_DIM)
    angle = places.astype(SINGLE_FLOAT)[:, None] * frequency[None, :]
    cosine, sine = jnp.cos(angle), jnp.sin(angle)
    cosine = jnp.concatenate([cosine, cosine], axis=1)
    sine = jnp.concatenate([-sine, sine], axis=1)
    segc, segr = segments[:, None], segments[None, :]
    qg, kg = query_gain[None, :], key_gain[None, :]
    own_places = jnp.arange(tokens, dtype=jnp.int32)
    own_places = jnp.where(
        own_places < tokens // 2,
        ctx_index * (tokens // 2) + own_places,
        (2 * ctx_count - 2 - ctx_index) * (tokens // 2) + own_places,
    )
    own_segments = segment_ids(doc_lengths[0], own_places)
    validity = own_segments < doc_lengths.shape[1]
    d_layer = jnp.where(validity[:, None], grad_output[0], 0.0).astype(BRAIN_FLOAT_TYPE)

    dout_all, normed, raw, q, k, v, attn, part = forward_gather(
        slack, d_layer, x_all, slabs, wo_all, attn_gain[None, :], qg, kg, cosine, sine, segc, segr, 7
    )
    branch = scatter_rows(part, 2)
    layer_in = inputs[0].astype(SINGLE_FLOAT)
    hidden_state = layer_in + branch
    mixed = rms_scale(hidden_state, ffn_gain).astype(BRAIN_FLOAT_TYPE)
    logits = jnp.dot(mixed, router_matrix, preferred_element_type=SINGLE_FLOAT)
    own_routes = routes[0]
    hit = jnp.any(
        own_routes[:, :, None] == jnp.arange(expert_count, dtype=jnp.int32)[None, None, :], axis=1
    )
    masked = jnp.where(hit, logits, MASK_FILL)
    exponent = jnp.exp(masked - jnp.max(masked, axis=-1, keepdims=True))
    gates = exponent / jnp.sum(exponent, axis=-1, keepdims=True)
    hits = hit.astype(BRAIN_FLOAT_TYPE)
    earlier = jnp.tril(jnp.ones((tokens, tokens), BRAIN_FLOAT_TYPE), -1)
    rank = jnp.dot(earlier, hits, preferred_element_type=SINGLE_FLOAT)
    rank = jnp.where(hit, rank, -1.0).astype(BRAIN_FLOAT_TYPE)
    gate_high = gates.astype(BRAIN_FLOAT_TYPE)
    gate_low = (gates - gate_high.astype(SINGLE_FLOAT)).astype(BRAIN_FLOAT_TYPE)
    payload = jnp.concatenate(
        [mixed, gate_high, gate_low, rank, jnp.zeros_like(rank)], axis=1
    )
    pay_all = gather_all(payload, 3)
    d_back, out_rows, out_pick, x_rows, d_rows, hidden, d_gate, d_up = expert_exchange(
        capacity, pay_all, dout_all, expert_gate[0], expert_up[0], expert_down[0], 4
    )
    grad_gate = dot_left_transposed(x_rows, d_gate)[None]
    grad_up = dot_left_transposed(x_rows, d_up)[None]
    grad_down = dot_left_transposed(hidden, d_rows)[None]

    table = d_back[:, width:]
    d_gates = table[:, :expert_count] + table[:, expert_count : 2 * expert_count]
    d_chosen = gates * (d_gates - jnp.sum(gates * d_gates, axis=-1, keepdims=True))
    d_logits = d_chosen.astype(BRAIN_FLOAT_TYPE)
    d_mixed = d_back[:, :width] + dot_right_transposed(
        d_logits, router_matrix
    )
    grad_router = dot_left_transposed(mixed, d_logits)
    d_state_norm, grad_ffn_gain = norm_backward(d_mixed, hidden_state, ffn_gain)
    d_state = d_layer.astype(SINGLE_FLOAT) + d_state_norm
    d_state_low = d_state.astype(BRAIN_FLOAT_TYPE)
    dh_all = gather_rows(d_state_low, 5)
    moe_sum, gwo, gw, dpart, ggain, gheads = backward_scatter(
        slack, out_rows, out_pick, dh_all, wo_all, attn, q, k, v, raw, normed, x_all, slabs, qg, kg, cosine, sine, segc, segr, 8
    )
    output = (hidden_state + moe_sum).astype(BRAIN_FLOAT_TYPE)
    blocks = (ctx_count, ws_count // 2, 2)
    small = jnp.concatenate(
        [
            ggain.reshape(device_count, owned),
            grad_ffn_gain.reshape(device_count, owned),
            gheads[0].reshape(device_count, few),
            gheads[1].reshape(device_count, few),
            grad_router.reshape(device_count, owned * expert_count),
        ],
        axis=1,
    )
    small = jnp.pad(small, ((0, 0), (0, 32 * 128 - small.shape[1]))).reshape(*blocks, 32, 128)
    d_normed, gw, grad_wo, small = scatter_end(
        dpart,
        gw.reshape(*blocks, owned, columns),
        gwo.reshape(*blocks[1:], w_out.shape[0], width),
        small,
        6,
    )
    small = small.reshape(-1)
    d_input_norm, _ = norm_backward(d_normed, layer_in, attn_gain)
    grad_input = d_state + d_input_norm
    gw = gw.astype(SINGLE_FLOAT)
    channels = heads * HEAD_DIM
    grad_wq = gw[:, :, :channels].transpose(1, 0, 2).reshape(owned, ctx_count * channels)
    shared = ctx_count // KEY_VALUE_HEADS
    kv = gw[:, :, channels:].reshape(KEY_VALUE_HEADS, shared, owned, 2, HEAD_DIM).sum(1)
    grad_wk = kv[:, :, 0].transpose(1, 0, 2).reshape(owned, KEY_VALUE_HEADS * HEAD_DIM)
    grad_wv = kv[:, :, 1].transpose(1, 0, 2).reshape(owned, KEY_VALUE_HEADS * HEAD_DIM)
    return (
        output[None],
        grad_input[None],
        small[:owned],
        grad_wq,
        grad_wk,
        grad_wv,
        small[2 * owned : at - few],
        small[at - few : at],
        grad_wo,
        small[owned : 2 * owned],
        small[at : at + owned * expert_count].reshape(owned, expert_count),
        grad_gate,
        grad_up,
        grad_down,
    )


def planned_body(mesh):
    if mesh.shape["ctx"] == 8 and mesh.shape["ws"] == 4:
        return tensor_body
    return general_body


def solution(mesh):
    placed = (
        P("ws", "ctx", None),
        P("ws", "ctx", None),
        P("ws", "ctx", None),
        P("ws", None),
        P(("ctx", "ws")),
        P(("ctx", "ws"), None),
        P(("ctx", "ws"), None),
        P(("ctx", "ws"), None),
        P(("ctx", "ws")),
        P(("ctx", "ws")),
        P(("ctx", "ws"), None),
        P(("ctx", "ws")),
        P(("ctx", "ws"), None),
        P(("ctx", "ws"), None, None),
        P(("ctx", "ws"), None, None),
        P(("ctx", "ws"), None, None),
    )
    return jax.shard_map(
        planned_body(mesh),
        mesh=mesh,
        in_specs=placed,
        out_specs=(
            P("ws", "ctx", None),
            P("ws", "ctx", None),
            P(("ctx", "ws")),
            P(("ctx", "ws"), None),
            P(("ctx", "ws"), None),
            P(("ctx", "ws"), None),
            P(("ctx", "ws")),
            P(("ctx", "ws")),
            P(("ctx", "ws"), None),
            P(("ctx", "ws")),
            P(("ctx", "ws"), None),
            P(("ctx", "ws"), None, None),
            P(("ctx", "ws"), None, None),
            P(("ctx", "ws"), None, None),
        ),
        check_vma=False,
    )
```

```python
import jax
import jax.numpy as jnp
from jax import lax
from jax.experimental import pallas as pl
from jax.experimental.pallas import tpu as pltpu
from jax.sharding import PartitionSpec as P

QUERY_HEADS = 32
KEY_VALUE_HEADS = 4
HEAD_DIM = 128
TOPK = 8


EPS = 1e-06
THETA = 1000000.0
MASK_FILL = -1e30
TOP_PRECISION = lax.Precision.HIGHEST
SINGLE_FLOAT = jnp.float32
BRAIN_FLOAT_TYPE = jnp.bfloat16


def rms_scale(values, norm_gain):
    return values * lax.rsqrt(jnp.mean(values * values, axis=-1, keepdims=True) + EPS) * norm_gain


def rotate(values, positions):
    half_dim = values.shape[-1] // 2
    frequency = THETA ** (-2.0 * jnp.arange(half_dim, dtype=jnp.float32) / values.shape[-1])
    angle = positions.astype(jnp.float32)[:, None] * frequency[None, :]
    cosine = jnp.cos(angle)[:, None, :]
    sine_part = jnp.sin(angle)[:, None, :]
    first_half = values[..., :half_dim]
    second_half = values[..., half_dim:]
    return jnp.concatenate(
        [
            first_half * cosine - second_half * sine_part,
            second_half * cosine + first_half * sine_part,
        ],
        axis=-1,
    )


def head_prepare(raw_heads, norm_gain, positions):
    return rotate(rms_scale(raw_heads, norm_gain), positions)


def swiglu(gate_part, up_part):
    return jax.nn.silu(gate_part) * up_part


def stored_positions(row_index, tokens_per_shard, ctx_count):
    device_row = row_index // tokens_per_shard
    within = row_index % tokens_per_shard
    half_block = tokens_per_shard // 2
    block_index = jnp.where(within < half_block, device_row, 2 * ctx_count - 1 - device_row)
    return block_index * half_block + within % half_block


def segment_ids(doc_lengths, positions):
    doc_ends = jnp.cumsum(doc_lengths, dtype=jnp.int32)
    return jnp.sum(
        (positions[:, None] >= doc_ends[None, :]).astype(jnp.int32), axis=1, dtype=jnp.int32
    )


def slot_ranks(flat_routes, expert_count):
    expert_hits = (
        flat_routes[:, None] == jnp.arange(expert_count, dtype=jnp.int32)[None, :]
    ).astype(jnp.int32)
    running = jnp.cumsum(expert_hits, axis=0, dtype=jnp.int32) - 1
    return jnp.sum(expert_hits * running, axis=1, dtype=jnp.int32)


def send_inputs(flat_rows):
    moved = lax.all_to_all(flat_rows, ("ctx", "ws"), split_axis=0, concat_axis=0, tiled=True)
    return moved


def send_outputs(flat_rows):
    moved = lax.all_to_all(flat_rows, ("ctx", "ws"), split_axis=0, concat_axis=0, tiled=True)
    return moved


def send_out_grads(flat_rows):
    moved = lax.all_to_all(flat_rows, ("ctx", "ws"), split_axis=0, concat_axis=0, tiled=True)
    return moved


def send_in_grads(flat_rows):
    moved = lax.all_to_all(flat_rows, ("ctx", "ws"), split_axis=0, concat_axis=0, tiled=True)
    return moved


def flat_rows(grid_sum):
    return grid_sum.reshape((-1,) + grid_sum.shape[3:])


def to_expert_major(arrived, expert_local):
    device_count, row_span, model_width = arrived.shape
    capacity = row_span // expert_local
    shaped = arrived.reshape(device_count, expert_local, capacity, model_width)
    return shaped.transpose(1, 0, 2, 3).reshape(expert_local, device_count * capacity, model_width)


def to_device_major(expert_rows, device_count):
    expert_local, row_span, model_width = expert_rows.shape
    capacity = row_span // device_count
    shaped = expert_rows.reshape(expert_local, device_count, capacity, model_width)
    return shaped.transpose(1, 0, 2, 3).reshape(device_count, expert_local * capacity, model_width)


def general_body(
    inputs,
    grad_output,
    routes,
    doc_lengths,
    norm_attn,
    w_query,
    key_projection,
    value_projection,
    query_norm,
    key_norm,
    w_out,
    norm_ffn,
    w_router,
    expert_gate,
    expert_up,
    expert_down,
):
    ctx_count = lax.axis_size("ctx")
    device_count = ctx_count * lax.axis_size("ws")
    tokens_per_shard = inputs.shape[1]
    model_width = inputs.shape[2]
    sequence_tokens = tokens_per_shard * ctx_count
    expert_count = w_router.shape[1]
    expert_local = expert_gate.shape[0]
    capacity = max(2, tokens_per_shard * TOPK * 3 // (2 * device_count))
    query_group_size = QUERY_HEADS // KEY_VALUE_HEADS
    logit_scale = HEAD_DIM ** (-0.5)
    single_key_block = min(512, sequence_tokens)
    count_of_blocks = sequence_tokens // single_key_block
    ctx_index = lax.axis_index("ctx")
    positions_all = stored_positions(
        jnp.arange(sequence_tokens, dtype=jnp.int32), tokens_per_shard, ctx_count
    )
    segments_all = segment_ids(doc_lengths[0], positions_all)
    local_positions = lax.dynamic_slice_in_dim(
        positions_all, ctx_index * tokens_per_shard, tokens_per_shard
    )
    segments_own = lax.dynamic_slice_in_dim(
        segments_all, ctx_index * tokens_per_shard, tokens_per_shard
    )
    validity = (segments_own < doc_lengths.shape[1]).astype(SINGLE_FLOAT)
    shards = (
        norm_attn,
        w_query,
        key_projection,
        value_projection,
        query_norm,
        key_norm,
        w_out,
        norm_ffn,
        w_router,
    )
    gathered = (
        lax.all_gather(shards[0], ("ctx", "ws"), axis=0, tiled=True),
        lax.all_gather(shards[1], ("ctx", "ws"), axis=0, tiled=True),
        lax.all_gather(shards[2], ("ctx", "ws"), axis=0, tiled=True),
        lax.all_gather(shards[3], ("ctx", "ws"), axis=0, tiled=True),
        lax.all_gather(shards[4], ("ctx", "ws"), axis=0, tiled=True),
        lax.all_gather(shards[5], ("ctx", "ws"), axis=0, tiled=True),
        lax.all_gather(shards[6], ("ctx", "ws"), axis=0, tiled=True),
        lax.all_gather(shards[7], ("ctx", "ws"), axis=0, tiled=True),
        lax.all_gather(shards[8], ("ctx", "ws"), axis=0, tiled=True),
    )
    (
        attn_gain,
        query_matrix,
        key_matrix,
        value_matrix,
        query_gain,
        key_norm_gain,
        output_matrix,
        ffn_gain,
        router_matrix,
    ) = gathered
    attn_gain = attn_gain.astype(SINGLE_FLOAT)
    query_gain = query_gain.astype(SINGLE_FLOAT)
    key_norm_gain = key_norm_gain.astype(SINGLE_FLOAT)
    ffn_gain = ffn_gain.astype(SINGLE_FLOAT)
    layer_in = inputs[0].astype(SINGLE_FLOAT)
    normalized_rows = rms_scale(layer_in, attn_gain).astype(BRAIN_FLOAT_TYPE)
    unnormed_queries = jnp.dot(
        normalized_rows, query_matrix, preferred_element_type=SINGLE_FLOAT
    ).reshape(tokens_per_shard, QUERY_HEADS, HEAD_DIM)
    unnormed_keys = jnp.dot(
        normalized_rows, key_matrix, preferred_element_type=SINGLE_FLOAT
    ).reshape(tokens_per_shard, KEY_VALUE_HEADS, HEAD_DIM)
    value_low = jnp.dot(normalized_rows, value_matrix, preferred_element_type=SINGLE_FLOAT).astype(
        BRAIN_FLOAT_TYPE
    )
    query_rows = head_prepare(unnormed_queries, query_gain, local_positions).astype(
        BRAIN_FLOAT_TYPE
    )
    key_low = (
        head_prepare(unnormed_keys, key_norm_gain, local_positions)
        .astype(BRAIN_FLOAT_TYPE)
        .reshape(tokens_per_shard, KEY_VALUE_HEADS * HEAD_DIM)
    )
    every_key, every_value = (
        lax.all_gather(key_low, "ctx", axis=0, tiled=True),
        lax.all_gather(value_low, "ctx", axis=0, tiled=True),
    )
    grouped_queries = query_rows.reshape(
        tokens_per_shard, KEY_VALUE_HEADS, query_group_size, HEAD_DIM
    )
    blocked_keys = every_key.reshape(count_of_blocks, single_key_block, KEY_VALUE_HEADS, HEAD_DIM)
    blocked_values = every_value.reshape(
        count_of_blocks, single_key_block, KEY_VALUE_HEADS, HEAD_DIM
    )
    position_blocks = positions_all.reshape(count_of_blocks, single_key_block)
    segment_blocks = segments_all.reshape(count_of_blocks, single_key_block)

    def scores_for(block_keys, block_positions, block_segments):
        raw_scores = (
            jnp.einsum(
                "tkgd,jkd->kgtj", grouped_queries, block_keys, preferred_element_type=SINGLE_FLOAT
            )
            * logit_scale
        )
        allowed = (segments_own[:, None] == block_segments[None, :]) & (
            block_positions[None, :] <= local_positions[:, None]
        )
        return (raw_scores, allowed[None, None])

    def stats_step(running, pieces):
        maximum, denominator = running
        block_keys, block_positions, block_segments = pieces
        raw_scores, allowed = scores_for(block_keys, block_positions, block_segments)
        masked = jnp.where(allowed, raw_scores, MASK_FILL)
        new_maximum = jnp.maximum(maximum, jnp.max(masked, axis=-1))
        weights = jnp.where(allowed, jnp.exp(masked - new_maximum[..., None]), 0.0)
        denominator = denominator * jnp.exp(maximum - new_maximum) + jnp.sum(weights, axis=-1)
        return ((new_maximum, denominator), None)

    stats_init = (
        jnp.full((KEY_VALUE_HEADS, query_group_size, tokens_per_shard), MASK_FILL, SINGLE_FLOAT),
        jnp.zeros((KEY_VALUE_HEADS, query_group_size, tokens_per_shard), SINGLE_FLOAT),
    )
    (maximum, denominator), _ = lax.scan(
        stats_step, stats_init, (blocked_keys, position_blocks, segment_blocks)
    )

    def probs_for(raw_scores, allowed):
        return (
            jnp.where(allowed, jnp.exp(raw_scores - maximum[..., None]), 0.0)
            / denominator[..., None]
        )

    def value_update(running, pieces):
        block_keys, block_values, block_positions, block_segments = pieces
        raw_scores, allowed = scores_for(block_keys, block_positions, block_segments)
        softmaxed = probs_for(raw_scores, allowed).astype(BRAIN_FLOAT_TYPE)
        running = running + jnp.einsum(
            "kgtj,jkd->tkgd", softmaxed, block_values, preferred_element_type=SINGLE_FLOAT
        )
        return (running, None)

    inputs_per_block = (blocked_keys, blocked_values, position_blocks, segment_blocks)
    attended, _ = lax.scan(
        value_update,
        jnp.zeros((tokens_per_shard, KEY_VALUE_HEADS, query_group_size, HEAD_DIM), SINGLE_FLOAT),
        inputs_per_block,
    )
    attn_low = attended.reshape(tokens_per_shard, QUERY_HEADS * HEAD_DIM).astype(BRAIN_FLOAT_TYPE)
    hidden_state = layer_in + jnp.dot(attn_low, output_matrix, preferred_element_type=SINGLE_FLOAT)
    combined_rows = rms_scale(hidden_state, ffn_gain).astype(BRAIN_FLOAT_TYPE)
    router_scores = jnp.dot(combined_rows, router_matrix, preferred_element_type=SINGLE_FLOAT)
    own_routes = routes[0]
    route_mask = (
        own_routes[:, :, None] == jnp.arange(expert_count, dtype=jnp.int32)[None, None, :]
    ).astype(SINGLE_FLOAT)
    chosen = jnp.einsum("tke,te->tk", route_mask, router_scores, precision=TOP_PRECISION)
    gate_share = jax.nn.softmax(chosen, axis=-1)
    flat_routes = own_routes.reshape(-1)
    slot_index = flat_routes * capacity + slot_ranks(flat_routes, expert_count)
    entries = tokens_per_shard * TOPK
    source_slot = (
        jnp.full((expert_count * capacity,), entries, jnp.int32)
        .at[slot_index]
        .set(jnp.arange(entries, dtype=jnp.int32))
    )
    padded_in = jnp.concatenate(
        [combined_rows, jnp.zeros((1, model_width), BRAIN_FLOAT_TYPE)], axis=0
    )
    outgoing = padded_in[source_slot // TOPK].reshape(device_count, -1, model_width)
    expert_in = to_expert_major(send_inputs(outgoing), expert_local)
    gate_hidden = jnp.einsum(
        "erd,edf->erf", expert_in, expert_gate, preferred_element_type=SINGLE_FLOAT
    )
    up_hidden = jnp.einsum(
        "erd,edf->erf", expert_in, expert_up, preferred_element_type=SINGLE_FLOAT
    )
    hidden = swiglu(gate_hidden, up_hidden).astype(BRAIN_FLOAT_TYPE)
    expert_out = jnp.einsum(
        "erf,efd->erd", hidden, expert_down, preferred_element_type=SINGLE_FLOAT
    ).astype(BRAIN_FLOAT_TYPE)
    returned = send_outputs(to_device_major(expert_out, device_count)).reshape(
        expert_count * capacity, model_width
    )
    picked = returned[slot_index].reshape(tokens_per_shard, TOPK, model_width)
    moe_sum = jnp.sum(gate_share[:, :, None] * picked.astype(SINGLE_FLOAT), axis=1)
    output = (hidden_state + moe_sum).astype(BRAIN_FLOAT_TYPE)
    d_layer = grad_output[0].astype(SINGLE_FLOAT) * validity[:, None]
    d_gate_share = jnp.sum(d_layer[:, None, :] * picked.astype(SINGLE_FLOAT), axis=-1)
    d_chosen = gate_share * (
        d_gate_share - jnp.sum(gate_share * d_gate_share, axis=-1, keepdims=True)
    )
    d_logits = jnp.einsum("tke,tk->te", route_mask, d_chosen, precision=TOP_PRECISION).astype(
        BRAIN_FLOAT_TYPE
    )
    d_copies = (
        (gate_share[:, :, None] * d_layer[:, None, :])
        .astype(BRAIN_FLOAT_TYPE)
        .reshape(entries, model_width)
    )
    d_padded = jnp.concatenate([d_copies, jnp.zeros((1, model_width), BRAIN_FLOAT_TYPE)], axis=0)
    d_outgoing = d_padded[source_slot].reshape(device_count, -1, model_width)
    d_expert_out = to_expert_major(send_out_grads(d_outgoing), expert_local)
    d_hidden = jnp.einsum(
        "erd,efd->erf", d_expert_out, expert_down, preferred_element_type=SINGLE_FLOAT
    )
    grad_down = jnp.einsum(
        "erf,erd->efd", hidden, d_expert_out, preferred_element_type=SINGLE_FLOAT
    )
    _, swiglu_back = jax.vjp(swiglu, gate_hidden, up_hidden)
    d_gate_hidden, d_up_hidden = swiglu_back(d_hidden)
    d_gate_low = d_gate_hidden.astype(BRAIN_FLOAT_TYPE)
    d_up_low = d_up_hidden.astype(BRAIN_FLOAT_TYPE)
    grad_gate = jnp.einsum(
        "erd,erf->edf", expert_in, d_gate_low, preferred_element_type=SINGLE_FLOAT
    )
    grad_up = jnp.einsum("erd,erf->edf", expert_in, d_up_low, preferred_element_type=SINGLE_FLOAT)
    d_expert_in = jnp.einsum(
        "erf,edf->erd", d_gate_low, expert_gate, preferred_element_type=SINGLE_FLOAT
    )
    d_expert_in = (
        d_expert_in
        + jnp.einsum("erf,edf->erd", d_up_low, expert_up, preferred_element_type=SINGLE_FLOAT)
    ).astype(BRAIN_FLOAT_TYPE)
    d_returned = send_in_grads(to_device_major(d_expert_in, device_count)).reshape(
        expert_count * capacity, model_width
    )
    d_slots = d_returned[slot_index].reshape(tokens_per_shard, TOPK, model_width)
    d_mixed = jnp.sum(d_slots.astype(SINGLE_FLOAT), axis=1) + jnp.einsum(
        "te,de->td", d_logits, router_matrix, preferred_element_type=SINGLE_FLOAT
    )
    grad_router = jnp.einsum(
        "td,te->de", combined_rows, d_logits, preferred_element_type=SINGLE_FLOAT
    )
    _, ffn_norm_back = jax.vjp(rms_scale, hidden_state, ffn_gain)
    d_state_norm, grad_ffn_gain = ffn_norm_back(d_mixed)
    d_state = d_layer + d_state_norm
    d_state_low = d_state.astype(BRAIN_FLOAT_TYPE)
    grad_out_weight = jnp.einsum(
        "tc,td->cd", attn_low, d_state_low, preferred_element_type=SINGLE_FLOAT
    )
    attention_gradient = jnp.einsum(
        "td,cd->tc", d_state_low, output_matrix, preferred_element_type=SINGLE_FLOAT
    ).astype(BRAIN_FLOAT_TYPE)
    attention_gradient = attention_gradient.reshape(
        tokens_per_shard, KEY_VALUE_HEADS, query_group_size, HEAD_DIM
    )
    row_delta = jnp.sum(attention_gradient.astype(SINGLE_FLOAT) * attended, axis=-1).transpose(
        1, 2, 0
    )

    def backward_step(d_query_acc, pieces):
        block_keys, block_values, block_positions, block_segments = pieces
        raw_scores, allowed = scores_for(block_keys, block_positions, block_segments)
        softmaxed = probs_for(raw_scores, allowed)
        d_probs = jnp.einsum(
            "tkgd,jkd->kgtj", attention_gradient, block_values, preferred_element_type=SINGLE_FLOAT
        )
        d_scores = (softmaxed * (d_probs - row_delta[..., None])).astype(BRAIN_FLOAT_TYPE)
        d_query_acc = d_query_acc + jnp.einsum(
            "kgtj,jkd->tkgd", d_scores, block_keys, preferred_element_type=SINGLE_FLOAT
        )
        d_key_block = jnp.einsum(
            "kgtj,tkgd->jkd", d_scores, grouped_queries, preferred_element_type=SINGLE_FLOAT
        )
        d_value_block = jnp.einsum(
            "kgtj,tkgd->jkd",
            softmaxed.astype(BRAIN_FLOAT_TYPE),
            attention_gradient,
            preferred_element_type=SINGLE_FLOAT,
        )
        return (d_query_acc, (d_key_block, d_value_block))

    d_query_acc, (key_block_gradients, value_block_gradients) = lax.scan(
        backward_step,
        jnp.zeros((tokens_per_shard, KEY_VALUE_HEADS, query_group_size, HEAD_DIM), SINGLE_FLOAT),
        inputs_per_block,
    )
    every_key_gradient = (key_block_gradients * logit_scale).reshape(
        sequence_tokens, KEY_VALUE_HEADS * HEAD_DIM
    )
    every_value_gradient = value_block_gradients.reshape(
        sequence_tokens, KEY_VALUE_HEADS * HEAD_DIM
    )
    key_gradients, d_values = (
        lax.psum_scatter(
            every_key_gradient.astype(jnp.bfloat16), "ctx", scatter_dimension=0, tiled=True
        ).astype(jnp.float32),
        lax.psum_scatter(
            every_value_gradient.astype(jnp.bfloat16), "ctx", scatter_dimension=0, tiled=True
        ).astype(jnp.float32),
    )
    _, query_back = jax.vjp(
        lambda raw_heads, norm_gain: head_prepare(raw_heads, norm_gain, local_positions),
        unnormed_queries,
        query_gain,
    )
    d_query_raw, grad_query_gain = query_back(
        (d_query_acc * logit_scale).reshape(tokens_per_shard, QUERY_HEADS, HEAD_DIM)
    )
    _, key_backward = jax.vjp(
        lambda raw_heads, norm_gain: head_prepare(raw_heads, norm_gain, local_positions),
        unnormed_keys,
        key_norm_gain,
    )
    raw_key_gradient, key_gain_gradient = key_backward(
        key_gradients.reshape(tokens_per_shard, KEY_VALUE_HEADS, HEAD_DIM)
    )
    d_query_low = d_query_raw.reshape(tokens_per_shard, QUERY_HEADS * HEAD_DIM).astype(
        BRAIN_FLOAT_TYPE
    )
    key_gradient_lowprec = raw_key_gradient.reshape(
        tokens_per_shard, KEY_VALUE_HEADS * HEAD_DIM
    ).astype(BRAIN_FLOAT_TYPE)
    d_value_low = d_values.astype(BRAIN_FLOAT_TYPE)
    grad_query_weight = jnp.einsum(
        "td,tc->dc", normalized_rows, d_query_low, preferred_element_type=SINGLE_FLOAT
    )
    grad_key_weight = jnp.einsum(
        "td,tc->dc", normalized_rows, key_gradient_lowprec, preferred_element_type=SINGLE_FLOAT
    )
    grad_value_weight = jnp.einsum(
        "td,tc->dc", normalized_rows, d_value_low, preferred_element_type=SINGLE_FLOAT
    )
    d_normed = jnp.einsum(
        "tc,dc->td", d_query_low, query_matrix, preferred_element_type=SINGLE_FLOAT
    )
    d_normed = d_normed + jnp.einsum(
        "tc,dc->td", key_gradient_lowprec, key_matrix, preferred_element_type=SINGLE_FLOAT
    )
    d_normed = d_normed + jnp.einsum(
        "tc,dc->td", d_value_low, value_matrix, preferred_element_type=SINGLE_FLOAT
    )
    _, attn_norm_back = jax.vjp(rms_scale, layer_in, attn_gain)
    d_input_norm, grad_attn_gain = attn_norm_back(d_normed)
    grad_input = d_state + d_input_norm
    reduced = (
        lax.psum_scatter(grad_attn_gain, ("ctx", "ws"), scatter_dimension=0, tiled=True),
        lax.psum_scatter(grad_query_weight, ("ctx", "ws"), scatter_dimension=0, tiled=True),
        lax.psum_scatter(grad_key_weight, ("ctx", "ws"), scatter_dimension=0, tiled=True),
        lax.psum_scatter(grad_value_weight, ("ctx", "ws"), scatter_dimension=0, tiled=True),
        lax.psum_scatter(grad_query_gain, ("ctx", "ws"), scatter_dimension=0, tiled=True),
        lax.psum_scatter(key_gain_gradient, ("ctx", "ws"), scatter_dimension=0, tiled=True),
        lax.psum_scatter(grad_out_weight, ("ctx", "ws"), scatter_dimension=0, tiled=True),
        lax.psum_scatter(grad_ffn_gain, ("ctx", "ws"), scatter_dimension=0, tiled=True),
        lax.psum_scatter(grad_router, ("ctx", "ws"), scatter_dimension=0, tiled=True),
    )
    return (
        output[None],
        grad_input[None],
        reduced[0],
        reduced[1],
        reduced[2],
        reduced[3],
        reduced[4],
        reduced[5],
        reduced[6],
        reduced[7],
        reduced[8],
        grad_gate,
        grad_up,
        grad_down,
    )


VMEM_WHOLE = pl.BlockSpec(memory_space=pltpu.VMEM)
VMEM_BYTES = 60 * 2**20
EXTRA = 128


def compiler_params():
    return pltpu.CompilerParams(vmem_limit_bytes=VMEM_BYTES)


def dot_rows(left, right):
    return lax.dot_general(
        left, right, (((1,), (0,)), ((), ())), preferred_element_type=SINGLE_FLOAT
    )


def dot_right_transposed(left, right):
    return lax.dot_general(
        left, right, (((1,), (1,)), ((), ())), preferred_element_type=SINGLE_FLOAT
    )


def dot_left_transposed(left, right):
    return lax.dot_general(
        left, right, (((0,), (0,)), ((), ())), preferred_element_type=SINGLE_FLOAT
    )


def key_range(tile, tile_rows, sequence_tokens, slack):
    half = sequence_tokens // 2
    first_row = tile * tile_rows
    low = 0 if first_row < half + slack else half
    return low, first_row + tile_rows


def stacked_heads(ref, rows, heads):
    return jnp.concatenate(
        [ref[rows, h * HEAD_DIM : (h + 1) * HEAD_DIM] for h in range(heads)], axis=0
    )


def tile_scores(q4, k_ref, segc_ref, segr_ref, low, high, first_row, tile_rows, heads):
    scale = HEAD_DIM ** (-0.5)
    scores = dot_right_transposed(q4, k_ref[low:high, :]) * scale
    span = high - low
    query_place = first_row + lax.broadcasted_iota(jnp.int32, (tile_rows, span), 0)
    key_place = low + lax.broadcasted_iota(jnp.int32, (tile_rows, span), 1)
    allowed = (segc_ref[first_row : first_row + tile_rows, :] == segr_ref[:, low:high]) & (
        key_place <= query_place
    )
    fill = jnp.where(allowed, 0.0, MASK_FILL)
    scores = scores + jnp.concatenate([fill] * heads, axis=0)
    exponent = jnp.exp(scores - jnp.max(scores, axis=-1, keepdims=True))
    return exponent * (1.0 / jnp.sum(exponent, axis=-1, keepdims=True))


def head_backward(turned_gradient, part, gain, cosine, sine):
    scaled_gradient = turned_gradient * cosine - (
        pltpu.roll(turned_gradient, HEAD_DIM // 2, 1) * sine
    )
    inverse = lax.rsqrt(jnp.mean(part * part, axis=-1, keepdims=True) + EPS)
    unit = part * inverse
    gain_gradient = jnp.sum(scaled_gradient * unit, axis=0, keepdims=True)
    unit_gradient = scaled_gradient * gain
    raw_gradient = inverse * (
        unit_gradient - unit * jnp.mean(unit * unit_gradient, axis=-1, keepdims=True)
    )
    return raw_gradient, gain_gradient


MESH = pl.DeviceIdType.MESH
ANYWHERE = pl.BlockSpec(memory_space=pl.ANY)
LINE = 4


def place():
    c, w = lax.axis_index("ctx"), lax.axis_index("ws")
    return c // 2, c % 2, w // 2, w % 2


def device_at(z, y, x, k):
    return (z * 2 + y, x * 2 + k)


def slot_of(z, y, x, k):
    return ((z * 2 + y) * 2 + x) * 2 + k


def line_order(z):
    upper = z // 2
    return [z, z + 1 - 2 * upper, 2 - 2 * (z % 2) + upper, 3 - 3 * upper]


def remote(source, target, send, recv, device):
    return pltpu.make_async_remote_copy(
        src_ref=source,
        dst_ref=target,
        send_sem=send,
        recv_sem=recv,
        device_id=device,
        device_id_type=MESH,
    )


def meet(z, y, x, k, around):
    barrier = pltpu.get_barrier_semaphore()

    def greet(device):
        pl.semaphore_signal(barrier, inc=1, device_id=device, device_id_type=MESH)

    @pl.when(z < LINE - 1)
    def _():
        greet(device_at(z + 1, y, x, k))

    @pl.when(z > 0)
    def _():
        greet(device_at(z - 1, y, x, k))

    for device in around:
        greet(device)
    pl.semaphore_wait(barrier, len(around) + 1 + z * (LINE - 1 - z) // 2)


class Sends:
    def __init__(self, semaphores):
        self.semaphores = semaphores
        self.started = []

    def start(self, source, target, recv, device, condition=None):
        copy = remote(source, target, self.semaphores.at[len(self.started)], recv, device)
        if condition is None:
            copy.start()
        else:
            pl.when(condition)(copy.start)
        self.started.append((condition, copy))

    def finish(self):
        for condition, copy in self.started:
            if condition is None:
                copy.wait_send()
            else:
                pl.when(condition)(copy.wait_send)


def arrived(target, recv, device):
    remote(target, target, recv, recv, device).wait_recv()


def along_line(z, y, x, k, block, i, order, start):
    if i == 0:
        up, down = z < LINE - 1, z > 0
    else:
        below = order[i] < z
        up, down = below & (z < LINE - 1), jnp.logical_not(below) & (z > 0)
    start(block, device_at(z + 1, y, x, k), up)
    start(block, device_at(z - 1, y, x, k), down)


class BlockGather:
    def __init__(self, source, out, local, send_sems, recv_sems):
        self.source, self.out, self.recv_sems = source, out, recv_sems
        z, y, x, k = self.at = place()
        self.order = line_order(z)
        self.along_x, self.along_y = device_at(z, y, 1 - x, k), device_at(z, 1 - y, x, k)
        self.sibling = device_at(z, y, x, 1 - k)
        self.sends = Sends(send_sems)
        self.mine = slot_of(z, y, x, k)
        self.own = pltpu.make_async_copy(source, out.at[self.mine], local)

    def pass_on(self, slot, device, condition=None):
        block = self.source if slot is self.mine else self.out.at[slot]
        self.sends.start(block, self.out.at[slot], self.recv_sems.at[slot], device, condition)

    def wait(self, slot):
        arrived(self.out.at[slot], self.recv_sems.at[slot], self.along_x)

    def line(self, i):
        z, y, x, k = self.at
        slot = slot_of(self.order[i], y, x, k)
        if i > 1:
            pl.when((z > 0) & (z < LINE - 1))(lambda: self.wait(slot))
        along_line(z, y, x, k, slot, i, self.order, self.pass_on)

    def column(self, i):
        z, y, x, k = self.at
        slot = self.mine if i == 0 else slot_of(self.order[i], y, x, k)
        if i == 0:
            along_line(z, y, x, k, slot, i, self.order, self.pass_on)
        elif i == 1:
            self.wait(slot)
            self.line(1)
        else:
            pl.when((z == 0) | (z == LINE - 1))(lambda: self.wait(slot))
        for device in (self.along_x, self.along_y, self.sibling):
            self.pass_on(slot, device)

    def across(self, i, on_x, on_y):
        z, y, x, k = self.at
        return slot_of(self.order[i], 1 - y if on_y else y, 1 - x if on_x else x, k)

    def receive(self, slot):
        self.wait(slot)
        self.pass_on(slot, self.sibling)

    def begin(self):
        meet(*self.at, (self.along_x, self.along_y, self.sibling))
        self.own.start()
        self.column(0)

    def advance(self, i):
        self.column(i)
        if i < 3:
            self.line(i + 1)
        self.receive(self.across(i - 1, True, False))
        self.receive(self.across(i - 1, False, True))

    def turn(self):
        self.receive(self.across(3, True, False))
        for j in (0, 1):
            self.pass_on(self.across(j, True, False), self.along_y)
        self.receive(self.across(3, False, True))
        for j in (2, 3):
            self.pass_on(self.across(j, False, True), self.along_x)

    def last(self, waited=()):
        for i in range(4):
            self.receive(self.across(i, True, True))
        z, y, x, k = self.at
        for i in range(4):
            for dy, dx in ((0, 0), (0, 1), (1, 0), (1, 1)):
                if (dy, dx) not in waited:
                    self.wait(
                        slot_of(self.order[i], 1 - y if dy else y, 1 - x if dx else x, 1 - k)
                    )
        self.sends.finish()

    def finish(self):
        self.turn()
        self.last()
        self.own.wait()


def add_blocks(target, *terms):
    rows = target.shape[0]

    def step(i, carry):
        part = pl.ds(pl.multiple_of(i * 16, 16), 16)
        total = terms[0][part, :].astype(SINGLE_FLOAT)
        for term in terms[1:]:
            total = total + term[part, :].astype(SINGLE_FLOAT)
        target[part, :] = total.astype(target.dtype)
        return carry

    lax.fori_loop(0, rows // 16, step, 0)


def scatter_line(z, y, x, k, order, total, owned, up_ref, down_ref, up_sems, down_sems, sends, out, after):
    above, below = device_at(z + 1, y, x, k), device_at(z - 1, y, x, k)
    for i in (3, 2, 1):
        total(i)
        chip = order[i]
        upward = chip > z
        block = owned(i)

        @pl.when(upward & (z > 0))
        def _():
            arrived(up_ref.at[chip], up_sems.at[chip], below)
            add_blocks(block, block, up_ref.at[chip])

        @pl.when(jnp.logical_not(upward) & (z < LINE - 1))
        def _():
            arrived(down_ref.at[chip], down_sems.at[chip], above)
            add_blocks(block, block, down_ref.at[chip])

        sends.start(block, up_ref.at[chip], up_sems.at[chip], above, upward)
        sends.start(
            block, down_ref.at[chip], down_sems.at[chip], below, jnp.logical_not(upward)
        )
        after(i)
    total(0)
    block = owned(0)

    @pl.when(z > 0)
    def _():
        arrived(up_ref.at[z], up_sems.at[z], below)

    @pl.when(z < LINE - 1)
    def _():
        arrived(down_ref.at[z], down_sems.at[z], above)

    @pl.when(z == 0)
    def _():
        add_blocks(out, block, down_ref.at[z])

    @pl.when(z == LINE - 1)
    def _():
        add_blocks(out, block, up_ref.at[z])

    @pl.when((z > 0) & (z < LINE - 1))
    def _():
        add_blocks(out, block, up_ref.at[z], down_ref.at[z])


class PickedSums:
    def __init__(self, rows_in, pick_in, out, scratch):
        (
            self.rows_ref,
            self.pick_ref,
            self.own_ref,
            self.corner_ref,
            self.x_ref,
            self.y_ref,
            self.up_ref,
            self.down_ref,
            load_sems,
            self.corner_sems,
            self.x_sems,
            self.y_sems,
            self.up_sems,
            self.down_sems,
            send_sems,
        ) = scratch
        self.out = out
        z, y, x, k = self.at = place()
        self.order = line_order(z)
        self.along_x, self.along_y = device_at(z, y, 1 - x, k), device_at(z, 1 - y, x, k)
        self.pick_load = pltpu.make_async_copy(pick_in, self.pick_ref, load_sems.at[16])
        self.turn = [i * 4 + r for r in (3, 1, 2, 0) for i in (3, 2, 1, 0)]
        self.loads = {
            j: pltpu.make_async_copy(rows_in.at[j], self.rows_ref.at[j], load_sems.at[j])
            for j in self.turn
        }
        self.sends = Sends(send_sems)

    def begin(self):
        self.pick_load.start()
        for j in self.turn:
            self.loads[j].start()
        meet(*self.at, (self.along_x, self.along_y))
        self.pick_load.wait()

    def gather(self, i, r, *extra):
        j = i * 4 + r
        self.loads[j].wait()
        block = self.own_ref.at[j]
        spread_rows(block, self.pick_ref.at[j], self.rows_ref.at[j], *extra)
        return block

    def corners(self):
        for i in (3, 2, 1, 0):
            self.sends.start(
                self.gather(i, 3),
                self.corner_ref.at[i],
                self.corner_sems.at[i],
                self.along_y if i < 2 else self.along_x,
            )

    def cross(self, i):
        arrived(self.corner_ref.at[i], self.corner_sems.at[i], self.along_x)
        extra = (self.corner_ref.at[i],)
        for_x = self.gather(i, 1, *(extra if i < 2 else ()))
        self.sends.start(for_x, self.x_ref.at[i], self.x_sems.at[i], self.along_x)
        for_y = self.gather(i, 2, *(extra if i >= 2 else ()))
        self.sends.start(for_y, self.y_ref.at[i], self.y_sems.at[i], self.along_y)

    def total(self, i):
        arrived(self.x_ref.at[i], self.x_sems.at[i], self.along_x)
        arrived(self.y_ref.at[i], self.y_sems.at[i], self.along_y)
        if i > 0:
            self.cross(i - 1)
        self.gather(i, 0, self.x_ref.at[i], self.y_ref.at[i])

    def finish(self, between=lambda i: None):
        scatter_line(
            *self.at, self.order, self.total, lambda i: self.own_ref.at[i * 4],
            self.up_ref, self.down_ref, self.up_sems, self.down_sems, self.sends, self.out,
            between,
        )
        self.sends.finish()


def picked_scratch(rows, pick):
    shape, low = (pick.shape[2], rows.shape[2]), rows.dtype
    return (
        [pltpu.VMEM(rows.shape, low), pltpu.VMEM(pick.shape, low)]
        + [pltpu.VMEM((n,) + shape, low) for n in (16, 4, 4, 4, 4, 4)]
        + [pltpu.SemaphoreType.DMA((n,)) for n in (17, 4, 4, 4, 4, 4, 24)]
    )


def halves(ref, z, y):
    half = ref.shape[0] // 16
    c = z * 2 + y
    return [
        ref.at[pl.ds(pl.multiple_of(half * b, half), half), :] for b in (c, 15 - c)
    ]


def split_rows(ref):
    half = ref.shape[0] // 2
    return [ref.at[0:half, :], ref.at[half : 2 * half, :]]


class RowGather:
    def __init__(self, source, out, sends, locals_, semaphores, at, order, along_y):
        self.source, self.out, self.sends, self.semaphores = source, out, sends, semaphores
        self.at, self.order, self.along_y = at, order, along_y
        z, y, x, k = at
        self.own = [
            pltpu.make_async_copy(a, b, locals_.at[n])
            for n, (a, b) in enumerate(zip(split_rows(source), halves(out, z, y)))
        ]
        for copy in self.own:
            copy.start()

    def send(self, i, along, across):
        z, y, x, k = self.at
        chip = self.order[i]
        pieces = halves(self.out, chip, y)
        for n in (0, 1):
            block = split_rows(self.source)[n] if i == 0 else pieces[n]
            recv = self.semaphores.at[n, chip * 2 + y]

            def start(_, device, condition=None):
                self.sends.start(block, pieces[n], recv, device, condition)

            if along:
                along_line(z, y, x, k, None, i, self.order, start)
            if across:
                start(None, self.along_y)

    def line(self, i):
        z, y = self.at[:2]
        pl.when((z > 0) & (z < LINE - 1))(lambda: self.wait(self.order[i], y))
        self.send(i, True, False)

    def column(self, i):
        z, y = self.at[:2]
        if i == 1:
            self.wait(self.order[i], y)
        elif i > 1:
            pl.when((z == 0) | (z == LINE - 1))(lambda: self.wait(self.order[i], y))
        self.send(i, i < 2, True)

    def wait(self, chip, y):
        for n, piece in enumerate(halves(self.out, chip, y)):
            arrived(piece, self.semaphores.at[n, chip * 2 + y], self.along_y)

    def finish(self):
        y = self.at[1]
        for i in range(4):
            self.wait(self.order[i], 1 - y)
        for copy in self.own:
            copy.wait()


def gather_rows_kernel(
    source,
    x_late,
    x_early,
    d_in,
    hidden_late,
    hidden_early,
    d_gate_in,
    d_up_in,
    out,
    gate_out,
    up_out,
    down_out,
    x_ref,
    d_ref,
    hidden_ref,
    d_gate_ref,
    d_up_ref,
    gate_ref,
    up_ref,
    down_ref,
    load_sems,
    store_sems,
    local_sems,
    send_sems,
    recv_sems,
):
    at = place()
    z, y, x, k = at
    along_y = device_at(z, 1 - y, x, k)
    late, early = x_late.shape[0], x_early.shape[0]
    loads = [
        pltpu.make_async_copy(a, b, load_sems.at[n])
        for n, (a, b) in enumerate(
            (
                (x_late, x_ref.at[pl.ds(0, late), :]),
                (x_early, x_ref.at[pl.ds(late, early), :]),
                (d_gate_in, d_gate_ref),
                (d_up_in, d_up_ref),
                (hidden_late, hidden_ref.at[pl.ds(0, late), :]),
                (hidden_early, hidden_ref.at[pl.ds(late, early), :]),
                (d_in, d_ref),
            )
        )
    ]
    stores = [
        pltpu.make_async_copy(a, b, store_sems.at[n])
        for n, (a, b) in enumerate(
            ((gate_ref, gate_out), (up_ref, up_out), (down_ref, down_out))
        )
    ]
    meet(z, y, x, k, (along_y,))
    sends = Sends(send_sems)
    rows = RowGather(source, out, sends, local_sems, recv_sems, at, line_order(z), along_y)
    rows.column(0)
    for copy in loads:
        copy.start()

    def inward(i, carry):
        part = pl.ds(pl.multiple_of(i * 256, 256), 256)
        left = x_ref[:, part]
        gate_ref[part, :] = dot_left_transposed(left, d_gate_ref[...]).astype(gate_ref.dtype)
        up_ref[part, :] = dot_left_transposed(left, d_up_ref[...]).astype(up_ref.dtype)
        return carry

    def outward(i, carry):
        part = pl.ds(pl.multiple_of(i * 256, 256), 256)
        down_ref[part, :] = dot_left_transposed(hidden_ref[:, part], d_ref[...]).astype(
            down_ref.dtype
        )
        return carry

    steps = x_ref.shape[1] // 256
    for copy in loads[:4]:
        copy.wait()
    lax.fori_loop(0, 3, inward, 0)
    rows.column(1)
    rows.line(2)
    lax.fori_loop(3, steps, inward, 0)
    for copy in stores[:2]:
        copy.start()
    rows.column(2)
    rows.line(3)
    for copy in loads[4:]:
        copy.wait()
    lax.fori_loop(0, hidden_ref.shape[1] // 256, outward, 0)
    stores[2].start()
    rows.column(3)
    rows.finish()
    for copy in stores:
        copy.wait()
    sends.finish()


def gather_rows(block, x_rows, d_rows, hidden, d_gate, d_up, collective_id):
    rows, width = block.shape
    ff, low = d_up.shape[1], block.dtype
    slots = d_up.shape[0]
    shape, vmem, dma = jax.ShapeDtypeStruct, pltpu.VMEM, pltpu.SemaphoreType.DMA
    inputs = (*x_rows, d_rows, *hidden, d_gate, d_up)
    held = ((slots, width), (slots, width), (slots, ff), (slots, ff), (slots, ff))
    grads = ((width, ff), (width, ff), (ff, width))
    return pl.pallas_call(
        gather_rows_kernel,
        out_shape=[shape((8 * rows, width), low)] + [shape(size, low) for size in grads],
        in_specs=[ANYWHERE] * 8,
        out_specs=[ANYWHERE] * 4,
        scratch_shapes=[vmem(size, low) for size in held]
        + [vmem(size, low) for size in grads]
        + [dma((7,)), dma((3,)), dma((2,)), dma((24,)), dma((2, 8))],
        compiler_params=pltpu.CompilerParams(
            collective_id=collective_id, has_side_effects=True, vmem_limit_bytes=VMEM_BYTES
        ),
        name="gather_rows",
    )(block, *inputs)


class RowScatter:
    def __init__(self, part, out, buffers, semaphores, sends, at, order, along_y):
        self.part, self.out, self.sends, self.at, self.order = part, out, sends, at, order
        self.along_y = along_y
        self.own_ref, self.y_ref, self.up_ref, self.down_ref = buffers
        self.load_sems, self.y_sems, self.up_sems, self.down_sems = semaphores
        z, y, x, k = at
        self.loads = {}
        for i in (3, 2, 1, 0):
            self.loads[i] = [
                pltpu.make_async_copy(a, b, self.load_sems.at[n, i])
                for n, (a, b) in enumerate(
                    zip(halves(part, order[i], y), split_rows(self.own_ref.at[i]))
                )
            ]
            for copy in self.loads[i]:
                copy.start()
        self.cross(3)

    def cross(self, i):
        y = self.at[1]
        for n, (a, b) in enumerate(
            zip(halves(self.part, self.order[i], 1 - y), split_rows(self.y_ref.at[i]))
        ):
            self.sends.start(a, b, self.y_sems.at[n, i], self.along_y)

    def total(self, i):
        for copy in self.loads[i]:
            copy.wait()
        for n, piece in enumerate(split_rows(self.y_ref.at[i])):
            arrived(piece, self.y_sems.at[n, i], self.along_y)
        if i > 0:
            self.cross(i - 1)
        add_blocks(self.own_ref.at[i], self.own_ref.at[i], self.y_ref.at[i])

    def run(self, after=lambda i: None):
        z, y, x, k = self.at
        scatter_line(
            z, y, x, k, self.order, self.total, lambda i: self.own_ref.at[i],
            self.up_ref, self.down_ref, self.up_sems, self.down_sems, self.sends, self.out,
            after,
        )


def row_scatter_scratch(rows, width, low):
    dma = pltpu.SemaphoreType.DMA
    return [pltpu.VMEM((4, rows, width), low)] * 4 + [
        dma((2, 4)),
        dma((2, 4)),
        dma((4,)),
        dma((4,)),
    ]


def scatter_rows_kernel(part, out, *scratch):
    at = place()
    z, y, x, k = at
    along_y = device_at(z, 1 - y, x, k)
    meet(z, y, x, k, (along_y,))
    sends = Sends(scratch[8])
    rows = RowScatter(part, out, scratch[:4], scratch[4:8], sends, at, line_order(z), along_y)
    rows.run()
    sends.finish()


def scatter_rows(part, collective_id):
    rows, width = part.shape[0] // 8, part.shape[1]
    return pl.pallas_call(
        scatter_rows_kernel,
        out_shape=jax.ShapeDtypeStruct((rows, width), SINGLE_FLOAT),
        in_specs=[ANYWHERE],
        out_specs=VMEM_WHOLE,
        scratch_shapes=row_scatter_scratch(rows, width, part.dtype)
        + [pltpu.SemaphoreType.DMA((16,))],
        compiler_params=pltpu.CompilerParams(
            collective_id=collective_id, has_side_effects=True, vmem_limit_bytes=VMEM_BYTES
        ),
        name="scatter_rows",
    )(part)


def ring_of(c, w):
    return [((c + t) % 8, w) for t in range(1, 8)]


def gather_start_kernel(
    x_in,
    slab_in,
    wo_in,
    x_out,
    slab_out,
    wo_out,
    local_sems,
    send_sems,
    x_sems,
    slab_sems,
    wo_sems,
):
    at = place()
    z, y, x, k = at
    c, w = z * 2 + y, x * 2 + k
    along_x, along_y = device_at(z, y, 1 - x, k), device_at(z, 1 - y, x, k)
    sibling = device_at(z, y, x, 1 - k)
    others = ring_of(c, w)
    barrier = pltpu.get_barrier_semaphore()
    for device in others + [along_x, sibling]:
        pl.semaphore_signal(barrier, inc=1, device_id=device, device_id_type=MESH)
    pl.semaphore_wait(barrier, 9)
    sends = Sends(send_sems)
    rows = RowGather(
        x_in, x_out, sends, local_sems.at[pl.ds(0, 2)], x_sems, at, line_order(z), along_y
    )
    wo_rows = wo_in.shape[0]

    def wo_at(w):
        return wo_out.at[pl.ds(pl.multiple_of(w * wo_rows, wo_rows), wo_rows), :]

    mine = c * 4 + w
    local = [
        pltpu.make_async_copy(slab_in.at[c], slab_out.at[mine], local_sems.at[2]),
        pltpu.make_async_copy(wo_in, wo_at(w), local_sems.at[3]),
    ]
    for copy in local:
        copy.start()

    def pass_on(slot, device, block=None):
        block = slab_out.at[slot] if block is None else block
        sends.start(block, slab_out.at[slot], slab_sems.at[slot], device)

    def take(source, w):
        slot = source * 4 + w
        arrived(slab_out.at[slot], slab_sems.at[slot], along_x)
        return slot

    rows.column(0)
    for device in (along_x, sibling):
        sends.start(wo_in, wo_at(w), wo_sems.at[w], device)
        pass_on(mine, device, slab_in.at[c])
    for device in others:
        sends.start(slab_in.at[device[0]], slab_out.at[mine], slab_sems.at[mine], device)

    def onward():
        for t in range(1, 8):
            slot = take((c + 8 - t) % 8, w)
            pass_on(slot, along_x)
            pass_on(slot, sibling)

    def across():
        beside = (1 - x) * 2 + k
        arrived(wo_at(beside), wo_sems.at[beside], along_x)
        sends.start(wo_at(beside), wo_at(beside), wo_sems.at[beside], sibling)
        for t in range(8):
            pass_on(take((c + 8 - t) % 8, beside), sibling)

    rows.column(1)
    rows.line(2)
    rows.column(2)
    rows.line(3)
    onward()
    rows.column(3)
    across()
    for other in (x * 2 + 1 - k, (1 - x) * 2 + 1 - k):
        for t in range(8):
            take((c + 8 - t) % 8, other)
        arrived(wo_at(other), wo_sems.at[other], along_x)
    rows.finish()
    for copy in local:
        copy.wait()
    sends.finish()


def gather_start(x, slabs, wo, collective_id):
    tokens, width = x.shape
    low = BRAIN_FLOAT_TYPE
    dma = pltpu.SemaphoreType.DMA
    return pl.pallas_call(
        gather_start_kernel,
        out_shape=(
            jax.ShapeDtypeStruct((8 * tokens, width), low),
            jax.ShapeDtypeStruct((32,) + slabs.shape[1:], low),
            jax.ShapeDtypeStruct((4 * wo.shape[0], width), low),
        ),
        in_specs=[ANYWHERE] * 3,
        out_specs=[ANYWHERE] * 3,
        scratch_shapes=[dma((4,)), dma((64,)), dma((2, 8)), dma((32,)), dma((4,))],
        compiler_params=pltpu.CompilerParams(collective_id=collective_id, has_side_effects=True),
        name="gather_start",
    )(x, slabs, wo)


def scatter_end_kernel(
    part,
    gw,
    gwo,
    small,
    rows_out,
    gw_out,
    gwo_out,
    small_out,
    *scratch,
):
    row_scratch, row_sems = scratch[:4], scratch[4:8]
    (
        send_sems,
        load_sems,
        core_sems,
        x_sems,
        to_sems,
        small_to_sems,
        gw_own,
        gw_core,
        gw_x,
        gwo_own,
        gwo_core,
        gwo_x,
        small_own,
        small_core,
        small_x,
        small_to,
    ) = scratch[8:]
    at = place()
    z, y, x, k = at
    c, w = z * 2 + y, x * 2 + k
    along_x, along_y = device_at(z, y, 1 - x, k), device_at(z, 1 - y, x, k)
    sibling = device_at(z, y, x, 1 - k)
    others = ring_of(c, w)
    barrier = pltpu.get_barrier_semaphore()
    for device in others + [along_x, sibling]:
        pl.semaphore_signal(barrier, inc=1, device_id=device, device_id_type=MESH)
    pl.semaphore_wait(barrier, 9)
    sends = Sends(send_sems)
    rows = RowScatter(
        part, rows_out, row_scratch, row_sems, sends, at, line_order(z), along_y
    )
    loads = []
    for n, (source, core, own) in enumerate(
        (
            (small, small_core, small_own),
            (gw, gw_core, gw_own),
            (gwo, gwo_core, gwo_own),
        )
    ):
        outer = (slice(None),) * (len(source.shape) - 3)
        sends.start(source.at[(*outer, 1 - k)], core, core_sems.at[n], sibling)
        loads.append(pltpu.make_async_copy(source.at[(*outer, k)], own, load_sems.at[n]))
        loads[-1].start()

    def fold(n, own, core):
        loads[n].wait()
        arrived(core, core_sems.at[n], sibling)
        flat = [(i,) for i in range(own.shape[0])]
        for extent in own.shape[1:-2]:
            flat = [index + (j,) for index in flat for j in range(extent)]
        for i in flat:
            add_blocks(own.at[i], own.at[i], core.at[i])

    fold(0, small_own, small_core)
    sends.start(small_own.at[:, 1 - x], small_x, x_sems.at[0], along_x)
    fold(1, gw_own, gw_core)
    sends.start(gw_own.at[:, 1 - x], gw_x, x_sems.at[1], along_x)
    fold(2, gwo_own, gwo_core)
    keep = []

    def weights(i):
        if i == 2:
            sends.start(gwo_own.at[1 - x], gwo_x, x_sems.at[2], along_x)
            spread()

    def spread():
        for n, own, far in ((0, small_own, small_x), (1, gw_own, gw_x)):
            arrived(far, x_sems.at[n], along_x)
            for i in range(8):
                add_blocks(own.at[i, x], own.at[i, x], far.at[i])
            target, sems = (small_to, small_to_sems) if n == 0 else (gw_out, to_sems)
            keep.append(
                pltpu.make_async_copy(own.at[c, x], target.at[c], load_sems.at[3 + n])
            )
            keep[-1].start()
            for device in others:
                sends.start(own.at[device[0], x], target.at[c], sems.at[c], device)

    rows.run(weights)
    arrived(gwo_x, x_sems.at[2], along_x)
    add_blocks(gwo_out, gwo_own.at[x], gwo_x)
    for copy in keep:
        copy.wait()
    for t in range(1, 8):
        source = (c + 8 - t) % 8
        arrived(small_to.at[source], small_to_sems.at[source], along_x)
        arrived(gw_out.at[source], to_sems.at[source], along_x)
    total = small_to[0]
    for i in range(1, 8):
        total = total + small_to[i]
    small_out[...] = total
    sends.finish()


def scatter_end(part, gw, gwo, small, collective_id):
    rows, width = part.shape[0] // 8, part.shape[1]
    low = part.dtype
    dma, vmem = pltpu.SemaphoreType.DMA, pltpu.VMEM
    r, n = gw.shape[3:]
    ro, no = gwo.shape[2:]
    rs, ns = small.shape[3:]
    return pl.pallas_call(
        scatter_end_kernel,
        out_shape=(
            jax.ShapeDtypeStruct((rows, width), SINGLE_FLOAT),
            jax.ShapeDtypeStruct((8, r, n), low),
            jax.ShapeDtypeStruct((ro, no), SINGLE_FLOAT),
            jax.ShapeDtypeStruct((rs, ns), SINGLE_FLOAT),
        ),
        in_specs=[ANYWHERE] * 4,
        out_specs=[VMEM_WHOLE, ANYWHERE, VMEM_WHOLE, VMEM_WHOLE],
        scratch_shapes=row_scatter_scratch(rows, width, low)
        + [dma((48,)), dma((5,)), dma((3,)), dma((3,)), dma((8,)), dma((8,))]
        + [vmem((8, 2, r, n), low), vmem((8, 2, r, n), low), vmem((8, r, n), low)]
        + [vmem((2, ro, no), low), vmem((2, ro, no), low), vmem((ro, no), low)]
        + [vmem((8, 2, rs, ns), SINGLE_FLOAT), vmem((8, 2, rs, ns), SINGLE_FLOAT)]
        + [vmem((8, rs, ns), SINGLE_FLOAT), vmem((8, rs, ns), SINGLE_FLOAT)],
        compiler_params=pltpu.CompilerParams(
            collective_id=collective_id, has_side_effects=True, vmem_limit_bytes=VMEM_BYTES
        ),
        name="scatter_end",
    )(part, gw, gwo, small)


def forward_gather_kernel(
    slack,
    block_in,
    x_in,
    slabs_in,
    wo_in,
    gain_ref,
    qg_ref,
    kg_ref,
    cos_ref,
    sin_ref,
    segc_ref,
    segr_ref,
    block_out,
    normed_out,
    raw_out,
    q_out,
    k_out,
    v_out,
    attn_out,
    part_out,
    *scratch,
):
    (
        x_ref,
        w_ref,
        wo_ref,
        normed_ref,
        raw_ref,
        q_ref,
        k_ref,
        v_ref,
        attn_ref,
        part_ref,
        in_sems,
        out_sems,
    ) = scratch[:12]
    tokens, width = x_ref.shape
    heads = q_ref.shape[1] // HEAD_DIM
    owned, columns = w_ref.shape[1:]
    rows_step = 256
    copies = [
        pltpu.make_async_copy(s, t, in_sems.at[n])
        for n, (s, t) in enumerate(
            ((x_in, x_ref), (slabs_in.at[:, pl.ds(0, owned), :], w_ref), (wo_in, wo_ref))
        )
    ]
    stores = [
        pltpu.make_async_copy(s, t, out_sems.at[n])
        for n, (s, t) in enumerate(
            (
                (normed_ref, normed_out),
                (raw_ref, raw_out),
                (q_ref, q_out),
                (k_ref, k_out),
                (v_ref, v_out),
                (attn_ref, attn_out),
                (part_ref, part_out),
            )
        )
    ]
    for copy in copies:
        copy.start()
    blocks = BlockGather(block_in, block_out, *scratch[12:])
    blocks.begin()
    copies[0].wait()
    copies[1].wait()

    def project(i, carry):
        rows = pl.ds(pl.multiple_of(i * rows_step, rows_step), rows_step)
        x = x_ref[rows, :].astype(SINGLE_FLOAT)
        inverse = lax.rsqrt(jnp.mean(x * x, axis=-1, keepdims=True) + EPS)
        normed = (x * inverse * gain_ref[...]).astype(BRAIN_FLOAT_TYPE)
        normed_ref[rows, :] = normed
        raw = dot_rows(normed, w_ref[...].reshape(width, columns))
        raw_ref[rows, :] = raw[:, : (heads + 1) * HEAD_DIM]
        v_ref[rows, :] = raw[:, (heads + 1) * HEAD_DIM :].astype(BRAIN_FLOAT_TYPE)
        cosine, sine = cos_ref[rows, :], sin_ref[rows, :]
        for h in range(heads + 1):
            part = raw[:, h * HEAD_DIM : (h + 1) * HEAD_DIM]
            gain = qg_ref[...] if h < heads else kg_ref[...]
            scaled = (
                part * lax.rsqrt(jnp.mean(part * part, axis=-1, keepdims=True) + EPS) * gain
            )
            turned = scaled * cosine + pltpu.roll(scaled, HEAD_DIM // 2, 1) * sine
            turned = turned.astype(BRAIN_FLOAT_TYPE)
            if h < heads:
                q_ref[rows, h * HEAD_DIM : (h + 1) * HEAD_DIM] = turned
            else:
                k_ref[rows, :] = turned
        return carry

    lax.fori_loop(0, tokens // rows_step, project, 0)
    for copy in stores[:5]:
        copy.start()
    blocks.advance(1)
    tile_rows = 128
    for tile in range(tokens // tile_rows):
        first_row = tile * tile_rows
        rows = slice(first_row, first_row + tile_rows)
        low, high = key_range(tile, tile_rows, tokens, slack)
        probs = tile_scores(
            stacked_heads(q_ref, rows, heads),
            k_ref,
            segc_ref,
            segr_ref,
            low,
            high,
            first_row,
            tile_rows,
            heads,
        )
        attended = dot_rows(probs.astype(BRAIN_FLOAT_TYPE), v_ref[low:high, :])
        for h in range(heads):
            attn_ref[rows, h * HEAD_DIM : (h + 1) * HEAD_DIM] = attended[
                h * tile_rows : (h + 1) * tile_rows
            ].astype(BRAIN_FLOAT_TYPE)
    stores[5].start()
    blocks.advance(2)
    copies[2].wait()

    def project_out(i, carry):
        rows = pl.ds(pl.multiple_of(i * rows_step, rows_step), rows_step)
        part_ref[rows, :] = dot_rows(attn_ref[rows, :], wo_ref[...]).astype(BRAIN_FLOAT_TYPE)
        return carry

    lax.fori_loop(0, tokens // rows_step, project_out, 0)
    stores[6].start()
    blocks.advance(3)
    blocks.finish()
    for copy in stores:
        copy.wait()


def forward_gather(slack, block, x, slabs, wo, gain, qg, kg, cosine, sine, segc, segr, collective_id):
    tokens, width = x.shape
    columns = slabs.shape[2]
    owned = width // slabs.shape[0]
    channels = columns - 2 * HEAD_DIM
    low = BRAIN_FLOAT_TYPE
    shape, vmem, dma = jax.ShapeDtypeStruct, pltpu.VMEM, pltpu.SemaphoreType.DMA
    sizes = (
        ((tokens, width), low),
        ((tokens, channels + HEAD_DIM), SINGLE_FLOAT),
        ((tokens, channels), low),
        ((tokens, HEAD_DIM), low),
        ((tokens, HEAD_DIM), low),
        ((tokens, channels), low),
        ((tokens, width), low),
    )

    def kernel(*refs):
        forward_gather_kernel(slack, *refs)

    return pl.pallas_call(
        kernel,
        out_shape=[shape((32,) + block.shape, low)] + [shape(*size) for size in sizes],
        in_specs=[ANYWHERE] * 4 + [VMEM_WHOLE] * 7,
        out_specs=[ANYWHERE] * 8,
        scratch_shapes=[
            vmem((tokens, width), low),
            vmem((slabs.shape[0], owned, columns), low),
            vmem(wo.shape, low),
        ]
        + [vmem(*size) for size in sizes]
        + [dma((3,)), dma((7,))]
        + [dma, dma((40,)), dma((32,))],
        compiler_params=pltpu.CompilerParams(
            collective_id=collective_id, has_side_effects=True, vmem_limit_bytes=VMEM_BYTES
        ),
        name="forward_gather",
    )(block, x, slabs, wo, gain, qg, kg, cosine, sine, segc, segr)


GROUPS = 8


def order_at(z, i):
    upper = z // 2
    inner = (z % 2) * (1 - upper) + (1 - z % 2) * upper
    along = i * (1 - inner) + inner * ((i + 1) % 3 + 2 * (i // 3))
    return 3 * upper + (1 - 2 * upper) * along


def group_blocks(g):
    later = ((g + 1) // 4) * (1 - g // 7)
    g = g * (1 - later) + later * (3 + g % 4)
    kind, turn = (g + 2) // 4, (g + 2) % 4
    far, side, near = 1 - (kind + 1) // 2, kind % 2, kind // 2
    return (
        (far * (turn - 2) + side * (3 - turn) + near * (3 - 2 * turn), 3 - 2 * kind + near),
        (far * turn + side * (3 - turn) + near * (2 - 2 * turn), 3 - kind - near),
    )


def spread_rows(target, pick, rows, *terms):
    step = 4 * HEAD_DIM
    width = target.shape[1]
    at = jnp.transpose(pick[...].astype(SINGLE_FLOAT)).astype(BRAIN_FLOAT_TYPE)
    for start in range(0, width, step):
        part = slice(start, min(start + step, width))
        total = dot_rows(at, rows[:, part])
        for term in terms:
            total = total + term[:, part].astype(SINGLE_FLOAT)
        target[:, part] = total.astype(target.dtype)


def blocks_at(at, g):
    z, y, x, k = at
    found = []
    for lane in (k, 1 - k):
        for i, r in group_blocks(g):
            dy, dx = r // 2, r % 2
            slot = slot_of(order_at(z, i), y + dy * (1 - 2 * y), x + dx * (1 - 2 * x), lane)
            found.append((slot, i * 4 + r))
    return found


def rank_mask(experts, e, extra):
    lane = lax.broadcasted_iota(jnp.int32, (8, extra), 1)
    return (lane == 2 * experts + e).astype(BRAIN_FLOAT_TYPE)


def picked(mask, pay, width, capacity):
    rank = dot_right_transposed(mask, pay[:, width:])
    slots = lax.broadcasted_iota(jnp.int32, (capacity, pay.shape[0]), 0).astype(SINGLE_FLOAT)
    return (rank[0:1, :] == slots).astype(BRAIN_FLOAT_TYPE)


def early_step(n):
    late = n // 3
    return (1 - late) * (7 - n) + late * (3 + (n + 1) % 2 - n // 5)


def gather_forward_kernel(
    capacity,
    payload_in,
    dout_all,
    wg_in,
    wu_in,
    wd_in,
    pay_all,
    x_out,
    d_out,
    extra_out,
    gh_out,
    uh_out,
    hid_out,
    eo_out,
    pick_out,
    wg_ref,
    wu_ref,
    wd_ref,
    pay_ref,
    dout_ref,
    x_ref,
    d_ref,
    extra_ref,
    gh_ref,
    uh_ref,
    hid_ref,
    eo_ref,
    pick_ref,
    weight_sems,
    load_sems,
    store_sems,
    local_sem,
    send_sems,
    recv_sems,
):
    blocks = BlockGather(payload_in, pay_all, local_sem, send_sems, recv_sems)
    blocks.begin()
    weights = [
        pltpu.make_async_copy(a, b, weight_sems.at[n])
        for n, (a, b) in enumerate(((wg_in, wg_ref), (wu_in, wu_ref), (wd_in, wd_ref)))
    ]
    for copy in weights:
        copy.start()
    width = wg_in.shape[0]
    tokens, payload = payload_in.shape
    experts = (payload - width) // 4
    rows = 4 * capacity
    mask = rank_mask(experts, blocks.mine, payload - width)

    def stores(n):
        g = early_step(n) - 2
        part = pl.ds(pl.multiple_of(g * rows, rows), rows)
        pairs = (
            (x_ref, x_out), (d_ref, d_out), (extra_ref, extra_out), (gh_ref, gh_out),
            (uh_ref, uh_out), (hid_ref, hid_out), (eo_ref, eo_out),
        )
        return [
            pltpu.make_async_copy(a, b.at[part, :], store_sems.at[m])
            for m, (a, b) in enumerate(pairs)
        ] + [pltpu.make_async_copy(pick_ref, pick_out.at[g], store_sems.at[7])]

    def group(n, carry):
        found = blocks_at(blocks.at, early_step(n))
        for slot, _ in found[2:]:
            blocks.wait(slot)
        loads = [
            (
                pltpu.make_async_copy(pay_all.at[slot], pay_ref.at[m], load_sems.at[m]),
                pltpu.make_async_copy(dout_all.at[slot], dout_ref.at[m], load_sems.at[4 + m]),
            )
            for m, (slot, _) in enumerate(found)
        ]
        for pair in loads:
            for copy in pair:
                copy.start()

        @pl.when(n > 0)
        def _():
            for copy in stores(n - 1):
                copy.wait()

        for m in range(4):
            for copy in loads[m]:
                copy.wait()
            part = slice(m * capacity, (m + 1) * capacity)
            pick = picked(mask, pay_ref.at[m], width, capacity)
            pick_ref[m] = pick
            chosen = dot_rows(pick, pay_ref[m]).astype(BRAIN_FLOAT_TYPE)
            x_ref[part, :] = chosen[:, :width]
            extra_ref[part, :] = chosen[:, width:]
            d_ref[part, :] = dot_rows(pick, dout_ref[m]).astype(BRAIN_FLOAT_TYPE)
        forward_rows(x_ref, wg_ref, wu_ref, wd_ref, gh_ref, uh_ref, hid_ref, eo_ref)
        for copy in stores(n):
            copy.start()
        return carry

    blocks.advance(1)
    blocks.own.wait()
    for copy in weights:
        copy.wait()
    lax.fori_loop(0, 1, group, 0)
    blocks.advance(2)
    lax.fori_loop(1, 2, group, 0)
    blocks.advance(3)
    lax.fori_loop(2, 3, group, 0)
    blocks.turn()
    lax.fori_loop(3, GROUPS - 2, group, 0)
    blocks.last(((0, 0), (0, 1), (1, 0)))
    for copy in stores(5):
        copy.wait()


def forward_rows(x_ref, wg_ref, wu_ref, wd_ref, gh_ref, uh_ref, hid_ref, eo_ref):
    x = x_ref[...]
    gate_hidden = dot_rows(x, wg_ref[...])
    up_hidden = dot_rows(x, wu_ref[...])
    gh_ref[...] = gate_hidden
    uh_ref[...] = up_hidden
    sigmoid = 1.0 / (1.0 + jnp.exp(-gate_hidden))
    hidden = (gate_hidden * sigmoid * up_hidden).astype(BRAIN_FLOAT_TYPE)
    hid_ref[...] = hidden
    eo_ref[...] = dot_rows(hidden, wd_ref[...]).astype(BRAIN_FLOAT_TYPE)


def gather_forward(capacity, payload, dout_all, wg, wu, wd, collective_id):
    tokens, wide = payload.shape
    width, ff = wg.shape
    low = BRAIN_FLOAT_TYPE
    rows = 4 * capacity
    early = (GROUPS - 2) * rows
    shape, vmem, dma = jax.ShapeDtypeStruct, pltpu.VMEM, pltpu.SemaphoreType.DMA
    extra = wide - width
    sizes = (
        (width, low), (width, low), (extra, low), (ff, SINGLE_FLOAT), (ff, SINGLE_FLOAT),
        (ff, low), (width, low),
    )

    def kernel(*refs):
        gather_forward_kernel(capacity, *refs)

    return pl.pallas_call(
        kernel,
        out_shape=[shape((32, tokens, wide), low)]
        + [shape((early, n), dtype) for n, dtype in sizes]
        + [shape((GROUPS - 2, 4, capacity, tokens), low)],
        in_specs=[ANYWHERE] * 5,
        out_specs=[ANYWHERE] * 9,
        scratch_shapes=[vmem((width, ff), low), vmem((width, ff), low), vmem((ff, width), low)]
        + [vmem((4, tokens, wide), low), vmem((4, tokens, width), low)]
        + [vmem((rows, n), dtype) for n, dtype in sizes]
        + [vmem((4, capacity, tokens), low)]
        + [dma((3,)), dma((8,)), dma((8,)), dma, dma((40,)), dma((32,))],
        compiler_params=pltpu.CompilerParams(
            collective_id=collective_id, has_side_effects=True, vmem_limit_bytes=VMEM_BYTES
        ),
        name="gather_forward",
    )(payload, dout_all, wg, wu, wd)


def expert_exchange_kernel(
    capacity,
    pay_all,
    dout_all,
    wg_in,
    wu_in,
    wd_in,
    d_early,
    extra_early,
    gh_early,
    uh_early,
    eo_early,
    pick_early,
    back_ref,
    rows_out,
    pick_out,
    x_out,
    hid_out,
    deo_out,
    dgl_out,
    dul_out,
    wg_ref,
    wu_ref,
    wd_ref,
    pay_ref,
    dout_ref,
    x_ref,
    hid_ref,
    deo_ref,
    dgl_ref,
    dul_ref,
    d_ref,
    extra_ref,
    gh_ref,
    uh_ref,
    eo_ref,
    far_pick_ref,
    far_d_ref,
    far_o_ref,
    near_o_ref,
    pick_ref,
    rows_ref,
    own_ref,
    corner_ref,
    x_sum_ref,
    y_sum_ref,
    up_ref,
    down_ref,
    weight_sems,
    load_sems,
    early_sems,
    row_sems,
    near_sems,
    far_sems,
    sibling_sems,
    corner_sems,
    x_sums,
    y_sums,
    up_sems,
    down_sems,
    sum_send_sems,
    pick_sem,
):
    z, y, x, k = place()
    order = line_order(z)
    along_x, along_y = device_at(z, y, 1 - x, k), device_at(z, 1 - y, x, k)
    sibling = device_at(z, y, x, 1 - k)
    weights = [
        pltpu.make_async_copy(a, b, weight_sems.at[n])
        for n, (a, b) in enumerate(((wg_in, wg_ref), (wu_in, wu_ref), (wd_in, wd_ref)))
    ]
    for copy in weights:
        copy.start()
    meet(z, y, x, k, (along_x, along_y, sibling))
    mine = slot_of(z, y, x, k)
    width = wg_in.shape[0]
    _, tokens, payload = pay_all.shape
    experts = (payload - width) // 4
    rows = 4 * capacity
    above, below = device_at(z + 1, y, x, k), device_at(z - 1, y, x, k)

    def far_copies(n, j, side):
        half = pl.ds(capacity, capacity)
        return [
            remote(a, b, far_sems.at[n, m], sibling_sems.at[m, j], sibling)
            for m, (a, b) in enumerate(
                (
                    (far_pick_ref.at[side, n], pick_ref.at[j, half, :]),
                    (far_d_ref.at[n], rows_ref.at[j, half, :]),
                    (far_o_ref.at[n], rows_out.at[j, half, :]),
                )
            )
        ]

    def gather(i, r, *extra):
        j = i * 4 + r
        for copy in far_copies(0, j, 0)[:2]:
            copy.wait_recv()
        spread_rows(own_ref.at[j], pick_ref.at[j], rows_ref.at[j], *extra)
        return own_ref.at[j]

    def sum_send(n, j, target, recv, device):
        return remote(own_ref.at[j], target, sum_send_sems.at[n], recv, device)

    corner_sends = [
        sum_send(i, i * 4 + 3, corner_ref.at[i], corner_sems.at[i], along_y if i < 2 else along_x)
        for i in range(4)
    ]
    x_sends = [
        sum_send(4 + i, i * 4 + 1, x_sum_ref.at[i], x_sums.at[i], along_x) for i in range(4)
    ]
    y_sends = [
        sum_send(8 + i, i * 4 + 2, y_sum_ref.at[i], y_sums.at[i], along_y) for i in range(4)
    ]
    line_sends = []
    for i in (1, 2, 3):
        chip = order[i]
        upward = chip > z
        line_sends.append(
            (upward, sum_send(12 + i, i * 4, up_ref.at[chip], up_sems.at[chip], above))
        )
        line_sends.append(
            (
                jnp.logical_not(upward),
                sum_send(16 + i, i * 4, down_ref.at[chip], down_sems.at[chip], below),
            )
        )

    def corners(*which):
        for i in which:
            gather(i, 3)
            corner_sends[i].start()

    def cross(i):
        arrived(corner_ref.at[i], corner_sems.at[i], along_x)
        extra = (corner_ref.at[i],)
        gather(i, 1, *(extra if i < 2 else ()))
        x_sends[i].start()
        gather(i, 2, *(extra if i >= 2 else ()))
        y_sends[i].start()

    def total(i):
        arrived(x_sum_ref.at[i], x_sums.at[i], along_x)
        arrived(y_sum_ref.at[i], y_sums.at[i], along_y)
        gather(i, 0, x_sum_ref.at[i], y_sum_ref.at[i])

    def along(i):
        total(i)
        chip, block = order[i], own_ref.at[i * 4]
        upward = chip > z

        @pl.when(upward & (z > 0))
        def _():
            arrived(up_ref.at[chip], up_sems.at[chip], below)
            add_blocks(block, block, up_ref.at[chip])

        @pl.when(jnp.logical_not(upward) & (z < LINE - 1))
        def _():
            arrived(down_ref.at[chip], down_sems.at[chip], above)
            add_blocks(block, block, down_ref.at[chip])

        for condition, copy in line_sends[2 * i - 2 : 2 * i]:
            pl.when(condition)(copy.start)

    def sixth():
        cross(1)
        along(3)

    def last():
        cross(0)
        along(2)

    at_start = {4: lambda: cross(3), 5: lambda: cross(2), 6: sixth, 7: last}
    at_middle = {1: lambda: corners(2, 0), 2: lambda: corners(3, 1)}

    def at(g, table):
        for n, work in table.items():
            pl.when(g == n)(work)

    for copy in weights:
        copy.wait()
    row_lane = lax.broadcasted_iota(jnp.int32, (capacity, payload - width), 1)
    e = mine
    all_lane = lax.broadcasted_iota(jnp.int32, (rows, payload - width), 1)
    is_gate = (all_lane == e) | (all_lane == experts + e)
    mask = rank_mask(experts, e, payload - width)
    at_here = (z, y, x, k)

    def row_copies(g):
        part = pl.ds(pl.multiple_of(g * rows, rows), rows)
        pairs = ((deo_ref, deo_out), (dgl_ref, dgl_out), (dul_ref, dul_out))
        return [
            pltpu.make_async_copy(a, b.at[part, :], row_sems.at[n])
            for n, (a, b) in enumerate(pairs)
        ]

    def late_copies(g):
        part = pl.ds(pl.multiple_of(g * rows, rows), rows)
        return [
            pltpu.make_async_copy(a, b.at[part, :], row_sems.at[3 + n])
            for n, (a, b) in enumerate(((x_ref, x_out), (hid_ref, hid_out)))
        ]

    def near_copies(g):
        return [
            pltpu.make_async_copy(
                near_o_ref.at[n],
                rows_out.at[blocks_at(at_here, g)[n][1], pl.ds(0, capacity), :],
                near_sems.at[n],
            )
            for n in (0, 1)
        ]

    def settle(g):
        for copy in row_copies(g) + near_copies(g):
            copy.wait()
        for n in (0, 1):
            for copy in far_copies(n, blocks_at(at_here, g)[2 + n][1], g % 2):
                copy.wait_send()

    def load_copies(g):
        copies = []
        for n, (slot, _) in enumerate(blocks_at(at_here, g)):
            copies.append(pltpu.make_async_copy(pay_all.at[slot], pay_ref.at[n], load_sems.at[n]))
            copies.append(
                pltpu.make_async_copy(dout_all.at[slot], dout_ref.at[n], load_sems.at[4 + n])
            )
        return copies

    def early_copies(g):
        side, at = g % 2, g - 2
        part = pl.ds(pl.multiple_of(at * rows, rows), rows)
        pairs = (
            (d_early, d_ref), (extra_early, extra_ref), (gh_early, gh_ref), (uh_early, uh_ref),
            (eo_early, eo_ref),
        )
        copies = [
            pltpu.make_async_copy(a.at[part, :], b.at[side], early_sems.at[side, n])
            for n, (a, b) in enumerate(pairs)
        ]
        for n, (_, j) in enumerate(blocks_at(at_here, g)):
            target = pick_ref.at[j, pl.ds(0, capacity), :] if n < 2 else far_pick_ref.at[side, n - 2]
            copies.append(
                pltpu.make_async_copy(pick_early.at[at, n], target, early_sems.at[side, 5 + n])
            )
        return copies

    def step(g, carry):
        blocks = blocks_at(at_here, g)
        side = g % 2
        at(g, at_start)

        @pl.when(g > 0)
        def _():
            settle(g - 1)

        @pl.when((g > 0) & (g < GROUPS - 1))
        def _():
            for copy in early_copies(g + 1):
                copy.start()

        @pl.when(g < 2)
        def _():
            @pl.when(g == 1)
            def _():
                for copy in late_copies(g - 1):
                    copy.wait()

            for copy in load_copies(g):
                copy.wait()
            for n in range(4):
                part = slice(n * capacity, (n + 1) * capacity)
                pick = picked(mask, pay_ref.at[n], width, capacity)
                if n < 2:
                    pick_ref[blocks[n][1], 0:capacity, :] = pick
                else:
                    far_pick_ref[side, n - 2] = pick
                chosen = dot_rows(pick, pay_ref[n]).astype(BRAIN_FLOAT_TYPE)
                x_ref[part, :] = chosen[:, :width]
                extra_ref[side, part, :] = chosen[:, width:]
                d_ref[side, part, :] = dot_rows(pick, dout_ref[n]).astype(BRAIN_FLOAT_TYPE)

            @pl.when(g == 0)
            def _():
                for copy in load_copies(g + 1):
                    copy.start()

            forward_rows(
                x_ref, wg_ref, wu_ref, wd_ref, gh_ref.at[side], uh_ref.at[side], hid_ref,
                eo_ref.at[side],
            )
            for copy in late_copies(g):
                copy.start()

        @pl.when(g >= 2)
        def _():
            for copy in early_copies(g):
                copy.wait()

        at(g, at_middle)
        gates = jnp.sum(
            jnp.where(is_gate, extra_ref[side].astype(SINGLE_FLOAT), 0.0), axis=-1, keepdims=True
        )
        deo_ref[...] = (gates * d_ref[side].astype(SINGLE_FLOAT)).astype(BRAIN_FLOAT_TYPE)
        gate_hidden, up_hidden = gh_ref[side], uh_ref[side]
        sigmoid = 1.0 / (1.0 + jnp.exp(-gate_hidden))
        silu = gate_hidden * sigmoid
        d_hidden = dot_right_transposed(deo_ref[...], wd_ref[...])
        d_gate = (d_hidden * up_hidden * sigmoid * (1.0 + gate_hidden * (1.0 - sigmoid))).astype(
            BRAIN_FLOAT_TYPE
        )
        d_up = (d_hidden * silu).astype(BRAIN_FLOAT_TYPE)
        dgl_ref[...] = d_gate
        dul_ref[...] = d_up
        for copy in row_copies(g):
            copy.start()
        d_copy = (
            dot_right_transposed(d_gate, wg_ref[...]) + dot_right_transposed(d_up, wu_ref[...])
        ).astype(BRAIN_FLOAT_TYPE)
        for n in (2, 3, 0, 1):
            j = blocks[n][1]
            part = slice(n * capacity, (n + 1) * capacity)
            e_rows = eo_ref[side, part, :].astype(SINGLE_FLOAT)
            d_gate_rows = jnp.sum(
                d_ref[side, part, :].astype(SINGLE_FLOAT) * e_rows, axis=-1, keepdims=True
            )
            high = d_gate_rows.astype(BRAIN_FLOAT_TYPE).astype(SINGLE_FLOAT)
            extra = jnp.where(row_lane == e, high, 0.0) + jnp.where(
                row_lane == experts + e, d_gate_rows - high, 0.0
            )
            if n >= 2:
                d_target, o_target = far_d_ref.at[n - 2], far_o_ref.at[n - 2]
            else:
                d_target, o_target = rows_ref.at[j, pl.ds(0, capacity), :], near_o_ref.at[n]
            d_target[:, :width] = d_copy[part]
            d_target[:, width:] = extra.astype(BRAIN_FLOAT_TYPE)
            o_target[...] = (gates[part] * e_rows).astype(BRAIN_FLOAT_TYPE)
            if n >= 2:
                for copy in far_copies(n - 2, j, side):
                    copy.start()
        for copy in near_copies(g):
            copy.start()
        return carry

    for copy in load_copies(0):
        copy.start()
    lax.fori_loop(0, GROUPS, step, 0)
    along(1)
    total(0)
    block = own_ref.at[0]

    @pl.when(z > 0)
    def _():
        arrived(up_ref.at[z], up_sems.at[z], below)

    @pl.when(z < LINE - 1)
    def _():
        arrived(down_ref.at[z], down_sems.at[z], above)

    @pl.when(z == 0)
    def _():
        add_blocks(back_ref, block, down_ref.at[z])

    @pl.when(z == LINE - 1)
    def _():
        add_blocks(back_ref, block, up_ref.at[z])

    @pl.when((z > 0) & (z < LINE - 1))
    def _():
        add_blocks(back_ref, block, up_ref.at[z], down_ref.at[z])

    settle(GROUPS - 1)
    for copy in late_copies(1):
        copy.wait()
    keep = pltpu.make_async_copy(pick_ref, pick_out, pick_sem)
    keep.start()
    for j in range(16):
        far_copies(0, j, 0)[2].wait_recv()
    keep.wait()
    for copy in corner_sends + x_sends + y_sends:
        copy.wait_send()
    for condition, copy in line_sends:
        pl.when(condition)(copy.wait_send)


def expert_exchange(capacity, pay_all, dout_all, wg, wu, wd, early, collective_id):
    _, tokens, wide = pay_all.shape
    width, ff = wg.shape
    low = BRAIN_FLOAT_TYPE
    rows = 4 * capacity
    total = GROUPS * rows
    dma, vmem = pltpu.SemaphoreType.DMA, pltpu.VMEM

    def kernel(*refs):
        expert_exchange_kernel(capacity, *refs)

    shape = jax.ShapeDtypeStruct
    return pl.pallas_call(
        kernel,
        out_shape=(
            shape((tokens, wide), SINGLE_FLOAT),
            shape((16, 2 * capacity, width), low),
            shape((16, 2 * capacity, tokens), low),
            shape((2 * rows, width), low),
            shape((2 * rows, ff), low),
            shape((total, width), low),
            shape((total, ff), low),
            shape((total, ff), low),
        ),
        in_specs=[ANYWHERE] * 11,
        out_specs=[VMEM_WHOLE] + [ANYWHERE] * 7,
        scratch_shapes=[vmem((width, ff), low), vmem((width, ff), low), vmem((ff, width), low)]
        + [vmem((4, tokens, wide), low), vmem((4, tokens, width), low)]
        + [vmem((rows, n), low) for n in (width, ff, width, ff, ff)]
        + [vmem((2, rows, width), low), vmem((2, rows, wide - width), low)]
        + [vmem((2, rows, ff), SINGLE_FLOAT)] * 2
        + [vmem((2, rows, width), low), vmem((2, 2, capacity, tokens), low)]
        + [vmem((2, capacity, n), low) for n in (wide, width, width)]
        + [vmem((16, 2 * capacity, tokens), low), vmem((16, 2 * capacity, wide), low)]
        + [vmem((n, tokens, wide), low) for n in (16, 4, 4, 4, 4, 4)]
        + [dma((3,)), dma((8,)), dma((2, 9)), dma((5,)), dma((2,)), dma((2, 3))]
        + [dma((3, 16)), dma((4,)), dma((4,)), dma((4,)), dma((4,)), dma((4,)), dma((20,)), dma],
        compiler_params=pltpu.CompilerParams(
            collective_id=collective_id, has_side_effects=True, vmem_limit_bytes=VMEM_BYTES
        ),
        name="expert_exchange",
    )(pay_all, dout_all, wg, wu, wd, *early)


def backward_scatter_kernel(
    slack,
    rows_in,
    pick_in,
    dh_in,
    wo_in,
    attn_in,
    q_in,
    k_in,
    v_in,
    raw_in,
    normed_in,
    x_in,
    w_in,
    qg_ref,
    kg_ref,
    cos_ref,
    sin_ref,
    segc_ref,
    segr_ref,
    out,
    gwo_out,
    gw_out,
    dpart_out,
    ggain_ref,
    gheads_ref,
    *scratch,
):
    (
        dh_ref,
        wo_ref,
        attn_ref,
        q_ref,
        k_ref,
        v_ref,
        raw_ref,
        normed_ref,
        w_ref,
        x_ref,
        gwo_ref,
        gw_ref,
        da_ref,
        draw_ref,
        dk_ref,
        dv_ref,
        in_sems,
        x_load_sems,
        gwo_sems,
        gw_sems,
        dpart_sems,
    ) = scratch[:21]
    exchange = PickedSums(rows_in, pick_in, out, scratch[21:])
    owned, columns = w_ref.shape[1:]
    w_rows = w_in.at[:, pl.ds(0, owned), :]
    inputs = (dh_in, wo_in, attn_in, q_in, k_in, v_in, raw_in, normed_in, w_rows)
    held = (dh_ref, wo_ref, attn_ref, q_ref, k_ref, v_ref, raw_ref, normed_ref, w_ref)
    copies = [pltpu.make_async_copy(s, t, in_sems.at[n]) for n, (s, t) in enumerate(zip(inputs, held))]
    tokens = dh_ref.shape[0]
    heads = q_ref.shape[1] // HEAD_DIM
    scale = HEAD_DIM ** (-0.5)
    rows_step = 256
    row_steps = tokens // rows_step

    def x_load(i):
        rows = pl.ds(pl.multiple_of(i * rows_step, rows_step), rows_step)
        return pltpu.make_async_copy(x_in.at[rows, :], x_ref.at[i % 2], x_load_sems.at[i % 2])

    def dpart_store(i):
        rows = pl.ds(pl.multiple_of(i * rows_step, rows_step), rows_step)
        return pltpu.make_async_copy(dh_ref.at[rows, :], dpart_out.at[rows, :], dpart_sems.at[i])

    def gwo_store(i):
        columns = pl.ds(pl.multiple_of(i * 512, 512), 512)
        return pltpu.make_async_copy(
            gwo_ref.at[i % 2], gwo_out.at[:, columns], gwo_sems.at[i % 2]
        )

    def gw_store(i):
        part = pl.ds(pl.multiple_of(i * 256, 256), 256)
        return pltpu.make_async_copy(gw_ref.at[i % 2], gw_out.at[part, :], gw_sems.at[i % 2])

    def attended_gradient():
        def body(i, carry):
            rows = pl.ds(pl.multiple_of(i * rows_step, rows_step), rows_step)
            da_ref[rows, :] = dot_right_transposed(dh_ref[rows, :], wo_ref[...]).astype(
                BRAIN_FLOAT_TYPE
            )
            return carry

        for copy in copies[:2]:
            copy.wait()
        lax.fori_loop(0, row_steps, body, 0)

    def out_weight():
        copies[2].wait()
        for i in range(dh_ref.shape[1] // 512):
            if i >= 2:
                gwo_store(i - 2).wait()
            gwo_ref[i % 2] = dot_left_transposed(
                attn_ref[...], dh_ref[:, i * 512 : (i + 1) * 512]
            ).astype(gwo_ref.dtype)
            gwo_store(i).start()

    tile_rows = 128
    gains = []

    def tiles(first, last):
        for tile in range(first, last):
            first_row = tile * tile_rows
            rows = slice(first_row, first_row + tile_rows)
            low, high = key_range(tile, tile_rows, tokens, slack)
            q4 = stacked_heads(q_ref, rows, heads)
            da4 = stacked_heads(da_ref, rows, heads)
            probs = tile_scores(
                q4, k_ref, segc_ref, segr_ref, low, high, first_row, tile_rows, heads
            )
            d_probs = dot_right_transposed(da4, v_ref[low:high, :])
            delta = jnp.sum(probs * d_probs, axis=-1, keepdims=True)
            d_scores = (probs * (d_probs - delta)).astype(BRAIN_FLOAT_TYPE)
            dq4 = dot_rows(d_scores, k_ref[low:high, :]) * scale
            dk_ref[low:high, :] += dot_left_transposed(d_scores, q4)
            dv_ref[low:high, :] += dot_left_transposed(probs.astype(BRAIN_FLOAT_TYPE), da4)
            for h in range(heads):
                columns = slice(h * HEAD_DIM, (h + 1) * HEAD_DIM)
                raw_gradient, gain_gradient = head_backward(
                    dq4[h * tile_rows : (h + 1) * tile_rows],
                    raw_ref[rows, columns],
                    qg_ref[...],
                    cos_ref[rows, :],
                    sin_ref[rows, :],
                )
                draw_ref[rows, columns] = raw_gradient.astype(BRAIN_FLOAT_TYPE)
                gains.append(gain_gradient)

    def keys():
        columns = slice(heads * HEAD_DIM, (heads + 1) * HEAD_DIM)
        raw_gradient, key_gain_gradient = head_backward(
            dk_ref[...] * scale, raw_ref[:, columns], kg_ref[...], cos_ref[...], sin_ref[...]
        )
        draw_ref[:, columns] = raw_gradient.astype(BRAIN_FLOAT_TYPE)
        draw_ref[:, (heads + 1) * HEAD_DIM :] = dv_ref[...].astype(BRAIN_FLOAT_TYPE)
        query_gain_gradient = gains[0]
        for gain in gains[1:]:
            query_gain_gradient = query_gain_gradient + gain
        gheads_ref[...] = jnp.concatenate(
            [query_gain_gradient, key_gain_gradient, jnp.zeros((6, HEAD_DIM), SINGLE_FLOAT)],
            axis=0,
        )

    def projection_weight():
        copies[7].wait()
        count = normed_ref.shape[1] // 256
        for i in range(count):
            if i >= 2:
                gw_store(i - 2).wait()
            gw_ref[i % 2] = dot_left_transposed(
                normed_ref[:, i * 256 : (i + 1) * 256], draw_ref[...]
            ).astype(gw_ref.dtype)
            gw_store(i).start()

    def input_gradient():
        copies[8].wait()
        ggain_ref[...] = jnp.zeros_like(ggain_ref)
        for i in range(row_steps):
            x_load(i).wait()
            rows = slice(i * rows_step, (i + 1) * rows_step)
            d_normed = dot_right_transposed(
                draw_ref[rows, :], w_ref[...].reshape(normed_ref.shape[1], columns)
            )
            dh_ref[rows, :] = d_normed.astype(BRAIN_FLOAT_TYPE)
            dpart_store(i).start()
            x = x_ref[i % 2].astype(SINGLE_FLOAT)
            inverse = lax.rsqrt(jnp.mean(x * x, axis=-1, keepdims=True) + EPS)
            ggain_ref[...] += jnp.sum(d_normed * (x * inverse), axis=0, keepdims=True)
            if i + 2 < row_steps:
                x_load(i + 2).start()

    exchange.begin()
    for copy in copies:
        copy.start()
    x_load(0).start()
    x_load(1).start()
    dk_ref[...] = jnp.zeros_like(dk_ref)
    dv_ref[...] = jnp.zeros_like(dv_ref)
    exchange.corners()
    attended_gradient()
    out_weight()
    for copy in copies[3:7]:
        copy.wait()
    tiles(0, 5)
    exchange.cross(3)
    tiles(5, 8)
    keys()

    def between(i):
        if i == 3:
            projection_weight()
        elif i == 2:
            input_gradient()

    exchange.finish(between)
    for i in (2, 3):
        gwo_store(i).wait()
    for i in (6, 7):
        gw_store(i).wait()
    for i in range(row_steps):
        dpart_store(i).wait()


def backward_scatter(
    slack, rows, pick, dh, wo, attn, q, k, v, raw, normed, x, w, qg, kg, cosine, sine, segc, segr,
    collective_id,
):
    tokens, width = x.shape
    channels = q.shape[1]
    columns = channels + 2 * HEAD_DIM
    low = BRAIN_FLOAT_TYPE
    shape, vmem, dma = jax.ShapeDtypeStruct, pltpu.VMEM, pltpu.SemaphoreType.DMA
    shapes = (
        shape((pick.shape[2], width), SINGLE_FLOAT),
        shape((channels, width), low),
        shape((width, columns), low),
        shape((tokens, width), low),
        shape((1, width), SINGLE_FLOAT),
        shape((8, HEAD_DIM), SINGLE_FLOAT),
    )

    def kernel(*refs):
        backward_scatter_kernel(slack, *refs)

    return pl.pallas_call(
        kernel,
        out_shape=shapes,
        in_specs=[ANYWHERE] * 12 + [VMEM_WHOLE] * 6,
        out_specs=[VMEM_WHOLE] + [ANYWHERE] * 3 + [VMEM_WHOLE] * 2,
        scratch_shapes=[
            vmem((tokens, width), low),
            vmem((channels, width), low),
            vmem((tokens, channels), low),
            vmem((tokens, channels), low),
            vmem((tokens, HEAD_DIM), low),
            vmem((tokens, HEAD_DIM), low),
            vmem((tokens, channels + HEAD_DIM), SINGLE_FLOAT),
            vmem((tokens, width), low),
            vmem((w.shape[0], width // w.shape[0], columns), low),
            vmem((2, 256, width), low),
            vmem((2, channels, 512), low),
            vmem((2, 256, columns), low),
            vmem((tokens, channels), low),
            vmem((tokens, columns), low),
            vmem((tokens, HEAD_DIM), SINGLE_FLOAT),
            vmem((tokens, HEAD_DIM), SINGLE_FLOAT),
            dma((9,)),
            dma((2,)),
            dma((2,)),
            dma((2,)),
            dma((4,)),
        ]
        + picked_scratch(rows, pick),
        compiler_params=pltpu.CompilerParams(
            collective_id=collective_id, has_side_effects=True, vmem_limit_bytes=VMEM_BYTES
        ),
        name="backward_scatter",
    )(rows, pick, dh, wo, attn, q, k, v, raw, normed, x, w, qg, kg, cosine, sine, segc, segr)


def natural_order(blocks):
    count, rows, width = blocks.shape
    half = rows // 2
    first = blocks[:, :half].reshape(count * half, width)
    second = blocks[::-1, half:].reshape(count * half, width)
    return jnp.concatenate([first, second], axis=0)


def device_order(rows, count):
    total, width = rows.shape
    half = total // count // 2
    first = rows[: total // 2].reshape(count, half, width)
    second = rows[total // 2 :].reshape(count, half, width)[::-1]
    return jnp.concatenate([first, second], axis=1)


def norm_backward(gradient, values, gain):
    inverse = lax.rsqrt(jnp.mean(values * values, axis=-1, keepdims=True) + EPS)
    unit = values * inverse
    scaled = gradient * gain
    d_values = inverse * (scaled - unit * jnp.mean(unit * scaled, axis=-1, keepdims=True))
    return d_values, jnp.sum(gradient * unit, axis=0)


def tensor_body(
    inputs,
    grad_output,
    routes,
    doc_lengths,
    norm_attn,
    w_query,
    key_projection,
    value_projection,
    query_norm,
    key_norm,
    w_out,
    norm_ffn,
    w_router,
    expert_gate,
    expert_up,
    expert_down,
):
    ctx_count = lax.axis_size("ctx")
    ws_count = lax.axis_size("ws")
    device_count = ctx_count * ws_count
    tokens = inputs.shape[1]
    width = inputs.shape[2]
    sequence_tokens = tokens * ctx_count
    expert_count = w_router.shape[1]
    capacity = tokens * TOPK * 3 // (2 * device_count)
    heads = QUERY_HEADS // ctx_count
    group = QUERY_HEADS // KEY_VALUE_HEADS
    slack = tokens // 2
    ctx_index = lax.axis_index("ctx")
    both = ("ctx", "ws")
    me = ctx_index * ws_count + lax.axis_index("ws")
    small = jnp.concatenate([norm_attn, norm_ffn, query_norm, key_norm, w_router.reshape(-1)])
    columns = (heads + 2) * HEAD_DIM
    small = jnp.pad(small, (0, 16 * columns - small.shape[0])).reshape(16, columns)
    slabs = []
    for c in range(ctx_count):
        kv = c * heads // group
        slab = jnp.concatenate(
            [
                w_query[:, c * heads * HEAD_DIM : (c + 1) * heads * HEAD_DIM],
                key_projection[:, kv * HEAD_DIM : (kv + 1) * HEAD_DIM],
                value_projection[:, kv * HEAD_DIM : (kv + 1) * HEAD_DIM],
            ],
            axis=1,
        )
        slabs.append(jnp.concatenate([slab, small], axis=0))
    owned, few = width // device_count, query_norm.shape[0]
    x_all, slabs, wo_all = gather_start(inputs[0], jnp.stack(slabs), w_out, 1)
    small = slabs[:, owned:].reshape(device_count, 16 * columns)
    attn_gain = small[:, :owned].reshape(width).astype(SINGLE_FLOAT)
    ffn_gain = small[:, owned : 2 * owned].reshape(width).astype(SINGLE_FLOAT)
    at = 2 * owned
    query_gain = small[:, at : at + few].reshape(HEAD_DIM).astype(SINGLE_FLOAT)
    key_gain = small[:, at + few : at + 2 * few].reshape(HEAD_DIM).astype(SINGLE_FLOAT)
    at = at + 2 * few
    router_matrix = small[:, at : at + owned * expert_count].reshape(width, expert_count)

    places = jnp.arange(sequence_tokens, dtype=jnp.int32)
    segments = segment_ids(doc_lengths[0], places)
    half = HEAD_DIM // 2
    frequency = THETA ** (-2.0 * jnp.arange(half, dtype=SINGLE_FLOAT) / HEAD_DIM)
    angle = places.astype(SINGLE_FLOAT)[:, None] * frequency[None, :]
    cosine, sine = jnp.cos(angle), jnp.sin(angle)
    cosine = jnp.concatenate([cosine, cosine], axis=1)
    sine = jnp.concatenate([-sine, sine], axis=1)
    segc, segr = segments[:, None], segments[None, :]
    qg, kg = query_gain[None, :], key_gain[None, :]
    own_places = jnp.arange(tokens, dtype=jnp.int32)
    own_places = jnp.where(
        own_places < tokens // 2,
        ctx_index * (tokens // 2) + own_places,
        (2 * ctx_count - 2 - ctx_index) * (tokens // 2) + own_places,
    )
    own_segments = segment_ids(doc_lengths[0], own_places)
    validity = own_segments < doc_lengths.shape[1]
    d_layer = jnp.where(validity[:, None], grad_output[0], 0.0).astype(BRAIN_FLOAT_TYPE)

    dout_all, normed, raw, q, k, v, attn, part = forward_gather(
        slack, d_layer, x_all, slabs, wo_all, attn_gain[None, :], qg, kg, cosine, sine, segc, segr, 7
    )
    branch = scatter_rows(part, 2)
    layer_in = inputs[0].astype(SINGLE_FLOAT)
    hidden_state = layer_in + branch
    mixed = rms_scale(hidden_state, ffn_gain).astype(BRAIN_FLOAT_TYPE)
    logits = jnp.dot(mixed, router_matrix, preferred_element_type=SINGLE_FLOAT)
    own_routes = routes[0]
    hit = jnp.any(
        own_routes[:, :, None] == jnp.arange(expert_count, dtype=jnp.int32)[None, None, :], axis=1
    )
    masked = jnp.where(hit, logits, MASK_FILL)
    exponent = jnp.exp(masked - jnp.max(masked, axis=-1, keepdims=True))
    gates = exponent / jnp.sum(exponent, axis=-1, keepdims=True)
    hits = hit.astype(BRAIN_FLOAT_TYPE)
    earlier = jnp.tril(jnp.ones((tokens, tokens), BRAIN_FLOAT_TYPE), -1)
    rank = jnp.dot(earlier, hits, preferred_element_type=SINGLE_FLOAT)
    rank = jnp.where(hit, rank, -1.0).astype(BRAIN_FLOAT_TYPE)
    gate_high = gates.astype(BRAIN_FLOAT_TYPE)
    gate_low = (gates - gate_high.astype(SINGLE_FLOAT)).astype(BRAIN_FLOAT_TYPE)
    payload = jnp.concatenate(
        [mixed, gate_high, gate_low, rank, jnp.zeros_like(rank)], axis=1
    )
    experts = (expert_gate[0], expert_up[0], expert_down[0])
    pay_all, x_early, d_early, extra_early, gh_early, uh_early, hid_early, eo_early, pick_early = (
        gather_forward(capacity, payload, dout_all, *experts, 3)
    )
    early = (d_early, extra_early, gh_early, uh_early, eo_early, pick_early)
    d_back, out_rows, out_pick, x_late, hid_late, d_rows, d_gate, d_up = expert_exchange(
        capacity, pay_all, dout_all, *experts, early, 4
    )
    table = d_back[:, width:]
    d_gates = table[:, :expert_count] + table[:, expert_count : 2 * expert_count]
    d_chosen = gates * (d_gates - jnp.sum(gates * d_gates, axis=-1, keepdims=True))
    d_logits = d_chosen.astype(BRAIN_FLOAT_TYPE)
    d_mixed = d_back[:, :width] + dot_right_transposed(
        d_logits, router_matrix
    )
    grad_router = dot_left_transposed(mixed, d_logits)
    d_state_norm, grad_ffn_gain = norm_backward(d_mixed, hidden_state, ffn_gain)
    d_state = d_layer.astype(SINGLE_FLOAT) + d_state_norm
    d_state_low = d_state.astype(BRAIN_FLOAT_TYPE)
    dh_all, grad_gate, grad_up, grad_down = gather_rows(
        d_state_low, (x_late, x_early), d_rows, (hid_late, hid_early), d_gate, d_up, 5
    )
    grad_gate, grad_up, grad_down = (
        grad[None].astype(SINGLE_FLOAT) for grad in (grad_gate, grad_up, grad_down)
    )
    moe_sum, gwo, gw, dpart, ggain, gheads = backward_scatter(
        slack, out_rows, out_pick, dh_all, wo_all, attn, q, k, v, raw, normed, x_all, slabs, qg, kg, cosine, sine, segc, segr, 8
    )
    output = (hidden_state + moe_sum).astype(BRAIN_FLOAT_TYPE)
    blocks = (ctx_count, ws_count // 2, 2)
    small = jnp.concatenate(
        [
            ggain.reshape(device_count, owned),
            grad_ffn_gain.reshape(device_count, owned),
            gheads[0].reshape(device_count, few),
            gheads[1].reshape(device_count, few),
            grad_router.reshape(device_count, owned * expert_count),
        ],
        axis=1,
    )
    small = jnp.pad(small, ((0, 0), (0, 32 * 128 - small.shape[1]))).reshape(*blocks, 32, 128)
    d_normed, gw, grad_wo, small = scatter_end(
        dpart,
        gw.reshape(*blocks, owned, columns),
        gwo.reshape(*blocks[1:], w_out.shape[0], width),
        small,
        6,
    )
    small = small.reshape(-1)
    d_input_norm, _ = norm_backward(d_normed, layer_in, attn_gain)
    grad_input = d_state + d_input_norm
    gw = gw.astype(SINGLE_FLOAT)
    channels = heads * HEAD_DIM
    grad_wq = gw[:, :, :channels].transpose(1, 0, 2).reshape(owned, ctx_count * channels)
    shared = ctx_count // KEY_VALUE_HEADS
    kv = gw[:, :, channels:].reshape(KEY_VALUE_HEADS, shared, owned, 2, HEAD_DIM).sum(1)
    grad_wk = kv[:, :, 0].transpose(1, 0, 2).reshape(owned, KEY_VALUE_HEADS * HEAD_DIM)
    grad_wv = kv[:, :, 1].transpose(1, 0, 2).reshape(owned, KEY_VALUE_HEADS * HEAD_DIM)
    return (
        output[None],
        grad_input[None],
        small[:owned],
        grad_wq,
        grad_wk,
        grad_wv,
        small[2 * owned : at - few],
        small[at - few : at],
        grad_wo,
        small[owned : 2 * owned],
        small[at : at + owned * expert_count].reshape(owned, expert_count),
        grad_gate,
        grad_up,
        grad_down,
    )


def planned_body(mesh):
    if mesh.shape["ctx"] == 8 and mesh.shape["ws"] == 4:
        return tensor_body
    return general_body


def solution(mesh):
    placed = (
        P("ws", "ctx", None),
        P("ws", "ctx", None),
        P("ws", "ctx", None),
        P("ws", None),
        P(("ctx", "ws")),
        P(("ctx", "ws"), None),
        P(("ctx", "ws"), None),
        P(("ctx", "ws"), None),
        P(("ctx", "ws")),
        P(("ctx", "ws")),
        P(("ctx", "ws"), None),
        P(("ctx", "ws")),
        P(("ctx", "ws"), None),
        P(("ctx", "ws"), None, None),
        P(("ctx", "ws"), None, None),
        P(("ctx", "ws"), None, None),
    )
    return jax.shard_map(
        planned_body(mesh),
        mesh=mesh,
        in_specs=placed,
        out_specs=(
            P("ws", "ctx", None),
            P("ws", "ctx", None),
            P(("ctx", "ws")),
            P(("ctx", "ws"), None),
            P(("ctx", "ws"), None),
            P(("ctx", "ws"), None),
            P(("ctx", "ws")),
            P(("ctx", "ws")),
            P(("ctx", "ws"), None),
            P(("ctx", "ws")),
            P(("ctx", "ws"), None),
            P(("ctx", "ws"), None, None),
            P(("ctx", "ws"), None, None),
            P(("ctx", "ws"), None, None),
        ),
        check_vma=False,
    )
```

```python
import jax
import jax.numpy as jnp
from jax import lax
from jax.experimental import pallas as pl
from jax.experimental.pallas import tpu as pltpu
from jax.sharding import PartitionSpec as P

QUERY_HEADS = 32
KEY_VALUE_HEADS = 4
HEAD_DIM = 128
TOPK = 8


EPS = 1e-06
THETA = 1000000.0
MASK_FILL = -1e30
TOP_PRECISION = lax.Precision.HIGHEST
SINGLE_FLOAT = jnp.float32
BRAIN_FLOAT_TYPE = jnp.bfloat16


def rms_scale(values, norm_gain):
    return values * lax.rsqrt(jnp.mean(values * values, axis=-1, keepdims=True) + EPS) * norm_gain


def rotate(values, positions):
    half_dim = values.shape[-1] // 2
    frequency = THETA ** (-2.0 * jnp.arange(half_dim, dtype=jnp.float32) / values.shape[-1])
    angle = positions.astype(jnp.float32)[:, None] * frequency[None, :]
    cosine = jnp.cos(angle)[:, None, :]
    sine_part = jnp.sin(angle)[:, None, :]
    first_half = values[..., :half_dim]
    second_half = values[..., half_dim:]
    return jnp.concatenate(
        [
            first_half * cosine - second_half * sine_part,
            second_half * cosine + first_half * sine_part,
        ],
        axis=-1,
    )


def head_prepare(raw_heads, norm_gain, positions):
    return rotate(rms_scale(raw_heads, norm_gain), positions)


def swiglu(gate_part, up_part):
    return jax.nn.silu(gate_part) * up_part


def stored_positions(row_index, tokens_per_shard, ctx_count):
    device_row = row_index // tokens_per_shard
    within = row_index % tokens_per_shard
    half_block = tokens_per_shard // 2
    block_index = jnp.where(within < half_block, device_row, 2 * ctx_count - 1 - device_row)
    return block_index * half_block + within % half_block


def segment_ids(doc_lengths, positions):
    doc_ends = jnp.cumsum(doc_lengths, dtype=jnp.int32)
    return jnp.sum(
        (positions[:, None] >= doc_ends[None, :]).astype(jnp.int32), axis=1, dtype=jnp.int32
    )


def slot_ranks(flat_routes, expert_count):
    expert_hits = (
        flat_routes[:, None] == jnp.arange(expert_count, dtype=jnp.int32)[None, :]
    ).astype(jnp.int32)
    running = jnp.cumsum(expert_hits, axis=0, dtype=jnp.int32) - 1
    return jnp.sum(expert_hits * running, axis=1, dtype=jnp.int32)


def send_inputs(flat_rows):
    moved = lax.all_to_all(flat_rows, ("ctx", "ws"), split_axis=0, concat_axis=0, tiled=True)
    return moved


def send_outputs(flat_rows):
    moved = lax.all_to_all(flat_rows, ("ctx", "ws"), split_axis=0, concat_axis=0, tiled=True)
    return moved


def send_out_grads(flat_rows):
    moved = lax.all_to_all(flat_rows, ("ctx", "ws"), split_axis=0, concat_axis=0, tiled=True)
    return moved


def send_in_grads(flat_rows):
    moved = lax.all_to_all(flat_rows, ("ctx", "ws"), split_axis=0, concat_axis=0, tiled=True)
    return moved


def flat_rows(grid_sum):
    return grid_sum.reshape((-1,) + grid_sum.shape[3:])


def to_expert_major(arrived, expert_local):
    device_count, row_span, model_width = arrived.shape
    capacity = row_span // expert_local
    shaped = arrived.reshape(device_count, expert_local, capacity, model_width)
    return shaped.transpose(1, 0, 2, 3).reshape(expert_local, device_count * capacity, model_width)


def to_device_major(expert_rows, device_count):
    expert_local, row_span, model_width = expert_rows.shape
    capacity = row_span // device_count
    shaped = expert_rows.reshape(expert_local, device_count, capacity, model_width)
    return shaped.transpose(1, 0, 2, 3).reshape(device_count, expert_local * capacity, model_width)


def general_body(
    inputs,
    grad_output,
    routes,
    doc_lengths,
    norm_attn,
    w_query,
    key_projection,
    value_projection,
    query_norm,
    key_norm,
    w_out,
    norm_ffn,
    w_router,
    expert_gate,
    expert_up,
    expert_down,
):
    ctx_count = lax.axis_size("ctx")
    device_count = ctx_count * lax.axis_size("ws")
    tokens_per_shard = inputs.shape[1]
    model_width = inputs.shape[2]
    sequence_tokens = tokens_per_shard * ctx_count
    expert_count = w_router.shape[1]
    expert_local = expert_gate.shape[0]
    capacity = max(2, tokens_per_shard * TOPK * 3 // (2 * device_count))
    query_group_size = QUERY_HEADS // KEY_VALUE_HEADS
    logit_scale = HEAD_DIM ** (-0.5)
    single_key_block = min(512, sequence_tokens)
    count_of_blocks = sequence_tokens // single_key_block
    ctx_index = lax.axis_index("ctx")
    positions_all = stored_positions(
        jnp.arange(sequence_tokens, dtype=jnp.int32), tokens_per_shard, ctx_count
    )
    segments_all = segment_ids(doc_lengths[0], positions_all)
    local_positions = lax.dynamic_slice_in_dim(
        positions_all, ctx_index * tokens_per_shard, tokens_per_shard
    )
    segments_own = lax.dynamic_slice_in_dim(
        segments_all, ctx_index * tokens_per_shard, tokens_per_shard
    )
    validity = (segments_own < doc_lengths.shape[1]).astype(SINGLE_FLOAT)
    shards = (
        norm_attn,
        w_query,
        key_projection,
        value_projection,
        query_norm,
        key_norm,
        w_out,
        norm_ffn,
        w_router,
    )
    gathered = (
        lax.all_gather(shards[0], ("ctx", "ws"), axis=0, tiled=True),
        lax.all_gather(shards[1], ("ctx", "ws"), axis=0, tiled=True),
        lax.all_gather(shards[2], ("ctx", "ws"), axis=0, tiled=True),
        lax.all_gather(shards[3], ("ctx", "ws"), axis=0, tiled=True),
        lax.all_gather(shards[4], ("ctx", "ws"), axis=0, tiled=True),
        lax.all_gather(shards[5], ("ctx", "ws"), axis=0, tiled=True),
        lax.all_gather(shards[6], ("ctx", "ws"), axis=0, tiled=True),
        lax.all_gather(shards[7], ("ctx", "ws"), axis=0, tiled=True),
        lax.all_gather(shards[8], ("ctx", "ws"), axis=0, tiled=True),
    )
    (
        attn_gain,
        query_matrix,
        key_matrix,
        value_matrix,
        query_gain,
        key_norm_gain,
        output_matrix,
        ffn_gain,
        router_matrix,
    ) = gathered
    attn_gain = attn_gain.astype(SINGLE_FLOAT)
    query_gain = query_gain.astype(SINGLE_FLOAT)
    key_norm_gain = key_norm_gain.astype(SINGLE_FLOAT)
    ffn_gain = ffn_gain.astype(SINGLE_FLOAT)
    layer_in = inputs[0].astype(SINGLE_FLOAT)
    normalized_rows = rms_scale(layer_in, attn_gain).astype(BRAIN_FLOAT_TYPE)
    unnormed_queries = jnp.dot(
        normalized_rows, query_matrix, preferred_element_type=SINGLE_FLOAT
    ).reshape(tokens_per_shard, QUERY_HEADS, HEAD_DIM)
    unnormed_keys = jnp.dot(
        normalized_rows, key_matrix, preferred_element_type=SINGLE_FLOAT
    ).reshape(tokens_per_shard, KEY_VALUE_HEADS, HEAD_DIM)
    value_low = jnp.dot(normalized_rows, value_matrix, preferred_element_type=SINGLE_FLOAT).astype(
        BRAIN_FLOAT_TYPE
    )
    query_rows = head_prepare(unnormed_queries, query_gain, local_positions).astype(
        BRAIN_FLOAT_TYPE
    )
    key_low = (
        head_prepare(unnormed_keys, key_norm_gain, local_positions)
        .astype(BRAIN_FLOAT_TYPE)
        .reshape(tokens_per_shard, KEY_VALUE_HEADS * HEAD_DIM)
    )
    every_key, every_value = (
        lax.all_gather(key_low, "ctx", axis=0, tiled=True),
        lax.all_gather(value_low, "ctx", axis=0, tiled=True),
    )
    grouped_queries = query_rows.reshape(
        tokens_per_shard, KEY_VALUE_HEADS, query_group_size, HEAD_DIM
    )
    blocked_keys = every_key.reshape(count_of_blocks, single_key_block, KEY_VALUE_HEADS, HEAD_DIM)
    blocked_values = every_value.reshape(
        count_of_blocks, single_key_block, KEY_VALUE_HEADS, HEAD_DIM
    )
    position_blocks = positions_all.reshape(count_of_blocks, single_key_block)
    segment_blocks = segments_all.reshape(count_of_blocks, single_key_block)

    def scores_for(block_keys, block_positions, block_segments):
        raw_scores = (
            jnp.einsum(
                "tkgd,jkd->kgtj", grouped_queries, block_keys, preferred_element_type=SINGLE_FLOAT
            )
            * logit_scale
        )
        allowed = (segments_own[:, None] == block_segments[None, :]) & (
            block_positions[None, :] <= local_positions[:, None]
        )
        return (raw_scores, allowed[None, None])

    def stats_step(running, pieces):
        maximum, denominator = running
        block_keys, block_positions, block_segments = pieces
        raw_scores, allowed = scores_for(block_keys, block_positions, block_segments)
        masked = jnp.where(allowed, raw_scores, MASK_FILL)
        new_maximum = jnp.maximum(maximum, jnp.max(masked, axis=-1))
        weights = jnp.where(allowed, jnp.exp(masked - new_maximum[..., None]), 0.0)
        denominator = denominator * jnp.exp(maximum - new_maximum) + jnp.sum(weights, axis=-1)
        return ((new_maximum, denominator), None)

    stats_init = (
        jnp.full((KEY_VALUE_HEADS, query_group_size, tokens_per_shard), MASK_FILL, SINGLE_FLOAT),
        jnp.zeros((KEY_VALUE_HEADS, query_group_size, tokens_per_shard), SINGLE_FLOAT),
    )
    (maximum, denominator), _ = lax.scan(
        stats_step, stats_init, (blocked_keys, position_blocks, segment_blocks)
    )

    def probs_for(raw_scores, allowed):
        return (
            jnp.where(allowed, jnp.exp(raw_scores - maximum[..., None]), 0.0)
            / denominator[..., None]
        )

    def value_update(running, pieces):
        block_keys, block_values, block_positions, block_segments = pieces
        raw_scores, allowed = scores_for(block_keys, block_positions, block_segments)
        softmaxed = probs_for(raw_scores, allowed).astype(BRAIN_FLOAT_TYPE)
        running = running + jnp.einsum(
            "kgtj,jkd->tkgd", softmaxed, block_values, preferred_element_type=SINGLE_FLOAT
        )
        return (running, None)

    inputs_per_block = (blocked_keys, blocked_values, position_blocks, segment_blocks)
    attended, _ = lax.scan(
        value_update,
        jnp.zeros((tokens_per_shard, KEY_VALUE_HEADS, query_group_size, HEAD_DIM), SINGLE_FLOAT),
        inputs_per_block,
    )
    attn_low = attended.reshape(tokens_per_shard, QUERY_HEADS * HEAD_DIM).astype(BRAIN_FLOAT_TYPE)
    hidden_state = layer_in + jnp.dot(attn_low, output_matrix, preferred_element_type=SINGLE_FLOAT)
    combined_rows = rms_scale(hidden_state, ffn_gain).astype(BRAIN_FLOAT_TYPE)
    router_scores = jnp.dot(combined_rows, router_matrix, preferred_element_type=SINGLE_FLOAT)
    own_routes = routes[0]
    route_mask = (
        own_routes[:, :, None] == jnp.arange(expert_count, dtype=jnp.int32)[None, None, :]
    ).astype(SINGLE_FLOAT)
    chosen = jnp.einsum("tke,te->tk", route_mask, router_scores, precision=TOP_PRECISION)
    gate_share = jax.nn.softmax(chosen, axis=-1)
    flat_routes = own_routes.reshape(-1)
    slot_index = flat_routes * capacity + slot_ranks(flat_routes, expert_count)
    entries = tokens_per_shard * TOPK
    source_slot = (
        jnp.full((expert_count * capacity,), entries, jnp.int32)
        .at[slot_index]
        .set(jnp.arange(entries, dtype=jnp.int32))
    )
    padded_in = jnp.concatenate(
        [combined_rows, jnp.zeros((1, model_width), BRAIN_FLOAT_TYPE)], axis=0
    )
    outgoing = padded_in[source_slot // TOPK].reshape(device_count, -1, model_width)
    expert_in = to_expert_major(send_inputs(outgoing), expert_local)
    gate_hidden = jnp.einsum(
        "erd,edf->erf", expert_in, expert_gate, preferred_element_type=SINGLE_FLOAT
    )
    up_hidden = jnp.einsum(
        "erd,edf->erf", expert_in, expert_up, preferred_element_type=SINGLE_FLOAT
    )
    hidden = swiglu(gate_hidden, up_hidden).astype(BRAIN_FLOAT_TYPE)
    expert_out = jnp.einsum(
        "erf,efd->erd", hidden, expert_down, preferred_element_type=SINGLE_FLOAT
    ).astype(BRAIN_FLOAT_TYPE)
    returned = send_outputs(to_device_major(expert_out, device_count)).reshape(
        expert_count * capacity, model_width
    )
    picked = returned[slot_index].reshape(tokens_per_shard, TOPK, model_width)
    moe_sum = jnp.sum(gate_share[:, :, None] * picked.astype(SINGLE_FLOAT), axis=1)
    output = (hidden_state + moe_sum).astype(BRAIN_FLOAT_TYPE)
    d_layer = grad_output[0].astype(SINGLE_FLOAT) * validity[:, None]
    d_gate_share = jnp.sum(d_layer[:, None, :] * picked.astype(SINGLE_FLOAT), axis=-1)
    d_chosen = gate_share * (
        d_gate_share - jnp.sum(gate_share * d_gate_share, axis=-1, keepdims=True)
    )
    d_logits = jnp.einsum("tke,tk->te", route_mask, d_chosen, precision=TOP_PRECISION).astype(
        BRAIN_FLOAT_TYPE
    )
    d_copies = (
        (gate_share[:, :, None] * d_layer[:, None, :])
        .astype(BRAIN_FLOAT_TYPE)
        .reshape(entries, model_width)
    )
    d_padded = jnp.concatenate([d_copies, jnp.zeros((1, model_width), BRAIN_FLOAT_TYPE)], axis=0)
    d_outgoing = d_padded[source_slot].reshape(device_count, -1, model_width)
    d_expert_out = to_expert_major(send_out_grads(d_outgoing), expert_local)
    d_hidden = jnp.einsum(
        "erd,efd->erf", d_expert_out, expert_down, preferred_element_type=SINGLE_FLOAT
    )
    grad_down = jnp.einsum(
        "erf,erd->efd", hidden, d_expert_out, preferred_element_type=SINGLE_FLOAT
    )
    _, swiglu_back = jax.vjp(swiglu, gate_hidden, up_hidden)
    d_gate_hidden, d_up_hidden = swiglu_back(d_hidden)
    d_gate_low = d_gate_hidden.astype(BRAIN_FLOAT_TYPE)
    d_up_low = d_up_hidden.astype(BRAIN_FLOAT_TYPE)
    grad_gate = jnp.einsum(
        "erd,erf->edf", expert_in, d_gate_low, preferred_element_type=SINGLE_FLOAT
    )
    grad_up = jnp.einsum("erd,erf->edf", expert_in, d_up_low, preferred_element_type=SINGLE_FLOAT)
    d_expert_in = jnp.einsum(
        "erf,edf->erd", d_gate_low, expert_gate, preferred_element_type=SINGLE_FLOAT
    )
    d_expert_in = (
        d_expert_in
        + jnp.einsum("erf,edf->erd", d_up_low, expert_up, preferred_element_type=SINGLE_FLOAT)
    ).astype(BRAIN_FLOAT_TYPE)
    d_returned = send_in_grads(to_device_major(d_expert_in, device_count)).reshape(
        expert_count * capacity, model_width
    )
    d_slots = d_returned[slot_index].reshape(tokens_per_shard, TOPK, model_width)
    d_mixed = jnp.sum(d_slots.astype(SINGLE_FLOAT), axis=1) + jnp.einsum(
        "te,de->td", d_logits, router_matrix, preferred_element_type=SINGLE_FLOAT
    )
    grad_router = jnp.einsum(
        "td,te->de", combined_rows, d_logits, preferred_element_type=SINGLE_FLOAT
    )
    _, ffn_norm_back = jax.vjp(rms_scale, hidden_state, ffn_gain)
    d_state_norm, grad_ffn_gain = ffn_norm_back(d_mixed)
    d_state = d_layer + d_state_norm
    d_state_low = d_state.astype(BRAIN_FLOAT_TYPE)
    grad_out_weight = jnp.einsum(
        "tc,td->cd", attn_low, d_state_low, preferred_element_type=SINGLE_FLOAT
    )
    attention_gradient = jnp.einsum(
        "td,cd->tc", d_state_low, output_matrix, preferred_element_type=SINGLE_FLOAT
    ).astype(BRAIN_FLOAT_TYPE)
    attention_gradient = attention_gradient.reshape(
        tokens_per_shard, KEY_VALUE_HEADS, query_group_size, HEAD_DIM
    )
    row_delta = jnp.sum(attention_gradient.astype(SINGLE_FLOAT) * attended, axis=-1).transpose(
        1, 2, 0
    )

    def backward_step(d_query_acc, pieces):
        block_keys, block_values, block_positions, block_segments = pieces
        raw_scores, allowed = scores_for(block_keys, block_positions, block_segments)
        softmaxed = probs_for(raw_scores, allowed)
        d_probs = jnp.einsum(
            "tkgd,jkd->kgtj", attention_gradient, block_values, preferred_element_type=SINGLE_FLOAT
        )
        d_scores = (softmaxed * (d_probs - row_delta[..., None])).astype(BRAIN_FLOAT_TYPE)
        d_query_acc = d_query_acc + jnp.einsum(
            "kgtj,jkd->tkgd", d_scores, block_keys, preferred_element_type=SINGLE_FLOAT
        )
        d_key_block = jnp.einsum(
            "kgtj,tkgd->jkd", d_scores, grouped_queries, preferred_element_type=SINGLE_FLOAT
        )
        d_value_block = jnp.einsum(
            "kgtj,tkgd->jkd",
            softmaxed.astype(BRAIN_FLOAT_TYPE),
            attention_gradient,
            preferred_element_type=SINGLE_FLOAT,
        )
        return (d_query_acc, (d_key_block, d_value_block))

    d_query_acc, (key_block_gradients, value_block_gradients) = lax.scan(
        backward_step,
        jnp.zeros((tokens_per_shard, KEY_VALUE_HEADS, query_group_size, HEAD_DIM), SINGLE_FLOAT),
        inputs_per_block,
    )
    every_key_gradient = (key_block_gradients * logit_scale).reshape(
        sequence_tokens, KEY_VALUE_HEADS * HEAD_DIM
    )
    every_value_gradient = value_block_gradients.reshape(
        sequence_tokens, KEY_VALUE_HEADS * HEAD_DIM
    )
    key_gradients, d_values = (
        lax.psum_scatter(
            every_key_gradient.astype(jnp.bfloat16), "ctx", scatter_dimension=0, tiled=True
        ).astype(jnp.float32),
        lax.psum_scatter(
            every_value_gradient.astype(jnp.bfloat16), "ctx", scatter_dimension=0, tiled=True
        ).astype(jnp.float32),
    )
    _, query_back = jax.vjp(
        lambda raw_heads, norm_gain: head_prepare(raw_heads, norm_gain, local_positions),
        unnormed_queries,
        query_gain,
    )
    d_query_raw, grad_query_gain = query_back(
        (d_query_acc * logit_scale).reshape(tokens_per_shard, QUERY_HEADS, HEAD_DIM)
    )
    _, key_backward = jax.vjp(
        lambda raw_heads, norm_gain: head_prepare(raw_heads, norm_gain, local_positions),
        unnormed_keys,
        key_norm_gain,
    )
    raw_key_gradient, key_gain_gradient = key_backward(
        key_gradients.reshape(tokens_per_shard, KEY_VALUE_HEADS, HEAD_DIM)
    )
    d_query_low = d_query_raw.reshape(tokens_per_shard, QUERY_HEADS * HEAD_DIM).astype(
        BRAIN_FLOAT_TYPE
    )
    key_gradient_lowprec = raw_key_gradient.reshape(
        tokens_per_shard, KEY_VALUE_HEADS * HEAD_DIM
    ).astype(BRAIN_FLOAT_TYPE)
    d_value_low = d_values.astype(BRAIN_FLOAT_TYPE)
    grad_query_weight = jnp.einsum(
        "td,tc->dc", normalized_rows, d_query_low, preferred_element_type=SINGLE_FLOAT
    )
    grad_key_weight = jnp.einsum(
        "td,tc->dc", normalized_rows, key_gradient_lowprec, preferred_element_type=SINGLE_FLOAT
    )
    grad_value_weight = jnp.einsum(
        "td,tc->dc", normalized_rows, d_value_low, preferred_element_type=SINGLE_FLOAT
    )
    d_normed = jnp.einsum(
        "tc,dc->td", d_query_low, query_matrix, preferred_element_type=SINGLE_FLOAT
    )
    d_normed = d_normed + jnp.einsum(
        "tc,dc->td", key_gradient_lowprec, key_matrix, preferred_element_type=SINGLE_FLOAT
    )
    d_normed = d_normed + jnp.einsum(
        "tc,dc->td", d_value_low, value_matrix, preferred_element_type=SINGLE_FLOAT
    )
    _, attn_norm_back = jax.vjp(rms_scale, layer_in, attn_gain)
    d_input_norm, grad_attn_gain = attn_norm_back(d_normed)
    grad_input = d_state + d_input_norm
    reduced = (
        lax.psum_scatter(grad_attn_gain, ("ctx", "ws"), scatter_dimension=0, tiled=True),
        lax.psum_scatter(grad_query_weight, ("ctx", "ws"), scatter_dimension=0, tiled=True),
        lax.psum_scatter(grad_key_weight, ("ctx", "ws"), scatter_dimension=0, tiled=True),
        lax.psum_scatter(grad_value_weight, ("ctx", "ws"), scatter_dimension=0, tiled=True),
        lax.psum_scatter(grad_query_gain, ("ctx", "ws"), scatter_dimension=0, tiled=True),
        lax.psum_scatter(key_gain_gradient, ("ctx", "ws"), scatter_dimension=0, tiled=True),
        lax.psum_scatter(grad_out_weight, ("ctx", "ws"), scatter_dimension=0, tiled=True),
        lax.psum_scatter(grad_ffn_gain, ("ctx", "ws"), scatter_dimension=0, tiled=True),
        lax.psum_scatter(grad_router, ("ctx", "ws"), scatter_dimension=0, tiled=True),
    )
    return (
        output[None],
        grad_input[None],
        reduced[0],
        reduced[1],
        reduced[2],
        reduced[3],
        reduced[4],
        reduced[5],
        reduced[6],
        reduced[7],
        reduced[8],
        grad_gate,
        grad_up,
        grad_down,
    )


VMEM_WHOLE = pl.BlockSpec(memory_space=pltpu.VMEM)
VMEM_BYTES = 60 * 2**20
EXTRA = 128


def compiler_params():
    return pltpu.CompilerParams(vmem_limit_bytes=VMEM_BYTES)


def dot_rows(left, right):
    return lax.dot_general(
        left, right, (((1,), (0,)), ((), ())), preferred_element_type=SINGLE_FLOAT
    )


def dot_right_transposed(left, right):
    return lax.dot_general(
        left, right, (((1,), (1,)), ((), ())), preferred_element_type=SINGLE_FLOAT
    )


def dot_left_transposed(left, right):
    return lax.dot_general(
        left, right, (((0,), (0,)), ((), ())), preferred_element_type=SINGLE_FLOAT
    )


def key_range(tile, tile_rows, sequence_tokens, slack):
    half = sequence_tokens // 2
    first_row = tile * tile_rows
    low = 0 if first_row < half + slack else half
    return low, first_row + tile_rows


def stacked_heads(ref, rows, heads):
    return jnp.concatenate(
        [ref[rows, h * HEAD_DIM : (h + 1) * HEAD_DIM] for h in range(heads)], axis=0
    )


def tile_scores(q4, k_ref, segc_ref, segr_ref, low, high, first_row, tile_rows, heads):
    scale = HEAD_DIM ** (-0.5)
    scores = dot_right_transposed(q4, k_ref[low:high, :]) * scale
    span = high - low
    query_place = first_row + lax.broadcasted_iota(jnp.int32, (tile_rows, span), 0)
    key_place = low + lax.broadcasted_iota(jnp.int32, (tile_rows, span), 1)
    allowed = (segc_ref[first_row : first_row + tile_rows, :] == segr_ref[:, low:high]) & (
        key_place <= query_place
    )
    fill = jnp.where(allowed, 0.0, MASK_FILL)
    scores = scores + jnp.concatenate([fill] * heads, axis=0)
    exponent = jnp.exp(scores - jnp.max(scores, axis=-1, keepdims=True))
    return exponent * (1.0 / jnp.sum(exponent, axis=-1, keepdims=True))


def head_backward(turned_gradient, part, gain, cosine, sine):
    scaled_gradient = turned_gradient * cosine - (
        pltpu.roll(turned_gradient, HEAD_DIM // 2, 1) * sine
    )
    inverse = lax.rsqrt(jnp.mean(part * part, axis=-1, keepdims=True) + EPS)
    unit = part * inverse
    gain_gradient = jnp.sum(scaled_gradient * unit, axis=0, keepdims=True)
    unit_gradient = scaled_gradient * gain
    raw_gradient = inverse * (
        unit_gradient - unit * jnp.mean(unit * unit_gradient, axis=-1, keepdims=True)
    )
    return raw_gradient, gain_gradient


MESH = pl.DeviceIdType.MESH
ANYWHERE = pl.BlockSpec(memory_space=pl.ANY)
LINE = 4


def place():
    c, w = lax.axis_index("ctx"), lax.axis_index("ws")
    return c // 2, c % 2, w // 2, w % 2


def device_at(z, y, x, k):
    return (z * 2 + y, x * 2 + k)


def slot_of(z, y, x, k):
    return ((z * 2 + y) * 2 + x) * 2 + k


def line_order(z):
    upper = z // 2
    return [z, z + 1 - 2 * upper, 2 - 2 * (z % 2) + upper, 3 - 3 * upper]


def remote(source, target, send, recv, device):
    return pltpu.make_async_remote_copy(
        src_ref=source,
        dst_ref=target,
        send_sem=send,
        recv_sem=recv,
        device_id=device,
        device_id_type=MESH,
    )


def meet(z, y, x, k, around):
    barrier = pltpu.get_barrier_semaphore()

    def greet(device):
        pl.semaphore_signal(barrier, inc=1, device_id=device, device_id_type=MESH)

    @pl.when(z < LINE - 1)
    def _():
        greet(device_at(z + 1, y, x, k))

    @pl.when(z > 0)
    def _():
        greet(device_at(z - 1, y, x, k))

    for device in around:
        greet(device)
    pl.semaphore_wait(barrier, len(around) + 1 + z * (LINE - 1 - z) // 2)


class Sends:
    def __init__(self, semaphores):
        self.semaphores = semaphores
        self.started = []

    def start(self, source, target, recv, device, condition=None):
        copy = remote(source, target, self.semaphores.at[len(self.started)], recv, device)
        if condition is None:
            copy.start()
        else:
            pl.when(condition)(copy.start)
        self.started.append((condition, copy))

    def finish(self):
        for condition, copy in self.started:
            if condition is None:
                copy.wait_send()
            else:
                pl.when(condition)(copy.wait_send)


def arrived(target, recv, device):
    remote(target, target, recv, recv, device).wait_recv()


def along_line(z, y, x, k, block, i, order, start):
    if i == 0:
        up, down = z < LINE - 1, z > 0
    else:
        below = order[i] < z
        up, down = below & (z < LINE - 1), jnp.logical_not(below) & (z > 0)
    start(block, device_at(z + 1, y, x, k), up)
    start(block, device_at(z - 1, y, x, k), down)


class BlockGather:
    def __init__(self, source, out, local, send_sems, recv_sems):
        self.source, self.out, self.recv_sems = source, out, recv_sems
        z, y, x, k = self.at = place()
        self.order = line_order(z)
        self.along_x, self.along_y = device_at(z, y, 1 - x, k), device_at(z, 1 - y, x, k)
        self.sibling = device_at(z, y, x, 1 - k)
        self.sends = Sends(send_sems)
        self.mine = slot_of(z, y, x, k)
        self.own = pltpu.make_async_copy(source, out.at[self.mine], local)

    def pass_on(self, slot, device, condition=None):
        block = self.source if slot is self.mine else self.out.at[slot]
        self.sends.start(block, self.out.at[slot], self.recv_sems.at[slot], device, condition)

    def wait(self, slot):
        arrived(self.out.at[slot], self.recv_sems.at[slot], self.along_x)

    def line(self, i):
        z, y, x, k = self.at
        slot = slot_of(self.order[i], y, x, k)
        if i > 1:
            pl.when((z > 0) & (z < LINE - 1))(lambda: self.wait(slot))
        along_line(z, y, x, k, slot, i, self.order, self.pass_on)

    def column(self, i):
        z, y, x, k = self.at
        slot = self.mine if i == 0 else slot_of(self.order[i], y, x, k)
        if i == 0:
            along_line(z, y, x, k, slot, i, self.order, self.pass_on)
        elif i == 1:
            self.wait(slot)
            self.line(1)
        else:
            pl.when((z == 0) | (z == LINE - 1))(lambda: self.wait(slot))
        for device in (self.along_x, self.along_y, self.sibling):
            self.pass_on(slot, device)

    def across(self, i, on_x, on_y):
        z, y, x, k = self.at
        return slot_of(self.order[i], 1 - y if on_y else y, 1 - x if on_x else x, k)

    def receive(self, slot):
        self.wait(slot)
        self.pass_on(slot, self.sibling)

    def begin(self):
        meet(*self.at, (self.along_x, self.along_y, self.sibling))
        self.own.start()
        self.column(0)

    def advance(self, i):
        self.column(i)
        if i < 3:
            self.line(i + 1)
        self.receive(self.across(i - 1, True, False))
        self.receive(self.across(i - 1, False, True))

    def turn(self):
        self.receive(self.across(3, True, False))
        for j in (0, 1):
            self.pass_on(self.across(j, True, False), self.along_y)
        self.receive(self.across(3, False, True))
        for j in (2, 3):
            self.pass_on(self.across(j, False, True), self.along_x)

    def last(self, waited=()):
        for i in range(4):
            self.receive(self.across(i, True, True))
        z, y, x, k = self.at
        for i in range(4):
            for dy, dx in ((0, 0), (0, 1), (1, 0), (1, 1)):
                if (dy, dx) not in waited:
                    self.wait(
                        slot_of(self.order[i], 1 - y if dy else y, 1 - x if dx else x, 1 - k)
                    )
        self.sends.finish()

    def finish(self):
        self.turn()
        self.last()
        self.own.wait()


def add_blocks(target, *terms):
    rows = target.shape[0]

    def step(i, carry):
        part = pl.ds(pl.multiple_of(i * 16, 16), 16)
        total = terms[0][part, :].astype(SINGLE_FLOAT)
        for term in terms[1:]:
            total = total + term[part, :].astype(SINGLE_FLOAT)
        target[part, :] = total.astype(target.dtype)
        return carry

    lax.fori_loop(0, rows // 16, step, 0)


def scatter_line(z, y, x, k, order, total, owned, up_ref, down_ref, up_sems, down_sems, sends, out, after):
    above, below = device_at(z + 1, y, x, k), device_at(z - 1, y, x, k)
    for i in (3, 2, 1):
        total(i)
        chip = order[i]
        upward = chip > z
        block = owned(i)

        @pl.when(upward & (z > 0))
        def _():
            arrived(up_ref.at[chip], up_sems.at[chip], below)
            add_blocks(block, block, up_ref.at[chip])

        @pl.when(jnp.logical_not(upward) & (z < LINE - 1))
        def _():
            arrived(down_ref.at[chip], down_sems.at[chip], above)
            add_blocks(block, block, down_ref.at[chip])

        sends.start(block, up_ref.at[chip], up_sems.at[chip], above, upward)
        sends.start(
            block, down_ref.at[chip], down_sems.at[chip], below, jnp.logical_not(upward)
        )
        after(i)
    total(0)
    block = owned(0)

    @pl.when(z > 0)
    def _():
        arrived(up_ref.at[z], up_sems.at[z], below)

    @pl.when(z < LINE - 1)
    def _():
        arrived(down_ref.at[z], down_sems.at[z], above)

    @pl.when(z == 0)
    def _():
        add_blocks(out, block, down_ref.at[z])

    @pl.when(z == LINE - 1)
    def _():
        add_blocks(out, block, up_ref.at[z])

    @pl.when((z > 0) & (z < LINE - 1))
    def _():
        add_blocks(out, block, up_ref.at[z], down_ref.at[z])


class PickedSums:
    def __init__(self, rows_in, pick_in, out, scratch):
        (
            self.rows_ref,
            self.pick_ref,
            self.own_ref,
            self.corner_ref,
            self.x_ref,
            self.y_ref,
            self.up_ref,
            self.down_ref,
            load_sems,
            self.corner_sems,
            self.x_sems,
            self.y_sems,
            self.up_sems,
            self.down_sems,
            send_sems,
        ) = scratch
        self.out = out
        z, y, x, k = self.at = place()
        self.order = line_order(z)
        self.along_x, self.along_y = device_at(z, y, 1 - x, k), device_at(z, 1 - y, x, k)
        self.pick_load = pltpu.make_async_copy(pick_in, self.pick_ref, load_sems.at[16])
        self.turn = [i * 4 + r for r in (3, 1, 2, 0) for i in (3, 2, 1, 0)]
        self.loads = {
            j: pltpu.make_async_copy(rows_in.at[j], self.rows_ref.at[j], load_sems.at[j])
            for j in self.turn
        }
        self.sends = Sends(send_sems)

    def begin(self):
        self.pick_load.start()
        for j in self.turn:
            self.loads[j].start()
        meet(*self.at, (self.along_x, self.along_y))
        self.pick_load.wait()

    def gather(self, i, r, *extra):
        j = i * 4 + r
        self.loads[j].wait()
        block = self.own_ref.at[j]
        spread_rows(block, self.pick_ref.at[j], self.rows_ref.at[j], *extra)
        return block

    def corners(self):
        for i in (3, 2, 1, 0):
            self.sends.start(
                self.gather(i, 3),
                self.corner_ref.at[i],
                self.corner_sems.at[i],
                self.along_y if i < 2 else self.along_x,
            )

    def cross(self, i):
        arrived(self.corner_ref.at[i], self.corner_sems.at[i], self.along_x)
        extra = (self.corner_ref.at[i],)
        for_x = self.gather(i, 1, *(extra if i < 2 else ()))
        self.sends.start(for_x, self.x_ref.at[i], self.x_sems.at[i], self.along_x)
        for_y = self.gather(i, 2, *(extra if i >= 2 else ()))
        self.sends.start(for_y, self.y_ref.at[i], self.y_sems.at[i], self.along_y)

    def total(self, i):
        arrived(self.x_ref.at[i], self.x_sems.at[i], self.along_x)
        arrived(self.y_ref.at[i], self.y_sems.at[i], self.along_y)
        if i > 0:
            self.cross(i - 1)
        self.gather(i, 0, self.x_ref.at[i], self.y_ref.at[i])

    def finish(self, between=lambda i: None):
        scatter_line(
            *self.at, self.order, self.total, lambda i: self.own_ref.at[i * 4],
            self.up_ref, self.down_ref, self.up_sems, self.down_sems, self.sends, self.out,
            between,
        )
        self.sends.finish()


def picked_scratch(rows, pick):
    shape, low = (pick.shape[2], rows.shape[2]), rows.dtype
    return (
        [pltpu.VMEM(rows.shape, low), pltpu.VMEM(pick.shape, low)]
        + [pltpu.VMEM((n,) + shape, low) for n in (16, 4, 4, 4, 4, 4)]
        + [pltpu.SemaphoreType.DMA((n,)) for n in (17, 4, 4, 4, 4, 4, 24)]
    )


def halves(ref, z, y):
    half = ref.shape[0] // 16
    c = z * 2 + y
    return [
        ref.at[pl.ds(pl.multiple_of(half * b, half), half), :] for b in (c, 15 - c)
    ]


def split_rows(ref):
    half = ref.shape[0] // 2
    return [ref.at[0:half, :], ref.at[half : 2 * half, :]]


class RowGather:
    def __init__(self, source, out, sends, locals_, semaphores, at, order, along_y):
        self.source, self.out, self.sends, self.semaphores = source, out, sends, semaphores
        self.at, self.order, self.along_y = at, order, along_y
        z, y, x, k = at
        self.own = [
            pltpu.make_async_copy(a, b, locals_.at[n])
            for n, (a, b) in enumerate(zip(split_rows(source), halves(out, z, y)))
        ]
        for copy in self.own:
            copy.start()

    def send(self, i, along, across):
        z, y, x, k = self.at
        chip = self.order[i]
        pieces = halves(self.out, chip, y)
        for n in (0, 1):
            block = split_rows(self.source)[n] if i == 0 else pieces[n]
            recv = self.semaphores.at[n, chip * 2 + y]

            def start(_, device, condition=None):
                self.sends.start(block, pieces[n], recv, device, condition)

            if along:
                along_line(z, y, x, k, None, i, self.order, start)
            if across:
                start(None, self.along_y)

    def line(self, i):
        z, y = self.at[:2]
        pl.when((z > 0) & (z < LINE - 1))(lambda: self.wait(self.order[i], y))
        self.send(i, True, False)

    def column(self, i):
        z, y = self.at[:2]
        if i == 1:
            self.wait(self.order[i], y)
        elif i > 1:
            pl.when((z == 0) | (z == LINE - 1))(lambda: self.wait(self.order[i], y))
        self.send(i, i < 2, True)

    def wait(self, chip, y):
        for n, piece in enumerate(halves(self.out, chip, y)):
            arrived(piece, self.semaphores.at[n, chip * 2 + y], self.along_y)

    def finish(self):
        y = self.at[1]
        for i in range(4):
            self.wait(self.order[i], 1 - y)
        for copy in self.own:
            copy.wait()


def gather_rows_kernel(
    source,
    x_late,
    x_early,
    d_in,
    hidden_late,
    hidden_early,
    d_gate_in,
    d_up_in,
    out,
    gate_out,
    up_out,
    down_out,
    x_ref,
    d_ref,
    hidden_ref,
    d_gate_ref,
    d_up_ref,
    gate_ref,
    up_ref,
    down_ref,
    load_sems,
    store_sems,
    local_sems,
    send_sems,
    recv_sems,
):
    at = place()
    z, y, x, k = at
    along_y = device_at(z, 1 - y, x, k)
    late, early = x_late.shape[0], x_early.shape[0]
    loads = [
        pltpu.make_async_copy(a, b, load_sems.at[n])
        for n, (a, b) in enumerate(
            (
                (x_late, x_ref.at[pl.ds(0, late), :]),
                (x_early, x_ref.at[pl.ds(late, early), :]),
                (d_gate_in, d_gate_ref),
                (d_up_in, d_up_ref),
                (hidden_late, hidden_ref.at[pl.ds(0, late), :]),
                (hidden_early, hidden_ref.at[pl.ds(late, early), :]),
                (d_in, d_ref),
            )
        )
    ]
    stores = [
        pltpu.make_async_copy(a, b, store_sems.at[n])
        for n, (a, b) in enumerate(
            ((gate_ref, gate_out), (up_ref, up_out), (down_ref, down_out))
        )
    ]
    meet(z, y, x, k, (along_y,))
    sends = Sends(send_sems)
    rows = RowGather(source, out, sends, local_sems, recv_sems, at, line_order(z), along_y)
    rows.column(0)
    for copy in loads:
        copy.start()

    def inward(i, carry):
        part = pl.ds(pl.multiple_of(i * 256, 256), 256)
        left = x_ref[:, part]
        gate_ref[part, :] = dot_left_transposed(left, d_gate_ref[...]).astype(gate_ref.dtype)
        up_ref[part, :] = dot_left_transposed(left, d_up_ref[...]).astype(up_ref.dtype)
        return carry

    def outward(i, carry):
        part = pl.ds(pl.multiple_of(i * 256, 256), 256)
        down_ref[part, :] = dot_left_transposed(hidden_ref[:, part], d_ref[...]).astype(
            down_ref.dtype
        )
        return carry

    steps = x_ref.shape[1] // 256
    for copy in loads[:4]:
        copy.wait()
    lax.fori_loop(0, 3, inward, 0)
    rows.column(1)
    rows.line(2)
    lax.fori_loop(3, steps, inward, 0)
    for copy in stores[:2]:
        copy.start()
    rows.column(2)
    rows.line(3)
    for copy in loads[4:]:
        copy.wait()
    lax.fori_loop(0, hidden_ref.shape[1] // 256, outward, 0)
    stores[2].start()
    rows.column(3)
    rows.finish()
    for copy in stores:
        copy.wait()
    sends.finish()


def gather_rows(block, x_rows, d_rows, hidden, d_gate, d_up, collective_id):
    rows, width = block.shape
    ff, low = d_up.shape[1], block.dtype
    slots = d_up.shape[0]
    shape, vmem, dma = jax.ShapeDtypeStruct, pltpu.VMEM, pltpu.SemaphoreType.DMA
    inputs = (*x_rows, d_rows, *hidden, d_gate, d_up)
    held = ((slots, width), (slots, width), (slots, ff), (slots, ff), (slots, ff))
    grads = ((width, ff), (width, ff), (ff, width))
    return pl.pallas_call(
        gather_rows_kernel,
        out_shape=[shape((8 * rows, width), low)] + [shape(size, low) for size in grads],
        in_specs=[ANYWHERE] * 8,
        out_specs=[ANYWHERE] * 4,
        scratch_shapes=[vmem(size, low) for size in held]
        + [vmem(size, low) for size in grads]
        + [dma((7,)), dma((3,)), dma((2,)), dma((24,)), dma((2, 8))],
        compiler_params=pltpu.CompilerParams(
            collective_id=collective_id, has_side_effects=True, vmem_limit_bytes=VMEM_BYTES
        ),
        name="gather_rows",
    )(block, *inputs)


class RowScatter:
    def __init__(self, part, out, buffers, semaphores, sends, at, order, along_y):
        self.part, self.out, self.sends, self.at, self.order = part, out, sends, at, order
        self.along_y = along_y
        self.own_ref, self.y_ref, self.up_ref, self.down_ref = buffers
        self.load_sems, self.y_sems, self.up_sems, self.down_sems = semaphores
        z, y, x, k = at
        self.loads = {}
        for i in (3, 2, 1, 0):
            self.loads[i] = [
                pltpu.make_async_copy(a, b, self.load_sems.at[n, i])
                for n, (a, b) in enumerate(
                    zip(halves(part, order[i], y), split_rows(self.own_ref.at[i]))
                )
            ]
            for copy in self.loads[i]:
                copy.start()
        self.cross(3)

    def cross(self, i):
        y = self.at[1]
        for n, (a, b) in enumerate(
            zip(halves(self.part, self.order[i], 1 - y), split_rows(self.y_ref.at[i]))
        ):
            self.sends.start(a, b, self.y_sems.at[n, i], self.along_y)

    def total(self, i):
        for copy in self.loads[i]:
            copy.wait()
        for n, piece in enumerate(split_rows(self.y_ref.at[i])):
            arrived(piece, self.y_sems.at[n, i], self.along_y)
        if i > 0:
            self.cross(i - 1)
        add_blocks(self.own_ref.at[i], self.own_ref.at[i], self.y_ref.at[i])

    def run(self, after=lambda i: None):
        z, y, x, k = self.at
        scatter_line(
            z, y, x, k, self.order, self.total, lambda i: self.own_ref.at[i],
            self.up_ref, self.down_ref, self.up_sems, self.down_sems, self.sends, self.out,
            after,
        )


def row_scatter_scratch(rows, width, low):
    dma = pltpu.SemaphoreType.DMA
    return [pltpu.VMEM((4, rows, width), low)] * 4 + [
        dma((2, 4)),
        dma((2, 4)),
        dma((4,)),
        dma((4,)),
    ]


def scatter_rows_kernel(part, out, *scratch):
    at = place()
    z, y, x, k = at
    along_y = device_at(z, 1 - y, x, k)
    meet(z, y, x, k, (along_y,))
    sends = Sends(scratch[8])
    rows = RowScatter(part, out, scratch[:4], scratch[4:8], sends, at, line_order(z), along_y)
    rows.run()
    sends.finish()


def scatter_rows(part, collective_id):
    rows, width = part.shape[0] // 8, part.shape[1]
    return pl.pallas_call(
        scatter_rows_kernel,
        out_shape=jax.ShapeDtypeStruct((rows, width), SINGLE_FLOAT),
        in_specs=[ANYWHERE],
        out_specs=VMEM_WHOLE,
        scratch_shapes=row_scatter_scratch(rows, width, part.dtype)
        + [pltpu.SemaphoreType.DMA((16,))],
        compiler_params=pltpu.CompilerParams(
            collective_id=collective_id, has_side_effects=True, vmem_limit_bytes=VMEM_BYTES
        ),
        name="scatter_rows",
    )(part)


def ring_of(c, w):
    return [((c + t) % 8, w) for t in range(1, 8)]


def gather_start_kernel(
    x_in,
    slab_in,
    wo_in,
    x_out,
    slab_out,
    wo_out,
    local_sems,
    send_sems,
    x_sems,
    slab_sems,
    wo_sems,
):
    at = place()
    z, y, x, k = at
    c, w = z * 2 + y, x * 2 + k
    along_x, along_y = device_at(z, y, 1 - x, k), device_at(z, 1 - y, x, k)
    sibling = device_at(z, y, x, 1 - k)
    others = ring_of(c, w)
    barrier = pltpu.get_barrier_semaphore()
    for device in others + [along_x, sibling]:
        pl.semaphore_signal(barrier, inc=1, device_id=device, device_id_type=MESH)
    pl.semaphore_wait(barrier, 9)
    sends = Sends(send_sems)
    rows = RowGather(
        x_in, x_out, sends, local_sems.at[pl.ds(0, 2)], x_sems, at, line_order(z), along_y
    )
    wo_rows = wo_in.shape[0]

    def wo_at(w):
        return wo_out.at[pl.ds(pl.multiple_of(w * wo_rows, wo_rows), wo_rows), :]

    mine = c * 4 + w
    local = [
        pltpu.make_async_copy(slab_in.at[c], slab_out.at[mine], local_sems.at[2]),
        pltpu.make_async_copy(wo_in, wo_at(w), local_sems.at[3]),
    ]
    for copy in local:
        copy.start()

    def pass_on(slot, device, block=None):
        block = slab_out.at[slot] if block is None else block
        sends.start(block, slab_out.at[slot], slab_sems.at[slot], device)

    def take(source, w):
        slot = source * 4 + w
        arrived(slab_out.at[slot], slab_sems.at[slot], along_x)
        return slot

    rows.column(0)
    for device in (along_x, sibling):
        sends.start(wo_in, wo_at(w), wo_sems.at[w], device)
        pass_on(mine, device, slab_in.at[c])
    for device in others:
        sends.start(slab_in.at[device[0]], slab_out.at[mine], slab_sems.at[mine], device)

    def onward():
        for t in range(1, 8):
            slot = take((c + 8 - t) % 8, w)
            pass_on(slot, along_x)
            pass_on(slot, sibling)

    def across():
        beside = (1 - x) * 2 + k
        arrived(wo_at(beside), wo_sems.at[beside], along_x)
        sends.start(wo_at(beside), wo_at(beside), wo_sems.at[beside], sibling)
        for t in range(8):
            pass_on(take((c + 8 - t) % 8, beside), sibling)

    rows.column(1)
    rows.line(2)
    rows.column(2)
    rows.line(3)
    onward()
    rows.column(3)
    across()
    for other in (x * 2 + 1 - k, (1 - x) * 2 + 1 - k):
        for t in range(8):
            take((c + 8 - t) % 8, other)
        arrived(wo_at(other), wo_sems.at[other], along_x)
    rows.finish()
    for copy in local:
        copy.wait()
    sends.finish()


def gather_start(x, slabs, wo, collective_id):
    tokens, width = x.shape
    low = BRAIN_FLOAT_TYPE
    dma = pltpu.SemaphoreType.DMA
    return pl.pallas_call(
        gather_start_kernel,
        out_shape=(
            jax.ShapeDtypeStruct((8 * tokens, width), low),
            jax.ShapeDtypeStruct((32,) + slabs.shape[1:], low),
            jax.ShapeDtypeStruct((4 * wo.shape[0], width), low),
        ),
        in_specs=[ANYWHERE] * 3,
        out_specs=[ANYWHERE] * 3,
        scratch_shapes=[dma((4,)), dma((64,)), dma((2, 8)), dma((32,)), dma((4,))],
        compiler_params=pltpu.CompilerParams(collective_id=collective_id, has_side_effects=True),
        name="gather_start",
    )(x, slabs, wo)


def scatter_end_kernel(
    part,
    gw,
    gwo,
    small,
    rows_out,
    gw_out,
    gwo_out,
    small_out,
    *scratch,
):
    row_scratch, row_sems = scratch[:4], scratch[4:8]
    (
        send_sems,
        load_sems,
        core_sems,
        x_sems,
        to_sems,
        small_to_sems,
        gw_own,
        gw_core,
        gw_x,
        gwo_own,
        gwo_core,
        gwo_x,
        small_own,
        small_core,
        small_x,
        small_to,
    ) = scratch[8:]
    at = place()
    z, y, x, k = at
    c, w = z * 2 + y, x * 2 + k
    along_x, along_y = device_at(z, y, 1 - x, k), device_at(z, 1 - y, x, k)
    sibling = device_at(z, y, x, 1 - k)
    others = ring_of(c, w)
    barrier = pltpu.get_barrier_semaphore()
    for device in others + [along_x, sibling]:
        pl.semaphore_signal(barrier, inc=1, device_id=device, device_id_type=MESH)
    pl.semaphore_wait(barrier, 9)
    sends = Sends(send_sems)
    rows = RowScatter(
        part, rows_out, row_scratch, row_sems, sends, at, line_order(z), along_y
    )
    loads = []
    for n, (source, core, own) in enumerate(
        (
            (small, small_core, small_own),
            (gw, gw_core, gw_own),
            (gwo, gwo_core, gwo_own),
        )
    ):
        outer = (slice(None),) * (len(source.shape) - 3)
        sends.start(source.at[(*outer, 1 - k)], core, core_sems.at[n], sibling)
        loads.append(pltpu.make_async_copy(source.at[(*outer, k)], own, load_sems.at[n]))
        loads[-1].start()

    def fold(n, own, core):
        loads[n].wait()
        arrived(core, core_sems.at[n], sibling)
        flat = [(i,) for i in range(own.shape[0])]
        for extent in own.shape[1:-2]:
            flat = [index + (j,) for index in flat for j in range(extent)]
        for i in flat:
            add_blocks(own.at[i], own.at[i], core.at[i])

    fold(0, small_own, small_core)
    sends.start(small_own.at[:, 1 - x], small_x, x_sems.at[0], along_x)
    fold(1, gw_own, gw_core)
    sends.start(gw_own.at[:, 1 - x], gw_x, x_sems.at[1], along_x)
    fold(2, gwo_own, gwo_core)
    keep = []

    def weights(i):
        if i == 2:
            sends.start(gwo_own.at[1 - x], gwo_x, x_sems.at[2], along_x)
            spread()

    def spread():
        for n, own, far in ((0, small_own, small_x), (1, gw_own, gw_x)):
            arrived(far, x_sems.at[n], along_x)
            for i in range(8):
                add_blocks(own.at[i, x], own.at[i, x], far.at[i])
            target, sems = (small_to, small_to_sems) if n == 0 else (gw_out, to_sems)
            keep.append(
                pltpu.make_async_copy(own.at[c, x], target.at[c], load_sems.at[3 + n])
            )
            keep[-1].start()
            for device in others:
                sends.start(own.at[device[0], x], target.at[c], sems.at[c], device)

    rows.run(weights)
    arrived(gwo_x, x_sems.at[2], along_x)
    add_blocks(gwo_out, gwo_own.at[x], gwo_x)
    for copy in keep:
        copy.wait()
    for t in range(1, 8):
        source = (c + 8 - t) % 8
        arrived(small_to.at[source], small_to_sems.at[source], along_x)
        arrived(gw_out.at[source], to_sems.at[source], along_x)
    total = small_to[0]
    for i in range(1, 8):
        total = total + small_to[i]
    small_out[...] = total
    sends.finish()


def scatter_end(part, gw, gwo, small, collective_id):
    rows, width = part.shape[0] // 8, part.shape[1]
    low = part.dtype
    dma, vmem = pltpu.SemaphoreType.DMA, pltpu.VMEM
    r, n = gw.shape[3:]
    ro, no = gwo.shape[2:]
    rs, ns = small.shape[3:]
    return pl.pallas_call(
        scatter_end_kernel,
        out_shape=(
            jax.ShapeDtypeStruct((rows, width), SINGLE_FLOAT),
            jax.ShapeDtypeStruct((8, r, n), low),
            jax.ShapeDtypeStruct((ro, no), SINGLE_FLOAT),
            jax.ShapeDtypeStruct((rs, ns), SINGLE_FLOAT),
        ),
        in_specs=[ANYWHERE] * 4,
        out_specs=[VMEM_WHOLE, ANYWHERE, VMEM_WHOLE, VMEM_WHOLE],
        scratch_shapes=row_scatter_scratch(rows, width, low)
        + [dma((48,)), dma((5,)), dma((3,)), dma((3,)), dma((8,)), dma((8,))]
        + [vmem((8, 2, r, n), low), vmem((8, 2, r, n), low), vmem((8, r, n), low)]
        + [vmem((2, ro, no), low), vmem((2, ro, no), low), vmem((ro, no), low)]
        + [vmem((8, 2, rs, ns), SINGLE_FLOAT), vmem((8, 2, rs, ns), SINGLE_FLOAT)]
        + [vmem((8, rs, ns), SINGLE_FLOAT), vmem((8, rs, ns), SINGLE_FLOAT)],
        compiler_params=pltpu.CompilerParams(
            collective_id=collective_id, has_side_effects=True, vmem_limit_bytes=VMEM_BYTES
        ),
        name="scatter_end",
    )(part, gw, gwo, small)


def forward_gather_kernel(
    slack,
    block_in,
    x_in,
    slabs_in,
    wo_in,
    gain_ref,
    qg_ref,
    kg_ref,
    cos_ref,
    sin_ref,
    segc_ref,
    segr_ref,
    block_out,
    normed_out,
    raw_out,
    q_out,
    k_out,
    v_out,
    attn_out,
    part_out,
    *scratch,
):
    (
        x_ref,
        w_ref,
        wo_ref,
        normed_ref,
        raw_ref,
        q_ref,
        k_ref,
        v_ref,
        attn_ref,
        part_ref,
        in_sems,
        out_sems,
    ) = scratch[:12]
    tokens, width = x_ref.shape
    heads = q_ref.shape[1] // HEAD_DIM
    owned, columns = w_ref.shape[1:]
    rows_step = 256
    copies = [
        pltpu.make_async_copy(s, t, in_sems.at[n])
        for n, (s, t) in enumerate(
            ((x_in, x_ref), (slabs_in.at[:, pl.ds(0, owned), :], w_ref), (wo_in, wo_ref))
        )
    ]
    stores = [
        pltpu.make_async_copy(s, t, out_sems.at[n])
        for n, (s, t) in enumerate(
            (
                (normed_ref, normed_out),
                (raw_ref, raw_out),
                (q_ref, q_out),
                (k_ref, k_out),
                (v_ref, v_out),
                (attn_ref, attn_out),
                (part_ref, part_out),
            )
        )
    ]
    for copy in copies:
        copy.start()
    blocks = BlockGather(block_in, block_out, *scratch[12:])
    blocks.begin()
    copies[0].wait()
    copies[1].wait()

    def project(i, carry):
        rows = pl.ds(pl.multiple_of(i * rows_step, rows_step), rows_step)
        x = x_ref[rows, :].astype(SINGLE_FLOAT)
        inverse = lax.rsqrt(jnp.mean(x * x, axis=-1, keepdims=True) + EPS)
        normed = (x * inverse * gain_ref[...]).astype(BRAIN_FLOAT_TYPE)
        normed_ref[rows, :] = normed
        raw = dot_rows(normed, w_ref[...].reshape(width, columns))
        raw_ref[rows, :] = raw[:, : (heads + 1) * HEAD_DIM]
        v_ref[rows, :] = raw[:, (heads + 1) * HEAD_DIM :].astype(BRAIN_FLOAT_TYPE)
        cosine, sine = cos_ref[rows, :], sin_ref[rows, :]
        for h in range(heads + 1):
            part = raw[:, h * HEAD_DIM : (h + 1) * HEAD_DIM]
            gain = qg_ref[...] if h < heads else kg_ref[...]
            scaled = (
                part * lax.rsqrt(jnp.mean(part * part, axis=-1, keepdims=True) + EPS) * gain
            )
            turned = scaled * cosine + pltpu.roll(scaled, HEAD_DIM // 2, 1) * sine
            turned = turned.astype(BRAIN_FLOAT_TYPE)
            if h < heads:
                q_ref[rows, h * HEAD_DIM : (h + 1) * HEAD_DIM] = turned
            else:
                k_ref[rows, :] = turned
        return carry

    lax.fori_loop(0, tokens // rows_step, project, 0)
    for copy in stores[:5]:
        copy.start()
    blocks.advance(1)
    tile_rows = 128
    for tile in range(tokens // tile_rows):
        first_row = tile * tile_rows
        rows = slice(first_row, first_row + tile_rows)
        low, high = key_range(tile, tile_rows, tokens, slack)
        probs = tile_scores(
            stacked_heads(q_ref, rows, heads),
            k_ref,
            segc_ref,
            segr_ref,
            low,
            high,
            first_row,
            tile_rows,
            heads,
        )
        attended = dot_rows(probs.astype(BRAIN_FLOAT_TYPE), v_ref[low:high, :])
        for h in range(heads):
            attn_ref[rows, h * HEAD_DIM : (h + 1) * HEAD_DIM] = attended[
                h * tile_rows : (h + 1) * tile_rows
            ].astype(BRAIN_FLOAT_TYPE)
    stores[5].start()
    blocks.advance(2)
    copies[2].wait()

    def project_out(i, carry):
        rows = pl.ds(pl.multiple_of(i * rows_step, rows_step), rows_step)
        part_ref[rows, :] = dot_rows(attn_ref[rows, :], wo_ref[...]).astype(BRAIN_FLOAT_TYPE)
        return carry

    lax.fori_loop(0, tokens // rows_step, project_out, 0)
    stores[6].start()
    blocks.advance(3)
    blocks.finish()
    for copy in stores:
        copy.wait()


def forward_gather(slack, block, x, slabs, wo, gain, qg, kg, cosine, sine, segc, segr, collective_id):
    tokens, width = x.shape
    columns = slabs.shape[2]
    owned = width // slabs.shape[0]
    channels = columns - 2 * HEAD_DIM
    low = BRAIN_FLOAT_TYPE
    shape, vmem, dma = jax.ShapeDtypeStruct, pltpu.VMEM, pltpu.SemaphoreType.DMA
    sizes = (
        ((tokens, width), low),
        ((tokens, channels + HEAD_DIM), SINGLE_FLOAT),
        ((tokens, channels), low),
        ((tokens, HEAD_DIM), low),
        ((tokens, HEAD_DIM), low),
        ((tokens, channels), low),
        ((tokens, width), low),
    )

    def kernel(*refs):
        forward_gather_kernel(slack, *refs)

    return pl.pallas_call(
        kernel,
        out_shape=[shape((32,) + block.shape, low)] + [shape(*size) for size in sizes],
        in_specs=[ANYWHERE] * 4 + [VMEM_WHOLE] * 7,
        out_specs=[ANYWHERE] * 8,
        scratch_shapes=[
            vmem((tokens, width), low),
            vmem((slabs.shape[0], owned, columns), low),
            vmem(wo.shape, low),
        ]
        + [vmem(*size) for size in sizes]
        + [dma((3,)), dma((7,))]
        + [dma, dma((40,)), dma((32,))],
        compiler_params=pltpu.CompilerParams(
            collective_id=collective_id, has_side_effects=True, vmem_limit_bytes=VMEM_BYTES
        ),
        name="forward_gather",
    )(block, x, slabs, wo, gain, qg, kg, cosine, sine, segc, segr)


GROUPS = 8


def order_at(z, i):
    upper = z // 2
    inner = (z % 2) * (1 - upper) + (1 - z % 2) * upper
    along = i * (1 - inner) + inner * ((i + 1) % 3 + 2 * (i // 3))
    return 3 * upper + (1 - 2 * upper) * along


def group_blocks(g):
    later = ((g + 1) // 4) * (1 - g // 7)
    g = g * (1 - later) + later * (3 + g % 4)
    kind, turn = (g + 2) // 4, (g + 2) % 4
    far, side, near = 1 - (kind + 1) // 2, kind % 2, kind // 2
    return (
        (far * (turn - 2) + side * (3 - turn) + near * (3 - 2 * turn), 3 - 2 * kind + near),
        (far * turn + side * (3 - turn) + near * (2 - 2 * turn), 3 - kind - near),
    )


def spread_rows(target, pick, rows, *terms):
    step = 4 * HEAD_DIM
    width = target.shape[1]
    at = jnp.transpose(pick[...].astype(SINGLE_FLOAT)).astype(BRAIN_FLOAT_TYPE)
    for start in range(0, width, step):
        part = slice(start, min(start + step, width))
        total = dot_rows(at, rows[:, part])
        for term in terms:
            total = total + term[:, part].astype(SINGLE_FLOAT)
        target[:, part] = total.astype(target.dtype)


def blocks_at(at, g):
    z, y, x, k = at
    found = []
    for lane in (k, 1 - k):
        for i, r in group_blocks(g):
            dy, dx = r // 2, r % 2
            slot = slot_of(order_at(z, i), y + dy * (1 - 2 * y), x + dx * (1 - 2 * x), lane)
            found.append((slot, i * 4 + r))
    return found


def rank_mask(experts, e, extra):
    lane = lax.broadcasted_iota(jnp.int32, (8, extra), 1)
    return (lane == 2 * experts + e).astype(BRAIN_FLOAT_TYPE)


def picked(mask, pay, width, capacity):
    rank = dot_right_transposed(mask, pay[:, width:])
    slots = lax.broadcasted_iota(jnp.int32, (capacity, pay.shape[0]), 0).astype(SINGLE_FLOAT)
    return (rank[0:1, :] == slots).astype(BRAIN_FLOAT_TYPE)


def early_step(n):
    late = n // 3
    return (1 - late) * (7 - n) + late * (3 + (n + 1) % 2 - n // 5)


def gather_forward_kernel(
    capacity,
    payload_in,
    dout_all,
    wg_in,
    wu_in,
    wd_in,
    pay_all,
    x_out,
    d_out,
    extra_out,
    gh_out,
    uh_out,
    hid_out,
    eo_out,
    pick_out,
    wg_ref,
    wu_ref,
    wd_ref,
    pay_ref,
    dout_ref,
    x_ref,
    d_ref,
    extra_ref,
    gh_ref,
    uh_ref,
    hid_ref,
    eo_ref,
    pick_ref,
    weight_sems,
    load_sems,
    store_sems,
    local_sem,
    send_sems,
    recv_sems,
):
    blocks = BlockGather(payload_in, pay_all, local_sem, send_sems, recv_sems)
    blocks.begin()
    weights = [
        pltpu.make_async_copy(a, b, weight_sems.at[n])
        for n, (a, b) in enumerate(((wg_in, wg_ref), (wu_in, wu_ref), (wd_in, wd_ref)))
    ]
    for copy in weights:
        copy.start()
    width = wg_in.shape[0]
    tokens, payload = payload_in.shape
    experts = (payload - width) // 4
    rows = 4 * capacity
    mask = rank_mask(experts, blocks.mine, payload - width)

    def stores(n):
        g = early_step(n) - 2
        part = pl.ds(pl.multiple_of(g * rows, rows), rows)
        pairs = (
            (x_ref, x_out), (d_ref, d_out), (extra_ref, extra_out), (gh_ref, gh_out),
            (uh_ref, uh_out), (hid_ref, hid_out), (eo_ref, eo_out),
        )
        return [
            pltpu.make_async_copy(a, b.at[part, :], store_sems.at[m])
            for m, (a, b) in enumerate(pairs)
        ] + [pltpu.make_async_copy(pick_ref, pick_out.at[g], store_sems.at[7])]

    def group(n, carry):
        found = blocks_at(blocks.at, early_step(n))
        for slot, _ in found[2:]:
            blocks.wait(slot)
        loads = [
            (
                pltpu.make_async_copy(pay_all.at[slot], pay_ref.at[m], load_sems.at[m]),
                pltpu.make_async_copy(dout_all.at[slot], dout_ref.at[m], load_sems.at[4 + m]),
            )
            for m, (slot, _) in enumerate(found)
        ]
        for pair in loads:
            for copy in pair:
                copy.start()

        @pl.when(n > 0)
        def _():
            for copy in stores(n - 1):
                copy.wait()

        for m in range(4):
            for copy in loads[m]:
                copy.wait()
            part = slice(m * capacity, (m + 1) * capacity)
            pick = picked(mask, pay_ref.at[m], width, capacity)
            pick_ref[m] = pick
            chosen = dot_rows(pick, pay_ref[m]).astype(BRAIN_FLOAT_TYPE)
            x_ref[part, :] = chosen[:, :width]
            extra_ref[part, :] = chosen[:, width:]
            d_ref[part, :] = dot_rows(pick, dout_ref[m]).astype(BRAIN_FLOAT_TYPE)
        forward_rows(x_ref, wg_ref, wu_ref, wd_ref, gh_ref, uh_ref, hid_ref, eo_ref)
        for copy in stores(n):
            copy.start()
        return carry

    blocks.advance(1)
    blocks.own.wait()
    for copy in weights:
        copy.wait()
    lax.fori_loop(0, 1, group, 0)
    blocks.advance(2)
    lax.fori_loop(1, 2, group, 0)
    blocks.advance(3)
    lax.fori_loop(2, 3, group, 0)
    blocks.turn()
    lax.fori_loop(3, GROUPS - 2, group, 0)
    blocks.last(((0, 0), (0, 1), (1, 0)))
    for copy in stores(5):
        copy.wait()


def forward_rows(x_ref, wg_ref, wu_ref, wd_ref, gh_ref, uh_ref, hid_ref, eo_ref):
    x = x_ref[...]
    gate_hidden = dot_rows(x, wg_ref[...])
    up_hidden = dot_rows(x, wu_ref[...])
    gh_ref[...] = gate_hidden
    uh_ref[...] = up_hidden
    sigmoid = 1.0 / (1.0 + jnp.exp(-gate_hidden))
    hidden = (gate_hidden * sigmoid * up_hidden).astype(BRAIN_FLOAT_TYPE)
    hid_ref[...] = hidden
    eo_ref[...] = dot_rows(hidden, wd_ref[...]).astype(BRAIN_FLOAT_TYPE)


def gather_forward(capacity, payload, dout_all, wg, wu, wd, collective_id):
    tokens, wide = payload.shape
    width, ff = wg.shape
    low = BRAIN_FLOAT_TYPE
    rows = 4 * capacity
    early = (GROUPS - 2) * rows
    shape, vmem, dma = jax.ShapeDtypeStruct, pltpu.VMEM, pltpu.SemaphoreType.DMA
    extra = wide - width
    sizes = (
        (width, low), (width, low), (extra, low), (ff, SINGLE_FLOAT), (ff, SINGLE_FLOAT),
        (ff, low), (width, low),
    )

    def kernel(*refs):
        gather_forward_kernel(capacity, *refs)

    return pl.pallas_call(
        kernel,
        out_shape=[shape((32, tokens, wide), low)]
        + [shape((early, n), dtype) for n, dtype in sizes]
        + [shape((GROUPS - 2, 4, capacity, tokens), low)],
        in_specs=[ANYWHERE] * 5,
        out_specs=[ANYWHERE] * 9,
        scratch_shapes=[vmem((width, ff), low), vmem((width, ff), low), vmem((ff, width), low)]
        + [vmem((4, tokens, wide), low), vmem((4, tokens, width), low)]
        + [vmem((rows, n), dtype) for n, dtype in sizes]
        + [vmem((4, capacity, tokens), low)]
        + [dma((3,)), dma((8,)), dma((8,)), dma, dma((40,)), dma((32,))],
        compiler_params=pltpu.CompilerParams(
            collective_id=collective_id, has_side_effects=True, vmem_limit_bytes=VMEM_BYTES
        ),
        name="gather_forward",
    )(payload, dout_all, wg, wu, wd)


def expert_exchange_kernel(
    capacity,
    pay_all,
    dout_all,
    wg_in,
    wu_in,
    wd_in,
    d_early,
    extra_early,
    gh_early,
    uh_early,
    eo_early,
    pick_early,
    back_ref,
    rows_out,
    pick_out,
    x_out,
    hid_out,
    deo_out,
    dgl_out,
    dul_out,
    wg_ref,
    wu_ref,
    wd_ref,
    pay_ref,
    dout_ref,
    x_ref,
    hid_ref,
    deo_ref,
    dgl_ref,
    dul_ref,
    d_ref,
    extra_ref,
    gh_ref,
    uh_ref,
    eo_ref,
    far_pick_ref,
    far_d_ref,
    far_o_ref,
    near_o_ref,
    pick_ref,
    rows_ref,
    own_ref,
    corner_ref,
    x_sum_ref,
    y_sum_ref,
    up_ref,
    down_ref,
    weight_sems,
    load_sems,
    early_sems,
    row_sems,
    near_sems,
    far_sems,
    sibling_sems,
    corner_sems,
    x_sums,
    y_sums,
    up_sems,
    down_sems,
    sum_send_sems,
    pick_sem,
):
    z, y, x, k = place()
    order = line_order(z)
    along_x, along_y = device_at(z, y, 1 - x, k), device_at(z, 1 - y, x, k)
    sibling = device_at(z, y, x, 1 - k)
    weights = [
        pltpu.make_async_copy(a, b, weight_sems.at[n])
        for n, (a, b) in enumerate(((wg_in, wg_ref), (wu_in, wu_ref), (wd_in, wd_ref)))
    ]
    for copy in weights:
        copy.start()
    meet(z, y, x, k, (along_x, along_y, sibling))
    mine = slot_of(z, y, x, k)
    width = wg_in.shape[0]
    _, tokens, payload = pay_all.shape
    experts = (payload - width) // 4
    rows = 4 * capacity
    above, below = device_at(z + 1, y, x, k), device_at(z - 1, y, x, k)

    def far_copies(n, j, side):
        half = pl.ds(capacity, capacity)
        return [
            remote(a, b, far_sems.at[n, m], sibling_sems.at[m, j], sibling)
            for m, (a, b) in enumerate(
                (
                    (far_pick_ref.at[side, n], pick_ref.at[j, half, :]),
                    (far_d_ref.at[n], rows_ref.at[j, half, :]),
                    (far_o_ref.at[n], rows_out.at[j, half, :]),
                )
            )
        ]

    def gather(i, r, *extra):
        j = i * 4 + r
        for copy in far_copies(0, j, 0)[:2]:
            copy.wait_recv()
        spread_rows(own_ref.at[j], pick_ref.at[j], rows_ref.at[j], *extra)
        return own_ref.at[j]

    def sum_send(n, j, target, recv, device):
        return remote(own_ref.at[j], target, sum_send_sems.at[n], recv, device)

    corner_sends = [
        sum_send(i, i * 4 + 3, corner_ref.at[i], corner_sems.at[i], along_y if i < 2 else along_x)
        for i in range(4)
    ]
    x_sends = [
        sum_send(4 + i, i * 4 + 1, x_sum_ref.at[i], x_sums.at[i], along_x) for i in range(4)
    ]
    y_sends = [
        sum_send(8 + i, i * 4 + 2, y_sum_ref.at[i], y_sums.at[i], along_y) for i in range(4)
    ]
    line_sends = []
    for i in (1, 2, 3):
        chip = order[i]
        upward = chip > z
        line_sends.append(
            (upward, sum_send(12 + i, i * 4, up_ref.at[chip], up_sems.at[chip], above))
        )
        line_sends.append(
            (
                jnp.logical_not(upward),
                sum_send(16 + i, i * 4, down_ref.at[chip], down_sems.at[chip], below),
            )
        )

    def corners(*which):
        for i in which:
            gather(i, 3)
            corner_sends[i].start()

    def cross(i):
        arrived(corner_ref.at[i], corner_sems.at[i], along_x)
        extra = (corner_ref.at[i],)
        gather(i, 1, *(extra if i < 2 else ()))
        x_sends[i].start()
        gather(i, 2, *(extra if i >= 2 else ()))
        y_sends[i].start()

    def total(i):
        arrived(x_sum_ref.at[i], x_sums.at[i], along_x)
        arrived(y_sum_ref.at[i], y_sums.at[i], along_y)
        gather(i, 0, x_sum_ref.at[i], y_sum_ref.at[i])

    def along(i):
        total(i)
        chip, block = order[i], own_ref.at[i * 4]
        upward = chip > z

        @pl.when(upward & (z > 0))
        def _():
            arrived(up_ref.at[chip], up_sems.at[chip], below)
            add_blocks(block, block, up_ref.at[chip])

        @pl.when(jnp.logical_not(upward) & (z < LINE - 1))
        def _():
            arrived(down_ref.at[chip], down_sems.at[chip], above)
            add_blocks(block, block, down_ref.at[chip])

        for condition, copy in line_sends[2 * i - 2 : 2 * i]:
            pl.when(condition)(copy.start)

    def sixth():
        cross(1)
        along(3)

    def last():
        cross(0)
        along(2)

    at_start = {
        1: lambda: corners(2, 0),
        2: lambda: corners(3, 1),
        4: lambda: cross(3),
        5: lambda: cross(2),
        6: sixth,
        7: last,
    }

    def at(g, table):
        for n, work in table.items():
            pl.when(g == n)(work)

    for copy in weights:
        copy.wait()
    row_lane = lax.broadcasted_iota(jnp.int32, (capacity, payload - width), 1)
    e = mine
    all_lane = lax.broadcasted_iota(jnp.int32, (rows, payload - width), 1)
    is_gate = (all_lane == e) | (all_lane == experts + e)
    mask = rank_mask(experts, e, payload - width)
    at_here = (z, y, x, k)

    def row_copies(g):
        part = pl.ds(pl.multiple_of(g * rows, rows), rows)
        pairs = ((deo_ref, deo_out), (dgl_ref, dgl_out), (dul_ref, dul_out))
        return [
            pltpu.make_async_copy(a, b.at[part, :], row_sems.at[n])
            for n, (a, b) in enumerate(pairs)
        ]

    def late_copies(g):
        part = pl.ds(pl.multiple_of(g * rows, rows), rows)
        return [
            pltpu.make_async_copy(a, b.at[part, :], row_sems.at[3 + n])
            for n, (a, b) in enumerate(((x_ref, x_out), (hid_ref, hid_out)))
        ]

    def near_copies(g):
        return [
            pltpu.make_async_copy(
                near_o_ref.at[n],
                rows_out.at[blocks_at(at_here, g)[n][1], pl.ds(0, capacity), :],
                near_sems.at[n],
            )
            for n in (0, 1)
        ]

    def settle(g):
        for copy in row_copies(g) + near_copies(g):
            copy.wait()
        for n in (0, 1):
            for copy in far_copies(n, blocks_at(at_here, g)[2 + n][1], g % 2):
                copy.wait_send()

    def load_copies(g):
        copies = []
        for n, (slot, _) in enumerate(blocks_at(at_here, g)):
            copies.append(pltpu.make_async_copy(pay_all.at[slot], pay_ref.at[n], load_sems.at[n]))
            copies.append(
                pltpu.make_async_copy(dout_all.at[slot], dout_ref.at[n], load_sems.at[4 + n])
            )
        return copies

    def early_copies(g):
        side, at = g % 2, g - 2
        part = pl.ds(pl.multiple_of(at * rows, rows), rows)
        pairs = (
            (d_early, d_ref), (extra_early, extra_ref), (gh_early, gh_ref), (uh_early, uh_ref),
            (eo_early, eo_ref),
        )
        copies = [
            pltpu.make_async_copy(a.at[part, :], b.at[side], early_sems.at[side, n])
            for n, (a, b) in enumerate(pairs)
        ]
        for n, (_, j) in enumerate(blocks_at(at_here, g)):
            target = pick_ref.at[j, pl.ds(0, capacity), :] if n < 2 else far_pick_ref.at[side, n - 2]
            copies.append(
                pltpu.make_async_copy(pick_early.at[at, n], target, early_sems.at[side, 5 + n])
            )
        return copies

    def step(g, carry):
        blocks = blocks_at(at_here, g)
        side = g % 2
        at(g, at_start)

        @pl.when(g > 0)
        def _():
            settle(g - 1)

        @pl.when((g > 0) & (g < GROUPS - 1))
        def _():
            for copy in early_copies(g + 1):
                copy.start()

        @pl.when(g < 2)
        def _():
            @pl.when(g == 1)
            def _():
                for copy in late_copies(g - 1):
                    copy.wait()

            for copy in load_copies(g):
                copy.wait()
            for n in range(4):
                part = slice(n * capacity, (n + 1) * capacity)
                pick = picked(mask, pay_ref.at[n], width, capacity)
                if n < 2:
                    pick_ref[blocks[n][1], 0:capacity, :] = pick
                else:
                    far_pick_ref[side, n - 2] = pick
                chosen = dot_rows(pick, pay_ref[n]).astype(BRAIN_FLOAT_TYPE)
                x_ref[part, :] = chosen[:, :width]
                extra_ref[side, part, :] = chosen[:, width:]
                d_ref[side, part, :] = dot_rows(pick, dout_ref[n]).astype(BRAIN_FLOAT_TYPE)

            @pl.when(g == 0)
            def _():
                for copy in load_copies(g + 1):
                    copy.start()

            forward_rows(
                x_ref, wg_ref, wu_ref, wd_ref, gh_ref.at[side], uh_ref.at[side], hid_ref,
                eo_ref.at[side],
            )
            for copy in late_copies(g):
                copy.start()

        @pl.when(g >= 2)
        def _():
            for copy in early_copies(g):
                copy.wait()

        gates = jnp.sum(
            jnp.where(is_gate, extra_ref[side].astype(SINGLE_FLOAT), 0.0), axis=-1, keepdims=True
        )
        deo_ref[...] = (gates * d_ref[side].astype(SINGLE_FLOAT)).astype(BRAIN_FLOAT_TYPE)
        gate_hidden, up_hidden = gh_ref[side], uh_ref[side]
        sigmoid = 1.0 / (1.0 + jnp.exp(-gate_hidden))
        silu = gate_hidden * sigmoid
        d_hidden = dot_right_transposed(deo_ref[...], wd_ref[...])
        d_gate = (d_hidden * up_hidden * sigmoid * (1.0 + gate_hidden * (1.0 - sigmoid))).astype(
            BRAIN_FLOAT_TYPE
        )
        d_up = (d_hidden * silu).astype(BRAIN_FLOAT_TYPE)
        dgl_ref[...] = d_gate
        dul_ref[...] = d_up
        for copy in row_copies(g):
            copy.start()
        d_copy = (
            dot_right_transposed(d_gate, wg_ref[...]) + dot_right_transposed(d_up, wu_ref[...])
        ).astype(BRAIN_FLOAT_TYPE)
        for n in (2, 3, 0, 1):
            j = blocks[n][1]
            part = slice(n * capacity, (n + 1) * capacity)
            e_rows = eo_ref[side, part, :].astype(SINGLE_FLOAT)
            d_gate_rows = jnp.sum(
                d_ref[side, part, :].astype(SINGLE_FLOAT) * e_rows, axis=-1, keepdims=True
            )
            high = d_gate_rows.astype(BRAIN_FLOAT_TYPE).astype(SINGLE_FLOAT)
            extra = jnp.where(row_lane == e, high, 0.0) + jnp.where(
                row_lane == experts + e, d_gate_rows - high, 0.0
            )
            if n >= 2:
                d_target, o_target = far_d_ref.at[n - 2], far_o_ref.at[n - 2]
            else:
                d_target, o_target = rows_ref.at[j, pl.ds(0, capacity), :], near_o_ref.at[n]
            d_target[:, :width] = d_copy[part]
            d_target[:, width:] = extra.astype(BRAIN_FLOAT_TYPE)
            o_target[...] = (gates[part] * e_rows).astype(BRAIN_FLOAT_TYPE)
            if n >= 2:
                for copy in far_copies(n - 2, j, side):
                    copy.start()
        for copy in near_copies(g):
            copy.start()
        return carry

    for copy in load_copies(0):
        copy.start()
    lax.fori_loop(0, GROUPS, step, 0)
    along(1)
    total(0)
    block = own_ref.at[0]

    @pl.when(z > 0)
    def _():
        arrived(up_ref.at[z], up_sems.at[z], below)

    @pl.when(z < LINE - 1)
    def _():
        arrived(down_ref.at[z], down_sems.at[z], above)

    @pl.when(z == 0)
    def _():
        add_blocks(back_ref, block, down_ref.at[z])

    @pl.when(z == LINE - 1)
    def _():
        add_blocks(back_ref, block, up_ref.at[z])

    @pl.when((z > 0) & (z < LINE - 1))
    def _():
        add_blocks(back_ref, block, up_ref.at[z], down_ref.at[z])

    settle(GROUPS - 1)
    for copy in late_copies(1):
        copy.wait()
    keep = pltpu.make_async_copy(pick_ref, pick_out, pick_sem)
    keep.start()
    for j in range(16):
        far_copies(0, j, 0)[2].wait_recv()
    keep.wait()
    for copy in corner_sends + x_sends + y_sends:
        copy.wait_send()
    for condition, copy in line_sends:
        pl.when(condition)(copy.wait_send)


def expert_exchange(capacity, pay_all, dout_all, wg, wu, wd, early, collective_id):
    _, tokens, wide = pay_all.shape
    width, ff = wg.shape
    low = BRAIN_FLOAT_TYPE
    rows = 4 * capacity
    total = GROUPS * rows
    dma, vmem = pltpu.SemaphoreType.DMA, pltpu.VMEM

    def kernel(*refs):
        expert_exchange_kernel(capacity, *refs)

    shape = jax.ShapeDtypeStruct
    return pl.pallas_call(
        kernel,
        out_shape=(
            shape((tokens, wide), SINGLE_FLOAT),
            shape((16, 2 * capacity, width), low),
            shape((16, 2 * capacity, tokens), low),
            shape((2 * rows, width), low),
            shape((2 * rows, ff), low),
            shape((total, width), low),
            shape((total, ff), low),
            shape((total, ff), low),
        ),
        in_specs=[ANYWHERE] * 11,
        out_specs=[VMEM_WHOLE] + [ANYWHERE] * 7,
        scratch_shapes=[vmem((width, ff), low), vmem((width, ff), low), vmem((ff, width), low)]
        + [vmem((4, tokens, wide), low), vmem((4, tokens, width), low)]
        + [vmem((rows, n), low) for n in (width, ff, width, ff, ff)]
        + [vmem((2, rows, width), low), vmem((2, rows, wide - width), low)]
        + [vmem((2, rows, ff), SINGLE_FLOAT)] * 2
        + [vmem((2, rows, width), low), vmem((2, 2, capacity, tokens), low)]
        + [vmem((2, capacity, n), low) for n in (wide, width, width)]
        + [vmem((16, 2 * capacity, tokens), low), vmem((16, 2 * capacity, wide), low)]
        + [vmem((n, tokens, wide), low) for n in (16, 4, 4, 4, 4, 4)]
        + [dma((3,)), dma((8,)), dma((2, 9)), dma((5,)), dma((2,)), dma((2, 3))]
        + [dma((3, 16)), dma((4,)), dma((4,)), dma((4,)), dma((4,)), dma((4,)), dma((20,)), dma],
        compiler_params=pltpu.CompilerParams(
            collective_id=collective_id, has_side_effects=True, vmem_limit_bytes=VMEM_BYTES
        ),
        name="expert_exchange",
    )(pay_all, dout_all, wg, wu, wd, *early)


def backward_scatter_kernel(
    slack,
    rows_in,
    pick_in,
    dh_in,
    wo_in,
    attn_in,
    q_in,
    k_in,
    v_in,
    raw_in,
    normed_in,
    x_in,
    w_in,
    qg_ref,
    kg_ref,
    cos_ref,
    sin_ref,
    segc_ref,
    segr_ref,
    out,
    gwo_out,
    gw_out,
    dpart_out,
    ggain_ref,
    gheads_ref,
    *scratch,
):
    (
        dh_ref,
        wo_ref,
        attn_ref,
        q_ref,
        k_ref,
        v_ref,
        raw_ref,
        normed_ref,
        w_ref,
        x_ref,
        gwo_ref,
        gw_ref,
        da_ref,
        draw_ref,
        dk_ref,
        dv_ref,
        in_sems,
        x_load_sems,
        gwo_sems,
        gw_sems,
        dpart_sems,
    ) = scratch[:21]
    exchange = PickedSums(rows_in, pick_in, out, scratch[21:])
    owned, columns = w_ref.shape[1:]
    w_rows = w_in.at[:, pl.ds(0, owned), :]
    inputs = (dh_in, wo_in, attn_in, q_in, k_in, v_in, raw_in, normed_in, w_rows)
    held = (dh_ref, wo_ref, attn_ref, q_ref, k_ref, v_ref, raw_ref, normed_ref, w_ref)
    copies = [pltpu.make_async_copy(s, t, in_sems.at[n]) for n, (s, t) in enumerate(zip(inputs, held))]
    tokens = dh_ref.shape[0]
    heads = q_ref.shape[1] // HEAD_DIM
    scale = HEAD_DIM ** (-0.5)
    rows_step = 256
    row_steps = tokens // rows_step

    def x_load(i):
        rows = pl.ds(pl.multiple_of(i * rows_step, rows_step), rows_step)
        return pltpu.make_async_copy(x_in.at[rows, :], x_ref.at[i % 2], x_load_sems.at[i % 2])

    def dpart_store(i):
        rows = pl.ds(pl.multiple_of(i * rows_step, rows_step), rows_step)
        return pltpu.make_async_copy(dh_ref.at[rows, :], dpart_out.at[rows, :], dpart_sems.at[i])

    def gwo_store(i):
        columns = pl.ds(pl.multiple_of(i * 512, 512), 512)
        return pltpu.make_async_copy(
            gwo_ref.at[i % 2], gwo_out.at[:, columns], gwo_sems.at[i % 2]
        )

    def gw_store(i):
        part = pl.ds(pl.multiple_of(i * 256, 256), 256)
        return pltpu.make_async_copy(gw_ref.at[i % 2], gw_out.at[part, :], gw_sems.at[i % 2])

    def attended_gradient():
        def body(i, carry):
            rows = pl.ds(pl.multiple_of(i * rows_step, rows_step), rows_step)
            da_ref[rows, :] = dot_right_transposed(dh_ref[rows, :], wo_ref[...]).astype(
                BRAIN_FLOAT_TYPE
            )
            return carry

        for copy in copies[:2]:
            copy.wait()
        lax.fori_loop(0, row_steps, body, 0)

    def out_weight():
        copies[2].wait()
        for i in range(dh_ref.shape[1] // 512):
            if i >= 2:
                gwo_store(i - 2).wait()
            gwo_ref[i % 2] = dot_left_transposed(
                attn_ref[...], dh_ref[:, i * 512 : (i + 1) * 512]
            ).astype(gwo_ref.dtype)
            gwo_store(i).start()

    tile_rows = 128
    gains = []

    def tiles(first, last):
        for tile in range(first, last):
            first_row = tile * tile_rows
            rows = slice(first_row, first_row + tile_rows)
            low, high = key_range(tile, tile_rows, tokens, slack)
            q4 = stacked_heads(q_ref, rows, heads)
            da4 = stacked_heads(da_ref, rows, heads)
            probs = tile_scores(
                q4, k_ref, segc_ref, segr_ref, low, high, first_row, tile_rows, heads
            )
            d_probs = dot_right_transposed(da4, v_ref[low:high, :])
            delta = jnp.sum(probs * d_probs, axis=-1, keepdims=True)
            d_scores = (probs * (d_probs - delta)).astype(BRAIN_FLOAT_TYPE)
            dq4 = dot_rows(d_scores, k_ref[low:high, :]) * scale
            dk_ref[low:high, :] += dot_left_transposed(d_scores, q4)
            dv_ref[low:high, :] += dot_left_transposed(probs.astype(BRAIN_FLOAT_TYPE), da4)
            for h in range(heads):
                columns = slice(h * HEAD_DIM, (h + 1) * HEAD_DIM)
                raw_gradient, gain_gradient = head_backward(
                    dq4[h * tile_rows : (h + 1) * tile_rows],
                    raw_ref[rows, columns],
                    qg_ref[...],
                    cos_ref[rows, :],
                    sin_ref[rows, :],
                )
                draw_ref[rows, columns] = raw_gradient.astype(BRAIN_FLOAT_TYPE)
                gains.append(gain_gradient)

    def keys():
        columns = slice(heads * HEAD_DIM, (heads + 1) * HEAD_DIM)
        raw_gradient, key_gain_gradient = head_backward(
            dk_ref[...] * scale, raw_ref[:, columns], kg_ref[...], cos_ref[...], sin_ref[...]
        )
        draw_ref[:, columns] = raw_gradient.astype(BRAIN_FLOAT_TYPE)
        draw_ref[:, (heads + 1) * HEAD_DIM :] = dv_ref[...].astype(BRAIN_FLOAT_TYPE)
        query_gain_gradient = gains[0]
        for gain in gains[1:]:
            query_gain_gradient = query_gain_gradient + gain
        gheads_ref[...] = jnp.concatenate(
            [query_gain_gradient, key_gain_gradient, jnp.zeros((6, HEAD_DIM), SINGLE_FLOAT)],
            axis=0,
        )

    def projection_weight():
        copies[7].wait()
        count = normed_ref.shape[1] // 256
        for i in range(count):
            if i >= 2:
                gw_store(i - 2).wait()
            gw_ref[i % 2] = dot_left_transposed(
                normed_ref[:, i * 256 : (i + 1) * 256], draw_ref[...]
            ).astype(gw_ref.dtype)
            gw_store(i).start()

    def input_gradient():
        copies[8].wait()
        ggain_ref[...] = jnp.zeros_like(ggain_ref)
        for i in range(row_steps):
            x_load(i).wait()
            rows = slice(i * rows_step, (i + 1) * rows_step)
            d_normed = dot_right_transposed(
                draw_ref[rows, :], w_ref[...].reshape(normed_ref.shape[1], columns)
            )
            dh_ref[rows, :] = d_normed.astype(BRAIN_FLOAT_TYPE)
            dpart_store(i).start()
            x = x_ref[i % 2].astype(SINGLE_FLOAT)
            inverse = lax.rsqrt(jnp.mean(x * x, axis=-1, keepdims=True) + EPS)
            ggain_ref[...] += jnp.sum(d_normed * (x * inverse), axis=0, keepdims=True)
            if i + 2 < row_steps:
                x_load(i + 2).start()

    exchange.begin()
    for copy in copies:
        copy.start()
    x_load(0).start()
    x_load(1).start()
    dk_ref[...] = jnp.zeros_like(dk_ref)
    dv_ref[...] = jnp.zeros_like(dv_ref)
    exchange.corners()
    attended_gradient()
    out_weight()
    for copy in copies[3:7]:
        copy.wait()
    tiles(0, 5)
    exchange.cross(3)
    tiles(5, 8)
    keys()

    def between(i):
        if i == 3:
            projection_weight()
        elif i == 2:
            input_gradient()

    exchange.finish(between)
    for i in (2, 3):
        gwo_store(i).wait()
    for i in (6, 7):
        gw_store(i).wait()
    for i in range(row_steps):
        dpart_store(i).wait()


def backward_scatter(
    slack, rows, pick, dh, wo, attn, q, k, v, raw, normed, x, w, qg, kg, cosine, sine, segc, segr,
    collective_id,
):
    tokens, width = x.shape
    channels = q.shape[1]
    columns = channels + 2 * HEAD_DIM
    low = BRAIN_FLOAT_TYPE
    shape, vmem, dma = jax.ShapeDtypeStruct, pltpu.VMEM, pltpu.SemaphoreType.DMA
    shapes = (
        shape((pick.shape[2], width), SINGLE_FLOAT),
        shape((channels, width), low),
        shape((width, columns), low),
        shape((tokens, width), low),
        shape((1, width), SINGLE_FLOAT),
        shape((8, HEAD_DIM), SINGLE_FLOAT),
    )

    def kernel(*refs):
        backward_scatter_kernel(slack, *refs)

    return pl.pallas_call(
        kernel,
        out_shape=shapes,
        in_specs=[ANYWHERE] * 12 + [VMEM_WHOLE] * 6,
        out_specs=[VMEM_WHOLE] + [ANYWHERE] * 3 + [VMEM_WHOLE] * 2,
        scratch_shapes=[
            vmem((tokens, width), low),
            vmem((channels, width), low),
            vmem((tokens, channels), low),
            vmem((tokens, channels), low),
            vmem((tokens, HEAD_DIM), low),
            vmem((tokens, HEAD_DIM), low),
            vmem((tokens, channels + HEAD_DIM), SINGLE_FLOAT),
            vmem((tokens, width), low),
            vmem((w.shape[0], width // w.shape[0], columns), low),
            vmem((2, 256, width), low),
            vmem((2, channels, 512), low),
            vmem((2, 256, columns), low),
            vmem((tokens, channels), low),
            vmem((tokens, columns), low),
            vmem((tokens, HEAD_DIM), SINGLE_FLOAT),
            vmem((tokens, HEAD_DIM), SINGLE_FLOAT),
            dma((9,)),
            dma((2,)),
            dma((2,)),
            dma((2,)),
            dma((4,)),
        ]
        + picked_scratch(rows, pick),
        compiler_params=pltpu.CompilerParams(
            collective_id=collective_id, has_side_effects=True, vmem_limit_bytes=VMEM_BYTES
        ),
        name="backward_scatter",
    )(rows, pick, dh, wo, attn, q, k, v, raw, normed, x, w, qg, kg, cosine, sine, segc, segr)


def natural_order(blocks):
    count, rows, width = blocks.shape
    half = rows // 2
    first = blocks[:, :half].reshape(count * half, width)
    second = blocks[::-1, half:].reshape(count * half, width)
    return jnp.concatenate([first, second], axis=0)


def device_order(rows, count):
    total, width = rows.shape
    half = total // count // 2
    first = rows[: total // 2].reshape(count, half, width)
    second = rows[total // 2 :].reshape(count, half, width)[::-1]
    return jnp.concatenate([first, second], axis=1)


def norm_backward(gradient, values, gain):
    inverse = lax.rsqrt(jnp.mean(values * values, axis=-1, keepdims=True) + EPS)
    unit = values * inverse
    scaled = gradient * gain
    d_values = inverse * (scaled - unit * jnp.mean(unit * scaled, axis=-1, keepdims=True))
    return d_values, jnp.sum(gradient * unit, axis=0)


def tensor_body(
    inputs,
    grad_output,
    routes,
    doc_lengths,
    norm_attn,
    w_query,
    key_projection,
    value_projection,
    query_norm,
    key_norm,
    w_out,
    norm_ffn,
    w_router,
    expert_gate,
    expert_up,
    expert_down,
):
    ctx_count = lax.axis_size("ctx")
    ws_count = lax.axis_size("ws")
    device_count = ctx_count * ws_count
    tokens = inputs.shape[1]
    width = inputs.shape[2]
    sequence_tokens = tokens * ctx_count
    expert_count = w_router.shape[1]
    capacity = tokens * TOPK * 3 // (2 * device_count)
    heads = QUERY_HEADS // ctx_count
    group = QUERY_HEADS // KEY_VALUE_HEADS
    slack = tokens // 2
    ctx_index = lax.axis_index("ctx")
    both = ("ctx", "ws")
    me = ctx_index * ws_count + lax.axis_index("ws")
    small = jnp.concatenate([norm_attn, norm_ffn, query_norm, key_norm, w_router.reshape(-1)])
    columns = (heads + 2) * HEAD_DIM
    small = jnp.pad(small, (0, 16 * columns - small.shape[0])).reshape(16, columns)
    slabs = []
    for c in range(ctx_count):
        kv = c * heads // group
        slab = jnp.concatenate(
            [
                w_query[:, c * heads * HEAD_DIM : (c + 1) * heads * HEAD_DIM],
                key_projection[:, kv * HEAD_DIM : (kv + 1) * HEAD_DIM],
                value_projection[:, kv * HEAD_DIM : (kv + 1) * HEAD_DIM],
            ],
            axis=1,
        )
        slabs.append(jnp.concatenate([slab, small], axis=0))
    owned, few = width // device_count, query_norm.shape[0]
    x_all, slabs, wo_all = gather_start(inputs[0], jnp.stack(slabs), w_out, 1)
    small = slabs[:, owned:].reshape(device_count, 16 * columns)
    attn_gain = small[:, :owned].reshape(width).astype(SINGLE_FLOAT)
    ffn_gain = small[:, owned : 2 * owned].reshape(width).astype(SINGLE_FLOAT)
    at = 2 * owned
    query_gain = small[:, at : at + few].reshape(HEAD_DIM).astype(SINGLE_FLOAT)
    key_gain = small[:, at + few : at + 2 * few].reshape(HEAD_DIM).astype(SINGLE_FLOAT)
    at = at + 2 * few
    router_matrix = small[:, at : at + owned * expert_count].reshape(width, expert_count)

    places = jnp.arange(sequence_tokens, dtype=jnp.int32)
    segments = segment_ids(doc_lengths[0], places)
    half = HEAD_DIM // 2
    frequency = THETA ** (-2.0 * jnp.arange(half, dtype=SINGLE_FLOAT) / HEAD_DIM)
    angle = places.astype(SINGLE_FLOAT)[:, None] * frequency[None, :]
    cosine, sine = jnp.cos(angle), jnp.sin(angle)
    cosine = jnp.concatenate([cosine, cosine], axis=1)
    sine = jnp.concatenate([-sine, sine], axis=1)
    segc, segr = segments[:, None], segments[None, :]
    qg, kg = query_gain[None, :], key_gain[None, :]
    own_places = jnp.arange(tokens, dtype=jnp.int32)
    own_places = jnp.where(
        own_places < tokens // 2,
        ctx_index * (tokens // 2) + own_places,
        (2 * ctx_count - 2 - ctx_index) * (tokens // 2) + own_places,
    )
    own_segments = segment_ids(doc_lengths[0], own_places)
    validity = own_segments < doc_lengths.shape[1]
    d_layer = jnp.where(validity[:, None], grad_output[0], 0.0).astype(BRAIN_FLOAT_TYPE)

    dout_all, normed, raw, q, k, v, attn, part = forward_gather(
        slack, d_layer, x_all, slabs, wo_all, attn_gain[None, :], qg, kg, cosine, sine, segc, segr, 7
    )
    branch = scatter_rows(part, 2)
    layer_in = inputs[0].astype(SINGLE_FLOAT)
    hidden_state = layer_in + branch
    mixed = rms_scale(hidden_state, ffn_gain).astype(BRAIN_FLOAT_TYPE)
    logits = jnp.dot(mixed, router_matrix, preferred_element_type=SINGLE_FLOAT)
    own_routes = routes[0]
    hit = jnp.any(
        own_routes[:, :, None] == jnp.arange(expert_count, dtype=jnp.int32)[None, None, :], axis=1
    )
    masked = jnp.where(hit, logits, MASK_FILL)
    exponent = jnp.exp(masked - jnp.max(masked, axis=-1, keepdims=True))
    gates = exponent / jnp.sum(exponent, axis=-1, keepdims=True)
    hits = hit.astype(BRAIN_FLOAT_TYPE)
    earlier = jnp.tril(jnp.ones((tokens, tokens), BRAIN_FLOAT_TYPE), -1)
    rank = jnp.dot(earlier, hits, preferred_element_type=SINGLE_FLOAT)
    rank = jnp.where(hit, rank, -1.0).astype(BRAIN_FLOAT_TYPE)
    gate_high = gates.astype(BRAIN_FLOAT_TYPE)
    gate_low = (gates - gate_high.astype(SINGLE_FLOAT)).astype(BRAIN_FLOAT_TYPE)
    payload = jnp.concatenate(
        [mixed, gate_high, gate_low, rank, jnp.zeros_like(rank)], axis=1
    )
    experts = (expert_gate[0], expert_up[0], expert_down[0])
    pay_all, x_early, d_early, extra_early, gh_early, uh_early, hid_early, eo_early, pick_early = (
        gather_forward(capacity, payload, dout_all, *experts, 3)
    )
    early = (d_early, extra_early, gh_early, uh_early, eo_early, pick_early)
    d_back, out_rows, out_pick, x_late, hid_late, d_rows, d_gate, d_up = expert_exchange(
        capacity, pay_all, dout_all, *experts, early, 4
    )
    table = d_back[:, width:]
    d_gates = table[:, :expert_count] + table[:, expert_count : 2 * expert_count]
    d_chosen = gates * (d_gates - jnp.sum(gates * d_gates, axis=-1, keepdims=True))
    d_logits = d_chosen.astype(BRAIN_FLOAT_TYPE)
    d_mixed = d_back[:, :width] + dot_right_transposed(
        d_logits, router_matrix
    )
    grad_router = dot_left_transposed(mixed, d_logits)
    d_state_norm, grad_ffn_gain = norm_backward(d_mixed, hidden_state, ffn_gain)
    d_state = d_layer.astype(SINGLE_FLOAT) + d_state_norm
    d_state_low = d_state.astype(BRAIN_FLOAT_TYPE)
    dh_all, grad_gate, grad_up, grad_down = gather_rows(
        d_state_low, (x_late, x_early), d_rows, (hid_late, hid_early), d_gate, d_up, 5
    )
    grad_gate, grad_up, grad_down = (
        grad[None].astype(SINGLE_FLOAT) for grad in (grad_gate, grad_up, grad_down)
    )
    moe_sum, gwo, gw, dpart, ggain, gheads = backward_scatter(
        slack, out_rows, out_pick, dh_all, wo_all, attn, q, k, v, raw, normed, x_all, slabs, qg, kg, cosine, sine, segc, segr, 8
    )
    output = (hidden_state + moe_sum).astype(BRAIN_FLOAT_TYPE)
    blocks = (ctx_count, ws_count // 2, 2)
    small = jnp.concatenate(
        [
            ggain.reshape(device_count, owned),
            grad_ffn_gain.reshape(device_count, owned),
            gheads[0].reshape(device_count, few),
            gheads[1].reshape(device_count, few),
            grad_router.reshape(device_count, owned * expert_count),
        ],
        axis=1,
    )
    small = jnp.pad(small, ((0, 0), (0, 32 * 128 - small.shape[1]))).reshape(*blocks, 32, 128)
    d_normed, gw, grad_wo, small = scatter_end(
        dpart,
        gw.reshape(*blocks, owned, columns),
        gwo.reshape(*blocks[1:], w_out.shape[0], width),
        small,
        6,
    )
    small = small.reshape(-1)
    d_input_norm, _ = norm_backward(d_normed, layer_in, attn_gain)
    grad_input = d_state + d_input_norm
    gw = gw.astype(SINGLE_FLOAT)
    channels = heads * HEAD_DIM
    grad_wq = gw[:, :, :channels].transpose(1, 0, 2).reshape(owned, ctx_count * channels)
    shared = ctx_count // KEY_VALUE_HEADS
    kv = gw[:, :, channels:].reshape(KEY_VALUE_HEADS, shared, owned, 2, HEAD_DIM).sum(1)
    grad_wk = kv[:, :, 0].transpose(1, 0, 2).reshape(owned, KEY_VALUE_HEADS * HEAD_DIM)
    grad_wv = kv[:, :, 1].transpose(1, 0, 2).reshape(owned, KEY_VALUE_HEADS * HEAD_DIM)
    return (
        output[None],
        grad_input[None],
        small[:owned],
        grad_wq,
        grad_wk,
        grad_wv,
        small[2 * owned : at - few],
        small[at - few : at],
        grad_wo,
        small[owned : 2 * owned],
        small[at : at + owned * expert_count].reshape(owned, expert_count),
        grad_gate,
        grad_up,
        grad_down,
    )


def planned_body(mesh):
    if mesh.shape["ctx"] == 8 and mesh.shape["ws"] == 4:
        return tensor_body
    return general_body


def solution(mesh):
    placed = (
        P("ws", "ctx", None),
        P("ws", "ctx", None),
        P("ws", "ctx", None),
        P("ws", None),
        P(("ctx", "ws")),
        P(("ctx", "ws"), None),
        P(("ctx", "ws"), None),
        P(("ctx", "ws"), None),
        P(("ctx", "ws")),
        P(("ctx", "ws")),
        P(("ctx", "ws"), None),
        P(("ctx", "ws")),
        P(("ctx", "ws"), None),
        P(("ctx", "ws"), None, None),
        P(("ctx", "ws"), None, None),
        P(("ctx", "ws"), None, None),
    )
    return jax.shard_map(
        planned_body(mesh),
        mesh=mesh,
        in_specs=placed,
        out_specs=(
            P("ws", "ctx", None),
            P("ws", "ctx", None),
            P(("ctx", "ws")),
            P(("ctx", "ws"), None),
            P(("ctx", "ws"), None),
            P(("ctx", "ws"), None),
            P(("ctx", "ws")),
            P(("ctx", "ws")),
            P(("ctx", "ws"), None),
            P(("ctx", "ws")),
            P(("ctx", "ws"), None),
            P(("ctx", "ws"), None, None),
            P(("ctx", "ws"), None, None),
            P(("ctx", "ws"), None, None),
        ),
        check_vma=False,
    )
```
